32 devices in a mesh: rows: 8 (over z, core), pos: 4 (over y, x).
Axes of the slice: x: 2, y: 2, z: 4, core: 2. Of those that a mesh axis runs over, the one named last changes fastest.
Arguments:
- activations: bfloat16 [8, 2048, 1024], P('rows', 'pos'), may hold values from -6 to 6
- out_grad: bfloat16 [8, 2048, 1024], P('rows', 'pos'), may hold values from -6 to 6
- doc_bounds: int32 [8, 3], P('rows'), may hold values from 0 to 2048, as said below
- doc_ids: int32 [8, 2048], P('rows'), may hold values from 0 to 2, as said below
- pre_gain: bfloat16 [1024], P(('rows', 'pos')), may hold values from 0.5 to 1.5
- pre_bias: bfloat16 [1024], P(('rows', 'pos')), may hold values from -1.25 to 1.25
- in_weight: bfloat16 [1024, 3, 1024], P(('rows', 'pos')), may hold values from -0.1875 to 0.1875
- in_bias: bfloat16 [3, 1024], P(None, ('rows', 'pos')), may hold values from -1.25 to 1.25
- short_weight: bfloat16 [3, 3, 1024], P(None, None, ('rows', 'pos')), may hold values from -3.5 to 3.5
- short_bias: bfloat16 [3, 1024], P(None, ('rows', 'pos')), may hold values from -1.25 to 1.25
- skip_gain: bfloat16 [1024], P(('rows', 'pos')), may hold values from -6 to 6
- out_weight: bfloat16 [1024, 1024], P(('rows', 'pos')), may hold values from -0.1875 to 0.1875
- out_bias: bfloat16 [1024], P(('rows', 'pos')), may hold values from -1.25 to 1.25
- post_gain: bfloat16 [1024], P(('rows', 'pos')), may hold values from 0.5 to 1.5
- post_bias: bfloat16 [1024], P(('rows', 'pos')), may hold values from -1.25 to 1.25
- up_weight: bfloat16 [1024, 4096], P(('rows', 'pos')), may hold values from -0.1875 to 0.1875
- up_bias: bfloat16 [4096], P(('rows', 'pos')), may hold values from -1.25 to 1.25
- down_weight: bfloat16 [4096, 1024], P(('rows', 'pos')), may hold values from -0.09375 to 0.09375
- down_bias: bfloat16 [1024], P(('rows', 'pos')), may hold values from -1.25 to 1.25
- filter_one: bfloat16 [33, 64], replicated, may hold values from -1 to 1
- filter_bias_one: bfloat16 [64], replicated, may hold values from -3 to 3
- filter_two: bfloat16 [64, 64], replicated, may hold values from -0.75 to 0.75
- filter_bias_two: bfloat16 [64], replicated, may hold values from -3 to 3
- filter_freq: bfloat16 [64], replicated, may hold values from 0.5 to 3
- filter_three: bfloat16 [64, 1024], P(None, ('rows', 'pos')), may hold values from -0.078125 to 0.078125
Outputs:
- result: bfloat16 [8, 2048, 1024], P('rows', 'pos')
- input_grad: bfloat16 [8, 2048, 1024], P('rows', 'pos')
- pre_gain_grad: float32 [1024], P(('rows', 'pos'))
- pre_bias_grad: float32 [1024], P(('rows', 'pos'))
- in_weight_grad: float32 [1024, 3, 1024], P(('rows', 'pos'))
- in_bias_grad: float32 [3, 1024], P(None, ('rows', 'pos'))
- short_weight_grad: float32 [3, 3, 1024], P(None, None, ('rows', 'pos'))
- short_bias_grad: float32 [3, 1024], P(None, ('rows', 'pos'))
- skip_gain_grad: float32 [1024], P(('rows', 'pos'))
- out_weight_grad: float32 [1024, 1024], P(('rows', 'pos'))
- out_bias_grad: float32 [1024], P(('rows', 'pos'))
- post_gain_grad: float32 [1024], P(('rows', 'pos'))
- post_bias_grad: float32 [1024], P(('rows', 'pos'))
- up_weight_grad: float32 [1024, 4096], P(('rows', 'pos'))
- up_bias_grad: float32 [4096], P(('rows', 'pos'))
- down_weight_grad: float32 [4096, 1024], P(('rows', 'pos'))
- down_bias_grad: float32 [1024], P(('rows', 'pos'))
- filter_one_grad: float32 [33, 64], replicated
- filter_bias_one_grad: float32 [64], replicated
- filter_two_grad: float32 [64, 64], replicated
- filter_bias_two_grad: float32 [64], replicated
- filter_freq_grad: float32 [64], replicated
- filter_three_grad: float32 [64, 1024], P(None, ('rows', 'pos'))
The draws below stay inside these ranges and needn't reach their ends.
Inputs may be any that keep to these rules, and one draw needn't show every extreme that they name: doc_bounds[r, 0] is 0 and the later entries of row r are the first tokens of its second, third and later documents, rising; a row holds 1 to 3 documents and the slots after its last document hold 2048; some row holds 3 documents and some row a single one. doc_ids[r, t] is the number of entries of doc_bounds[r, 1:] that are at most t.
All inputs are finite; a program needn't handle non-finite values.
Results may differ from the reference program's by a relative error of at most 0.011.
Values may be sent and summed in bfloat16 or wider, within the bound.
A program may use at most 320 MiB of HBM per device.

```python
import math
import jax
import jax.numpy as jnp
from jax import lax

D = 1024
FF = 4096
FORDER = 64
EMB = 33
TAPS = 3
LEN = 2048
DOCS = 3
ROWS = 8


def doc_layout(key):
    count_key = jax.random.fold_in(key, 101)
    cut_key = jax.random.fold_in(key, 202)
    counts = jax.random.randint(count_key, (ROWS,), 1, DOCS + 1)
    counts = counts.at[0].set(DOCS).at[1].set(1)
    row_keys = jax.random.split(cut_key, ROWS)
    shuffled = jax.vmap(lambda row_key: jax.random.permutation(row_key, LEN - 1))(row_keys) + 1
    cuts = jnp.sort(shuffled[:, :DOCS - 1], axis=1)
    slot_index = jnp.arange(DOCS - 1)[None, :]
    cuts = jnp.where(slot_index < counts[:, None] - 1, cuts, LEN).astype(jnp.int32)
    bounds = jnp.concatenate([jnp.zeros((ROWS, 1), jnp.int32), cuts], axis=1)
    places = jnp.arange(LEN).astype(jnp.int32)[None, :, None]
    doc_rows = jnp.sum((places >= bounds[:, None, 1:]).astype(jnp.int32), axis=2)
    return (bounds, doc_rows.astype(jnp.int32))


def draw_doc_bounds(key, part):
    return doc_layout(key)[0]


def draw_doc_ids(key, part):
    return doc_layout(key)[1]


def steps_of(rng, shape, shards, smallest, largest):
    gain, own = 1.0, jax.random.fold_in(rng, 6)
    for axis_at, parts in shards:
        draws = jnp.exp(jax.random.uniform(jax.random.fold_in(own, axis_at), (parts,), jnp.float32, smallest / len(shards), largest / len(shards)))
        gain = gain * jnp.repeat(draws, shape[axis_at] // parts).reshape([-1 if axis == axis_at else 1 for axis in range(len(shape))])
    return gain


def gaussian(stream_key, extent, scale, limit, cuts=(), kind=jnp.bfloat16):
    entries = scale * jax.random.normal(stream_key, extent, jnp.float32)
    if cuts:
        entries = entries * steps_of(stream_key, extent, cuts, -0.22, 0.18)
    return jnp.clip(entries, -limit, limit).astype(kind)


def setup_inputs(seed: int = 0) -> dict:
    key_of = jax.random.split(jax.random.key(seed), 26)
    activations = gaussian(key_of[0], (ROWS, LEN, D), 1.0, 6.0, ((0, 8), (1, 4)))
    out_grad = gaussian(key_of[1], (ROWS, LEN, D), 1.0, 6.0, ((0, 8), (1, 4)))
    doc_bounds = draw_doc_bounds(jax.random.fold_in(key_of[25], 71), 0)
    doc_ids = draw_doc_ids(jax.random.fold_in(key_of[25], 71), 0)
    pre_gain = jnp.clip(1.0 + 0.1 * jax.random.normal(key_of[4], (D,), jnp.float32), 0.5, 1.5).astype(jnp.bfloat16)
    pre_bias = gaussian(key_of[5], (D,), 0.2, 1.25, ((0, 32),))
    in_weight = gaussian(key_of[6], (D, 3, D), D ** -0.5, 0.1875, ((0, 32),))
    in_bias = gaussian(key_of[7], (3, D), 0.2, 1.25, ((1, 32),))
    short_weight = gaussian(key_of[8], (TAPS, 3, D), 0.6, 3.5, ((2, 32),))
    short_bias = gaussian(key_of[9], (3, D), 0.2, 1.25, ((1, 32),))
    skip_gain = gaussian(key_of[10], (D,), 1.0, 6.0, ((0, 32),))
    out_weight = gaussian(key_of[11], (D, D), D ** -0.5, 0.1875, ((0, 32),))
    out_bias = gaussian(key_of[12], (D,), 0.2, 1.25, ((0, 32),))
    post_gain = jnp.clip(1.0 + 0.1 * jax.random.normal(key_of[13], (D,), jnp.float32), 0.5, 1.5).astype(jnp.bfloat16)
    post_bias = gaussian(key_of[14], (D,), 0.2, 1.25, ((0, 32),))
    up_weight = gaussian(key_of[15], (D, FF), D ** -0.5, 0.1875, ((0, 32),))
    up_bias = gaussian(key_of[16], (FF,), 0.2, 1.25, ((0, 32),))
    down_weight = gaussian(key_of[17], (FF, D), FF ** -0.5, 0.09375, ((0, 32),))
    down_bias = gaussian(key_of[18], (D,), 0.2, 1.25, ((0, 32),))
    filter_one = gaussian(key_of[19], (EMB, FORDER), EMB ** -0.5, 1.0)
    filter_bias_one = gaussian(key_of[20], (FORDER,), 0.5, 3.0)
    filter_two = gaussian(key_of[21], (FORDER, FORDER), FORDER ** -0.5, 0.75)
    filter_bias_two = gaussian(key_of[22], (FORDER,), 0.5, 3.0)
    filter_freq = jnp.clip(jnp.exp(jax.random.uniform(key_of[23], (FORDER,), jnp.float32, math.log(0.5), math.log(3.0))), 0.5, 3.0).astype(jnp.bfloat16)
    filter_three = gaussian(key_of[24], (FORDER, D), 0.0125, 0.078125, ((1, 32),))
    return {"activations": activations, "out_grad": out_grad, "doc_bounds": doc_bounds, "doc_ids": doc_ids, "pre_gain": pre_gain, "pre_bias": pre_bias, "in_weight": in_weight, "in_bias": in_bias, "short_weight": short_weight, "short_bias": short_bias, "skip_gain": skip_gain, "out_weight": out_weight, "out_bias": out_bias, "post_gain": post_gain, "post_bias": post_bias, "up_weight": up_weight, "up_bias": up_bias, "down_weight": down_weight, "down_bias": down_bias, "filter_one": filter_one, "filter_bias_one": filter_bias_one, "filter_two": filter_two, "filter_bias_two": filter_bias_two, "filter_freq": filter_freq, "filter_three": filter_three}


HIGHEST = lax.Precision.HIGHEST

@jax.custom_vjp
def low(v):
    return lax.optimization_barrier(v.astype(jnp.bfloat16)).astype(jnp.float32)

@jax.custom_vjp
def low_back(v):
    return v

def low_keep(v):
    return (low(v), None)

def low_pass(kept, grad):
    return (grad,)

def back_keep(v):
    return (v, None)

def back_low(kept, grad):
    return (low(grad),)
low.defvjp(low_keep, low_pass)
low_back.defvjp(back_keep, back_low)

def layer_norm(values, norm_gain, norm_shift):
    centre = values - lax.optimization_barrier(jnp.mean(values, axis=-1, keepdims=True))
    spread = lax.optimization_barrier(jnp.mean(centre * centre, axis=-1, keepdims=True))
    return centre * lax.rsqrt(spread + 1e-05) * norm_gain + norm_shift

def gelu_tanh(values):
    return jax.nn.gelu(values, approximate=True)

def filter_net(places, channels, length, model_width, w_one, b_one, w_two, b_two, frequency, w_three):
    scaled = places / (length - 1)
    band_count = (w_one.shape[0] - 1) // 2
    ladder = 0.0001 + (band_count - 1 - 0.0001) * jnp.arange(band_count).astype(places.dtype) / (band_count - 1)
    angles = 2.0 * math.pi / length * places[:, None] * ladder[None, :]
    embedding = jnp.concatenate([scaled[:, None], jnp.cos(angles), -jnp.sin(angles)], axis=1)
    layer_one = jnp.sin(frequency * (jnp.dot(embedding, w_one, precision=HIGHEST) + b_one))
    layer_two = jnp.sin(frequency * (jnp.dot(layer_one, w_two, precision=HIGHEST) + b_two))
    kernel = jnp.dot(layer_two, w_three, precision=HIGHEST)
    slow_rate = math.log(0.01) / 1.5
    fast_rate = math.log(0.01) / 0.3
    decay_rates = jnp.abs(slow_rate + (fast_rate - slow_rate) * channels / (model_width - 1))
    return kernel * (jnp.exp(-scaled[:, None] * decay_rates[None, :]) + 0.05)

def doc_offsets(bounds, length):
    places = jnp.arange(length).astype(jnp.int32)
    starts = lax.optimization_barrier(jnp.max(jnp.where(bounds[:, None, :] <= places[None, :, None], bounds[:, None, :], 0), axis=2))
    return places[None, :] - starts

def short_conv(mixed, tap_weight, tap_bias, offsets):
    length = mixed.shape[1]
    total = jnp.zeros_like(mixed) + tap_bias
    for tap_index in range(tap_weight.shape[0]):
        moved = jnp.pad(mixed, ((0, 0), (tap_index, 0), (0, 0), (0, 0)))[:, :length]
        usable = (offsets >= tap_index)[:, :, None, None]
        total = total + tap_weight[tap_index] * jnp.where(usable, moved, 0.0)
    return total

def long_conv(signal, filt, doc_rows):
    total_len = 2 * LEN
    filt_spec = jnp.fft.rfft(filt, n=total_len, axis=0)
    total = jnp.zeros_like(signal)
    for doc_slot in range(DOCS):
        inside = (doc_rows == doc_slot)[:, :, None]
        masked = jnp.where(inside, signal, 0.0)
        spec = jnp.fft.rfft(masked, n=total_len, axis=1)
        piece = jnp.fft.irfft(spec * filt_spec[None], n=total_len, axis=1)[:, :LEN]
        total = total + jnp.where(inside, piece, 0.0)
    return total

def block_forward(inputs, bounds, doc_rows, weights, filt):
    pre_gain, pre_bias, in_weight, in_bias, short_weight, short_bias, skip_gain, out_weight, out_bias, post_gain, post_bias, up_weight, up_bias, down_weight, down_bias = weights
    normed = low(layer_norm(inputs, pre_gain, pre_bias))
    projected = low(low_back(jnp.einsum('gtd,dke->gtke', normed, in_weight, precision=HIGHEST) + in_bias))
    conv = short_conv(projected, short_weight, short_bias, doc_offsets(bounds, LEN))
    post_gate = conv[:, :, 0]
    pre_gate = conv[:, :, 1]
    values = conv[:, :, 2]
    gated = values * pre_gate
    mixed = long_conv(gated, filt, doc_rows) + skip_gain * gated
    branch = low(low_back(post_gate * mixed))
    residual = inputs + low_back(jnp.einsum('gtc,cd->gtd', branch, out_weight, precision=HIGHEST)) + out_bias
    normed_two = low(layer_norm(residual, post_gain, post_bias))
    hidden_pre = low_back(jnp.einsum('gtd,df->gtf', normed_two, up_weight, precision=HIGHEST)) + up_bias
    hidden = low(gelu_tanh(hidden_pre))
    return residual + jnp.einsum('gtf,fd->gtd', hidden, down_weight, precision=HIGHEST) + down_bias

def reference(activations, out_grad, doc_bounds, doc_ids, pre_gain, pre_bias, in_weight, in_bias, short_weight, short_bias, skip_gain, out_weight, out_bias, post_gain, post_bias, up_weight, up_bias, down_weight, down_bias, filter_one, filter_bias_one, filter_two, filter_bias_two, filter_freq, filter_three):
    single = jnp.float32
    params = (pre_gain.astype(single), pre_bias.astype(single), in_weight.astype(single), in_bias.astype(single), short_weight.astype(single), short_bias.astype(single), skip_gain.astype(single), out_weight.astype(single), out_bias.astype(single), post_gain.astype(single), post_bias.astype(single), up_weight.astype(single), up_bias.astype(single), down_weight.astype(single), down_bias.astype(single), filter_one.astype(single), filter_bias_one.astype(single), filter_two.astype(single), filter_bias_two.astype(single), filter_freq.astype(single), filter_three.astype(single))
    group_size = 2 if ROWS % 2 == 0 else 1
    group_count = ROWS // group_size
    bounds_groups = doc_bounds.reshape(group_count, group_size, DOCS)
    ids_groups = doc_ids.reshape(group_count, group_size, LEN)

    def forward(inputs, *weights):
        places = jnp.arange(LEN).astype(inputs.dtype)
        channels = jnp.arange(D).astype(inputs.dtype)
        filt = filter_net(places, channels, LEN, D, *weights[15:])

        def run_group(pieces):
            block_in, block_bounds, block_ids = pieces
            return block_forward(block_in, block_bounds, block_ids, weights[:15], filt)
        outputs = lax.map(jax.checkpoint(run_group), (inputs.reshape(group_count, group_size, LEN, D), bounds_groups, ids_groups))
        return outputs.reshape(ROWS, LEN, D)
    result, backward = jax.vjp(forward, activations.astype(single), *params)
    grads = backward(out_grad.astype(single))
    return (result.astype(jnp.bfloat16), grads[0].astype(jnp.bfloat16), grads[1], grads[2], grads[3], grads[4], grads[5], grads[6], grads[7], grads[8], grads[9], grads[10], grads[11], grads[12], grads[13], grads[14], grads[15], grads[16], grads[17], grads[18], grads[19], grads[20], grads[21])
```

```python
import functools
import math

import jax
import jax.numpy as jnp
import ml_dtypes
import numpy as np
from jax import lax
from jax.experimental import pallas as pl
from jax.experimental.pallas import tpu as pltpu
from jax.sharding import Mesh
from jax.sharding import PartitionSpec as P

HIGHEST = lax.Precision.HIGHEST
F32 = jnp.float32
BF16 = jnp.bfloat16
BLOCK = 256
FREQ_CHUNK = 64
VMEM_LIMIT = 60 * 1024 * 1024


def layer_norm(values, norm_gain, norm_shift):
    centre = values - jnp.mean(values, axis=-1, keepdims=True)
    spread = jnp.mean(centre * centre, axis=-1, keepdims=True)
    return centre * lax.rsqrt(spread + 1e-05) * norm_gain + norm_shift


def positions_table(length, features):
    band_count = (features - 1) // 2
    places = np.arange(length, dtype=np.float64)
    ladder = 0.0001 + (band_count - 1 - 0.0001) * np.arange(band_count) / (band_count - 1)
    angles = 2.0 * math.pi / length * places[:, None] * ladder[None, :]
    table = np.concatenate(
        [places[:, None] / (length - 1), np.cos(angles), -np.sin(angles)], axis=1
    )
    return jnp.asarray(table.astype(np.float32))


def decay_of(length, channels, model_width):
    scaled = jnp.arange(length, dtype=F32) / (length - 1)
    slow_rate = math.log(0.01) / 1.5
    fast_rate = math.log(0.01) / 0.3
    rates = jnp.abs(slow_rate + (fast_rate - slow_rate) * channels / (model_width - 1))
    return jnp.exp(-scaled[:, None] * rates[None, :]) + 0.05


def filter_net(embedding, decay, w_one, b_one, w_two, b_two, frequency, w_three):
    layer_one = jnp.sin(frequency * (jnp.dot(embedding, w_one, precision=HIGHEST) + b_one))
    layer_two = jnp.sin(frequency * (jnp.dot(layer_one, w_two, precision=HIGHEST) + b_two))
    return jnp.dot(layer_two, w_three, precision=HIGHEST) * decay


def transform_tables():
    order = np.concatenate([np.arange(0, BLOCK, 2), np.arange(1, BLOCK, 2)])
    angle = math.pi / BLOCK * (order[:, None] + 0.5) * np.arange(BLOCK)[None, :]
    forward = np.concatenate([np.cos(angle), -np.sin(angle)], axis=0)
    tables = []
    for table in (forward, forward.T / BLOCK):
        high = table.astype(ml_dtypes.bfloat16)
        low = (table - high.astype(np.float64)).astype(ml_dtypes.bfloat16)
        tables.append(jnp.asarray(np.concatenate([high, high, low], axis=1)))
    return tables


def unit_table(bounds, length):
    docs = bounds.shape[0]
    units = length // BLOCK + docs - 1
    ends = jnp.concatenate([bounds[1:], jnp.full((1,), length, jnp.int32)])
    first = bounds // BLOCK
    count = jnp.where(ends > bounds, (ends - 1) // BLOCK - first + 1, 0)
    earlier = jnp.arange(docs)[:, None] >= jnp.arange(docs)[None, :]
    stops = jnp.sum(jnp.where(earlier, count[None, :], 0), axis=1)
    starts = stops - count
    unit = jnp.arange(units, dtype=jnp.int32)
    doc = jnp.sum((unit[:, None] >= stops[None, :]).astype(jnp.int32), axis=1)
    doc = jnp.minimum(doc, docs - 1)
    pick = (doc[:, None] == jnp.arange(docs)[None, :]).astype(jnp.int32)

    def of_doc(values):
        return jnp.sum(pick * values[None, :], axis=1)

    block = jnp.clip(of_doc(first - starts) + unit, 0, length // BLOCK - 1)
    return jnp.concatenate(
        [
            block,
            of_doc(bounds),
            of_doc(ends),
            of_doc(starts),
            of_doc(stops),
            starts,
            stops,
            bounds,
            stops[docs - 1 :],
        ]
    ).astype(jnp.int32)


class Units:
    def __init__(self, meta, length, docs):
        self.meta = meta
        self.docs = docs
        self.units = length // BLOCK + docs - 1

    def block(self, unit):
        return self.meta[unit]

    def low(self, unit):
        return self.meta[self.units + unit]

    def high(self, unit):
        return self.meta[2 * self.units + unit]

    def start(self, unit):
        return self.meta[3 * self.units + unit]

    def stop(self, unit):
        return self.meta[4 * self.units + unit]

    def doc_start(self, doc):
        return self.meta[5 * self.units + doc]

    def doc_stop(self, doc):
        return self.meta[5 * self.units + self.docs + doc]

    def bound(self, doc):
        return self.meta[5 * self.units + 2 * self.docs + doc]

    def total(self):
        return self.meta[5 * self.units + 3 * self.docs]

    def inside(self, unit, width):
        place = lax.broadcasted_iota(jnp.int32, (BLOCK, width), 0) + self.block(unit) * BLOCK
        return (place >= self.low(unit)) & (place < self.high(unit))


def rows_of(block):
    return pl.ds(pl.multiple_of(block * BLOCK, BLOCK), BLOCK)


def times(table, value):
    high = value.astype(BF16)
    low = (value - high.astype(F32)).astype(BF16)
    return jnp.dot(
        table[...], jnp.concatenate([high, low, high], axis=0), preferred_element_type=F32
    )


def tap_masks(units, block, width, ahead=0):
    place = lax.broadcasted_iota(jnp.int32, (BLOCK, width), 0) + (block * BLOCK + ahead)
    first = place == units.bound(0)
    second = place == units.bound(0) + 1
    for doc in range(1, units.docs):
        first = first | (place == units.bound(doc))
        second = second | (place == units.bound(doc) + 1)
    return jnp.logical_not(first), jnp.logical_not(first | second)


def delayed(ref, block):
    start = block * BLOCK
    here = ref[rows_of(block), :].astype(F32)
    before = ref[pl.ds(pl.multiple_of(jnp.maximum(start - 16, 0), 16), 16), :].astype(F32)
    joined = jnp.concatenate([before, here], axis=0)
    return (here, pltpu.roll(joined, 1, 0)[16:], pltpu.roll(joined, 2, 0)[16:])


def short_conv(parts, small, branch, masks):
    total = small[9 + branch : 10 + branch, :] + small[branch : branch + 1, :] * parts[0]
    total += jnp.where(masks[0], small[3 + branch : 4 + branch, :] * parts[1], 0.0)
    total += jnp.where(masks[1], small[6 + branch : 7 + branch, :] * parts[2], 0.0)
    return total


def mixer_forward_kernel(
    docs, meta, post, pre, val, filt, small, fwd, inv, branch, mixed, gated, spec, taps, prod
):
    length, width = gated.shape
    blocks = length // BLOCK
    units = Units(meta, length, docs)

    def gate(block, _):
        masks = tap_masks(units, block, width)
        part = short_conv(delayed(val, block), small, 2, masks)
        part *= short_conv(delayed(pre, block), small, 1, masks)
        gated[rows_of(block), :] = part
        mixed[rows_of(block), :] = small[12:13, :] * part
        taps[block] = times(fwd, filt[rows_of(block), :])
        return 0

    lax.fori_loop(0, blocks, gate, 0)

    def transform(unit, _):
        value = gated[rows_of(units.block(unit)), :]
        spec[unit] = times(fwd, jnp.where(units.inside(unit, width), value, 0.0))
        return 0

    lax.fori_loop(0, units.total(), transform, 0)

    def multiply(unit, _):
        for low in range(0, BLOCK, FREQ_CHUNK):
            re, im = pl.ds(low, FREQ_CHUNK), pl.ds(BLOCK + low, FREQ_CHUNK)

            def step(back, total):
                at = unit - back
                s_re, s_im, t_re, t_im = spec[at, re], spec[at, im], taps[back, re], taps[back, im]
                return (
                    total[0] + (s_re * t_re - s_im * t_im),
                    total[1] + (s_re * t_im + s_im * t_re),
                )

            zero = jnp.zeros((FREQ_CHUNK, width), F32)
            total = lax.fori_loop(0, unit - units.start(unit) + 1, step, (zero, zero))
            prod[unit, re] = total[0]
            prod[unit, im] = total[1]
        return 0

    lax.fori_loop(0, units.total(), multiply, 0)

    half = BLOCK // 2

    def bring_back(unit, _):
        last = jnp.maximum(unit - 1, 0)
        old = jnp.where(unit > units.start(unit), prod[last], 0.0)
        new = prod[unit]
        joined = jnp.concatenate(
            [
                new[:half] - old[BLOCK : BLOCK + half],
                new[half:BLOCK] + old[BLOCK + half :],
                new[BLOCK : BLOCK + half] + old[:half],
                new[BLOCK + half :] - old[half:BLOCK],
            ],
            axis=0,
        )
        value = times(inv, joined)
        rows = rows_of(units.block(unit))
        mixed[rows, :] += jnp.where(units.inside(unit, width), value, 0.0)
        return 0

    lax.fori_loop(0, units.total(), bring_back, 0)

    def finish(block, _):
        masks = tap_masks(units, block, width)
        gate_value = short_conv(delayed(post, block), small, 0, masks)
        branch[rows_of(block), :] = (gate_value * mixed[rows_of(block), :]).astype(BF16)
        return 0

    lax.fori_loop(0, blocks, finish, 0)


def mixer_backward_kernel(
    docs,
    meta,
    post,
    pre,
    val,
    filt,
    small,
    fwd,
    inv,
    mixed,
    branch_grad,
    proj_grad,
    filt_grad,
    sums,
    gated,
    gm,
    conv_grad,
    spec,
    taps,
    prod,
):
    length, width = gated.shape
    blocks = length // BLOCK
    units = Units(meta, length, docs)
    half = BLOCK // 2
    sums[...] = jnp.zeros_like(sums)

    def total_rows(value):
        return jnp.sum(value, axis=0, keepdims=True)

    def gate(block, _):
        rows = rows_of(block)
        masks = tap_masks(units, block, width)
        part = short_conv(delayed(val, block), small, 2, masks)
        part *= short_conv(delayed(pre, block), small, 1, masks)
        gated[rows, :] = part
        grad = branch_grad[rows, :].astype(F32)
        mix_grad = grad * short_conv(delayed(post, block), small, 0, masks)
        gm[rows, :] = mix_grad
        conv_grad[0, rows, :] = grad * mixed[rows, :]
        conv_grad[1, rows, :] = small[12:13, :] * mix_grad
        sums[15:16, :] += total_rows(part * mix_grad)
        taps[block] = times(fwd, filt[rows, :])
        return 0

    lax.fori_loop(0, blocks, gate, 0)

    def transform(unit, _):
        rows = rows_of(units.block(unit))
        inside = units.inside(unit, width)
        spec[unit] = times(fwd, jnp.where(inside, gated[rows, :], 0.0))
        prod[unit] = times(fwd, jnp.where(inside, gm[rows, :], 0.0))
        return 0

    lax.fori_loop(0, units.total(), transform, 0)

    def spread(unit, _):
        after = jnp.minimum(unit + 1, units.units - 1)
        new = jnp.where(unit + 1 < units.stop(unit), prod[after], 0.0)
        prod[unit, pl.ds(0, half)] += new[BLOCK : BLOCK + half]
        prod[unit, pl.ds(half, half)] -= new[BLOCK + half :]
        prod[unit, pl.ds(BLOCK, half)] -= new[:half]
        prod[unit, pl.ds(BLOCK + half, half)] += new[half:BLOCK]
        return 0

    lax.fori_loop(0, units.total(), spread, 0)

    def signal_grad(unit, _):
        pieces = []
        for low in range(0, BLOCK, FREQ_CHUNK):
            re, im = pl.ds(low, FREQ_CHUNK), pl.ds(BLOCK + low, FREQ_CHUNK)

            def step(ahead, total):
                at = unit + ahead
                g_re, g_im, t_re, t_im = (
                    prod[at, re],
                    prod[at, im],
                    taps[ahead, re],
                    taps[ahead, im],
                )
                return (
                    total[0] + (g_re * t_re + g_im * t_im),
                    total[1] + (g_im * t_re - g_re * t_im),
                )

            zero = jnp.zeros((FREQ_CHUNK, width), F32)
            pieces.append(lax.fori_loop(0, units.stop(unit) - unit, step, (zero, zero)))
        joined = jnp.concatenate([piece[0] for piece in pieces] + [piece[1] for piece in pieces])
        value = times(inv, joined)
        rows = rows_of(units.block(unit))
        conv_grad[1, rows, :] += jnp.where(units.inside(unit, width), value, 0.0)
        return 0

    lax.fori_loop(0, units.total(), signal_grad, 0)

    def tap_grad(back, _):
        pieces = []
        for low in range(0, BLOCK, FREQ_CHUNK):
            re, im = pl.ds(low, FREQ_CHUNK), pl.ds(BLOCK + low, FREQ_CHUNK)

            def step(unit, total):
                at = unit - back
                g_re, g_im, s_re, s_im = (
                    prod[unit, re],
                    prod[unit, im],
                    spec[at, re],
                    spec[at, im],
                )
                return (
                    total[0] + (g_re * s_re + g_im * s_im),
                    total[1] + (g_im * s_re - g_re * s_im),
                )

            zero = jnp.zeros((FREQ_CHUNK, width), F32)
            total = (zero, zero)
            for doc in range(docs):
                total = lax.fori_loop(
                    units.doc_start(doc) + back, units.doc_stop(doc), step, total
                )
            pieces.append(total)
        joined = jnp.concatenate([piece[0] for piece in pieces] + [piece[1] for piece in pieces])
        filt_grad[rows_of(back), :] = times(inv, joined)
        return 0

    lax.fori_loop(0, blocks, tap_grad, 0)

    def conv_back(block, _):
        rows = rows_of(block)
        masks = tap_masks(units, block, width)
        val_parts, pre_parts, post_parts = (
            delayed(val, block),
            delayed(pre, block),
            delayed(post, block),
        )
        gated_grad = conv_grad[1, rows, :]
        pre_grad = gated_grad * short_conv(val_parts, small, 2, masks)
        val_grad = gated_grad * short_conv(pre_parts, small, 1, masks)
        post_grad = conv_grad[0, rows, :]
        conv_grad[1, rows, :] = pre_grad
        conv_grad[2, rows, :] = val_grad
        for branch, (grad, parts) in enumerate(
            ((post_grad, post_parts), (pre_grad, pre_parts), (val_grad, val_parts))
        ):
            sums[branch : branch + 1, :] += total_rows(grad * parts[0])
            sums[3 + branch : 4 + branch, :] += total_rows(
                jnp.where(masks[0], grad * parts[1], 0.0)
            )
            sums[6 + branch : 7 + branch, :] += total_rows(
                jnp.where(masks[1], grad * parts[2], 0.0)
            )
            sums[9 + branch : 10 + branch, :] += total_rows(grad)
        return 0

    lax.fori_loop(0, blocks, conv_back, 0)

    def spread_taps(block, _):
        start = block * BLOCK
        one, _two = tap_masks(units, block, width, 1)
        _one, two = tap_masks(units, block, width, 2)
        place = lax.broadcasted_iota(jnp.int32, (BLOCK, width), 0) + start
        one = one & (place + 1 < length)
        two = two & (place + 2 < length)
        for branch in range(3):
            here = conv_grad[branch, rows_of(block), :]
            after = conv_grad[
                branch, pl.ds(pl.multiple_of(jnp.minimum(start + BLOCK, length - 8), 8), 8), :
            ]
            joined = jnp.concatenate([here, after], axis=0)
            size = BLOCK + 8
            next_one = pltpu.roll(joined, size - 1, 0)[:BLOCK]
            next_two = pltpu.roll(joined, size - 2, 0)[:BLOCK]
            total = small[branch : branch + 1, :] * here
            total += jnp.where(one, small[3 + branch : 4 + branch, :] * next_one, 0.0)
            total += jnp.where(two, small[6 + branch : 7 + branch, :] * next_two, 0.0)
            rounded = total.astype(BF16)
            proj_grad[rows_of(block), branch * width : (branch + 1) * width] = rounded
            sums[12 + branch : 13 + branch, :] += total_rows(rounded.astype(F32))
        return 0

    lax.fori_loop(0, blocks, spread_taps, 0)


def whole_spec(shape, column=0):
    return pl.BlockSpec(shape, lambda i, meta: (0, column), pipeline_mode=pl.Buffered(1))


def mixer_forward(meta, docs, projected, filt, small, tables):
    length, width = filt.shape
    units = length // BLOCK + docs - 1
    column = [whole_spec((length, width), at) for at in range(3)]
    return pl.pallas_call(
        functools.partial(mixer_forward_kernel, docs),
        out_shape=(
            jax.ShapeDtypeStruct((length, width), BF16),
            jax.ShapeDtypeStruct((length, width), F32),
        ),
        grid_spec=pltpu.PrefetchScalarGridSpec(
            num_scalar_prefetch=1,
            grid=(1,),
            in_specs=column
            + [whole_spec(value.shape) for value in (filt, small, tables[0], tables[1])],
            out_specs=(column[0], column[0]),
            scratch_shapes=[
                pltpu.VMEM((length, width), F32),
                pltpu.VMEM((units, 2 * BLOCK, width), F32),
                pltpu.VMEM((length // BLOCK, 2 * BLOCK, width), F32),
                pltpu.VMEM((units, 2 * BLOCK, width), F32),
            ],
        ),
        compiler_params=pltpu.CompilerParams(vmem_limit_bytes=VMEM_LIMIT),
        cost_estimate=pl.CostEstimate(
            flops=40 * 10**9, bytes_accessed=10 * 10**6, transcendentals=0
        ),
        name="mixer_forward",
    )(meta, projected, projected, projected, filt, small, *tables)


def mixer_backward(meta, docs, projected, filt, small, tables, mixed, branch_grad):
    length, width = filt.shape
    units = length // BLOCK + docs - 1
    column = [whole_spec((length, width), at) for at in range(3)]
    return pl.pallas_call(
        functools.partial(mixer_backward_kernel, docs),
        out_shape=(
            jax.ShapeDtypeStruct((length, 3 * width), BF16),
            jax.ShapeDtypeStruct((length, width), F32),
            jax.ShapeDtypeStruct((16, width), F32),
        ),
        grid_spec=pltpu.PrefetchScalarGridSpec(
            num_scalar_prefetch=1,
            grid=(1,),
            in_specs=column
            + [
                whole_spec(value.shape)
                for value in (filt, small, tables[0], tables[1], mixed, branch_grad)
            ],
            out_specs=(
                whole_spec((length, 3 * width)),
                column[0],
                whole_spec((16, width)),
            ),
            scratch_shapes=[
                pltpu.VMEM((length, width), F32),
                pltpu.VMEM((length, width), F32),
                pltpu.VMEM((3, length, width), F32),
                pltpu.VMEM((units, 2 * BLOCK, width), F32),
                pltpu.VMEM((length // BLOCK, 2 * BLOCK, width), F32),
                pltpu.VMEM((units, 2 * BLOCK, width), F32),
            ],
        ),
        compiler_params=pltpu.CompilerParams(vmem_limit_bytes=VMEM_LIMIT),
        cost_estimate=pl.CostEstimate(
            flops=80 * 10**9, bytes_accessed=16 * 10**6, transcendentals=0
        ),
        name="mixer_backward",
    )(meta, projected, projected, projected, filt, small, *tables, mixed, branch_grad)


def norm_parts(values):
    centre = values - jnp.mean(values, axis=-1, keepdims=True)
    spread = jnp.mean(centre * centre, axis=-1, keepdims=True)
    scale = lax.rsqrt(spread + 1e-05)
    return centre * scale, scale


def project_kernel(inputs, norm, weight, bias, out):
    unit, _ = norm_parts(inputs[...].astype(F32))
    normed = (unit * norm[0:1, :] + norm[1:2, :]).astype(BF16)
    total = jnp.dot(normed, weight[...], preferred_element_type=F32) + bias[...]
    out[...] = total.astype(BF16)


def project(inputs, norm, weight, bias):
    length, depth = inputs.shape
    width = weight.shape[1]
    return pl.pallas_call(
        project_kernel,
        out_shape=jax.ShapeDtypeStruct((length, width), BF16),
        grid=(length // BLOCK,),
        in_specs=[
            pl.BlockSpec((BLOCK, depth), lambda i: (i, 0)),
            pl.BlockSpec(norm.shape, lambda i: (0, 0)),
            pl.BlockSpec(weight.shape, lambda i: (0, 0)),
            pl.BlockSpec(bias.shape, lambda i: (0, 0)),
        ],
        out_specs=pl.BlockSpec((BLOCK, width), lambda i: (i, 0)),
        compiler_params=pltpu.CompilerParams(vmem_limit_bytes=VMEM_LIMIT),
        cost_estimate=pl.CostEstimate(
            flops=2 * length * depth * width, bytes_accessed=10 * 10**6, transcendentals=0
        ),
        name="project",
    )(inputs, norm, weight, bias)


def project_back_kernel(inputs, norm, weight, grad, normed_grad, weight_grad, sums, total):
    @pl.when(pl.program_id(0) == 0)
    def _():
        total[...] = jnp.zeros_like(total)
        sums[...] = jnp.zeros_like(sums)

    unit, _ = norm_parts(inputs[...].astype(F32))
    normed = (unit * norm[0:1, :] + norm[1:2, :]).astype(BF16)
    cotangent = lax.dot_general(
        grad[...], weight[...], (((1,), (1,)), ((), ())), preferred_element_type=F32
    )
    normed_grad[...] = cotangent.astype(BF16)
    sums[0:1, :] += jnp.sum(cotangent * unit, axis=0, keepdims=True)
    sums[1:2, :] += jnp.sum(cotangent, axis=0, keepdims=True)
    total[...] += lax.dot_general(
        normed, grad[...], (((0,), (0,)), ((), ())), preferred_element_type=F32
    )

    @pl.when(pl.program_id(0) == pl.num_programs(0) - 1)
    def _():
        weight_grad[...] = total[...].astype(BF16)


def project_back(inputs, norm, weight, grad):
    length, depth = inputs.shape
    width = weight.shape[1]
    return pl.pallas_call(
        project_back_kernel,
        out_shape=(
            jax.ShapeDtypeStruct((length, depth), BF16),
            jax.ShapeDtypeStruct((depth, width), BF16),
            jax.ShapeDtypeStruct((8, depth), F32),
        ),
        grid=(length // BLOCK,),
        in_specs=[
            pl.BlockSpec((BLOCK, depth), lambda i: (i, 0)),
            pl.BlockSpec(norm.shape, lambda i: (0, 0)),
            pl.BlockSpec(weight.shape, lambda i: (0, 0)),
            pl.BlockSpec((BLOCK, width), lambda i: (i, 0)),
        ],
        out_specs=(
            pl.BlockSpec((BLOCK, depth), lambda i: (i, 0)),
            pl.BlockSpec((depth, width), lambda i: (0, 0)),
            pl.BlockSpec((8, depth), lambda i: (0, 0)),
        ),
        scratch_shapes=[pltpu.VMEM((depth, width), F32)],
        compiler_params=pltpu.CompilerParams(vmem_limit_bytes=VMEM_LIMIT),
        cost_estimate=pl.CostEstimate(
            flops=4 * length * depth * width, bytes_accessed=16 * 10**6, transcendentals=0
        ),
        name="project_back",
    )(inputs, norm, weight, grad)


def gelu_pair(u):
    root = math.sqrt(2.0 / math.pi)
    square = u * u
    curve = jnp.tanh(root * (u + 0.044715 * (u * square)))
    value = 0.5 * u * (1.0 + curve)
    slope = 0.5 * (1.0 + curve) + 0.5 * u * (1.0 - curve * curve) * (
        root * (1.0 + 3.0 * 0.044715 * square)
    )
    return value, slope


def feed_forward_kernel(
    normed_own,
    normed_other,
    grad_own,
    grad_other,
    up,
    up_bias,
    down,
    out_own,
    out_other,
    back_own,
    back_other,
    up_grad,
    down_grad,
    bias_grad,
    normed,
    grad,
    out_total,
    back_total,
):
    rows = normed_own.shape[0]
    at = pl.program_id(0)

    @pl.when(at == 0)
    def _():
        normed[:rows] = normed_own[...]
        normed[rows:] = normed_other[...]
        grad[:rows] = grad_own[...]
        grad[rows:] = grad_other[...]
        out_total[...] = jnp.zeros_like(out_total)
        back_total[...] = jnp.zeros_like(back_total)

    pre = jnp.dot(normed[...], up[...], preferred_element_type=F32) + up_bias[...]
    hidden, slope = gelu_pair(pre)
    hidden = hidden.astype(BF16)
    hidden_grad = lax.dot_general(
        grad[...], down[...], (((1,), (1,)), ((), ())), preferred_element_type=F32
    )
    pre_grad = hidden_grad * slope
    bias_grad[...] = jnp.sum(pre_grad, axis=0, keepdims=True)
    pre_grad = pre_grad.astype(BF16)
    out_total[...] += jnp.dot(hidden, down[...], preferred_element_type=F32)
    back_total[...] += lax.dot_general(
        pre_grad, up[...], (((1,), (1,)), ((), ())), preferred_element_type=F32
    )
    down_grad[...] = lax.dot_general(
        hidden, grad[...], (((0,), (0,)), ((), ())), preferred_element_type=F32
    ).astype(BF16)
    up_grad[...] = lax.dot_general(
        normed[...], pre_grad, (((0,), (0,)), ((), ())), preferred_element_type=F32
    ).astype(BF16)

    @pl.when(at == pl.num_programs(0) - 1)
    def _():
        out_own[...] = out_total[:rows]
        out_other[...] = out_total[rows:].astype(BF16)
        back_own[...] = back_total[:rows]
        back_other[...] = back_total[rows:].astype(BF16)


def feed_forward(normed_own, normed_other, grad_own, grad_other, up, up_bias, down):
    rows, depth = normed_own.shape
    width = up.shape[1]
    tile = 256
    fixed = pl.BlockSpec((rows, depth), lambda i: (0, 0), pipeline_mode=pl.Buffered(1))
    return pl.pallas_call(
        feed_forward_kernel,
        out_shape=(
            jax.ShapeDtypeStruct((rows, depth), F32),
            jax.ShapeDtypeStruct((rows, depth), BF16),
            jax.ShapeDtypeStruct((rows, depth), F32),
            jax.ShapeDtypeStruct((rows, depth), BF16),
            jax.ShapeDtypeStruct((depth, width), BF16),
            jax.ShapeDtypeStruct((width, depth), BF16),
            jax.ShapeDtypeStruct((1, width), F32),
        ),
        grid=(width // tile,),
        in_specs=[
            fixed,
            fixed,
            fixed,
            fixed,
            pl.BlockSpec((depth, tile), lambda i: (0, i)),
            pl.BlockSpec((1, tile), lambda i: (0, i)),
            pl.BlockSpec((tile, depth), lambda i: (i, 0)),
        ],
        out_specs=(
            fixed,
            fixed,
            fixed,
            fixed,
            pl.BlockSpec((depth, tile), lambda i: (0, i)),
            pl.BlockSpec((tile, depth), lambda i: (i, 0)),
            pl.BlockSpec((1, tile), lambda i: (0, i)),
        ),
        scratch_shapes=[
            pltpu.VMEM((2 * rows, depth), BF16),
            pltpu.VMEM((2 * rows, depth), BF16),
            pltpu.VMEM((2 * rows, depth), F32),
            pltpu.VMEM((2 * rows, depth), F32),
        ],
        compiler_params=pltpu.CompilerParams(vmem_limit_bytes=VMEM_LIMIT),
        cost_estimate=pl.CostEstimate(
            flops=12 * 2 * rows * depth * width,
            bytes_accessed=30 * 10**6,
            transcendentals=2 * rows * width,
        ),
        name="feed_forward",
    )(normed_own, normed_other, grad_own, grad_other, up, up_bias, down)


def swap(value, axis, bit):
    count = lax.axis_size(axis)
    return lax.ppermute(value, axis, [(at, at ^ bit) for at in range(count)])


def gather_halving(value, axis, bits):
    count = lax.axis_size(axis)
    me = lax.axis_index(axis)
    held = value[None]
    for bit in bits:
        held = jnp.concatenate([held, swap(held, axis, bit)], axis=0)
    order = [0]
    for bit in bits:
        order = order + [mask ^ bit for mask in order]
    place = {mask: at for at, mask in enumerate(order)}
    held = jnp.stack([held[place[mask]] for mask in range(count)])
    shape = held.shape
    bit = 1
    while bit < count:
        parts = held.reshape((count // (2 * bit), 2, bit) + shape[1:])
        held = jnp.where((me & bit) != 0, parts[:, ::-1], parts).reshape(shape)
        bit *= 2
    return held


def bits_of(count):
    return [1 << at for at in range(count.bit_length() - 1)]


def on_device(
    activations,
    out_grad,
    doc_bounds,
    doc_ids,
    pre_gain,
    pre_bias,
    in_weight,
    in_bias,
    short_weight,
    short_bias,
    skip_gain,
    out_weight,
    out_bias,
    post_gain,
    post_bias,
    up_weight,
    up_bias,
    down_weight,
    down_bias,
    filter_one,
    filter_bias_one,
    filter_two,
    filter_bias_two,
    filter_freq,
    filter_three,
):
    rz_count, pos_count = lax.axis_size("rz"), lax.axis_size("pos")
    pos, core = lax.axis_index("pos"), lax.axis_index("core")
    everything = ("rz", "core", "pos")
    owners = rz_count * 2 * pos_count
    own_at = (lax.axis_index("rz") * 2 + core) * pos_count + pos
    part_len, model_width = activations.shape[1:]
    length = part_len * pos_count
    own_width = pre_gain.shape[0]
    chan = model_width // pos_count
    ff_own = down_weight.shape[0]
    ff_half = rz_count * pos_count * ff_own
    docs = doc_bounds.shape[1]
    order = filter_two.shape[0]
    tables = transform_tables()
    meta = unit_table(doc_bounds[0], length)

    vectors = [
        pre_gain,
        pre_bias,
        out_bias,
        post_gain,
        post_bias,
        down_bias,
        skip_gain,
        in_bias,
        short_weight,
        short_bias,
        filter_three,
    ]
    small = jnp.concatenate(
        [value.reshape(-1, own_width) for value in vectors] + [up_bias.reshape(-1, own_width)]
    )
    small = lax.all_gather(small, "pos")
    small = lax.all_gather(small, "core")
    small = lax.all_gather(small, "rz").reshape(rz_count, 2, pos_count, -1, own_width)
    lines = small.transpose(3, 0, 1, 2, 4)
    lines = lines.reshape(-1, model_width).astype(F32)
    (
        pre_gain_all,
        pre_bias_all,
        out_bias_all,
        post_gain_all,
        post_bias_all,
        down_bias_all,
    ) = (lines[at] for at in range(6))
    up_lines = lines.shape[0] - ff_own // own_width
    up_bias_all = lines[up_lines:].reshape(ff_own // own_width, rz_count, 2, pos_count, own_width)
    up_bias_all = up_bias_all.transpose(2, 1, 3, 0, 4).reshape(2, ff_half)
    up_bias_half = lax.dynamic_index_in_dim(up_bias_all, core, 0)
    mine = lax.dynamic_slice_in_dim(lines[6:up_lines], pos * chan, chan, 1)
    proj_bias = mine[1:4].reshape(1, 3 * chan)
    taps = jnp.concatenate([mine[4:16], mine[0:1], jnp.zeros((3, chan), F32)])
    three = mine[16:]

    weight_in = in_weight.reshape(own_width, 3, pos_count, chan)
    weight_in = lax.all_to_all(weight_in, "pos", split_axis=2, concat_axis=0, tiled=True)
    weight_in = weight_in.reshape(pos_count * own_width, 3 * chan)
    weight_in = lax.all_gather(weight_in, ("rz", "core"), axis=0, tiled=True)

    up_parts = up_weight.reshape(own_width, rz_count, 2, pos_count * ff_own)
    up_keep = lax.dynamic_index_in_dim(up_parts, core, 2, False).reshape(own_width, ff_half)
    up_send = lax.dynamic_index_in_dim(up_parts, 1 - core, 2, False).reshape(own_width, ff_half)
    up_got = swap(up_send, "core", 1)
    up_pair = jnp.where(core == 0, jnp.stack([up_keep, up_got]), jnp.stack([up_got, up_keep]))
    up_all = lax.all_gather(up_pair, ("rz", "pos"))
    up_all = up_all.reshape(rz_count, pos_count, 2, own_width, ff_half)
    up_all = up_all.transpose(0, 2, 1, 3, 4).reshape(model_width, ff_half)
    down_all = lax.all_gather(down_weight, ("rz", "pos"), axis=0, tiled=True)
    out_all = lax.all_gather(out_weight, ("rz", "pos"))
    out_other = swap(out_all, "core", 1)
    out_all = jnp.where(
        core == 0, jnp.stack([out_all, out_other], 1), jnp.stack([out_other, out_all], 1)
    )
    out_all = out_all.reshape(rz_count, pos_count, 2, own_width, model_width)
    out_all = out_all.transpose(0, 2, 1, 3, 4).reshape(model_width, model_width)

    embedding = positions_table(length, filter_one.shape[0])
    channels = (pos * chan + jnp.arange(chan, dtype=jnp.int32)).astype(F32)
    decay = decay_of(length, channels, model_width)
    filt, filter_back = jax.vjp(
        functools.partial(filter_net, embedding, decay),
        filter_one.astype(F32),
        filter_bias_one.astype(F32),
        filter_two.astype(F32),
        filter_bias_two.astype(F32),
        filter_freq.astype(F32),
        three,
    )

    own_in = activations[0]
    bits = bits_of(pos_count)
    half = model_width // 2
    left = gather_halving(own_in[:, :half], "pos", bits)
    right = gather_halving(own_in[:, half:], "pos", bits[::-1])
    row_in = jnp.concatenate([left, right], axis=2).reshape(length, model_width)
    norm_one = jnp.stack([pre_gain_all, pre_bias_all])
    projected = project(row_in, norm_one, weight_in, proj_bias)
    branch, mixed = mixer_forward(meta, docs, projected, filt, taps, tables)
    branch_tokens = lax.all_to_all(
        branch.reshape(pos_count, part_len, chan), "pos", split_axis=0, concat_axis=0, tiled=True
    )
    branch_tokens = branch_tokens.transpose(1, 0, 2).reshape(part_len, model_width)

    inputs_f = own_in.astype(F32)
    residual = inputs_f + jnp.dot(branch_tokens, out_all, preferred_element_type=F32) + out_bias_all
    normed_two, post_back = jax.vjp(layer_norm, residual, post_gain_all, post_bias_all)
    normed_two = normed_two.astype(BF16)
    own_grad = out_grad[0]
    other_grad = swap(own_grad, "core", 1)
    ff_own_out, ff_other_out, back_own, back_other, up_grad, down_grad, up_bias_grad = feed_forward(
        normed_two,
        swap(normed_two, "core", 1),
        own_grad,
        other_grad,
        up_all,
        up_bias_half,
        down_all,
    )
    result = residual + (ff_own_out + swap(ff_other_out, "core", 1).astype(F32)) + down_bias_all
    result = result.astype(BF16)[None]
    grad_normed_two = back_own + swap(back_other, "core", 1).astype(F32)
    grad_out_f = own_grad.astype(F32)
    down_bias_grad = jnp.sum(grad_out_f, axis=0)
    grad_res_part, post_gain_grad, post_bias_grad = post_back(grad_normed_two)
    grad_residual = grad_out_f + grad_res_part
    out_bias_grad = jnp.sum(grad_residual, axis=0)
    grad_res_q = grad_residual.astype(BF16)
    branch_grad = lax.dot_general(
        grad_res_q, out_all, (((1,), (1,)), ((), ())), preferred_element_type=F32
    ).astype(BF16)
    branch_grad = lax.all_to_all(
        branch_grad.reshape(part_len, pos_count, chan).transpose(1, 0, 2),
        "pos",
        split_axis=0,
        concat_axis=0,
        tiled=True,
    ).reshape(length, chan)
    out_weight_grad = lax.dot_general(
        branch_tokens, grad_res_q, (((0,), (0,)), ((), ())), preferred_element_type=F32
    ).astype(BF16)

    def scatter(value, axes):
        return lax.psum_scatter(value, axes, scatter_dimension=0, tiled=False)

    out_parts = out_weight_grad.reshape(rz_count, 2, pos_count, own_width, model_width)
    out_keep = lax.dynamic_index_in_dim(out_parts, core, 1, False)
    out_send = lax.dynamic_index_in_dim(out_parts, 1 - core, 1, False)
    out_sum = (out_keep.astype(F32) + swap(out_send, "core", 1).astype(F32)).astype(BF16)
    up_parts = up_grad.reshape(rz_count, 2, pos_count, own_width, ff_half).transpose(0, 2, 1, 3, 4)
    bundle = jnp.concatenate(
        [
            up_parts.reshape(rz_count, pos_count, -1, model_width),
            down_grad.reshape(rz_count, pos_count, ff_own, model_width),
            out_sum,
        ],
        axis=2,
    ).transpose(1, 0, 2, 3)
    bundle = scatter(scatter(bundle, "pos"), "rz").astype(F32)
    up_rows = 2 * own_width * ff_half // model_width
    up_sum = bundle[:up_rows].reshape(2, own_width, ff_half)
    down_weight_grad = bundle[up_rows : up_rows + ff_own]
    out_weight_grad = bundle[up_rows + ff_own :]
    up_keep = lax.dynamic_index_in_dim(up_sum, core, 0, False)
    up_send = lax.dynamic_index_in_dim(up_sum, 1 - core, 0, False).astype(BF16)
    up_got = swap(up_send, "core", 1).astype(F32)
    up_pair = jnp.where(core == 0, jnp.stack([up_keep, up_got]), jnp.stack([up_got, up_keep]))
    up_weight_grad = up_pair.reshape(2, own_width, rz_count, pos_count * ff_own)
    up_weight_grad = up_weight_grad.transpose(1, 2, 0, 3).reshape(own_width, owners * ff_own)

    proj_grad, filt_grad, chan_sums = mixer_backward(
        meta, docs, projected, filt, taps, tables, mixed, branch_grad
    )
    normed_grad, weight_in_grad, pre_sums = project_back(row_in, norm_one, weight_in, proj_grad)
    normed_grad = scatter(
        normed_grad.reshape(pos_count, part_len, model_width), "pos"
    ).astype(F32)
    unit, scale = norm_parts(inputs_f)
    scaled = normed_grad * pre_gain_all
    grad_input = scale * (
        scaled
        - jnp.mean(scaled, axis=-1, keepdims=True)
        - unit * jnp.mean(scaled * unit, axis=-1, keepdims=True)
    )
    input_grad = (grad_residual + grad_input).astype(BF16)[None]
    weight_in_grad = scatter(
        weight_in_grad.reshape(rz_count * 2, pos_count * own_width, 3 * chan), ("rz", "core")
    )
    weight_in_grad = lax.all_to_all(
        weight_in_grad.reshape(pos_count, own_width, 3, chan),
        "pos",
        split_axis=0,
        concat_axis=0,
        tiled=True,
    )
    weight_in_grad = weight_in_grad.transpose(1, 2, 0, 3).reshape(own_width, 3, model_width)
    weight_in_grad = weight_in_grad.astype(F32)
    inner = filter_back(filt_grad)

    wide = jnp.concatenate([chan_sums, inner[5]])
    wide = lax.dynamic_update_slice_in_dim(
        jnp.zeros((wide.shape[0], model_width), F32), wide, pos * chan, 1
    )
    up_bias_wide = jnp.where(
        jnp.arange(2)[:, None] == core, jnp.broadcast_to(up_bias_grad, (2, ff_half)), 0.0
    )
    token_sums = jnp.stack(
        [
            pre_sums[0],
            pre_sums[1],
            out_bias_grad,
            post_gain_grad,
            post_bias_grad,
            down_bias_grad,
        ]
    )
    wide, up_bias_wide, token_sums, inner_sum = lax.psum(
        (wide, up_bias_wide, token_sums, tuple(inner[:5])), everything
    )
    wide = lax.dynamic_slice_in_dim(wide, own_at * own_width, own_width, 1)
    token_sums = lax.dynamic_slice_in_dim(token_sums, own_at * own_width, own_width, 1)
    up_bias_sum = up_bias_wide.reshape(2, rz_count, pos_count, ff_own)
    up_bias_sum = up_bias_sum.transpose(1, 0, 2, 3).reshape(-1)
    up_bias_sum = lax.dynamic_slice_in_dim(up_bias_sum, own_at * ff_own, ff_own, 0)
    return (
        result,
        input_grad,
        token_sums[0],
        token_sums[1],
        weight_in_grad,
        wide[12:15],
        wide[0:9].reshape(3, 3, own_width),
        wide[9:12],
        wide[15],
        out_weight_grad,
        token_sums[2],
        token_sums[3],
        token_sums[4],
        up_weight_grad,
        up_bias_sum,
        down_weight_grad,
        token_sums[5],
        *inner_sum,
        wide[16:],
    )


def solution(mesh):
    rows_count, pos_count = mesh.devices.shape
    fine = Mesh(mesh.devices.reshape(rows_count // 2, 2, pos_count), ("rz", "core", "pos"))
    rows = ("rz", "core")
    every = ("rz", "core", "pos")
    tokens = P(rows, "pos", None)
    vector = P(every)
    matrix = P(every, None)
    return jax.shard_map(
        on_device,
        mesh=fine,
        in_specs=(
            tokens,
            tokens,
            P(rows, None),
            P(rows, None),
            vector,
            vector,
            P(every, None, None),
            P(None, every),
            P(None, None, every),
            P(None, every),
            vector,
            matrix,
            vector,
            vector,
            vector,
            matrix,
            vector,
            matrix,
            vector,
            P(),
            P(),
            P(),
            P(),
            P(),
            P(None, every),
        ),
        out_specs=(
            tokens,
            tokens,
            vector,
            vector,
            P(every, None, None),
            P(None, every),
            P(None, None, every),
            P(None, every),
            vector,
            matrix,
            vector,
            vector,
            vector,
            matrix,
            vector,
            matrix,
            vector,
            P(),
            P(),
            P(),
            P(),
            P(),
            P(None, every),
        ),
        check_vma=False,
    )
```

```python
import functools
import math

import jax
import jax.numpy as jnp
import ml_dtypes
import numpy as np
from jax import lax
from jax.experimental import pallas as pl
from jax.experimental.pallas import tpu as pltpu
from jax.sharding import Mesh
from jax.sharding import PartitionSpec as P

HIGHEST = lax.Precision.HIGHEST
F32 = jnp.float32
BF16 = jnp.bfloat16
BLOCK = 256
FREQ_CHUNK = 64
VMEM_LIMIT = 60 * 1024 * 1024


def layer_norm(values, norm_gain, norm_shift):
    centre = values - jnp.mean(values, axis=-1, keepdims=True)
    spread = jnp.mean(centre * centre, axis=-1, keepdims=True)
    return centre * lax.rsqrt(spread + 1e-05) * norm_gain + norm_shift


def positions_table(length, features):
    band_count = (features - 1) // 2
    places = np.arange(length, dtype=np.float64)
    ladder = 0.0001 + (band_count - 1 - 0.0001) * np.arange(band_count) / (band_count - 1)
    angles = 2.0 * math.pi / length * places[:, None] * ladder[None, :]
    table = np.concatenate(
        [places[:, None] / (length - 1), np.cos(angles), -np.sin(angles)], axis=1
    )
    return jnp.asarray(table.astype(np.float32))


def decay_of(length, channels, model_width):
    scaled = jnp.arange(length, dtype=F32) / (length - 1)
    slow_rate = math.log(0.01) / 1.5
    fast_rate = math.log(0.01) / 0.3
    rates = jnp.abs(slow_rate + (fast_rate - slow_rate) * channels / (model_width - 1))
    return jnp.exp(-scaled[:, None] * rates[None, :]) + 0.05


def filter_net(embedding, decay, w_one, b_one, w_two, b_two, frequency, w_three):
    layer_one = jnp.sin(frequency * (jnp.dot(embedding, w_one, precision=HIGHEST) + b_one))
    layer_two = jnp.sin(frequency * (jnp.dot(layer_one, w_two, precision=HIGHEST) + b_two))
    return jnp.dot(layer_two, w_three, precision=HIGHEST) * decay


def transform_tables():
    order = np.concatenate([np.arange(0, BLOCK, 2), np.arange(1, BLOCK, 2)])
    angle = math.pi / BLOCK * (order[:, None] + 0.5) * np.arange(BLOCK)[None, :]
    forward = np.concatenate([np.cos(angle), -np.sin(angle)], axis=0)
    tables = []
    for table in (forward, forward.T / BLOCK):
        high = table.astype(ml_dtypes.bfloat16)
        low = (table - high.astype(np.float64)).astype(ml_dtypes.bfloat16)
        tables.append(jnp.asarray(np.concatenate([high, high, low], axis=1)))
    return tables


def unit_table(bounds, length):
    docs = bounds.shape[0]
    units = length // BLOCK + docs - 1
    ends = jnp.concatenate([bounds[1:], jnp.full((1,), length, jnp.int32)])
    first = bounds // BLOCK
    count = jnp.where(ends > bounds, (ends - 1) // BLOCK - first + 1, 0)
    earlier = jnp.arange(docs)[:, None] >= jnp.arange(docs)[None, :]
    stops = jnp.sum(jnp.where(earlier, count[None, :], 0), axis=1)
    starts = stops - count
    unit = jnp.arange(units, dtype=jnp.int32)
    doc = jnp.sum((unit[:, None] >= stops[None, :]).astype(jnp.int32), axis=1)
    doc = jnp.minimum(doc, docs - 1)
    pick = (doc[:, None] == jnp.arange(docs)[None, :]).astype(jnp.int32)

    def of_doc(values):
        return jnp.sum(pick * values[None, :], axis=1)

    block = jnp.clip(of_doc(first - starts) + unit, 0, length // BLOCK - 1)
    return jnp.concatenate(
        [
            block,
            of_doc(bounds),
            of_doc(ends),
            of_doc(starts),
            of_doc(stops),
            starts,
            stops,
            bounds,
            stops[docs - 1 :],
        ]
    ).astype(jnp.int32)


class Units:
    def __init__(self, meta, length, docs):
        self.meta = meta
        self.docs = docs
        self.units = length // BLOCK + docs - 1

    def block(self, unit):
        return self.meta[unit]

    def low(self, unit):
        return self.meta[self.units + unit]

    def high(self, unit):
        return self.meta[2 * self.units + unit]

    def start(self, unit):
        return self.meta[3 * self.units + unit]

    def stop(self, unit):
        return self.meta[4 * self.units + unit]

    def doc_start(self, doc):
        return self.meta[5 * self.units + doc]

    def doc_stop(self, doc):
        return self.meta[5 * self.units + self.docs + doc]

    def bound(self, doc):
        return self.meta[5 * self.units + 2 * self.docs + doc]

    def total(self):
        return self.meta[5 * self.units + 3 * self.docs]

    def inside(self, unit, width):
        place = lax.broadcasted_iota(jnp.int32, (BLOCK, width), 0) + self.block(unit) * BLOCK
        return (place >= self.low(unit)) & (place < self.high(unit))


def rows_of(block):
    return pl.ds(pl.multiple_of(block * BLOCK, BLOCK), BLOCK)


def times(table, value):
    high = value.astype(BF16)
    low = (value - high.astype(F32)).astype(BF16)
    return jnp.dot(
        table[...], jnp.concatenate([high, low, high], axis=0), preferred_element_type=F32
    )


def tap_masks(units, block, width, ahead=0):
    place = lax.broadcasted_iota(jnp.int32, (BLOCK, width), 0) + (block * BLOCK + ahead)
    first = place == units.bound(0)
    second = place == units.bound(0) + 1
    for doc in range(1, units.docs):
        first = first | (place == units.bound(doc))
        second = second | (place == units.bound(doc) + 1)
    return jnp.logical_not(first), jnp.logical_not(first | second)


def delayed(ref, block):
    start = block * BLOCK
    here = ref[rows_of(block), :].astype(F32)
    before = ref[pl.ds(pl.multiple_of(jnp.maximum(start - 16, 0), 16), 16), :].astype(F32)
    joined = jnp.concatenate([before, here], axis=0)
    return (here, pltpu.roll(joined, 1, 0)[16:], pltpu.roll(joined, 2, 0)[16:])


def short_conv(parts, small, branch, masks):
    total = small[9 + branch : 10 + branch, :] + small[branch : branch + 1, :] * parts[0]
    total += jnp.where(masks[0], small[3 + branch : 4 + branch, :] * parts[1], 0.0)
    total += jnp.where(masks[1], small[6 + branch : 7 + branch, :] * parts[2], 0.0)
    return total


def mixer_forward_kernel(
    docs, meta, post, pre, val, filt, small, fwd, inv, branch, mixed, gated, spec, taps, prod
):
    length, width = gated.shape
    blocks = length // BLOCK
    units = Units(meta, length, docs)

    def gate(block, _):
        masks = tap_masks(units, block, width)
        part = short_conv(delayed(val, block), small, 2, masks)
        part *= short_conv(delayed(pre, block), small, 1, masks)
        gated[rows_of(block), :] = part
        mixed[rows_of(block), :] = small[12:13, :] * part
        taps[block] = times(fwd, filt[rows_of(block), :])
        return 0

    lax.fori_loop(0, blocks, gate, 0)

    def transform(unit, _):
        value = gated[rows_of(units.block(unit)), :]
        spec[unit] = times(fwd, jnp.where(units.inside(unit, width), value, 0.0))
        return 0

    lax.fori_loop(0, units.total(), transform, 0)

    def multiply(unit, _):
        for low in range(0, BLOCK, FREQ_CHUNK):
            re, im = pl.ds(low, FREQ_CHUNK), pl.ds(BLOCK + low, FREQ_CHUNK)

            def step(back, total):
                at = unit - back
                s_re, s_im, t_re, t_im = spec[at, re], spec[at, im], taps[back, re], taps[back, im]
                return (
                    total[0] + (s_re * t_re - s_im * t_im),
                    total[1] + (s_re * t_im + s_im * t_re),
                )

            zero = jnp.zeros((FREQ_CHUNK, width), F32)
            total = lax.fori_loop(0, unit - units.start(unit) + 1, step, (zero, zero))
            prod[unit, re] = total[0]
            prod[unit, im] = total[1]
        return 0

    lax.fori_loop(0, units.total(), multiply, 0)

    half = BLOCK // 2

    def bring_back(unit, _):
        last = jnp.maximum(unit - 1, 0)
        old = jnp.where(unit > units.start(unit), prod[last], 0.0)
        new = prod[unit]
        joined = jnp.concatenate(
            [
                new[:half] - old[BLOCK : BLOCK + half],
                new[half:BLOCK] + old[BLOCK + half :],
                new[BLOCK : BLOCK + half] + old[:half],
                new[BLOCK + half :] - old[half:BLOCK],
            ],
            axis=0,
        )
        value = times(inv, joined)
        rows = rows_of(units.block(unit))
        mixed[rows, :] += jnp.where(units.inside(unit, width), value, 0.0)
        return 0

    lax.fori_loop(0, units.total(), bring_back, 0)

    def finish(block, _):
        masks = tap_masks(units, block, width)
        gate_value = short_conv(delayed(post, block), small, 0, masks)
        branch[rows_of(block), :] = (gate_value * mixed[rows_of(block), :]).astype(BF16)
        return 0

    lax.fori_loop(0, blocks, finish, 0)


def mixer_backward_kernel(
    docs,
    meta,
    post,
    pre,
    val,
    filt,
    small,
    fwd,
    inv,
    mixed,
    branch_grad,
    proj_grad,
    filt_grad,
    sums,
    gated,
    gm,
    conv_grad,
    spec,
    taps,
    prod,
):
    length, width = gated.shape
    blocks = length // BLOCK
    units = Units(meta, length, docs)
    half = BLOCK // 2
    sums[...] = jnp.zeros_like(sums)

    def total_rows(value):
        return jnp.sum(value, axis=0, keepdims=True)

    def gate(block, _):
        rows = rows_of(block)
        masks = tap_masks(units, block, width)
        part = short_conv(delayed(val, block), small, 2, masks)
        part *= short_conv(delayed(pre, block), small, 1, masks)
        gated[rows, :] = part
        grad = branch_grad[rows, :].astype(F32)
        mix_grad = grad * short_conv(delayed(post, block), small, 0, masks)
        gm[rows, :] = mix_grad
        conv_grad[0, rows, :] = grad * mixed[rows, :]
        conv_grad[1, rows, :] = small[12:13, :] * mix_grad
        sums[15:16, :] += total_rows(part * mix_grad)
        taps[block] = times(fwd, filt[rows, :])
        return 0

    lax.fori_loop(0, blocks, gate, 0)

    def transform(unit, _):
        rows = rows_of(units.block(unit))
        inside = units.inside(unit, width)
        spec[unit] = times(fwd, jnp.where(inside, gated[rows, :], 0.0))
        prod[unit] = times(fwd, jnp.where(inside, gm[rows, :], 0.0))
        return 0

    lax.fori_loop(0, units.total(), transform, 0)

    def spread(unit, _):
        after = jnp.minimum(unit + 1, units.units - 1)
        new = jnp.where(unit + 1 < units.stop(unit), prod[after], 0.0)
        prod[unit, pl.ds(0, half)] += new[BLOCK : BLOCK + half]
        prod[unit, pl.ds(half, half)] -= new[BLOCK + half :]
        prod[unit, pl.ds(BLOCK, half)] -= new[:half]
        prod[unit, pl.ds(BLOCK + half, half)] += new[half:BLOCK]
        return 0

    lax.fori_loop(0, units.total(), spread, 0)

    def signal_grad(unit, _):
        pieces = []
        for low in range(0, BLOCK, FREQ_CHUNK):
            re, im = pl.ds(low, FREQ_CHUNK), pl.ds(BLOCK + low, FREQ_CHUNK)

            def step(ahead, total):
                at = unit + ahead
                g_re, g_im, t_re, t_im = (
                    prod[at, re],
                    prod[at, im],
                    taps[ahead, re],
                    taps[ahead, im],
                )
                return (
                    total[0] + (g_re * t_re + g_im * t_im),
                    total[1] + (g_im * t_re - g_re * t_im),
                )

            zero = jnp.zeros((FREQ_CHUNK, width), F32)
            pieces.append(lax.fori_loop(0, units.stop(unit) - unit, step, (zero, zero)))
        joined = jnp.concatenate([piece[0] for piece in pieces] + [piece[1] for piece in pieces])
        value = times(inv, joined)
        rows = rows_of(units.block(unit))
        conv_grad[1, rows, :] += jnp.where(units.inside(unit, width), value, 0.0)
        return 0

    lax.fori_loop(0, units.total(), signal_grad, 0)

    def tap_grad(back, _):
        pieces = []
        for low in range(0, BLOCK, FREQ_CHUNK):
            re, im = pl.ds(low, FREQ_CHUNK), pl.ds(BLOCK + low, FREQ_CHUNK)

            def step(unit, total):
                at = unit - back
                g_re, g_im, s_re, s_im = (
                    prod[unit, re],
                    prod[unit, im],
                    spec[at, re],
                    spec[at, im],
                )
                return (
                    total[0] + (g_re * s_re + g_im * s_im),
                    total[1] + (g_im * s_re - g_re * s_im),
                )

            zero = jnp.zeros((FREQ_CHUNK, width), F32)
            total = (zero, zero)
            for doc in range(docs):
                total = lax.fori_loop(
                    units.doc_start(doc) + back, units.doc_stop(doc), step, total
                )
            pieces.append(total)
        joined = jnp.concatenate([piece[0] for piece in pieces] + [piece[1] for piece in pieces])
        filt_grad[rows_of(back), :] = times(inv, joined)
        return 0

    lax.fori_loop(0, blocks, tap_grad, 0)

    def conv_back(block, _):
        rows = rows_of(block)
        masks = tap_masks(units, block, width)
        val_parts, pre_parts, post_parts = (
            delayed(val, block),
            delayed(pre, block),
            delayed(post, block),
        )
        gated_grad = conv_grad[1, rows, :]
        pre_grad = gated_grad * short_conv(val_parts, small, 2, masks)
        val_grad = gated_grad * short_conv(pre_parts, small, 1, masks)
        post_grad = conv_grad[0, rows, :]
        conv_grad[1, rows, :] = pre_grad
        conv_grad[2, rows, :] = val_grad
        for branch, (grad, parts) in enumerate(
            ((post_grad, post_parts), (pre_grad, pre_parts), (val_grad, val_parts))
        ):
            sums[branch : branch + 1, :] += total_rows(grad * parts[0])
            sums[3 + branch : 4 + branch, :] += total_rows(
                jnp.where(masks[0], grad * parts[1], 0.0)
            )
            sums[6 + branch : 7 + branch, :] += total_rows(
                jnp.where(masks[1], grad * parts[2], 0.0)
            )
            sums[9 + branch : 10 + branch, :] += total_rows(grad)
        return 0

    lax.fori_loop(0, blocks, conv_back, 0)

    def spread_taps(block, _):
        start = block * BLOCK
        one, _two = tap_masks(units, block, width, 1)
        _one, two = tap_masks(units, block, width, 2)
        place = lax.broadcasted_iota(jnp.int32, (BLOCK, width), 0) + start
        one = one & (place + 1 < length)
        two = two & (place + 2 < length)
        for branch in range(3):
            here = conv_grad[branch, rows_of(block), :]
            after = conv_grad[
                branch, pl.ds(pl.multiple_of(jnp.minimum(start + BLOCK, length - 8), 8), 8), :
            ]
            joined = jnp.concatenate([here, after], axis=0)
            size = BLOCK + 8
            next_one = pltpu.roll(joined, size - 1, 0)[:BLOCK]
            next_two = pltpu.roll(joined, size - 2, 0)[:BLOCK]
            total = small[branch : branch + 1, :] * here
            total += jnp.where(one, small[3 + branch : 4 + branch, :] * next_one, 0.0)
            total += jnp.where(two, small[6 + branch : 7 + branch, :] * next_two, 0.0)
            rounded = total.astype(BF16)
            proj_grad[rows_of(block), branch * width : (branch + 1) * width] = rounded
            sums[12 + branch : 13 + branch, :] += total_rows(rounded.astype(F32))
        return 0

    lax.fori_loop(0, blocks, spread_taps, 0)


def whole_spec(shape, column=0):
    return pl.BlockSpec(shape, lambda i, meta: (0, column), pipeline_mode=pl.Buffered(1))


def mixer_forward(meta, docs, projected, filt, small, tables):
    length, width = filt.shape
    units = length // BLOCK + docs - 1
    column = [whole_spec((length, width), at) for at in range(3)]
    return pl.pallas_call(
        functools.partial(mixer_forward_kernel, docs),
        out_shape=(
            jax.ShapeDtypeStruct((length, width), BF16),
            jax.ShapeDtypeStruct((length, width), F32),
        ),
        grid_spec=pltpu.PrefetchScalarGridSpec(
            num_scalar_prefetch=1,
            grid=(1,),
            in_specs=column
            + [whole_spec(value.shape) for value in (filt, small, tables[0], tables[1])],
            out_specs=(column[0], column[0]),
            scratch_shapes=[
                pltpu.VMEM((length, width), F32),
                pltpu.VMEM((units, 2 * BLOCK, width), F32),
                pltpu.VMEM((length // BLOCK, 2 * BLOCK, width), F32),
                pltpu.VMEM((units, 2 * BLOCK, width), F32),
            ],
        ),
        compiler_params=pltpu.CompilerParams(vmem_limit_bytes=VMEM_LIMIT),
        cost_estimate=pl.CostEstimate(
            flops=40 * 10**9, bytes_accessed=10 * 10**6, transcendentals=0
        ),
        name="mixer_forward",
    )(meta, projected, projected, projected, filt, small, *tables)


def mixer_backward(meta, docs, projected, filt, small, tables, mixed, branch_grad):
    length, width = filt.shape
    units = length // BLOCK + docs - 1
    column = [whole_spec((length, width), at) for at in range(3)]
    return pl.pallas_call(
        functools.partial(mixer_backward_kernel, docs),
        out_shape=(
            jax.ShapeDtypeStruct((length, 3 * width), BF16),
            jax.ShapeDtypeStruct((length, width), F32),
            jax.ShapeDtypeStruct((16, width), F32),
        ),
        grid_spec=pltpu.PrefetchScalarGridSpec(
            num_scalar_prefetch=1,
            grid=(1,),
            in_specs=column
            + [
                whole_spec(value.shape)
                for value in (filt, small, tables[0], tables[1], mixed, branch_grad)
            ],
            out_specs=(
                whole_spec((length, 3 * width)),
                column[0],
                whole_spec((16, width)),
            ),
            scratch_shapes=[
                pltpu.VMEM((length, width), F32),
                pltpu.VMEM((length, width), F32),
                pltpu.VMEM((3, length, width), F32),
                pltpu.VMEM((units, 2 * BLOCK, width), F32),
                pltpu.VMEM((length // BLOCK, 2 * BLOCK, width), F32),
                pltpu.VMEM((units, 2 * BLOCK, width), F32),
            ],
        ),
        compiler_params=pltpu.CompilerParams(vmem_limit_bytes=VMEM_LIMIT),
        cost_estimate=pl.CostEstimate(
            flops=80 * 10**9, bytes_accessed=16 * 10**6, transcendentals=0
        ),
        name="mixer_backward",
    )(meta, projected, projected, projected, filt, small, *tables, mixed, branch_grad)


def norm_parts(values):
    centre = values - jnp.mean(values, axis=-1, keepdims=True)
    spread = jnp.mean(centre * centre, axis=-1, keepdims=True)
    scale = lax.rsqrt(spread + 1e-05)
    return centre * scale, scale


def project_kernel(inputs, norm, weight, bias, out):
    unit, _ = norm_parts(inputs[...].astype(F32))
    normed = (unit * norm[0:1, :] + norm[1:2, :]).astype(BF16)
    total = jnp.dot(normed, weight[...], preferred_element_type=F32) + bias[...]
    out[...] = total.astype(BF16)


def project(inputs, norm, weight, bias):
    length, depth = inputs.shape
    width = weight.shape[1]
    return pl.pallas_call(
        project_kernel,
        out_shape=jax.ShapeDtypeStruct((length, width), BF16),
        grid=(length // BLOCK,),
        in_specs=[
            pl.BlockSpec((BLOCK, depth), lambda i: (i, 0)),
            pl.BlockSpec(norm.shape, lambda i: (0, 0)),
            pl.BlockSpec(weight.shape, lambda i: (0, 0)),
            pl.BlockSpec(bias.shape, lambda i: (0, 0)),
        ],
        out_specs=pl.BlockSpec((BLOCK, width), lambda i: (i, 0)),
        compiler_params=pltpu.CompilerParams(vmem_limit_bytes=VMEM_LIMIT),
        cost_estimate=pl.CostEstimate(
            flops=2 * length * depth * width, bytes_accessed=10 * 10**6, transcendentals=0
        ),
        name="project",
    )(inputs, norm, weight, bias)


def project_back_kernel(inputs, norm, weight, grad, normed_grad, weight_grad, sums, total):
    @pl.when(pl.program_id(0) == 0)
    def _():
        total[...] = jnp.zeros_like(total)
        sums[...] = jnp.zeros_like(sums)

    unit, _ = norm_parts(inputs[...].astype(F32))
    normed = (unit * norm[0:1, :] + norm[1:2, :]).astype(BF16)
    cotangent = lax.dot_general(
        grad[...], weight[...], (((1,), (1,)), ((), ())), preferred_element_type=F32
    )
    normed_grad[...] = cotangent.astype(BF16)
    sums[0:1, :] += jnp.sum(cotangent * unit, axis=0, keepdims=True)
    sums[1:2, :] += jnp.sum(cotangent, axis=0, keepdims=True)
    total[...] += lax.dot_general(
        normed, grad[...], (((0,), (0,)), ((), ())), preferred_element_type=F32
    )

    @pl.when(pl.program_id(0) == pl.num_programs(0) - 1)
    def _():
        weight_grad[...] = total[...].astype(BF16)


def project_back(inputs, norm, weight, grad):
    length, depth = inputs.shape
    width = weight.shape[1]
    return pl.pallas_call(
        project_back_kernel,
        out_shape=(
            jax.ShapeDtypeStruct((length, depth), BF16),
            jax.ShapeDtypeStruct((depth, width), BF16),
            jax.ShapeDtypeStruct((8, depth), F32),
        ),
        grid=(length // BLOCK,),
        in_specs=[
            pl.BlockSpec((BLOCK, depth), lambda i: (i, 0)),
            pl.BlockSpec(norm.shape, lambda i: (0, 0)),
            pl.BlockSpec(weight.shape, lambda i: (0, 0)),
            pl.BlockSpec((BLOCK, width), lambda i: (i, 0)),
        ],
        out_specs=(
            pl.BlockSpec((BLOCK, depth), lambda i: (i, 0)),
            pl.BlockSpec((depth, width), lambda i: (0, 0)),
            pl.BlockSpec((8, depth), lambda i: (0, 0)),
        ),
        scratch_shapes=[pltpu.VMEM((depth, width), F32)],
        compiler_params=pltpu.CompilerParams(vmem_limit_bytes=VMEM_LIMIT),
        cost_estimate=pl.CostEstimate(
            flops=4 * length * depth * width, bytes_accessed=16 * 10**6, transcendentals=0
        ),
        name="project_back",
    )(inputs, norm, weight, grad)


def gelu_pair(u):
    root = math.sqrt(2.0 / math.pi)
    square = u * u
    curve = jnp.tanh(root * (u + 0.044715 * (u * square)))
    value = 0.5 * u * (1.0 + curve)
    slope = 0.5 * (1.0 + curve) + 0.5 * u * (1.0 - curve * curve) * (
        root * (1.0 + 3.0 * 0.044715 * square)
    )
    return value, slope


def feed_forward_kernel(
    masks,
    place,
    normed_own,
    normed_other,
    grad_own,
    grad_other,
    up_bias,
    *rest,
):
    count = 2 * len(masks)
    pieces, rest = rest[:count], rest[count:]
    out_own, out_other, back_own, back_other, bias_grad = rest[:5]
    piece_grads, rest = rest[5 : 5 + count], rest[5 + count :]
    normed, grad, out_total, back_total, weights, grads, load_sems, store_sems = rest
    rows, depth = normed_own.shape
    tiles, pos_count, units, own_width, width = weights.shape
    half = tiles // 2
    columns = depth // width
    down_units = (units - 2 * tiles) // columns
    loads = [
        (normed_own, normed.at[pl.ds(0, rows)]),
        (normed_other, normed.at[pl.ds(rows, rows)]),
        (grad_own, grad.at[pl.ds(0, rows)]),
        (grad_other, grad.at[pl.ds(rows, rows)]),
    ]
    stores = []
    for at, mask in enumerate(masks):
        origin = jnp.bitwise_xor(place[0], mask)
        for side in range(2):
            part = pl.ds(side * half, half)
            loads.append((pieces[2 * at + side], weights.at[part, origin]))
            stores.append((grads.at[part, origin], piece_grads[2 * at + side]))
    loads = [
        pltpu.make_async_copy(source, target, load_sems.at[at])
        for at, (source, target) in enumerate(loads)
    ]
    for copy in loads:
        copy.start()
    out_total[...] = jnp.zeros_like(out_total)
    back_total[...] = jnp.zeros_like(back_total)
    for copy in loads:
        copy.wait()

    def step(tile, _):
        up = jnp.concatenate(
            [
                weights[block, :, side * tiles + tile].reshape(pos_count * own_width, width)
                for block in range(tiles)
                for side in range(2)
            ],
            axis=0,
        )
        down = jnp.concatenate(
            [
                weights[
                    tile, :, 2 * tiles + at * down_units : 2 * tiles + (at + 1) * down_units
                ].reshape(width, width)
                for at in range(columns)
            ],
            axis=1,
        )
        pre = jnp.dot(normed[...], up, preferred_element_type=F32) + up_bias[pl.ds(tile, 1), :]
        hidden, slope = gelu_pair(pre)
        hidden = hidden.astype(BF16)
        hidden_grad = lax.dot_general(
            grad[...], down, (((1,), (1,)), ((), ())), preferred_element_type=F32
        )
        pre_grad = hidden_grad * slope
        bias_grad[pl.ds(tile, 1), :] = jnp.sum(pre_grad, axis=0, keepdims=True)
        pre_grad = pre_grad.astype(BF16)
        out_total[...] += jnp.dot(hidden, down, preferred_element_type=F32)
        back_total[...] += lax.dot_general(
            pre_grad, up, (((1,), (1,)), ((), ())), preferred_element_type=F32
        )
        down_grad = lax.dot_general(
            hidden, grad[...], (((0,), (0,)), ((), ())), preferred_element_type=F32
        ).astype(BF16)
        for at in range(columns):
            grads[tile, :, 2 * tiles + at * down_units : 2 * tiles + (at + 1) * down_units] = (
                down_grad[:, at * width : (at + 1) * width].reshape(
                    pos_count, down_units, own_width, width
                )
            )
        up_grad = lax.dot_general(
            normed[...], pre_grad, (((0,), (0,)), ((), ())), preferred_element_type=F32
        ).astype(BF16)
        size = pos_count * own_width
        for block in range(tiles):
            for side in range(2):
                low = (2 * block + side) * size
                grads[block, :, side * tiles + tile] = up_grad[low : low + size].reshape(
                    pos_count, own_width, width
                )
        return 0

    lax.fori_loop(0, tiles, step, 0)
    normed[:rows] = out_total[rows:].astype(BF16)
    normed[rows:] = back_total[rows:].astype(BF16)
    stores += [
        (back_total.at[pl.ds(0, rows)], back_own),
        (normed.at[pl.ds(rows, rows)], back_other),
        (out_total.at[pl.ds(0, rows)], out_own),
        (normed.at[pl.ds(0, rows)], out_other),
    ]
    stores = [
        pltpu.make_async_copy(source, target, store_sems.at[at])
        for at, (source, target) in enumerate(stores)
    ]
    for copy in stores:
        copy.start()
    for copy in stores:
        copy.wait()


def feed_forward(place, masks, normed_own, normed_other, grad_own, grad_other, up_bias, pieces):
    rows, depth = normed_own.shape
    tiles, width = up_bias.shape
    piece = pieces[0].shape
    whole = (tiles, len(masks)) + piece[1:]
    anywhere = pl.BlockSpec(memory_space=pl.ANY)
    bias = pl.BlockSpec((tiles, width), lambda i, place: (0, 0))
    count = len(pieces)
    return pl.pallas_call(
        functools.partial(feed_forward_kernel, masks),
        out_shape=(
            jax.ShapeDtypeStruct((rows, depth), F32),
            jax.ShapeDtypeStruct((rows, depth), BF16),
            jax.ShapeDtypeStruct((rows, depth), F32),
            jax.ShapeDtypeStruct((rows, depth), BF16),
            jax.ShapeDtypeStruct((tiles, width), F32),
        )
        + (jax.ShapeDtypeStruct(piece, BF16),) * count,
        grid_spec=pltpu.PrefetchScalarGridSpec(
            num_scalar_prefetch=1,
            grid=(1,),
            in_specs=[anywhere] * 4 + [bias] + [anywhere] * count,
            out_specs=(anywhere,) * 4 + (bias,) + (anywhere,) * count,
            scratch_shapes=[
                pltpu.VMEM((2 * rows, depth), BF16),
                pltpu.VMEM((2 * rows, depth), BF16),
                pltpu.VMEM((2 * rows, depth), F32),
                pltpu.VMEM((2 * rows, depth), F32),
                pltpu.VMEM(whole, BF16),
                pltpu.VMEM(whole, BF16),
                pltpu.SemaphoreType.DMA((4 + count,)),
                pltpu.SemaphoreType.DMA((4 + count,)),
            ],
        ),
        compiler_params=pltpu.CompilerParams(vmem_limit_bytes=VMEM_LIMIT),
        cost_estimate=pl.CostEstimate(
            flops=12 * 2 * rows * depth * width * tiles,
            bytes_accessed=30 * 10**6,
            transcendentals=2 * rows * width * tiles,
        ),
        name="feed_forward",
    )(place, normed_own, normed_other, grad_own, grad_other, up_bias, *pieces)


def swap(value, axis, bit):
    count = lax.axis_size(axis)
    return lax.ppermute(value, axis, [(at, at ^ bit) for at in range(count)])


def gather_halving(value, axis, bits):
    count = lax.axis_size(axis)
    me = lax.axis_index(axis)
    held = value[None]
    for bit in bits:
        held = jnp.concatenate([held, swap(held, axis, bit)], axis=0)
    order = [0]
    for bit in bits:
        order = order + [mask ^ bit for mask in order]
    place = {mask: at for at, mask in enumerate(order)}
    held = jnp.stack([held[place[mask]] for mask in range(count)])
    shape = held.shape
    bit = 1
    while bit < count:
        parts = held.reshape((count // (2 * bit), 2, bit) + shape[1:])
        held = jnp.where((me & bit) != 0, parts[:, ::-1], parts).reshape(shape)
        bit *= 2
    return held


def spread_pieces(own, bits):
    held = {0: own}
    for bit in bits:
        held.update({mask ^ bit: swap(value, "pos", bit) for mask, value in list(held.items())})
    return held


def reduce_pieces(pieces, bits):
    for bit in bits:
        moved = {mask: swap(value, "pos", bit) for mask, value in pieces.items() if mask & bit}
        pieces = {
            mask: (value.astype(F32) + moved[mask ^ bit].astype(F32)).astype(BF16)
            for mask, value in pieces.items()
            if not mask & bit
        }
    return pieces[0]


def reduce_line(chunks, axis):
    count = lax.axis_size(axis)
    me = lax.axis_index(axis)

    def chunk(at):
        return lax.dynamic_index_in_dim(chunks, jnp.clip(at, 0, count - 1), 0, False).astype(F32)

    right = left = None
    for step in range(1, count):
        go_right = chunk(count - step + me)
        go_left = chunk(step - count + me)
        if step > 1:
            go_right += right.astype(F32)
            go_left += left.astype(F32)
        right = lax.ppermute(
            go_right.astype(BF16), axis, [(at, at + 1) for at in range(min(step, count - 1))]
        )
        left = lax.ppermute(
            go_left.astype(BF16),
            axis,
            [(count - 1 - at, count - 2 - at) for at in range(min(step, count - 1))],
        )
    return chunk(me) + (right.astype(F32) + left.astype(F32))


def small_sums_kernel(sizes, lines, send, total, shared, got, mine, send_sems, got_sems, share_sems, shared_sems):
    rz_count, pos_count = sizes
    owners = rz_count * 2 * pos_count
    me = (lax.axis_index("rz") * 2 + lax.axis_index("core")) * pos_count + lax.axis_index("pos")

    def device(at):
        return (at // (2 * pos_count), (at // pos_count) % 2, at % pos_count)

    barrier = pltpu.get_barrier_semaphore()

    def greet(step, _):
        pl.semaphore_signal(
            barrier,
            inc=1,
            device_id=device((me + step) % owners),
            device_id_type=pl.DeviceIdType.MESH,
        )
        return 0

    lax.fori_loop(1, owners, greet, 0)
    pl.semaphore_wait(barrier, owners - 1)

    def part(step):
        to = (me + step) % owners
        return pltpu.make_async_remote_copy(
            src_ref=send.at[to],
            dst_ref=got.at[step],
            send_sem=send_sems.at[step],
            recv_sem=got_sems.at[step],
            device_id=device(to),
            device_id_type=pl.DeviceIdType.MESH,
        )

    def share(step):
        to = (me + step) % owners
        return pltpu.make_async_remote_copy(
            src_ref=mine,
            dst_ref=shared.at[me],
            send_sem=share_sems.at[step],
            recv_sem=shared_sems.at[step],
            device_id=device(to),
            device_id_type=pl.DeviceIdType.MESH,
        )

    def start(step, _):
        part(step).start()
        return 0

    lax.fori_loop(1, owners, start, 0)
    total[...] = send[me]

    def add(step, _):
        part(step).wait_recv()
        total[...] += got[step]
        return 0

    lax.fori_loop(1, owners, add, 0)
    mine[...] = total[lines:]
    shared[me] = total[lines:]

    def start_share(step, _):
        share(step).start()
        return 0

    lax.fori_loop(1, owners, start_share, 0)

    def finish(step, _):
        part(step).wait_send()
        share(step).wait()
        return 0

    lax.fori_loop(1, owners, finish, 0)


def small_sums(sizes, send, lines):
    owners, rows, _ = send.shape
    return pl.pallas_call(
        functools.partial(small_sums_kernel, sizes, lines),
        out_shape=(
            jax.ShapeDtypeStruct((rows, 128), F32),
            jax.ShapeDtypeStruct((owners, rows - lines, 128), F32),
        ),
        in_specs=[pl.BlockSpec(memory_space=pltpu.VMEM)],
        out_specs=(
            pl.BlockSpec(memory_space=pltpu.VMEM),
            pl.BlockSpec(memory_space=pltpu.VMEM),
        ),
        scratch_shapes=[
            pltpu.VMEM((owners, rows, 128), F32),
            pltpu.VMEM((rows - lines, 128), F32),
            pltpu.SemaphoreType.DMA((owners,)),
            pltpu.SemaphoreType.DMA((owners,)),
            pltpu.SemaphoreType.DMA((owners,)),
            pltpu.SemaphoreType.DMA((owners,)),
        ],
        compiler_params=pltpu.CompilerParams(
            collective_id=0, has_side_effects=True, vmem_limit_bytes=32 * 1024 * 1024
        ),
        cost_estimate=pl.CostEstimate(flops=10**6, bytes_accessed=4 * 10**6, transcendentals=0),
        name="small_sums",
    )(send)


def bits_of(count):
    return [1 << at for at in range(count.bit_length() - 1)]


def on_device(
    activations,
    out_grad,
    doc_bounds,
    doc_ids,
    pre_gain,
    pre_bias,
    in_weight,
    in_bias,
    short_weight,
    short_bias,
    skip_gain,
    out_weight,
    out_bias,
    post_gain,
    post_bias,
    up_weight,
    up_bias,
    down_weight,
    down_bias,
    filter_one,
    filter_bias_one,
    filter_two,
    filter_bias_two,
    filter_freq,
    filter_three,
):
    rz_count, pos_count = lax.axis_size("rz"), lax.axis_size("pos")
    pos, core = lax.axis_index("pos"), lax.axis_index("core")
    everything = ("rz", "core", "pos")
    owners = rz_count * 2 * pos_count
    own_at = (lax.axis_index("rz") * 2 + core) * pos_count + pos
    part_len, model_width = activations.shape[1:]
    length = part_len * pos_count
    own_width = pre_gain.shape[0]
    chan = model_width // pos_count
    ff_own = down_weight.shape[0]
    ff_half = rz_count * pos_count * ff_own
    docs = doc_bounds.shape[1]
    order = filter_two.shape[0]
    tables = transform_tables()
    meta = unit_table(doc_bounds[0], length)

    vectors = [
        pre_gain,
        pre_bias,
        out_bias,
        post_gain,
        post_bias,
        down_bias,
        skip_gain,
        in_bias,
        short_weight,
        short_bias,
        filter_three,
    ]
    small = jnp.concatenate(
        [value.reshape(-1, own_width) for value in vectors] + [up_bias.reshape(-1, own_width)]
    )
    small = lax.all_gather(small, "pos")
    small = lax.all_gather(small, "core")
    small = lax.all_gather(small, "rz").reshape(rz_count, 2, pos_count, -1, own_width)
    lines = small.transpose(3, 0, 1, 2, 4)
    lines = lines.reshape(-1, model_width).astype(F32)
    (
        pre_gain_all,
        pre_bias_all,
        out_bias_all,
        post_gain_all,
        post_bias_all,
        down_bias_all,
    ) = (lines[at] for at in range(6))
    up_lines = lines.shape[0] - ff_own // own_width
    up_bias_all = lines[up_lines:].reshape(ff_own // own_width, rz_count, 2, pos_count, own_width)
    up_bias_all = up_bias_all.transpose(2, 1, 3, 0, 4).reshape(2, ff_half)
    up_bias_half = lax.dynamic_index_in_dim(up_bias_all, core, 0, False)
    up_bias_half = up_bias_half.reshape(rz_count, pos_count * ff_own)
    mine = lax.dynamic_slice_in_dim(lines[6:up_lines], pos * chan, chan, 1)
    proj_bias = mine[1:4].reshape(1, 3 * chan)
    taps = jnp.concatenate([mine[4:16], mine[0:1], jnp.zeros((3, chan), F32)])
    three = mine[16:]

    weight_in = in_weight.reshape(own_width, 3, pos_count, chan)
    weight_in = lax.all_to_all(weight_in, "pos", split_axis=2, concat_axis=0, tiled=True)
    weight_in = weight_in.reshape(pos_count * own_width, 3 * chan)
    weight_in = lax.all_gather(weight_in, ("rz", "core"), axis=0, tiled=True)

    tile = pos_count * ff_own
    columns = model_width // tile
    bits = bits_of(pos_count)
    orders = (bits, bits[::-1])
    place = jnp.reshape(pos, (1,)).astype(jnp.int32)
    up_parts = up_weight.reshape(own_width, rz_count, 2, tile).transpose(2, 1, 0, 3)
    up_keep = lax.dynamic_index_in_dim(up_parts, core, 0, False)
    up_got = swap(lax.dynamic_index_in_dim(up_parts, 1 - core, 0, False), "core", 1)
    up_first = jnp.where(core == 0, up_keep, up_got)
    up_second = jnp.where(core == 0, up_got, up_keep)
    down_parts = down_weight.reshape(ff_own // own_width, own_width, columns, tile)
    down_parts = down_parts.transpose(2, 0, 1, 3).reshape(-1, own_width, tile)
    bundle = jnp.concatenate([up_first, up_second, down_parts])
    bundle = lax.all_gather(bundle, "rz")
    sides = [
        spread_pieces(bundle[: rz_count // 2], orders[0]),
        spread_pieces(bundle[rz_count // 2 :], orders[1]),
    ]
    masks = sorted(sides[0])
    pieces = [sides[side][mask] for mask in masks for side in range(2)]
    out_all = lax.all_gather(out_weight, ("rz", "pos"))
    out_other = swap(out_all, "core", 1)
    out_all = jnp.where(
        core == 0, jnp.stack([out_all, out_other], 1), jnp.stack([out_other, out_all], 1)
    )
    out_all = out_all.reshape(rz_count, pos_count, 2, own_width, model_width)
    out_all = out_all.transpose(0, 2, 1, 3, 4).reshape(model_width, model_width)

    embedding = positions_table(length, filter_one.shape[0])
    channels = (pos * chan + jnp.arange(chan, dtype=jnp.int32)).astype(F32)
    decay = decay_of(length, channels, model_width)
    filt, filter_back = jax.vjp(
        functools.partial(filter_net, embedding, decay),
        filter_one.astype(F32),
        filter_bias_one.astype(F32),
        filter_two.astype(F32),
        filter_bias_two.astype(F32),
        filter_freq.astype(F32),
        three,
    )

    own_in = activations[0]
    half = model_width // 2
    left = gather_halving(own_in[:, :half], "pos", bits)
    right = gather_halving(own_in[:, half:], "pos", bits[::-1])
    row_in = jnp.concatenate([left, right], axis=2).reshape(length, model_width)
    norm_one = jnp.stack([pre_gain_all, pre_bias_all])
    projected = project(row_in, norm_one, weight_in, proj_bias)
    branch, mixed = mixer_forward(meta, docs, projected, filt, taps, tables)
    branch_tokens = lax.all_to_all(
        branch.reshape(pos_count, part_len, chan), "pos", split_axis=0, concat_axis=0, tiled=True
    )
    branch_tokens = branch_tokens.transpose(1, 0, 2).reshape(part_len, model_width)

    inputs_f = own_in.astype(F32)
    residual = inputs_f + jnp.dot(branch_tokens, out_all, preferred_element_type=F32) + out_bias_all
    normed_two, post_back = jax.vjp(layer_norm, residual, post_gain_all, post_bias_all)
    normed_two = normed_two.astype(BF16)
    own_grad = out_grad[0]
    other_grad = swap(own_grad, "core", 1)
    ff_own_out, ff_other_out, back_own, back_other, up_bias_grad, *piece_grads = feed_forward(
        place,
        masks,
        normed_two,
        swap(normed_two, "core", 1),
        own_grad,
        other_grad,
        up_bias_half,
        pieces,
    )
    result = residual + (ff_own_out + swap(ff_other_out, "core", 1).astype(F32)) + down_bias_all
    result = result.astype(BF16)[None]
    grad_normed_two = back_own + swap(back_other, "core", 1).astype(F32)
    grad_out_f = own_grad.astype(F32)
    down_bias_grad = jnp.sum(grad_out_f, axis=0)
    grad_res_part, post_gain_grad, post_bias_grad = post_back(grad_normed_two)
    grad_residual = grad_out_f + grad_res_part
    out_bias_grad = jnp.sum(grad_residual, axis=0)
    grad_res_q = grad_residual.astype(BF16)
    branch_grad = lax.dot_general(
        grad_res_q, out_all, (((1,), (1,)), ((), ())), preferred_element_type=F32
    ).astype(BF16)
    branch_grad = lax.all_to_all(
        branch_grad.reshape(part_len, pos_count, chan).transpose(1, 0, 2),
        "pos",
        split_axis=0,
        concat_axis=0,
        tiled=True,
    ).reshape(length, chan)
    out_weight_grad = lax.dot_general(
        branch_tokens, grad_res_q, (((0,), (0,)), ((), ())), preferred_element_type=F32
    ).astype(BF16)

    def scatter(value, axes):
        return lax.psum_scatter(value, axes, scatter_dimension=0, tiled=False)

    sums = [
        reduce_pieces(
            {mask: piece_grads[2 * at + side] for at, mask in enumerate(masks)}, orders[side]
        )
        for side in range(2)
    ]
    bundle = reduce_line(jnp.concatenate(sums), "rz")
    up_sum = bundle[: 2 * rz_count].reshape(2, rz_count, own_width, tile)
    up_keep = lax.dynamic_index_in_dim(up_sum, core, 0, False)
    up_send = lax.dynamic_index_in_dim(up_sum, 1 - core, 0, False).astype(BF16)
    up_got = swap(up_send, "core", 1).astype(F32)
    up_pair = jnp.where(
        core == 0, jnp.stack([up_keep, up_got], 1), jnp.stack([up_got, up_keep], 1)
    )
    up_weight_grad = up_pair.transpose(2, 0, 1, 3).reshape(own_width, owners * ff_own)
    down_weight_grad = bundle[2 * rz_count :].reshape(columns, ff_own, tile)
    down_weight_grad = down_weight_grad.transpose(1, 0, 2).reshape(ff_own, model_width)

    out_parts = out_weight_grad.reshape(rz_count, 2, pos_count, own_width, model_width)
    out_keep = lax.dynamic_index_in_dim(out_parts, core, 1, False)
    out_send = lax.dynamic_index_in_dim(out_parts, 1 - core, 1, False)
    out_sum = out_keep.astype(F32) + swap(out_send, "core", 1).astype(F32)
    out_sum = jnp.stack(
        [
            lax.dynamic_index_in_dim(out_sum, jnp.bitwise_xor(pos, mask), 1, False)
            for mask in masks
        ]
    ).astype(BF16)
    middle = rz_count // 2
    out_sums = [
        reduce_pieces({mask: out_sum[at, :middle] for at, mask in enumerate(masks)}, orders[0]),
        reduce_pieces({mask: out_sum[at, middle:] for at, mask in enumerate(masks)}, orders[1]),
    ]
    out_weight_grad = reduce_line(jnp.concatenate(out_sums), "rz")

    proj_grad, filt_grad, chan_sums = mixer_backward(
        meta, docs, projected, filt, taps, tables, mixed, branch_grad
    )
    normed_grad, weight_in_grad, pre_sums = project_back(row_in, norm_one, weight_in, proj_grad)
    normed_grad = scatter(
        normed_grad.reshape(pos_count, part_len, model_width), "pos"
    ).astype(F32)
    unit, scale = norm_parts(inputs_f)
    scaled = normed_grad * pre_gain_all
    grad_input = scale * (
        scaled
        - jnp.mean(scaled, axis=-1, keepdims=True)
        - unit * jnp.mean(scaled * unit, axis=-1, keepdims=True)
    )
    input_grad = (grad_residual + grad_input).astype(BF16)[None]
    weight_in_grad = scatter(
        weight_in_grad.reshape(rz_count * 2, pos_count * own_width, 3 * chan), ("rz", "core")
    )
    weight_in_grad = lax.all_to_all(
        weight_in_grad.reshape(pos_count, own_width, 3, chan),
        "pos",
        split_axis=0,
        concat_axis=0,
        tiled=True,
    )
    weight_in_grad = weight_in_grad.transpose(1, 2, 0, 3).reshape(own_width, 3, model_width)
    weight_in_grad = weight_in_grad.astype(F32)
    inner = filter_back(filt_grad)

    wide = jnp.concatenate([chan_sums, inner[5]])
    wide = lax.dynamic_update_slice_in_dim(
        jnp.zeros((wide.shape[0], model_width), F32), wide, pos * chan, 1
    )
    token_sums = jnp.stack(
        [
            pre_sums[0],
            pre_sums[1],
            out_bias_grad,
            post_gain_grad,
            post_bias_grad,
            down_bias_grad,
        ]
    )
    up_bias_wide = jnp.where(
        jnp.arange(2)[None, :, None] == core, up_bias_grad.reshape(rz_count, 1, tile), 0.0
    ).reshape(owners, ff_own)
    by_owner = jnp.concatenate([token_sums, wide]).reshape(-1, owners, own_width)
    count = by_owner.shape[0] * own_width
    line_rows = -(-(count + ff_own) // 1024) * 8
    by_owner = jnp.concatenate(
        [
            by_owner.transpose(1, 0, 2).reshape(owners, count),
            up_bias_wide,
            jnp.zeros((owners, line_rows * 128 - count - ff_own), F32),
        ],
        axis=1,
    ).reshape(owners, line_rows, 128)
    flat = jnp.concatenate([value.reshape(-1) for value in inner[:5]])
    share = -(-flat.shape[0] // owners)
    flat = jnp.pad(flat, (0, share * owners - flat.shape[0])).reshape(owners, share)
    inner_rows = -(-share // 1024) * 8
    flat = jnp.pad(flat, ((0, 0), (0, inner_rows * 128 - share)))
    send = jnp.concatenate([by_owner, flat.reshape(owners, inner_rows, 128)], axis=1)
    total, shared = small_sums((rz_count, pos_count), send, line_rows)
    total = total[:line_rows].reshape(-1)
    up_bias_sum = total[count : count + ff_own]
    total = total[:count].reshape(-1, own_width)
    token_sums, wide = total[:6], total[6:]
    shared = shared.reshape(owners, inner_rows * 128)[:, :share].reshape(-1)
    inner_sum, start = [], 0
    for value in inner[:5]:
        inner_sum.append(shared[start : start + value.size].reshape(value.shape))
        start += value.size
    return (
        result,
        input_grad,
        token_sums[0],
        token_sums[1],
        weight_in_grad,
        wide[12:15],
        wide[0:9].reshape(3, 3, own_width),
        wide[9:12],
        wide[15],
        out_weight_grad,
        token_sums[2],
        token_sums[3],
        token_sums[4],
        up_weight_grad,
        up_bias_sum,
        down_weight_grad,
        token_sums[5],
        *inner_sum,
        wide[16:],
    )


def solution(mesh):
    rows_count, pos_count = mesh.devices.shape
    fine = Mesh(mesh.devices.reshape(rows_count // 2, 2, pos_count), ("rz", "core", "pos"))
    rows = ("rz", "core")
    every = ("rz", "core", "pos")
    tokens = P(rows, "pos", None)
    vector = P(every)
    matrix = P(every, None)
    return jax.shard_map(
        on_device,
        mesh=fine,
        in_specs=(
            tokens,
            tokens,
            P(rows, None),
            P(rows, None),
            vector,
            vector,
            P(every, None, None),
            P(None, every),
            P(None, None, every),
            P(None, every),
            vector,
            matrix,
            vector,
            vector,
            vector,
            matrix,
            vector,
            matrix,
            vector,
            P(),
            P(),
            P(),
            P(),
            P(),
            P(None, every),
        ),
        out_specs=(
            tokens,
            tokens,
            vector,
            vector,
            P(every, None, None),
            P(None, every),
            P(None, None, every),
            P(None, every),
            vector,
            matrix,
            vector,
            vector,
            vector,
            matrix,
            vector,
            matrix,
            vector,
            P(),
            P(),
            P(),
            P(),
            P(),
            P(None, every),
        ),
        check_vma=False,
    )
```

```python
import functools
import math

import jax
import jax.numpy as jnp
import ml_dtypes
import numpy as np
from jax import lax
from jax.experimental import pallas as pl
from jax.experimental.pallas import tpu as pltpu
from jax.sharding import Mesh
from jax.sharding import PartitionSpec as P

HIGHEST = lax.Precision.HIGHEST
F32 = jnp.float32
BF16 = jnp.bfloat16
BLOCK = 256
FREQ_CHUNK = 64
VMEM_LIMIT = 60 * 1024 * 1024


def layer_norm(values, norm_gain, norm_shift):
    centre = values - jnp.mean(values, axis=-1, keepdims=True)
    spread = jnp.mean(centre * centre, axis=-1, keepdims=True)
    return centre * lax.rsqrt(spread + 1e-05) * norm_gain + norm_shift


def positions_table(length, features):
    band_count = (features - 1) // 2
    places = np.arange(length, dtype=np.float64)
    ladder = 0.0001 + (band_count - 1 - 0.0001) * np.arange(band_count) / (band_count - 1)
    angles = 2.0 * math.pi / length * places[:, None] * ladder[None, :]
    table = np.concatenate(
        [places[:, None] / (length - 1), np.cos(angles), -np.sin(angles)], axis=1
    )
    return jnp.asarray(table.astype(np.float32))


def decay_of(length, channels, model_width):
    scaled = jnp.arange(length, dtype=F32) / (length - 1)
    slow_rate = math.log(0.01) / 1.5
    fast_rate = math.log(0.01) / 0.3
    rates = jnp.abs(slow_rate + (fast_rate - slow_rate) * channels / (model_width - 1))
    return jnp.exp(-scaled[:, None] * rates[None, :]) + 0.05


def filter_net(embedding, decay, w_one, b_one, w_two, b_two, frequency, w_three):
    layer_one = jnp.sin(frequency * (jnp.dot(embedding, w_one, precision=HIGHEST) + b_one))
    layer_two = jnp.sin(frequency * (jnp.dot(layer_one, w_two, precision=HIGHEST) + b_two))
    return jnp.dot(layer_two, w_three, precision=HIGHEST) * decay


def transform_tables():
    order = np.concatenate([np.arange(0, BLOCK, 2), np.arange(1, BLOCK, 2)])
    angle = math.pi / BLOCK * (order[:, None] + 0.5) * np.arange(BLOCK)[None, :]
    forward = np.concatenate([np.cos(angle), -np.sin(angle)], axis=0)
    tables = []
    for table in (forward, forward.T / BLOCK):
        high = table.astype(ml_dtypes.bfloat16)
        low = (table - high.astype(np.float64)).astype(ml_dtypes.bfloat16)
        tables.append(jnp.asarray(np.concatenate([high, high, low], axis=1)))
    return tables


def unit_table(bounds, length):
    docs = bounds.shape[0]
    units = length // BLOCK + docs - 1
    ends = jnp.concatenate([bounds[1:], jnp.full((1,), length, jnp.int32)])
    first = bounds // BLOCK
    count = jnp.where(ends > bounds, (ends - 1) // BLOCK - first + 1, 0)
    earlier = jnp.arange(docs)[:, None] >= jnp.arange(docs)[None, :]
    stops = jnp.sum(jnp.where(earlier, count[None, :], 0), axis=1)
    starts = stops - count
    unit = jnp.arange(units, dtype=jnp.int32)
    doc = jnp.sum((unit[:, None] >= stops[None, :]).astype(jnp.int32), axis=1)
    doc = jnp.minimum(doc, docs - 1)
    pick = (doc[:, None] == jnp.arange(docs)[None, :]).astype(jnp.int32)

    def of_doc(values):
        return jnp.sum(pick * values[None, :], axis=1)

    block = jnp.clip(of_doc(first - starts) + unit, 0, length // BLOCK - 1)
    return jnp.concatenate(
        [
            block,
            of_doc(bounds),
            of_doc(ends),
            of_doc(starts),
            of_doc(stops),
            starts,
            stops,
            bounds,
            stops[docs - 1 :],
        ]
    ).astype(jnp.int32)


class Units:
    def __init__(self, meta, length, docs):
        self.meta = meta
        self.docs = docs
        self.units = length // BLOCK + docs - 1

    def block(self, unit):
        return self.meta[unit]

    def low(self, unit):
        return self.meta[self.units + unit]

    def high(self, unit):
        return self.meta[2 * self.units + unit]

    def start(self, unit):
        return self.meta[3 * self.units + unit]

    def stop(self, unit):
        return self.meta[4 * self.units + unit]

    def doc_start(self, doc):
        return self.meta[5 * self.units + doc]

    def doc_stop(self, doc):
        return self.meta[5 * self.units + self.docs + doc]

    def bound(self, doc):
        return self.meta[5 * self.units + 2 * self.docs + doc]

    def total(self):
        return self.meta[5 * self.units + 3 * self.docs]

    def inside(self, unit, width):
        place = lax.broadcasted_iota(jnp.int32, (BLOCK, width), 0) + self.block(unit) * BLOCK
        return (place >= self.low(unit)) & (place < self.high(unit))


def rows_of(block):
    return pl.ds(pl.multiple_of(block * BLOCK, BLOCK), BLOCK)


def times(table, value):
    high = value.astype(BF16)
    low = (value - high.astype(F32)).astype(BF16)
    return jnp.dot(
        table[...], jnp.concatenate([high, low, high], axis=0), preferred_element_type=F32
    )


def tap_masks(units, block, width, ahead=0):
    place = lax.broadcasted_iota(jnp.int32, (BLOCK, width), 0) + (block * BLOCK + ahead)
    first = place == units.bound(0)
    second = place == units.bound(0) + 1
    for doc in range(1, units.docs):
        first = first | (place == units.bound(doc))
        second = second | (place == units.bound(doc) + 1)
    return jnp.logical_not(first), jnp.logical_not(first | second)


def delayed(ref, block):
    start = block * BLOCK
    here = ref[rows_of(block), :].astype(F32)
    before = ref[pl.ds(pl.multiple_of(jnp.maximum(start - 16, 0), 16), 16), :].astype(F32)
    joined = jnp.concatenate([before, here], axis=0)
    return (here, pltpu.roll(joined, 1, 0)[16:], pltpu.roll(joined, 2, 0)[16:])


def short_conv(parts, small, branch, masks):
    total = small[9 + branch : 10 + branch, :] + small[branch : branch + 1, :] * parts[0]
    total += jnp.where(masks[0], small[3 + branch : 4 + branch, :] * parts[1], 0.0)
    total += jnp.where(masks[1], small[6 + branch : 7 + branch, :] * parts[2], 0.0)
    return total


def mixer_forward_kernel(
    docs, meta, post, pre, val, filt, small, fwd, inv, branch, mixed, gated, spec, taps, prod
):
    length, width = gated.shape
    blocks = length // BLOCK
    units = Units(meta, length, docs)

    def gate(block, _):
        masks = tap_masks(units, block, width)
        part = short_conv(delayed(val, block), small, 2, masks)
        part *= short_conv(delayed(pre, block), small, 1, masks)
        gated[rows_of(block), :] = part
        mixed[rows_of(block), :] = small[12:13, :] * part
        taps[block] = times(fwd, filt[rows_of(block), :])
        return 0

    lax.fori_loop(0, blocks, gate, 0)

    def transform(unit, _):
        value = gated[rows_of(units.block(unit)), :]
        spec[unit] = times(fwd, jnp.where(units.inside(unit, width), value, 0.0))
        return 0

    lax.fori_loop(0, units.total(), transform, 0)

    def multiply(unit, _):
        for low in range(0, BLOCK, FREQ_CHUNK):
            re, im = pl.ds(low, FREQ_CHUNK), pl.ds(BLOCK + low, FREQ_CHUNK)

            def step(back, total):
                at = unit - back
                s_re, s_im, t_re, t_im = spec[at, re], spec[at, im], taps[back, re], taps[back, im]
                return (
                    total[0] + (s_re * t_re - s_im * t_im),
                    total[1] + (s_re * t_im + s_im * t_re),
                )

            zero = jnp.zeros((FREQ_CHUNK, width), F32)
            total = lax.fori_loop(0, unit - units.start(unit) + 1, step, (zero, zero))
            prod[unit, re] = total[0]
            prod[unit, im] = total[1]
        return 0

    lax.fori_loop(0, units.total(), multiply, 0)

    half = BLOCK // 2

    def bring_back(unit, _):
        last = jnp.maximum(unit - 1, 0)
        old = jnp.where(unit > units.start(unit), prod[last], 0.0)
        new = prod[unit]
        joined = jnp.concatenate(
            [
                new[:half] - old[BLOCK : BLOCK + half],
                new[half:BLOCK] + old[BLOCK + half :],
                new[BLOCK : BLOCK + half] + old[:half],
                new[BLOCK + half :] - old[half:BLOCK],
            ],
            axis=0,
        )
        value = times(inv, joined)
        rows = rows_of(units.block(unit))
        mixed[rows, :] += jnp.where(units.inside(unit, width), value, 0.0)
        return 0

    lax.fori_loop(0, units.total(), bring_back, 0)

    def finish(block, _):
        masks = tap_masks(units, block, width)
        gate_value = short_conv(delayed(post, block), small, 0, masks)
        branch[rows_of(block), :] = (gate_value * mixed[rows_of(block), :]).astype(BF16)
        return 0

    lax.fori_loop(0, blocks, finish, 0)


def mixer_backward_kernel(
    docs,
    meta,
    post,
    pre,
    val,
    filt,
    small,
    fwd,
    inv,
    mixed,
    branch_grad,
    proj_grad,
    filt_grad,
    sums,
    gated,
    gm,
    conv_grad,
    spec,
    taps,
    prod,
):
    length, width = gated.shape
    blocks = length // BLOCK
    units = Units(meta, length, docs)
    half = BLOCK // 2
    sums[...] = jnp.zeros_like(sums)

    def total_rows(value):
        return jnp.sum(value, axis=0, keepdims=True)

    def gate(block, _):
        rows = rows_of(block)
        masks = tap_masks(units, block, width)
        part = short_conv(delayed(val, block), small, 2, masks)
        part *= short_conv(delayed(pre, block), small, 1, masks)
        gated[rows, :] = part
        grad = branch_grad[rows, :].astype(F32)
        mix_grad = grad * short_conv(delayed(post, block), small, 0, masks)
        gm[rows, :] = mix_grad
        conv_grad[0, rows, :] = grad * mixed[rows, :]
        conv_grad[1, rows, :] = small[12:13, :] * mix_grad
        sums[15:16, :] += total_rows(part * mix_grad)
        taps[block] = times(fwd, filt[rows, :])
        return 0

    lax.fori_loop(0, blocks, gate, 0)

    def transform(unit, _):
        rows = rows_of(units.block(unit))
        inside = units.inside(unit, width)
        spec[unit] = times(fwd, jnp.where(inside, gated[rows, :], 0.0))
        prod[unit] = times(fwd, jnp.where(inside, gm[rows, :], 0.0))
        return 0

    lax.fori_loop(0, units.total(), transform, 0)

    def spread(unit, _):
        after = jnp.minimum(unit + 1, units.units - 1)
        new = jnp.where(unit + 1 < units.stop(unit), prod[after], 0.0)
        prod[unit, pl.ds(0, half)] += new[BLOCK : BLOCK + half]
        prod[unit, pl.ds(half, half)] -= new[BLOCK + half :]
        prod[unit, pl.ds(BLOCK, half)] -= new[:half]
        prod[unit, pl.ds(BLOCK + half, half)] += new[half:BLOCK]
        return 0

    lax.fori_loop(0, units.total(), spread, 0)

    def signal_grad(unit, _):
        pieces = []
        for low in range(0, BLOCK, FREQ_CHUNK):
            re, im = pl.ds(low, FREQ_CHUNK), pl.ds(BLOCK + low, FREQ_CHUNK)

            def step(ahead, total):
                at = unit + ahead
                g_re, g_im, t_re, t_im = (
                    prod[at, re],
                    prod[at, im],
                    taps[ahead, re],
                    taps[ahead, im],
                )
                return (
                    total[0] + (g_re * t_re + g_im * t_im),
                    total[1] + (g_im * t_re - g_re * t_im),
                )

            zero = jnp.zeros((FREQ_CHUNK, width), F32)
            pieces.append(lax.fori_loop(0, units.stop(unit) - unit, step, (zero, zero)))
        joined = jnp.concatenate([piece[0] for piece in pieces] + [piece[1] for piece in pieces])
        value = times(inv, joined)
        rows = rows_of(units.block(unit))
        conv_grad[1, rows, :] += jnp.where(units.inside(unit, width), value, 0.0)
        return 0

    lax.fori_loop(0, units.total(), signal_grad, 0)

    def tap_grad(back, _):
        pieces = []
        for low in range(0, BLOCK, FREQ_CHUNK):
            re, im = pl.ds(low, FREQ_CHUNK), pl.ds(BLOCK + low, FREQ_CHUNK)

            def step(unit, total):
                at = unit - back
                g_re, g_im, s_re, s_im = (
                    prod[unit, re],
                    prod[unit, im],
                    spec[at, re],
                    spec[at, im],
                )
                return (
                    total[0] + (g_re * s_re + g_im * s_im),
                    total[1] + (g_im * s_re - g_re * s_im),
                )

            zero = jnp.zeros((FREQ_CHUNK, width), F32)
            total = (zero, zero)
            for doc in range(docs):
                total = lax.fori_loop(
                    units.doc_start(doc) + back, units.doc_stop(doc), step, total
                )
            pieces.append(total)
        joined = jnp.concatenate([piece[0] for piece in pieces] + [piece[1] for piece in pieces])
        filt_grad[rows_of(back), :] = times(inv, joined)
        return 0

    lax.fori_loop(0, blocks, tap_grad, 0)

    def conv_back(block, _):
        rows = rows_of(block)
        masks = tap_masks(units, block, width)
        val_parts, pre_parts, post_parts = (
            delayed(val, block),
            delayed(pre, block),
            delayed(post, block),
        )
        gated_grad = conv_grad[1, rows, :]
        pre_grad = gated_grad * short_conv(val_parts, small, 2, masks)
        val_grad = gated_grad * short_conv(pre_parts, small, 1, masks)
        post_grad = conv_grad[0, rows, :]
        conv_grad[1, rows, :] = pre_grad
        conv_grad[2, rows, :] = val_grad
        for branch, (grad, parts) in enumerate(
            ((post_grad, post_parts), (pre_grad, pre_parts), (val_grad, val_parts))
        ):
            sums[branch : branch + 1, :] += total_rows(grad * parts[0])
            sums[3 + branch : 4 + branch, :] += total_rows(
                jnp.where(masks[0], grad * parts[1], 0.0)
            )
            sums[6 + branch : 7 + branch, :] += total_rows(
                jnp.where(masks[1], grad * parts[2], 0.0)
            )
            sums[9 + branch : 10 + branch, :] += total_rows(grad)
        return 0

    lax.fori_loop(0, blocks, conv_back, 0)

    def spread_taps(block, _):
        start = block * BLOCK
        one, _two = tap_masks(units, block, width, 1)
        _one, two = tap_masks(units, block, width, 2)
        place = lax.broadcasted_iota(jnp.int32, (BLOCK, width), 0) + start
        one = one & (place + 1 < length)
        two = two & (place + 2 < length)
        for branch in range(3):
            here = conv_grad[branch, rows_of(block), :]
            after = conv_grad[
                branch, pl.ds(pl.multiple_of(jnp.minimum(start + BLOCK, length - 8), 8), 8), :
            ]
            joined = jnp.concatenate([here, after], axis=0)
            size = BLOCK + 8
            next_one = pltpu.roll(joined, size - 1, 0)[:BLOCK]
            next_two = pltpu.roll(joined, size - 2, 0)[:BLOCK]
            total = small[branch : branch + 1, :] * here
            total += jnp.where(one, small[3 + branch : 4 + branch, :] * next_one, 0.0)
            total += jnp.where(two, small[6 + branch : 7 + branch, :] * next_two, 0.0)
            rounded = total.astype(BF16)
            proj_grad[rows_of(block), branch * width : (branch + 1) * width] = rounded
            sums[12 + branch : 13 + branch, :] += total_rows(rounded.astype(F32))
        return 0

    lax.fori_loop(0, blocks, spread_taps, 0)


def whole_spec(shape, column=0):
    return pl.BlockSpec(shape, lambda i, meta: (0, column), pipeline_mode=pl.Buffered(1))


def mixer_forward(meta, docs, projected, filt, small, tables):
    length, width = filt.shape
    units = length // BLOCK + docs - 1
    column = [whole_spec((length, width), at) for at in range(3)]
    return pl.pallas_call(
        functools.partial(mixer_forward_kernel, docs),
        out_shape=(
            jax.ShapeDtypeStruct((length, width), BF16),
            jax.ShapeDtypeStruct((length, width), F32),
        ),
        grid_spec=pltpu.PrefetchScalarGridSpec(
            num_scalar_prefetch=1,
            grid=(1,),
            in_specs=column
            + [whole_spec(value.shape) for value in (filt, small, tables[0], tables[1])],
            out_specs=(column[0], column[0]),
            scratch_shapes=[
                pltpu.VMEM((length, width), F32),
                pltpu.VMEM((units, 2 * BLOCK, width), F32),
                pltpu.VMEM((length // BLOCK, 2 * BLOCK, width), F32),
                pltpu.VMEM((units, 2 * BLOCK, width), F32),
            ],
        ),
        compiler_params=pltpu.CompilerParams(vmem_limit_bytes=VMEM_LIMIT),
        cost_estimate=pl.CostEstimate(
            flops=40 * 10**9, bytes_accessed=10 * 10**6, transcendentals=0
        ),
        name="mixer_forward",
    )(meta, projected, projected, projected, filt, small, *tables)


def mixer_backward(meta, docs, projected, filt, small, tables, mixed, branch_grad):
    length, width = filt.shape
    units = length // BLOCK + docs - 1
    column = [whole_spec((length, width), at) for at in range(3)]
    return pl.pallas_call(
        functools.partial(mixer_backward_kernel, docs),
        out_shape=(
            jax.ShapeDtypeStruct((length, 3 * width), BF16),
            jax.ShapeDtypeStruct((length, width), F32),
            jax.ShapeDtypeStruct((16, width), F32),
        ),
        grid_spec=pltpu.PrefetchScalarGridSpec(
            num_scalar_prefetch=1,
            grid=(1,),
            in_specs=column
            + [
                whole_spec(value.shape)
                for value in (filt, small, tables[0], tables[1], mixed, branch_grad)
            ],
            out_specs=(
                whole_spec((length, 3 * width)),
                column[0],
                whole_spec((16, width)),
            ),
            scratch_shapes=[
                pltpu.VMEM((length, width), F32),
                pltpu.VMEM((length, width), F32),
                pltpu.VMEM((3, length, width), F32),
                pltpu.VMEM((units, 2 * BLOCK, width), F32),
                pltpu.VMEM((length // BLOCK, 2 * BLOCK, width), F32),
                pltpu.VMEM((units, 2 * BLOCK, width), F32),
            ],
        ),
        compiler_params=pltpu.CompilerParams(vmem_limit_bytes=VMEM_LIMIT),
        cost_estimate=pl.CostEstimate(
            flops=80 * 10**9, bytes_accessed=16 * 10**6, transcendentals=0
        ),
        name="mixer_backward",
    )(meta, projected, projected, projected, filt, small, *tables, mixed, branch_grad)


def norm_parts(values):
    centre = values - jnp.mean(values, axis=-1, keepdims=True)
    spread = jnp.mean(centre * centre, axis=-1, keepdims=True)
    scale = lax.rsqrt(spread + 1e-05)
    return centre * scale, scale


def project_kernel(inputs, norm, weight, bias, out):
    unit, _ = norm_parts(inputs[...].astype(F32))
    normed = (unit * norm[0:1, :] + norm[1:2, :]).astype(BF16)
    total = jnp.dot(normed, weight[...], preferred_element_type=F32) + bias[...]
    out[...] = total.astype(BF16)


def project(inputs, norm, weight, bias):
    length, depth = inputs.shape
    width = weight.shape[1]
    return pl.pallas_call(
        project_kernel,
        out_shape=jax.ShapeDtypeStruct((length, width), BF16),
        grid=(length // BLOCK,),
        in_specs=[
            pl.BlockSpec((BLOCK, depth), lambda i: (i, 0)),
            pl.BlockSpec(norm.shape, lambda i: (0, 0)),
            pl.BlockSpec(weight.shape, lambda i: (0, 0)),
            pl.BlockSpec(bias.shape, lambda i: (0, 0)),
        ],
        out_specs=pl.BlockSpec((BLOCK, width), lambda i: (i, 0)),
        compiler_params=pltpu.CompilerParams(vmem_limit_bytes=VMEM_LIMIT),
        cost_estimate=pl.CostEstimate(
            flops=2 * length * depth * width, bytes_accessed=10 * 10**6, transcendentals=0
        ),
        name="project",
    )(inputs, norm, weight, bias)


def gelu_pair(u):
    root = math.sqrt(2.0 / math.pi)
    square = u * u
    curve = jnp.tanh(root * (u + 0.044715 * (u * square)))
    value = 0.5 * u * (1.0 + curve)
    slope = 0.5 * (1.0 + curve) + 0.5 * u * (1.0 - curve * curve) * (
        root * (1.0 + 3.0 * 0.044715 * square)
    )
    return value, slope


def feed_forward_kernel(
    masks,
    place,
    normed_own,
    normed_other,
    grad_own,
    grad_other,
    up_bias,
    *rest,
):
    count = 2 * len(masks)
    pieces, rest = rest[:count], rest[count:]
    out_own, out_other, back_own, back_other, bias_grad = rest[:5]
    piece_grads, rest = rest[5 : 5 + count], rest[5 + count :]
    normed, grad, out_total, back_total, weights, grads, load_sems, store_sems = rest
    rows, depth = normed_own.shape
    tiles, pos_count, units, own_width, width = weights.shape
    half = tiles // 2
    columns = depth // width
    down_units = (units - 2 * tiles) // columns
    loads = [
        (normed_own, normed.at[pl.ds(0, rows)]),
        (normed_other, normed.at[pl.ds(rows, rows)]),
        (grad_own, grad.at[pl.ds(0, rows)]),
        (grad_other, grad.at[pl.ds(rows, rows)]),
    ]
    stores = []
    for at, mask in enumerate(masks):
        origin = jnp.bitwise_xor(place[0], mask)
        for side in range(2):
            part = pl.ds(side * half, half)
            loads.append((pieces[2 * at + side], weights.at[part, origin]))
            stores.append((grads.at[part, origin], piece_grads[2 * at + side]))
    loads = [
        pltpu.make_async_copy(source, target, load_sems.at[at])
        for at, (source, target) in enumerate(loads)
    ]
    for copy in loads:
        copy.start()
    out_total[...] = jnp.zeros_like(out_total)
    back_total[...] = jnp.zeros_like(back_total)
    for copy in loads:
        copy.wait()

    def step(tile, _):
        up = jnp.concatenate(
            [
                weights[block, :, side * tiles + tile].reshape(pos_count * own_width, width)
                for block in range(tiles)
                for side in range(2)
            ],
            axis=0,
        )
        down = jnp.concatenate(
            [
                weights[
                    tile, :, 2 * tiles + at * down_units : 2 * tiles + (at + 1) * down_units
                ].reshape(width, width)
                for at in range(columns)
            ],
            axis=1,
        )
        pre = jnp.dot(normed[...], up, preferred_element_type=F32) + up_bias[pl.ds(tile, 1), :]
        hidden, slope = gelu_pair(pre)
        hidden = hidden.astype(BF16)
        hidden_grad = lax.dot_general(
            grad[...], down, (((1,), (1,)), ((), ())), preferred_element_type=F32
        )
        pre_grad = hidden_grad * slope
        bias_grad[pl.ds(tile, 1), :] = jnp.sum(pre_grad, axis=0, keepdims=True)
        pre_grad = pre_grad.astype(BF16)
        out_total[...] += jnp.dot(hidden, down, preferred_element_type=F32)
        back_total[...] += lax.dot_general(
            pre_grad, up, (((1,), (1,)), ((), ())), preferred_element_type=F32
        )
        down_grad = lax.dot_general(
            hidden, grad[...], (((0,), (0,)), ((), ())), preferred_element_type=F32
        ).astype(BF16)
        for at in range(columns):
            grads[tile, :, 2 * tiles + at * down_units : 2 * tiles + (at + 1) * down_units] = (
                down_grad[:, at * width : (at + 1) * width].reshape(
                    pos_count, down_units, own_width, width
                )
            )
        up_grad = lax.dot_general(
            normed[...], pre_grad, (((0,), (0,)), ((), ())), preferred_element_type=F32
        ).astype(BF16)
        size = pos_count * own_width
        for block in range(tiles):
            for side in range(2):
                low = (2 * block + side) * size
                grads[block, :, side * tiles + tile] = up_grad[low : low + size].reshape(
                    pos_count, own_width, width
                )
        return 0

    lax.fori_loop(0, tiles, step, 0)
    normed[:rows] = out_total[rows:].astype(BF16)
    normed[rows:] = back_total[rows:].astype(BF16)
    stores += [
        (back_total.at[pl.ds(0, rows)], back_own),
        (normed.at[pl.ds(rows, rows)], back_other),
        (out_total.at[pl.ds(0, rows)], out_own),
        (normed.at[pl.ds(0, rows)], out_other),
    ]
    stores = [
        pltpu.make_async_copy(source, target, store_sems.at[at])
        for at, (source, target) in enumerate(stores)
    ]
    for copy in stores:
        copy.start()
    for copy in stores:
        copy.wait()


def feed_forward(place, masks, normed_own, normed_other, grad_own, grad_other, up_bias, pieces):
    rows, depth = normed_own.shape
    tiles, width = up_bias.shape
    piece = pieces[0].shape
    whole = (tiles, len(masks)) + piece[1:]
    anywhere = pl.BlockSpec(memory_space=pl.ANY)
    bias = pl.BlockSpec((tiles, width), lambda i, place: (0, 0))
    count = len(pieces)
    return pl.pallas_call(
        functools.partial(feed_forward_kernel, masks),
        out_shape=(
            jax.ShapeDtypeStruct((rows, depth), F32),
            jax.ShapeDtypeStruct((rows, depth), BF16),
            jax.ShapeDtypeStruct((rows, depth), F32),
            jax.ShapeDtypeStruct((rows, depth), BF16),
            jax.ShapeDtypeStruct((tiles, width), F32),
        )
        + (jax.ShapeDtypeStruct(piece, BF16),) * count,
        grid_spec=pltpu.PrefetchScalarGridSpec(
            num_scalar_prefetch=1,
            grid=(1,),
            in_specs=[anywhere] * 4 + [bias] + [anywhere] * count,
            out_specs=(anywhere,) * 4 + (bias,) + (anywhere,) * count,
            scratch_shapes=[
                pltpu.VMEM((2 * rows, depth), BF16),
                pltpu.VMEM((2 * rows, depth), BF16),
                pltpu.VMEM((2 * rows, depth), F32),
                pltpu.VMEM((2 * rows, depth), F32),
                pltpu.VMEM(whole, BF16),
                pltpu.VMEM(whole, BF16),
                pltpu.SemaphoreType.DMA((4 + count,)),
                pltpu.SemaphoreType.DMA((4 + count,)),
            ],
        ),
        compiler_params=pltpu.CompilerParams(vmem_limit_bytes=VMEM_LIMIT),
        cost_estimate=pl.CostEstimate(
            flops=12 * 2 * rows * depth * width * tiles,
            bytes_accessed=30 * 10**6,
            transcendentals=2 * rows * width * tiles,
        ),
        name="feed_forward",
    )(place, normed_own, normed_other, grad_own, grad_other, up_bias, *pieces)


def swap(value, axis, bit):
    count = lax.axis_size(axis)
    return lax.ppermute(value, axis, [(at, at ^ bit) for at in range(count)])


class Copies:
    def __init__(self, local_sems, send_sems, got_sems):
        self.local_sems, self.send_sems, self.got_sems = local_sems, send_sems, got_sems
        self.locals = 0
        self.names = {}
        self.pending = []

    def local(self, source, target):
        copy = pltpu.make_async_copy(source, target, self.local_sems.at[self.locals])
        self.locals += 1
        copy.start()
        return copy

    def remote(self, name, source, target, device):
        at = self.names.setdefault(name, len(self.names))
        return pltpu.make_async_remote_copy(
            src_ref=source,
            dst_ref=target,
            send_sem=self.send_sems.at[at],
            recv_sem=self.got_sems.at[at],
            device_id=device,
            device_id_type=pl.DeviceIdType.MESH,
        )

    def send(self, name, source, target, device, when=None):
        copy = self.remote(name, source, target, device)
        if when is None:
            copy.start()
        else:
            pl.when(when)(copy.start)
        self.pending.append((copy, when))

    def got(self, name, target, device):
        self.remote(name, target, target, device).wait_recv()

    def finish(self):
        for copy, when in self.pending:
            if when is None:
                copy.wait_send()
            else:
                pl.when(when)(copy.wait_send)


def greet(devices):
    barrier = pltpu.get_barrier_semaphore()
    for device in devices:
        pl.semaphore_signal(
            barrier, inc=1, device_id=device, device_id_type=pl.DeviceIdType.MESH
        )
    pl.semaphore_wait(barrier, len(devices))


def lane_masks(bits):
    masks, found = [0], []
    for bit in bits:
        found += [(mask ^ bit, bit) for mask in masks]
        masks += [mask ^ bit for mask in masks]
    return found


def gather_kernel(
    dims,
    inputs,
    weight,
    up,
    down,
    out,
    small,
    row_in,
    weight_in,
    bundle,
    owned,
    local_sems,
    send_sems,
    got_sems,
):
    rz_count, pos_count = dims
    z, core, pos = lax.axis_index("rz"), lax.axis_index("core"), lax.axis_index("pos")
    bits = bits_of(pos_count)
    lanes = [lane_masks(bits), lane_masks(bits[::-1])]
    own_width, model_width = out.shape
    chan = model_width // pos_count
    tile = bundle.shape[3]
    columns = model_width // tile
    half = model_width // 2
    middle = rz_count // 2
    copies = Copies(local_sems, send_sems, got_sems)
    other = {"core": 1 - core}
    right, left = {"rz": z + 1}, {"rz": z - 1}
    has_right, has_left = z + 1 < rz_count, z > 0
    greet(
        [other]
        + [{"rz": (z + step) % rz_count} for step in range(1, rz_count)]
        + [{"pos": jnp.bitwise_xor(pos, mask)} for mask in range(1, pos_count)]
    )

    def branch_cols(owner):
        return pl.ds(pl.multiple_of(owner * chan, chan), chan)

    for mask in range(1, pos_count):
        owner = jnp.bitwise_xor(pos, mask)
        for at in range(3):
            copies.send(
                ("in", mask, at),
                weight.at[at, :, branch_cols(owner)],
                weight_in.at[z, core, pos, :, pl.ds(at * chan, chan)],
                {"pos": owner},
            )

    def lane_cols(lane):
        return pl.ds(lane * half, half)

    def send_rows(lane, mask, bit):
        origin = jnp.bitwise_xor(pos, mask ^ bit)
        cols = lane_cols(lane)
        source = inputs.at[:, cols] if mask == bit else row_in.at[origin, :, cols]
        copies.send(
            ("rows", lane, mask),
            source,
            row_in.at[origin, :, cols],
            {"pos": jnp.bitwise_xor(pos, bit)},
        )

    for at in range(len(bits)):
        for lane in range(2):
            bit = (bits, bits[::-1])[lane][at]
            send_rows(lane, bit, bit)

    def up_cols(at, side):
        return pl.ds(pl.multiple_of((2 * at + side) * tile, tile), tile)

    for at in range(rz_count):
        copies.send(
            ("up", at),
            up.at[:, up_cols(at, 1 - core)],
            bundle.at[z, core * rz_count + at],
            other,
        )
    local_in = [
        copies.local(
            weight.at[at, :, branch_cols(pos)],
            weight_in.at[z, core, pos, :, pl.ds(at * chan, chan)],
        )
        for at in range(3)
    ]
    local_owned = [
        copies.local(out, owned.at[core, pos, z, pl.ds(0, own_width)]),
        copies.local(small, owned.at[core, pos, z, pl.ds(own_width, small.shape[0])]),
    ]
    local_bundle = [
        copies.local(up.at[:, up_cols(at, core)], bundle.at[z, core * rz_count + at])
        for at in range(rz_count)
    ]
    down_units = down.shape[0] // own_width
    for col in range(columns):
        for at in range(down_units):
            local_bundle.append(
                copies.local(
                    down.at[pl.ds(at * own_width, own_width), pl.ds(col * tile, tile)],
                    bundle.at[z, 2 * rz_count + col * down_units + at],
                )
            )
    local_rows = copies.local(inputs, row_in.at[pos])

    flows = {
        "in": lambda origin: weight_in.at[origin, core],
        "owned": lambda origin: owned.at[core, pos, origin],
        "bundle": lambda origin: bundle.at[origin],
    }

    def line_start(flow):
        block = flows[flow](z)
        copies.send((flow, "right", 1), block, block, right, has_right)
        copies.send((flow, "left", 1), block, block, left, has_left)

    def line_step(flow, distance, arrived=None):
        for side, origin, there, onward, has_next in (
            ("right", z - distance, z >= distance, right, has_right),
            ("left", z + distance, z + distance < rz_count, left, has_left),
        ):
            safe = jnp.clip(origin, 0, rz_count - 1)
            block = flows[flow](safe)

            def wait(block=block, side=side, onward=onward):
                copies.got((flow, side, distance), block, onward)

            pl.when(there)(wait)
            if distance + 1 < rz_count:
                copies.send((flow, side, distance + 1), block, block, onward, there & has_next)
            if arrived is not None:
                arrived(side, distance, safe, there)

    def share_in(side, distance, origin, there):
        block = weight_in.at[origin, core]
        copies.send(("in core", side, distance), block, block, other, there)

    for copy in local_in:
        copy.wait()
    for mask in range(1, pos_count):
        owner = jnp.bitwise_xor(pos, mask)
        for at in range(3):
            copies.got(
                ("in", mask, at),
                weight_in.at[z, core, owner, :, pl.ds(at * chan, chan)],
                {"pos": owner},
            )
    line_start("in")
    block = weight_in.at[z, core]
    copies.send(("in core", "own", 0), block, block, other)
    for copy in local_owned:
        copy.wait()
    line_start("owned")
    for copy in local_bundle:
        copy.wait()
    for at in range(rz_count):
        copies.got(("up", at), bundle.at[z, (1 - core) * rz_count + at], other)
    line_start("bundle")
    for distance in range(1, rz_count):
        line_step("in", distance, share_in)
        line_step("owned", distance)

    def owned_half(side, origin, lane):
        return owned.at[side, origin, pl.ds(lane * middle, middle)]

    def send_owned(lane, mask, bit):
        block = owned_half(core, jnp.bitwise_xor(pos, mask ^ bit), lane)
        copies.send(
            ("owned pos", lane, mask), block, block, {"pos": jnp.bitwise_xor(pos, bit)}
        )

    def share_owned(lane, mask):
        block = owned_half(core, jnp.bitwise_xor(pos, mask), lane)
        copies.send(("owned core", lane, mask), block, block, other)

    def got_rows(lane, mask, bit):
        block = row_in.at[jnp.bitwise_xor(pos, mask), :, lane_cols(lane)]
        copies.got(("rows", lane, mask), block, {"pos": jnp.bitwise_xor(pos, bit)})
        later = (bits, bits[::-1])[lane]
        for onward in later[later.index(bit) + 1 :]:
            send_rows(lane, mask ^ onward, onward)

    def got_owned(lane, mask, bit):
        block = owned_half(core, jnp.bitwise_xor(pos, mask), lane)
        copies.got(("owned pos", lane, mask), block, {"pos": jnp.bitwise_xor(pos, bit)})
        later = (bits, bits[::-1])[lane]
        for onward in later[later.index(bit) + 1 :]:
            send_owned(lane, mask ^ onward, onward)
        share_owned(lane, mask)

    first = [lanes[lane][0] for lane in range(2)]
    for lane in range(2):
        got_rows(lane, *first[lane])
    for at in range(len(bits)):
        for lane in range(2):
            bit = (bits, bits[::-1])[lane][at]
            send_owned(lane, bit, bit)
    for lane in range(2):
        share_owned(lane, 0)
    for distance in range(1, rz_count - 1):
        line_step("bundle", distance)
    for at in range(1, pos_count - 1):
        for lane in range(2):
            got_rows(lane, *lanes[lane][at])
    for at in range(pos_count - 1):
        for lane in range(2):
            got_owned(lane, *lanes[lane][at])
    line_step("bundle", rz_count - 1)
    local_rows.wait()
    for at in range(pos_count):
        for lane in range(2):
            copies.got(
                ("owned core", lane, at), owned_half(1 - core, jnp.bitwise_xor(pos, at), lane), other
            )
    copies.got(("in core", "own", 0), weight_in.at[z, 1 - core], other)
    for distance in range(1, rz_count):
        for side, origin, there in (
            ("right", z - distance, z >= distance),
            ("left", z + distance, z + distance < rz_count),
        ):
            block = weight_in.at[jnp.clip(origin, 0, rz_count - 1), 1 - core]

            def wait(block=block, side=side, distance=distance):
                copies.got(("in core", side, distance), block, other)

            pl.when(there)(wait)
    copies.finish()


def gather(dims, inputs, weight, up, down, out, small):
    rz_count, pos_count = dims
    part_len, model_width = inputs.shape
    own_width = out.shape[0]
    tile = pos_count * down.shape[0]
    units = 2 * rz_count + (down.shape[0] // own_width) * (model_width // tile)
    anywhere = pl.BlockSpec(memory_space=pl.ANY)
    locals_count = 3 + 2 + units + 1
    remote_count = (
        3 * (pos_count - 1)
        + 2 * (pos_count - 1)
        + rz_count
        + 3 * 2 * rz_count
        + 2 * rz_count
        + 2 * 2 * pos_count
    )
    return pl.pallas_call(
        functools.partial(gather_kernel, dims),
        out_shape=(
            jax.ShapeDtypeStruct((pos_count, part_len, model_width), BF16),
            jax.ShapeDtypeStruct(
                (rz_count, 2, pos_count, own_width, 3 * model_width // pos_count), BF16
            ),
            jax.ShapeDtypeStruct((rz_count, units, own_width, tile), BF16),
            jax.ShapeDtypeStruct(
                (2, pos_count, rz_count, own_width + small.shape[0], model_width), BF16
            ),
        ),
        in_specs=[pl.BlockSpec(memory_space=pltpu.VMEM)] * 6,
        out_specs=(anywhere,) * 4,
        scratch_shapes=[
            pltpu.SemaphoreType.DMA((locals_count,)),
            pltpu.SemaphoreType.DMA((remote_count,)),
            pltpu.SemaphoreType.DMA((remote_count,)),
        ],
        compiler_params=pltpu.CompilerParams(collective_id=1, has_side_effects=True),
        cost_estimate=pl.CostEstimate(flops=10**6, bytes_accessed=10**7, transcendentals=0),
        name="gather",
    )(inputs, weight, up, down, out, small)


class LineSum:
    def __init__(self, copies, name, count, z, chunk, sent, got):
        self.copies, self.name, self.count, self.z = copies, name, count, z
        self.chunk, self.sent, self.got_ref = chunk, sent, got

    def sides(self):
        last = self.count - 1
        return (
            (0, self.z, 1, {"rz": self.z + 1}, {"rz": self.z - 1}),
            (1, last - self.z, -1, {"rz": self.z - 1}, {"rz": self.z + 1}),
        )

    def step(self, step):
        count = self.count
        for side, place, direction, onward, back in self.sides():
            sends = (place < step) & (place + 1 < count)
            at = count - step + place
            at = jnp.clip(at if direction == 1 else count - 1 - at, 0, count - 1)
            target = self.sent.at[side, step - 1]

            def first(at=at, side=side):
                self.sent[side, step - 1] = self.chunk(at).astype(BF16)

            def later(at=at, side=side, back=back):
                self.copies.got((self.name, side, step - 1), self.got_ref.at[side, step - 2], back)
                self.sent[side, step - 1] = (
                    self.chunk(at) + self.got_ref[side, step - 2].astype(F32)
                ).astype(BF16)

            pl.when(sends & (place == 0))(first)
            if step > 1:
                pl.when(sends & (place > 0))(later)
            self.copies.send(
                (self.name, side, step), target, self.got_ref.at[side, step - 1], onward, sends
            )

    def total(self, result):
        last = self.count - 1
        result[...] = self.chunk(self.z)
        for side, place, _, _, back in self.sides():

            def add(side=side, back=back):
                self.copies.got((self.name, side, last), self.got_ref.at[side, last - 1], back)
                result[...] += self.got_ref[side, last - 1].astype(F32)

            pl.when(place > 0)(add)


class PieceSum:
    def __init__(self, copies, name, pos, orders, piece, got):
        self.copies, self.name, self.pos, self.orders = copies, name, pos, orders
        self.piece, self.got_ref = piece, got

    def masks(self, side, stage):
        order = self.orders[side]
        found = [0]
        for bit in order[stage:]:
            found += [mask ^ bit for mask in found]
        return [mask for mask in found if mask & order[stage]]

    def device(self, side, stage):
        return {"pos": jnp.bitwise_xor(self.pos, self.orders[side][stage])}

    def send(self, side, stage, mask):
        self.copies.send(
            (self.name, side, mask),
            self.piece(side, mask),
            self.got_ref(side, mask),
            self.device(side, stage),
        )

    def got(self, side, stage, mask):
        self.copies.got(
            (self.name, side, mask), self.got_ref(side, mask), self.device(side, stage)
        )

    def add(self, side, stage, mask):
        target = self.piece(side, mask ^ self.orders[side][stage])
        target[...] = (
            target[...].astype(F32) + self.got_ref(side, mask)[...].astype(F32)
        ).astype(BF16)

    def settle(self, stage):
        for side in range(2):
            onward = self.masks(side, stage + 1) if stage + 1 < len(self.orders[side]) else []
            masks = self.masks(side, stage)
            bit = self.orders[side][stage]
            for mask in sorted(masks, key=lambda mask: (mask ^ bit) not in onward):
                self.got(side, stage, mask)
                self.add(side, stage, mask)
                if mask ^ bit in onward:
                    self.send(side, stage + 1, mask ^ bit)


def last_sums_kernel(
    dims,
    kept,
    row_in,
    proj_grad,
    weight_in,
    norm,
    grad_residual,
    out_parts,
    token_lines,
    chan_lines,
    inner,
    *rest,
):
    rz_count, pos_count = dims
    count = 2 * len(kept[0])
    own_pieces, moved_pieces, rest = rest[:count], rest[count : 2 * count], rest[2 * count :]
    input_grad, in_grad, up_grad, down_grad, out_grad, lines_out, inner_out = rest[:7]
    rest = rest[7:]
    (
        rows_v,
        proj_v,
        pieces_v,
        moved_v,
        pieces_got,
        bundle_sent,
        bundle_got,
        bundle_total,
        up_sent,
        up_got,
        e_v,
        e_got,
        in_total,
        in_sent,
        in_got,
        in_line_sent,
        in_line_got,
        in_mine,
        in_out,
        in_back,
        outs_v,
        outs_got,
        outs_line_sent,
        outs_line_got,
        outs_total,
        packed,
        packed_got,
        packed_pos,
        packed_total,
        local_sems,
        send_sems,
        got_sems,
    ) = rest
    z, core, pos = lax.axis_index("rz"), lax.axis_index("core"), lax.axis_index("pos")
    rows_count = 2 * rz_count
    row = z * 2 + core
    bits = bits_of(pos_count)
    orders = (bits, bits[::-1])
    middle = rz_count // 2
    part_len, model_width = grad_residual.shape
    half = model_width // 2
    own_width, tile = up_sent.shape[1:]
    width = weight_in.shape[1]
    chan = width // 3
    columns = model_width // tile
    copies = Copies(local_sems, send_sems, got_sems)
    other = {"core": 1 - core}

    def row_device(at):
        return {"rz": at // 2, "core": at % 2}

    loads = []
    for side in range(2):
        for mask in kept[side]:
            at = 2 * kept[side].index(mask) + side
            part = pl.ds(side * middle, middle)
            loads.append(copies.local(own_pieces[at], pieces_v.at[kept[side].index(mask), part]))
            loads.append(copies.local(moved_pieces[at], moved_v.at[kept[side].index(mask), part]))
    masks = sorted(range(pos_count), key=lambda mask: -bin(mask).count("1"))
    row_loads = []
    for mask in masks:
        block = pl.ds(pl.multiple_of(jnp.bitwise_xor(pos, mask) * part_len, part_len), part_len)
        row_loads.append(
            (
                copies.local(row_in.at[block], rows_v.at[mask]),
                copies.local(proj_grad.at[block], proj_v.at[mask]),
            )
        )
    greet(
        [row_device((row + step) % rows_count) for step in range(1, rows_count)]
        + [{"pos": jnp.bitwise_xor(pos, mask)} for mask in range(1, pos_count)]
    )

    def half_ref(ref, slot, side):
        return ref.at[slot, pl.ds(side * middle, middle)]

    bundle = PieceSum(
        copies,
        "bundle",
        pos,
        orders,
        lambda side, mask: half_ref(pieces_v, kept[side].index(mask), side),
        lambda side, mask: half_ref(pieces_got, kept[side].index(mask), side),
    )
    for copy in loads:
        copy.wait()
    for side in range(2):
        second = bundle.masks(side, 1)
        for mask in sorted(kept[side], key=lambda mask: mask not in second):
            slot = kept[side].index(mask)
            for at in range(middle):
                place = side * middle + at
                pieces_v[slot, place] = (
                    pieces_v[slot, place].astype(F32) + moved_v[slot, place].astype(F32)
                ).astype(BF16)
            if mask in second:
                bundle.send(side, 1, mask)

    outs = PieceSum(
        copies,
        "outs",
        pos,
        orders,
        lambda side, mask: outs_v.at[pl.ds(side * middle, middle), jnp.bitwise_xor(pos, mask)],
        lambda side, mask: outs_got.at[mask, pl.ds(side * middle, middle)],
    )
    outs_v[...] = out_parts[...]
    for side in range(2):
        for mask in outs.masks(side, 0):
            outs.send(side, 0, mask)

    e_sums = PieceSum(
        copies,
        "rows",
        pos,
        orders,
        lambda side, mask: e_v.at[side, mask],
        lambda side, mask: e_got.at[side, mask],
    )
    in_total[...] = jnp.zeros_like(in_total)
    packed_total[...] = jnp.zeros_like(packed_total)
    packed[...] = jnp.zeros_like(packed)
    sums = (jnp.zeros((1, model_width), F32), jnp.zeros((1, model_width), F32))
    for mask, row_load in zip(masks, row_loads, strict=True):
        for copy in row_load:
            copy.wait()

        def tile_step(at, sums, mask=mask):
            rows = pl.ds(pl.multiple_of(at * BLOCK, BLOCK), BLOCK)
            unit, _ = norm_parts(rows_v[mask, rows].astype(F32))
            normed = (unit * norm[0:1, :] + norm[1:2, :]).astype(BF16)
            grad = proj_v[mask, rows]
            cotangent = lax.dot_general(
                grad, weight_in[...], (((1,), (1,)), ((), ())), preferred_element_type=F32
            )
            e_v[0, mask, rows] = cotangent[:, :half].astype(BF16)
            e_v[1, mask, rows] = cotangent[:, half:].astype(BF16)
            in_total[...] += lax.dot_general(
                normed, grad, (((0,), (0,)), ((), ())), preferred_element_type=F32
            )
            return (
                sums[0] + jnp.sum(cotangent * unit, axis=0, keepdims=True),
                sums[1] + jnp.sum(cotangent, axis=0, keepdims=True),
            )

        sums = lax.fori_loop(0, part_len // BLOCK, tile_step, sums)
        for side in range(2):
            if mask in e_sums.masks(side, 0):
                e_sums.send(side, 0, mask)

    block_rows = pos_count * own_width
    for at in range(rz_count):
        rows = pl.ds(pl.multiple_of((2 * at + 1 - core) * block_rows, block_rows), block_rows)
        in_sent[at] = in_total[rows, :].astype(BF16)
    copies.send(("in core",), in_sent, in_got, other)

    groups = model_width // 128
    per = rows_count // groups
    token_rows, chan_rows = token_lines.shape[0], chan_lines.shape[0]
    inner_rows = inner.shape[0] // groups
    line_rows = token_rows + chan_rows
    for at in range(groups):
        lanes = pl.ds(at * 128, 128)
        packed[at, 0:token_rows] = token_lines[:, lanes]
        packed[at, 0:1] = sums[0][:, at * 128 : (at + 1) * 128]
        packed[at, 1:2] = sums[1][:, at * 128 : (at + 1) * 128]
        packed[at, line_rows:] = inner[pl.ds(at * inner_rows, inner_rows), :]
    for at in range(chan // 128):
        packed[pos * (chan // 128) + at, token_rows:line_rows] = chan_lines[
            :, pl.ds(at * 128, 128)
        ]

    def owns(at):
        return None if per == 1 else at % per == 0

    def when(condition, action):
        if condition is None:
            action()
        else:
            pl.when(condition)(action)

    for step in range(1, rows_count):
        to = (row + step) % rows_count
        copies.send(
            ("lines", step), packed.at[to // per], packed_got.at[step], row_device(to), owns(to)
        )

    for stage in range(1, len(bits)):
        bundle.settle(stage)
    outs.settle(0)
    zero_slot = kept[0].index(0)
    bundle_line = LineSum(
        copies,
        "bundle line",
        rz_count,
        z,
        lambda at: pieces_v[zero_slot, at].astype(F32),
        bundle_sent,
        bundle_got,
    )
    bundle_line.step(1)
    copies.got(("in core",), in_got, other)

    def in_chunk(at):
        rows = pl.ds(pl.multiple_of((2 * at + core) * block_rows, block_rows), block_rows)
        return in_total[rows, :] + in_got[at].astype(F32)

    in_line = LineSum(copies, "in line", rz_count, z, in_chunk, in_line_sent, in_line_got)
    in_line.step(1)
    e_sums.settle(0)

    def add_lines():
        packed_total[...] = packed[row // per]
        for step in range(1, rows_count):
            copies.got(("lines", step), packed_got.at[step], row_device((row - step) % rows_count))
            packed_total[...] += packed_got[step]
        packed_pos[pos] = packed_total[...]

    when(owns(row), add_lines)
    for mask in range(1, pos_count):
        copies.send(
            ("lines pos", mask),
            packed_total,
            packed_pos.at[pos],
            {"pos": jnp.bitwise_xor(pos, mask)},
            owns(row),
        )
    for stage in range(1, len(bits)):
        outs.settle(stage)
    outs_line = LineSum(
        copies,
        "outs line",
        rz_count,
        z,
        lambda at: outs_v[at, pos].astype(F32),
        outs_line_sent,
        outs_line_got,
    )
    outs_line.step(1)
    for step in range(2, rz_count):
        in_line.step(step)
        outs_line.step(step)
        bundle_line.step(step)
        if step == 2:
            for stage in range(1, len(bits)):
                e_sums.settle(stage)

    def input_step(at, _):
        rows = pl.ds(pl.multiple_of(at * BLOCK, BLOCK), BLOCK)
        unit, scale = norm_parts(rows_v[0, rows].astype(F32))
        cotangent = jnp.concatenate(
            [e_v[0, 0, rows].astype(F32), e_v[1, 0, rows].astype(F32)], axis=1
        )
        scaled = cotangent * norm[0:1, :]
        grad = scale * (
            scaled
            - jnp.mean(scaled, axis=-1, keepdims=True)
            - unit * jnp.mean(scaled * unit, axis=-1, keepdims=True)
        )
        input_grad[rows, :] = (grad_residual[rows, :] + grad).astype(BF16)
        return 0

    lax.fori_loop(0, part_len // BLOCK, input_step, 0)

    def sum_lines():
        for mask in range(1, pos_count):
            owner = jnp.bitwise_xor(pos, mask)
            copies.got(("lines pos", mask), packed_pos.at[owner], {"pos": owner})
        total = packed_pos[0]
        for at in range(1, pos_count):
            total = total + packed_pos[at]
        lines_out[...] = total[:line_rows]
        inner_out[row // per] = total[line_rows:]

    when(owns(row), sum_lines)
    for step in range(1, rows_count):
        to = (row + step) % rows_count
        block = inner_out.at[row // per]
        copies.send(("inner", step), block, block, row_device(to), owns(row))
        if step < per:
            copies.send(
                ("lines row", step),
                lines_out,
                lines_out,
                row_device(to),
                owns(row),
            )

    in_line.total(in_mine)
    for mask in range(1, pos_count):
        owner = jnp.bitwise_xor(pos, mask)
        rows = pl.ds(pl.multiple_of(owner * own_width, own_width), own_width)
        in_out[mask] = in_mine[rows, :].astype(BF16)
        copies.send(("in pos", mask), in_out.at[mask], in_back.at[mask], {"pos": owner})
    mine = in_mine[pl.ds(pl.multiple_of(pos * own_width, own_width), own_width), :]
    cols = pl.ds(pl.multiple_of(pos * chan, chan), chan)
    for at in range(3):
        in_grad[at, :, cols] = mine[:, at * chan : (at + 1) * chan]

    outs_line.total(outs_total)
    out_grad[...] = outs_total[...]
    bundle_line.total(bundle_total)
    up_sent[...] = bundle_total[
        pl.ds(pl.multiple_of((1 - core) * rz_count, rz_count), rz_count)
    ].astype(BF16)
    copies.send(("up core",), up_sent, up_got, other)
    down_units = (bundle_total.shape[0] - 2 * rz_count) // columns
    for col in range(columns):
        for at in range(down_units):
            down_grad[at * own_width : (at + 1) * own_width, col * tile : (col + 1) * tile] = (
                bundle_total[2 * rz_count + col * down_units + at]
            )
    for at in range(rz_count):
        cols = pl.ds(pl.multiple_of((2 * at + core) * tile, tile), tile)
        up_grad[:, cols] = bundle_total[core * rz_count + at]
    for mask in range(1, pos_count):
        owner = jnp.bitwise_xor(pos, mask)
        copies.got(("in pos", mask), in_back.at[mask], {"pos": owner})
        cols = pl.ds(pl.multiple_of(owner * chan, chan), chan)
        for at in range(3):
            in_grad[at, :, cols] = in_back[mask, :, at * chan : (at + 1) * chan].astype(F32)
    copies.got(("up core",), up_got, other)
    for at in range(rz_count):
        cols = pl.ds(pl.multiple_of((2 * at + 1 - core) * tile, tile), tile)
        up_grad[:, cols] = up_got[at].astype(F32)
    for step in range(1, rows_count):
        origin = (row - step) % rows_count

        def take(step=step, origin=origin):
            copies.got(("inner", step), inner_out.at[origin // per], row_device(origin))

        when(owns(origin), take)
        if step < per:

            def take_lines(step=step, origin=origin):
                copies.got(("lines row", step), lines_out, row_device(origin))

            when(origin == row // per * per, take_lines)
    copies.finish()


def last_sums(
    dims,
    kept,
    row_in,
    proj_grad,
    weight_in,
    norm,
    grad_residual,
    out_parts,
    token_lines,
    chan_lines,
    inner,
    own_pieces,
    moved_pieces,
):
    rz_count, pos_count = dims
    part_len, model_width = grad_residual.shape
    piece = own_pieces[0].shape
    units, own_width, tile = piece[1:]
    width = weight_in.shape[1]
    block_rows = pos_count * own_width
    groups = model_width // 128
    line_rows = token_lines.shape[0] + chan_lines.shape[0]
    inner_rows = inner.shape[0] // groups
    slots = len(kept[0])
    steps = rz_count - 1
    rows_count = 2 * rz_count
    ff_own = (units - 2 * rz_count) * own_width * tile // model_width
    anywhere = pl.BlockSpec(memory_space=pl.ANY)
    inside = pl.BlockSpec(memory_space=pltpu.VMEM)
    local_count = 4 * len(kept[0]) + 2 * pos_count
    remote_count = (
        3 * 2 * pos_count + 3 * 2 * steps + 2 + 3 * rows_count + 3 * pos_count
    )
    half = model_width // 2
    vmem = pltpu.VMEM
    return pl.pallas_call(
        functools.partial(last_sums_kernel, dims, kept),
        out_shape=(
            jax.ShapeDtypeStruct((part_len, model_width), BF16),
            jax.ShapeDtypeStruct((3, own_width, model_width), F32),
            jax.ShapeDtypeStruct((own_width, 2 * rz_count * tile), F32),
            jax.ShapeDtypeStruct((ff_own, model_width), F32),
            jax.ShapeDtypeStruct((own_width, model_width), F32),
            jax.ShapeDtypeStruct((line_rows, 128), F32),
            jax.ShapeDtypeStruct((groups, inner_rows, 128), F32),
        ),
        in_specs=[anywhere, anywhere] + [inside] * 7 + [anywhere] * (2 * len(own_pieces)),
        out_specs=(inside,) * 7,
        scratch_shapes=[
            vmem((pos_count, part_len, model_width), BF16),
            vmem((pos_count, part_len, width), BF16),
            vmem((slots, rz_count, units, own_width, tile), BF16),
            vmem((slots, rz_count, units, own_width, tile), BF16),
            vmem((slots, rz_count, units, own_width, tile), BF16),
            vmem((2, steps, units, own_width, tile), BF16),
            vmem((2, steps, units, own_width, tile), BF16),
            vmem((units, own_width, tile), F32),
            vmem((rz_count, own_width, tile), BF16),
            vmem((rz_count, own_width, tile), BF16),
            vmem((2, pos_count, part_len, half), BF16),
            vmem((2, pos_count, part_len, half), BF16),
            vmem((model_width, width), F32),
            vmem((rz_count, block_rows, width), BF16),
            vmem((rz_count, block_rows, width), BF16),
            vmem((2, steps, block_rows, width), BF16),
            vmem((2, steps, block_rows, width), BF16),
            vmem((block_rows, width), F32),
            vmem((pos_count, own_width, width), BF16),
            vmem((pos_count, own_width, width), BF16),
            vmem((rz_count, pos_count, own_width, model_width), BF16),
            vmem((pos_count, rz_count, own_width, model_width), BF16),
            vmem((2, steps, own_width, model_width), BF16),
            vmem((2, steps, own_width, model_width), BF16),
            vmem((own_width, model_width), F32),
            vmem((groups, line_rows + inner_rows, 128), F32),
            vmem((rows_count, line_rows + inner_rows, 128), F32),
            vmem((pos_count, line_rows + inner_rows, 128), F32),
            vmem((line_rows + inner_rows, 128), F32),
            pltpu.SemaphoreType.DMA((local_count,)),
            pltpu.SemaphoreType.DMA((remote_count,)),
            pltpu.SemaphoreType.DMA((remote_count,)),
        ],
        compiler_params=pltpu.CompilerParams(
            collective_id=0, has_side_effects=True, vmem_limit_bytes=VMEM_LIMIT
        ),
        cost_estimate=pl.CostEstimate(flops=10**7, bytes_accessed=10**7, transcendentals=0),
        name="last_sums",
    )(
        row_in,
        proj_grad,
        weight_in,
        norm,
        grad_residual,
        out_parts,
        token_lines,
        chan_lines,
        inner,
        *own_pieces,
        *moved_pieces,
    )


def bits_of(count):
    return [1 << at for at in range(count.bit_length() - 1)]


def on_device(
    activations,
    out_grad,
    doc_bounds,
    doc_ids,
    pre_gain,
    pre_bias,
    in_weight,
    in_bias,
    short_weight,
    short_bias,
    skip_gain,
    out_weight,
    out_bias,
    post_gain,
    post_bias,
    up_weight,
    up_bias,
    down_weight,
    down_bias,
    filter_one,
    filter_bias_one,
    filter_two,
    filter_bias_two,
    filter_freq,
    filter_three,
):
    rz_count, pos_count = lax.axis_size("rz"), lax.axis_size("pos")
    pos, core = lax.axis_index("pos"), lax.axis_index("core")
    everything = ("rz", "core", "pos")
    owners = rz_count * 2 * pos_count
    own_at = (lax.axis_index("rz") * 2 + core) * pos_count + pos
    part_len, model_width = activations.shape[1:]
    length = part_len * pos_count
    own_width = pre_gain.shape[0]
    chan = model_width // pos_count
    ff_own = down_weight.shape[0]
    ff_half = rz_count * pos_count * ff_own
    docs = doc_bounds.shape[1]
    order = filter_two.shape[0]
    tables = transform_tables()
    meta = unit_table(doc_bounds[0], length)

    vectors = [
        pre_gain,
        pre_bias,
        out_bias,
        post_gain,
        post_bias,
        down_bias,
        skip_gain,
        in_bias,
        short_weight,
        short_bias,
        filter_three,
    ]
    small = jnp.concatenate([value.reshape(-1) for value in vectors + [up_bias]])
    count = small.shape[0]
    small_rows = -(-count // (model_width * 16)) * 16
    small = jnp.pad(small, (0, small_rows * model_width - count)).reshape(small_rows, model_width)
    row_in, weight_in, bundle, owned = gather(
        (rz_count, pos_count),
        activations[0],
        in_weight.transpose(1, 0, 2),
        up_weight,
        down_weight,
        out_weight,
        small,
    )
    row_in = row_in.reshape(length, model_width)
    weight_in = weight_in.reshape(model_width, -1)
    used = -(-count // model_width)
    small = owned[:, :, :, own_width : own_width + used].reshape(2, pos_count, rz_count, -1)
    small = small[..., :count].reshape(2, pos_count, rz_count, -1, own_width)
    lines = small.transpose(3, 2, 0, 1, 4).reshape(-1, model_width).astype(F32)
    out_all = owned[:, :, :, :own_width].transpose(2, 0, 1, 3, 4)
    out_all = out_all.reshape(model_width, model_width)
    (
        pre_gain_all,
        pre_bias_all,
        out_bias_all,
        post_gain_all,
        post_bias_all,
        down_bias_all,
    ) = (lines[at] for at in range(6))
    up_lines = lines.shape[0] - ff_own // own_width
    up_bias_all = lines[up_lines:].reshape(ff_own // own_width, rz_count, 2, pos_count, own_width)
    up_bias_all = up_bias_all.transpose(2, 1, 3, 0, 4).reshape(2, ff_half)
    up_bias_half = lax.dynamic_index_in_dim(up_bias_all, core, 0, False)
    up_bias_half = up_bias_half.reshape(rz_count, pos_count * ff_own)
    mine = lax.dynamic_slice_in_dim(lines[6:up_lines], pos * chan, chan, 1)
    proj_bias = mine[1:4].reshape(1, 3 * chan)
    taps = jnp.concatenate([mine[4:16], mine[0:1], jnp.zeros((3, chan), F32)])
    three = mine[16:]

    tile = pos_count * ff_own
    columns = model_width // tile
    bits = bits_of(pos_count)
    orders = (bits, bits[::-1])
    place = jnp.reshape(pos, (1,)).astype(jnp.int32)

    embedding = positions_table(length, filter_one.shape[0])
    channels = (pos * chan + jnp.arange(chan, dtype=jnp.int32)).astype(F32)
    decay = decay_of(length, channels, model_width)
    filt, filter_back = jax.vjp(
        functools.partial(filter_net, embedding, decay),
        filter_one.astype(F32),
        filter_bias_one.astype(F32),
        filter_two.astype(F32),
        filter_bias_two.astype(F32),
        filter_freq.astype(F32),
        three,
    )

    own_in = activations[0]
    norm_one = jnp.stack([pre_gain_all, pre_bias_all])
    projected = project(row_in, norm_one, weight_in, proj_bias)
    branch, mixed = mixer_forward(meta, docs, projected, filt, taps, tables)
    sides = [{0: bundle[: rz_count // 2]}, {0: bundle[rz_count // 2 :]}]
    firsts = [[swap(sides[side][0], "pos", bit) for bit in bits] for side in range(2)]
    branch, firsts = lax.optimization_barrier((branch, firsts))
    for side in range(2):
        sides[side].update(zip(bits, firsts[side], strict=True))
        known = [0]
        for bit in orders[side]:
            for mask in known[1:]:
                sides[side][mask ^ bit] = swap(sides[side][mask], "pos", bit)
            known += [mask ^ bit for mask in known]
    masks = sorted(sides[0])
    pieces = [sides[side][mask] for mask in masks for side in range(2)]
    branch_tokens = lax.all_to_all(
        branch.reshape(pos_count, part_len, chan), "pos", split_axis=0, concat_axis=0, tiled=True
    )
    branch_tokens = branch_tokens.transpose(1, 0, 2).reshape(part_len, model_width)

    inputs_f = own_in.astype(F32)
    residual = inputs_f + jnp.dot(branch_tokens, out_all, preferred_element_type=F32) + out_bias_all
    normed_two, post_back = jax.vjp(layer_norm, residual, post_gain_all, post_bias_all)
    normed_two = normed_two.astype(BF16)
    own_grad = out_grad[0]
    other_grad = swap(own_grad, "core", 1)
    ff_own_out, ff_other_out, back_own, back_other, up_bias_grad, *piece_grads = feed_forward(
        place,
        masks,
        normed_two,
        swap(normed_two, "core", 1),
        own_grad,
        other_grad,
        up_bias_half,
        pieces,
    )
    result = residual + (ff_own_out + swap(ff_other_out, "core", 1).astype(F32)) + down_bias_all
    result = result.astype(BF16)[None]
    grad_normed_two = back_own + swap(back_other, "core", 1).astype(F32)
    grad_out_f = own_grad.astype(F32)
    down_bias_grad = jnp.sum(grad_out_f, axis=0)
    grad_res_part, post_gain_grad, post_bias_grad = post_back(grad_normed_two)
    grad_residual = grad_out_f + grad_res_part
    out_bias_grad = jnp.sum(grad_residual, axis=0)
    grad_res_q = grad_residual.astype(BF16)
    branch_grad = lax.dot_general(
        grad_res_q, out_all, (((1,), (1,)), ((), ())), preferred_element_type=F32
    ).astype(BF16)
    branch_grad = lax.all_to_all(
        branch_grad.reshape(part_len, pos_count, chan).transpose(1, 0, 2),
        "pos",
        split_axis=0,
        concat_axis=0,
        tiled=True,
    ).reshape(length, chan)
    out_weight_grad = lax.dot_general(
        branch_tokens, grad_res_q, (((0,), (0,)), ((), ())), preferred_element_type=F32
    ).astype(BF16)

    kept = [[mask for mask in masks if not mask & orders[side][0]] for side in range(2)]
    by_mask = {
        (side, mask): piece_grads[2 * at + side]
        for at, mask in enumerate(masks)
        for side in range(2)
    }
    own_pieces = [by_mask[side, kept[side][at]] for at in range(len(kept[0])) for side in range(2)]
    moved_pieces = [
        swap(by_mask[side, kept[side][at] ^ orders[side][0]], "pos", orders[side][0])
        for at in range(len(kept[0]))
        for side in range(2)
    ]
    out_parts = out_weight_grad.reshape(rz_count, 2, pos_count, own_width, model_width)
    out_keep = lax.dynamic_index_in_dim(out_parts, core, 1, False)
    out_send = lax.dynamic_index_in_dim(out_parts, 1 - core, 1, False)
    out_parts = (out_keep.astype(F32) + swap(out_send, "core", 1).astype(F32)).astype(BF16)
    groups = model_width // 128
    up_lines = jnp.where(
        jnp.arange(2)[None, :, None] == core, up_bias_grad.reshape(rz_count, 1, tile), 0.0
    )
    up_lines = up_lines.reshape(groups, -1, 128).transpose(1, 0, 2).reshape(-1, model_width)
    token_lines = jnp.concatenate(
        [
            jnp.zeros((2, model_width), F32),
            jnp.stack([out_bias_grad, post_gain_grad, post_bias_grad, down_bias_grad]),
            up_lines,
        ]
    )
    token_lines = jnp.pad(token_lines, ((0, -token_lines.shape[0] % 8), (0, 0)))

    proj_grad, filt_grad, chan_sums = mixer_backward(
        meta, docs, projected, filt, taps, tables, mixed, branch_grad
    )
    inner = filter_back(filt_grad)
    chan_lines = jnp.concatenate([chan_sums, inner[5]])
    vectors = [value.reshape(-1, filter_two.shape[1]) for value in inner[:5]]
    flat = jnp.concatenate(vectors)
    flat = jnp.pad(
        flat, ((0, -flat.shape[0] % (8 * groups)), (0, 128 - filter_two.shape[1]))
    )
    input_grad, weight_in_grad, up_weight_grad, down_weight_grad, out_weight_grad, total, shared = (
        last_sums(
            (rz_count, pos_count),
            kept,
            row_in,
            proj_grad,
            weight_in,
            norm_one,
            grad_residual,
            out_parts,
            token_lines,
            chan_lines,
            flat,
            own_pieces,
            moved_pieces,
        )
    )
    input_grad = input_grad[None]
    weight_in_grad = weight_in_grad.transpose(1, 0, 2)
    shared = shared.reshape(-1, 128)[:, : filter_two.shape[1]]
    inner_sum, start = [], 0
    for value, rows in zip(inner[:5], vectors, strict=True):
        inner_sum.append(shared[start : start + rows.shape[0]].reshape(value.shape))
        start += rows.shape[0]
    lane = lax.rem(own_at * own_width, 128)
    mine = lax.dynamic_slice_in_dim(total, lane, own_width, 1)
    token_sums, wide = mine[:6], mine[token_lines.shape[0] :]
    up_bias_sum = total[6 : 6 + up_lines.shape[0]].reshape(-1)
    up_bias_sum = lax.dynamic_slice_in_dim(
        up_bias_sum, lax.rem(own_at * ff_own, up_bias_sum.shape[0]), ff_own, 0
    )
    return (
        result,
        input_grad,
        token_sums[0],
        token_sums[1],
        weight_in_grad,
        wide[12:15],
        wide[0:9].reshape(3, 3, own_width),
        wide[9:12],
        wide[15],
        out_weight_grad,
        token_sums[2],
        token_sums[3],
        token_sums[4],
        up_weight_grad,
        up_bias_sum,
        down_weight_grad,
        token_sums[5],
        *inner_sum,
        wide[16:],
    )


def solution(mesh):
    rows_count, pos_count = mesh.devices.shape
    fine = Mesh(mesh.devices.reshape(rows_count // 2, 2, pos_count), ("rz", "core", "pos"))
    rows = ("rz", "core")
    every = ("rz", "core", "pos")
    tokens = P(rows, "pos", None)
    vector = P(every)
    matrix = P(every, None)
    return jax.shard_map(
        on_device,
        mesh=fine,
        in_specs=(
            tokens,
            tokens,
            P(rows, None),
            P(rows, None),
            vector,
            vector,
            P(every, None, None),
            P(None, every),
            P(None, None, every),
            P(None, every),
            vector,
            matrix,
            vector,
            vector,
            vector,
            matrix,
            vector,
            matrix,
            vector,
            P(),
            P(),
            P(),
            P(),
            P(),
            P(None, every),
        ),
        out_specs=(
            tokens,
            tokens,
            vector,
            vector,
            P(every, None, None),
            P(None, every),
            P(None, None, every),
            P(None, every),
            vector,
            matrix,
            vector,
            vector,
            vector,
            matrix,
            vector,
            matrix,
            vector,
            P(),
            P(),
            P(),
            P(),
            P(),
            P(None, every),
        ),
        check_vma=False,
    )
```

```python
import functools
import math

import jax
import jax.numpy as jnp
import ml_dtypes
import numpy as np
from jax import lax
from jax.experimental import pallas as pl
from jax.experimental.pallas import tpu as pltpu
from jax.sharding import Mesh
from jax.sharding import PartitionSpec as P

HIGHEST = lax.Precision.HIGHEST
F32 = jnp.float32
BF16 = jnp.bfloat16
BLOCK = 256
FREQ_CHUNK = 64
VMEM_LIMIT = 60 * 1024 * 1024


def layer_norm(values, norm_gain, norm_shift):
    centre = values - jnp.mean(values, axis=-1, keepdims=True)
    spread = jnp.mean(centre * centre, axis=-1, keepdims=True)
    return centre * lax.rsqrt(spread + 1e-05) * norm_gain + norm_shift


FEATURES = 64
THREE_ROW, NORM_ROW, UP_ROW, LINES = 16, 80, 86, 96


def positions_table(length, features):
    band_count = (features - 1) // 2
    places = np.arange(length, dtype=np.float64)
    ladder = 0.0001 + (band_count - 1 - 0.0001) * np.arange(band_count) / (band_count - 1)
    angles = 2.0 * math.pi / length * places[:, None] * ladder[None, :]
    table = np.zeros((FEATURES, length), np.float32)
    table[0] = places / (length - 1)
    table[1 : 1 + band_count] = np.cos(angles).T
    table[1 + band_count : features] = -np.sin(angles).T
    return jnp.asarray(table)


def decay_of(block, length, first_channel, model_width, width):
    place = lax.broadcasted_iota(jnp.int32, (BLOCK, width), 0) + block * BLOCK
    channel = lax.broadcasted_iota(jnp.int32, (BLOCK, width), 1) + first_channel
    slow_rate = math.log(0.01) / 1.5
    fast_rate = math.log(0.01) / 0.3
    rates = jnp.abs(
        slow_rate + (fast_rate - slow_rate) * channel.astype(F32) * (1.0 / (model_width - 1))
    )
    return jnp.exp(-(place.astype(F32) * (1.0 / (length - 1))) * rates) + 0.05


def exact(left, right, contract):
    return lax.dot_general(
        left, right, (contract, ((), ())), precision=HIGHEST, preferred_element_type=F32
    )


def filter_block(layers, lines, block, units, length, width, model_width):
    layer_two = layers[1, :, rows_of(block)]
    three = lines[THREE_ROW : THREE_ROW + layer_two.shape[0], :]
    decay = decay_of(block, length, units.channel(), model_width, width)
    return exact(layer_two, three, ((0,), (0,))), decay


def transform_tables():
    order = np.concatenate([np.arange(0, BLOCK, 2), np.arange(1, BLOCK, 2)])
    angle = math.pi / BLOCK * (order[:, None] + 0.5) * np.arange(BLOCK)[None, :]
    forward = np.concatenate([np.cos(angle), -np.sin(angle)], axis=0)
    tables = []
    for table in (forward, forward.T / BLOCK):
        high = table.astype(ml_dtypes.bfloat16)
        low = (table - high.astype(np.float64)).astype(ml_dtypes.bfloat16)
        tables.append(jnp.asarray(np.concatenate([high, high, low], axis=1)))
    return tables


def unit_table(bounds, length, first_channel):
    docs = bounds.shape[0]
    units = length // BLOCK + docs - 1
    ends = jnp.concatenate([bounds[1:], jnp.full((1,), length, jnp.int32)])
    first = bounds // BLOCK
    count = jnp.where(ends > bounds, (ends - 1) // BLOCK - first + 1, 0)
    earlier = jnp.arange(docs)[:, None] >= jnp.arange(docs)[None, :]
    stops = jnp.sum(jnp.where(earlier, count[None, :], 0), axis=1)
    starts = stops - count
    unit = jnp.arange(units, dtype=jnp.int32)
    doc = jnp.sum((unit[:, None] >= stops[None, :]).astype(jnp.int32), axis=1)
    doc = jnp.minimum(doc, docs - 1)
    pick = (doc[:, None] == jnp.arange(docs)[None, :]).astype(jnp.int32)

    def of_doc(values):
        return jnp.sum(pick * values[None, :], axis=1)

    block = jnp.clip(of_doc(first - starts) + unit, 0, length // BLOCK - 1)
    return jnp.concatenate(
        [
            block,
            of_doc(bounds),
            of_doc(ends),
            of_doc(starts),
            of_doc(stops),
            starts,
            stops,
            bounds,
            stops[docs - 1 :],
            jnp.reshape(first_channel, (1,)),
        ]
    ).astype(jnp.int32)


class Units:
    def __init__(self, meta, length, docs):
        self.meta = meta
        self.docs = docs
        self.units = length // BLOCK + docs - 1

    def block(self, unit):
        return self.meta[unit]

    def low(self, unit):
        return self.meta[self.units + unit]

    def high(self, unit):
        return self.meta[2 * self.units + unit]

    def start(self, unit):
        return self.meta[3 * self.units + unit]

    def stop(self, unit):
        return self.meta[4 * self.units + unit]

    def doc_start(self, doc):
        return self.meta[5 * self.units + doc]

    def doc_stop(self, doc):
        return self.meta[5 * self.units + self.docs + doc]

    def bound(self, doc):
        return self.meta[5 * self.units + 2 * self.docs + doc]

    def total(self):
        return self.meta[5 * self.units + 3 * self.docs]

    def channel(self):
        return self.meta[5 * self.units + 3 * self.docs + 1]

    def inside(self, unit, width):
        place = lax.broadcasted_iota(jnp.int32, (BLOCK, width), 0) + self.block(unit) * BLOCK
        return (place >= self.low(unit)) & (place < self.high(unit))


def rows_of(block):
    return pl.ds(pl.multiple_of(block * BLOCK, BLOCK), BLOCK)


def times(table, value):
    high = value.astype(BF16)
    low = (value - high.astype(F32)).astype(BF16)
    return jnp.dot(
        table[...], jnp.concatenate([high, low, high], axis=0), preferred_element_type=F32
    )


def tap_masks(units, block, width, ahead=0):
    place = lax.broadcasted_iota(jnp.int32, (BLOCK, width), 0) + (block * BLOCK + ahead)
    first = place == units.bound(0)
    second = place == units.bound(0) + 1
    for doc in range(1, units.docs):
        first = first | (place == units.bound(doc))
        second = second | (place == units.bound(doc) + 1)
    return jnp.logical_not(first), jnp.logical_not(first | second)


def delayed(ref, block):
    start = block * BLOCK
    here = ref[rows_of(block), :].astype(F32)
    before = ref[pl.ds(pl.multiple_of(jnp.maximum(start - 16, 0), 16), 16), :].astype(F32)
    joined = jnp.concatenate([before, here], axis=0)
    return (here, pltpu.roll(joined, 1, 0)[16:], pltpu.roll(joined, 2, 0)[16:])


def short_conv(parts, small, branch, masks):
    total = small[9 + branch : 10 + branch, :] + small[branch : branch + 1, :] * parts[0]
    total += jnp.where(masks[0], small[3 + branch : 4 + branch, :] * parts[1], 0.0)
    total += jnp.where(masks[1], small[6 + branch : 7 + branch, :] * parts[2], 0.0)
    return total


def mixer_forward_kernel(
    docs, model_width, meta, post, pre, val, layers, small, fwd, inv, branch, mixed, gated, spec, taps, prod
):
    length, width = gated.shape
    blocks = length // BLOCK
    units = Units(meta, length, docs)

    def gate(block, _):
        masks = tap_masks(units, block, width)
        part = short_conv(delayed(val, block), small, 2, masks)
        part *= short_conv(delayed(pre, block), small, 1, masks)
        gated[rows_of(block), :] = part
        mixed[rows_of(block), :] = small[12:13, :] * part
        filt, decay = filter_block(layers, small, block, units, length, width, model_width)
        taps[block] = times(fwd, filt * decay)
        return 0

    lax.fori_loop(0, blocks, gate, 0)

    def transform(unit, _):
        value = gated[rows_of(units.block(unit)), :]
        spec[unit] = times(fwd, jnp.where(units.inside(unit, width), value, 0.0))
        return 0

    lax.fori_loop(0, units.total(), transform, 0)

    def multiply(unit, _):
        for low in range(0, BLOCK, FREQ_CHUNK):
            re, im = pl.ds(low, FREQ_CHUNK), pl.ds(BLOCK + low, FREQ_CHUNK)

            def step(back, total):
                at = unit - back
                s_re, s_im, t_re, t_im = spec[at, re], spec[at, im], taps[back, re], taps[back, im]
                return (
                    total[0] + (s_re * t_re - s_im * t_im),
                    total[1] + (s_re * t_im + s_im * t_re),
                )

            zero = jnp.zeros((FREQ_CHUNK, width), F32)
            total = lax.fori_loop(0, unit - units.start(unit) + 1, step, (zero, zero))
            prod[unit, re] = total[0]
            prod[unit, im] = total[1]
        return 0

    lax.fori_loop(0, units.total(), multiply, 0)

    half = BLOCK // 2

    def bring_back(unit, _):
        last = jnp.maximum(unit - 1, 0)
        old = jnp.where(unit > units.start(unit), prod[last], 0.0)
        new = prod[unit]
        joined = jnp.concatenate(
            [
                new[:half] - old[BLOCK : BLOCK + half],
                new[half:BLOCK] + old[BLOCK + half :],
                new[BLOCK : BLOCK + half] + old[:half],
                new[BLOCK + half :] - old[half:BLOCK],
            ],
            axis=0,
        )
        value = times(inv, joined)
        rows = rows_of(units.block(unit))
        mixed[rows, :] += jnp.where(units.inside(unit, width), value, 0.0)
        return 0

    lax.fori_loop(0, units.total(), bring_back, 0)

    def finish(block, _):
        masks = tap_masks(units, block, width)
        gate_value = short_conv(delayed(post, block), small, 0, masks)
        branch[rows_of(block), :] = (gate_value * mixed[rows_of(block), :]).astype(BF16)
        return 0

    lax.fori_loop(0, blocks, finish, 0)


def mixer_backward_kernel(
    docs,
    model_width,
    meta,
    post,
    pre,
    val,
    layers,
    small,
    fwd,
    inv,
    mixed,
    branch_grad,
    proj_grad,
    filt_grad,
    sums,
    gated,
    gm,
    conv_grad,
    spec,
    taps,
    prod,
):
    length, width = gated.shape
    blocks = length // BLOCK
    units = Units(meta, length, docs)
    half = BLOCK // 2
    sums[...] = jnp.zeros_like(sums)

    def total_rows(value):
        return jnp.sum(value, axis=0, keepdims=True)

    def gate(block, _):
        rows = rows_of(block)
        masks = tap_masks(units, block, width)
        part = short_conv(delayed(val, block), small, 2, masks)
        part *= short_conv(delayed(pre, block), small, 1, masks)
        gated[rows, :] = part
        grad = branch_grad[rows, :].astype(F32)
        mix_grad = grad * short_conv(delayed(post, block), small, 0, masks)
        gm[rows, :] = mix_grad
        conv_grad[0, rows, :] = grad * mixed[rows, :]
        conv_grad[1, rows, :] = small[12:13, :] * mix_grad
        sums[15:16, :] += total_rows(part * mix_grad)
        filt, decay = filter_block(layers, small, block, units, length, width, model_width)
        taps[block] = times(fwd, filt * decay)
        return 0

    lax.fori_loop(0, blocks, gate, 0)

    def transform(unit, _):
        rows = rows_of(units.block(unit))
        inside = units.inside(unit, width)
        spec[unit] = times(fwd, jnp.where(inside, gated[rows, :], 0.0))
        prod[unit] = times(fwd, jnp.where(inside, gm[rows, :], 0.0))
        return 0

    lax.fori_loop(0, units.total(), transform, 0)

    def spread(unit, _):
        after = jnp.minimum(unit + 1, units.units - 1)
        new = jnp.where(unit + 1 < units.stop(unit), prod[after], 0.0)
        prod[unit, pl.ds(0, half)] += new[BLOCK : BLOCK + half]
        prod[unit, pl.ds(half, half)] -= new[BLOCK + half :]
        prod[unit, pl.ds(BLOCK, half)] -= new[:half]
        prod[unit, pl.ds(BLOCK + half, half)] += new[half:BLOCK]
        return 0

    lax.fori_loop(0, units.total(), spread, 0)

    def signal_grad(unit, _):
        pieces = []
        for low in range(0, BLOCK, FREQ_CHUNK):
            re, im = pl.ds(low, FREQ_CHUNK), pl.ds(BLOCK + low, FREQ_CHUNK)

            def step(ahead, total):
                at = unit + ahead
                g_re, g_im, t_re, t_im = (
                    prod[at, re],
                    prod[at, im],
                    taps[ahead, re],
                    taps[ahead, im],
                )
                return (
                    total[0] + (g_re * t_re + g_im * t_im),
                    total[1] + (g_im * t_re - g_re * t_im),
                )

            zero = jnp.zeros((FREQ_CHUNK, width), F32)
            pieces.append(lax.fori_loop(0, units.stop(unit) - unit, step, (zero, zero)))
        joined = jnp.concatenate([piece[0] for piece in pieces] + [piece[1] for piece in pieces])
        value = times(inv, joined)
        rows = rows_of(units.block(unit))
        conv_grad[1, rows, :] += jnp.where(units.inside(unit, width), value, 0.0)
        return 0

    lax.fori_loop(0, units.total(), signal_grad, 0)

    def tap_grad(back, _):
        pieces = []
        for low in range(0, BLOCK, FREQ_CHUNK):
            re, im = pl.ds(low, FREQ_CHUNK), pl.ds(BLOCK + low, FREQ_CHUNK)

            def step(unit, total):
                at = unit - back
                g_re, g_im, s_re, s_im = (
                    prod[unit, re],
                    prod[unit, im],
                    spec[at, re],
                    spec[at, im],
                )
                return (
                    total[0] + (g_re * s_re + g_im * s_im),
                    total[1] + (g_im * s_re - g_re * s_im),
                )

            zero = jnp.zeros((FREQ_CHUNK, width), F32)
            total = (zero, zero)
            for doc in range(docs):
                total = lax.fori_loop(
                    units.doc_start(doc) + back, units.doc_stop(doc), step, total
                )
            pieces.append(total)
        joined = jnp.concatenate([piece[0] for piece in pieces] + [piece[1] for piece in pieces])
        decay = decay_of(back, length, units.channel(), model_width, width)
        filt_grad[rows_of(back), :] = times(inv, joined) * decay
        return 0

    lax.fori_loop(0, blocks, tap_grad, 0)

    def conv_back(block, _):
        rows = rows_of(block)
        masks = tap_masks(units, block, width)
        val_parts, pre_parts, post_parts = (
            delayed(val, block),
            delayed(pre, block),
            delayed(post, block),
        )
        gated_grad = conv_grad[1, rows, :]
        pre_grad = gated_grad * short_conv(val_parts, small, 2, masks)
        val_grad = gated_grad * short_conv(pre_parts, small, 1, masks)
        post_grad = conv_grad[0, rows, :]
        conv_grad[1, rows, :] = pre_grad
        conv_grad[2, rows, :] = val_grad
        for branch, (grad, parts) in enumerate(
            ((post_grad, post_parts), (pre_grad, pre_parts), (val_grad, val_parts))
        ):
            sums[branch : branch + 1, :] += total_rows(grad * parts[0])
            sums[3 + branch : 4 + branch, :] += total_rows(
                jnp.where(masks[0], grad * parts[1], 0.0)
            )
            sums[6 + branch : 7 + branch, :] += total_rows(
                jnp.where(masks[1], grad * parts[2], 0.0)
            )
            sums[9 + branch : 10 + branch, :] += total_rows(grad)
        return 0

    lax.fori_loop(0, blocks, conv_back, 0)

    def spread_taps(block, _):
        start = block * BLOCK
        one, _two = tap_masks(units, block, width, 1)
        _one, two = tap_masks(units, block, width, 2)
        place = lax.broadcasted_iota(jnp.int32, (BLOCK, width), 0) + start
        one = one & (place + 1 < length)
        two = two & (place + 2 < length)
        for branch in range(3):
            here = conv_grad[branch, rows_of(block), :]
            after = conv_grad[
                branch, pl.ds(pl.multiple_of(jnp.minimum(start + BLOCK, length - 8), 8), 8), :
            ]
            joined = jnp.concatenate([here, after], axis=0)
            size = BLOCK + 8
            next_one = pltpu.roll(joined, size - 1, 0)[:BLOCK]
            next_two = pltpu.roll(joined, size - 2, 0)[:BLOCK]
            total = small[branch : branch + 1, :] * here
            total += jnp.where(one, small[3 + branch : 4 + branch, :] * next_one, 0.0)
            total += jnp.where(two, small[6 + branch : 7 + branch, :] * next_two, 0.0)
            rounded = total.astype(BF16)
            proj_grad[rows_of(block), branch * width : (branch + 1) * width] = rounded
            sums[12 + branch : 13 + branch, :] += total_rows(rounded.astype(F32))
        return 0

    lax.fori_loop(0, blocks, spread_taps, 0)


def whole_spec(shape, column=0):
    place = (0,) * (len(shape) - 1) + (column,)
    return pl.BlockSpec(shape, lambda i, meta: place, pipeline_mode=pl.Buffered(1))


def mixer_forward(meta, docs, projected, layers, small, model_width, tables):
    length, width = layers.shape[2], small.shape[1]
    units = length // BLOCK + docs - 1
    column = [whole_spec((length, width), at) for at in range(3)]
    return pl.pallas_call(
        functools.partial(mixer_forward_kernel, docs, model_width),
        out_shape=(
            jax.ShapeDtypeStruct((length, width), BF16),
            jax.ShapeDtypeStruct((length, width), F32),
        ),
        grid_spec=pltpu.PrefetchScalarGridSpec(
            num_scalar_prefetch=1,
            grid=(1,),
            in_specs=column
            + [whole_spec(value.shape) for value in (layers, small, tables[0], tables[1])],
            out_specs=(column[0], column[0]),
            scratch_shapes=[
                pltpu.VMEM((length, width), F32),
                pltpu.VMEM((units, 2 * BLOCK, width), F32),
                pltpu.VMEM((length // BLOCK, 2 * BLOCK, width), F32),
                pltpu.VMEM((units, 2 * BLOCK, width), F32),
            ],
        ),
        compiler_params=pltpu.CompilerParams(vmem_limit_bytes=VMEM_LIMIT),
        cost_estimate=pl.CostEstimate(
            flops=40 * 10**9, bytes_accessed=10 * 10**6, transcendentals=0
        ),
        name="mixer_forward",
    )(meta, projected, projected, projected, layers, small, *tables)


def mixer_backward(meta, docs, projected, layers, small, model_width, tables, mixed, branch_grad):
    length, width = layers.shape[2], small.shape[1]
    units = length // BLOCK + docs - 1
    column = [whole_spec((length, width), at) for at in range(3)]
    return pl.pallas_call(
        functools.partial(mixer_backward_kernel, docs, model_width),
        out_shape=(
            jax.ShapeDtypeStruct((length, 3 * width), BF16),
            jax.ShapeDtypeStruct((length, width), F32),
            jax.ShapeDtypeStruct((16, width), F32),
        ),
        grid_spec=pltpu.PrefetchScalarGridSpec(
            num_scalar_prefetch=1,
            grid=(1,),
            in_specs=column
            + [
                whole_spec(value.shape)
                for value in (layers, small, tables[0], tables[1], mixed, branch_grad)
            ],
            out_specs=(
                whole_spec((length, 3 * width)),
                column[0],
                whole_spec((16, width)),
            ),
            scratch_shapes=[
                pltpu.VMEM((length, width), F32),
                pltpu.VMEM((length, width), F32),
                pltpu.VMEM((3, length, width), F32),
                pltpu.VMEM((units, 2 * BLOCK, width), F32),
                pltpu.VMEM((length // BLOCK, 2 * BLOCK, width), F32),
                pltpu.VMEM((units, 2 * BLOCK, width), F32),
            ],
        ),
        compiler_params=pltpu.CompilerParams(vmem_limit_bytes=VMEM_LIMIT),
        cost_estimate=pl.CostEstimate(
            flops=80 * 10**9, bytes_accessed=16 * 10**6, transcendentals=0
        ),
        name="mixer_backward",
    )(meta, projected, projected, projected, layers, small, *tables, mixed, branch_grad)


def norm_parts(values):
    centre = values - jnp.mean(values, axis=-1, keepdims=True)
    spread = jnp.mean(centre * centre, axis=-1, keepdims=True)
    scale = lax.rsqrt(spread + 1e-05)
    return centre * scale, scale


def project_kernel(inputs, norm, weight, lines, out):
    unit, _ = norm_parts(inputs[...].astype(F32))
    normed = (unit * norm[0:1, :] + norm[1:2, :]).astype(BF16)
    bias = jnp.concatenate([lines[13 + at : 14 + at, :] for at in range(3)], axis=1)
    total = jnp.dot(normed, weight[...], preferred_element_type=F32) + bias
    out[...] = total.astype(BF16)


def project(inputs, lines, weight, mine):
    length, depth = inputs.shape
    width = weight.shape[1]
    return pl.pallas_call(
        project_kernel,
        out_shape=jax.ShapeDtypeStruct((length, width), BF16),
        grid=(length // BLOCK,),
        in_specs=[
            pl.BlockSpec((BLOCK, depth), lambda i: (i, 0)),
            pl.BlockSpec((8, depth), lambda i: (NORM_ROW // 8, 0)),
            pl.BlockSpec(weight.shape, lambda i: (0, 0)),
            pl.BlockSpec((16, mine.shape[1]), lambda i: (0, 0)),
        ],
        out_specs=pl.BlockSpec((BLOCK, width), lambda i: (i, 0)),
        compiler_params=pltpu.CompilerParams(vmem_limit_bytes=VMEM_LIMIT),
        cost_estimate=pl.CostEstimate(
            flops=2 * length * depth * width, bytes_accessed=10 * 10**6, transcendentals=0
        ),
        name="project",
    )(inputs, lines, weight, mine)


def gelu_pair(u):
    root = math.sqrt(2.0 / math.pi)
    square = u * u
    curve = jnp.tanh(root * (u + 0.044715 * (u * square)))
    value = 0.5 * u * (1.0 + curve)
    slope = 0.5 * (1.0 + curve) + 0.5 * u * (1.0 - curve * curve) * (
        root * (1.0 + 3.0 * 0.044715 * square)
    )
    return value, slope


class Copies:
    def __init__(self, local_sems, send_sems, got_sems):
        self.local_sems, self.send_sems, self.got_sems = local_sems, send_sems, got_sems
        self.locals = 0
        self.names = {}
        self.pending = []

    def local(self, source, target):
        copy = pltpu.make_async_copy(source, target, self.local_sems.at[self.locals])
        self.locals += 1
        copy.start()
        return copy

    def remote(self, name, source, target, device):
        at = self.names.setdefault(name, len(self.names))
        return pltpu.make_async_remote_copy(
            src_ref=source,
            dst_ref=target,
            send_sem=self.send_sems.at[at],
            recv_sem=self.got_sems.at[at],
            device_id=device,
            device_id_type=pl.DeviceIdType.MESH,
        )

    def send(self, name, source, target, device, when=None):
        copy = self.remote(name, source, target, device)
        if when is None:
            copy.start()
        else:
            pl.when(when)(copy.start)
        self.pending.append((name, copy, when))

    def got(self, name, target, device):
        self.remote(name, target, target, device).wait_recv()

    def local_when(self, source, target, when):
        copy = pltpu.make_async_copy(source, target, self.local_sems.at[self.locals])
        self.locals += 1
        pl.when(when)(copy.start)
        return copy

    def settle(self, name):
        for at, (found, copy, when) in enumerate(self.pending):
            if found == name:
                copy.wait_send()
                del self.pending[at]
                return

    def finish(self):
        for _, copy, when in self.pending:
            if when is None:
                copy.wait_send()
            else:
                pl.when(when)(copy.wait_send)


def greet(devices):
    barrier = pltpu.get_barrier_semaphore()
    for device in devices:
        pl.semaphore_signal(
            barrier, inc=1, device_id=device, device_id_type=pl.DeviceIdType.MESH
        )
    pl.semaphore_wait(barrier, len(devices))


def lane_masks(bits):
    masks, found = [0], []
    for bit in bits:
        found += [(mask ^ bit, bit) for mask in masks]
        masks += [mask ^ bit for mask in masks]
    return found


def middle_kernel(
    dims,
    given,
    branch,
    inputs,
    out_weight,
    lines,
    out_grad,
    up_bias,
    *rest,
):
    rz_count, pos_count = dims
    count = 2 * len(given)
    pieces, rest = rest[:count], rest[count:]
    steps = rz_count - 1
    extras, rest = rest[: 2 * steps - 1], rest[2 * steps - 1 :]
    result, residual, branch_grad, out_parts, token_lines = rest[:5]
    piece_grads, rest = rest[5 : 5 + 2 * pos_count], rest[5 + 2 * pos_count :]
    (
        tokens,
        normed,
        grad,
        out_total,
        back_total,
        weights,
        grads,
        out_got,
        back_got,
        grad_q,
        turned_got,
        bias_grad,
        local_sems,
        send_sems,
        got_sems,
    ) = rest
    z, core, pos = lax.axis_index("rz"), lax.axis_index("core"), lax.axis_index("pos")
    rows, depth = inputs.shape
    tiles, _, units, own_width, width = weights.shape
    middle = tiles // 2
    columns = depth // width
    chan = branch.shape[1]
    down_units = (units - 2 * tiles) // columns
    bits = bits_of(pos_count)
    orders = (bits, bits[::-1])
    copies = Copies(local_sems, send_sems, got_sems)
    other = {"core": 1 - core}
    peers = [jnp.bitwise_xor(pos, mask) for mask in range(pos_count)]

    def token_rows(owner):
        return pl.ds(pl.multiple_of(owner * rows, rows), rows)

    def channels(owner):
        return pl.ds(pl.multiple_of(owner * chan, chan), chan)

    grad_load = copies.local(out_grad, grad.at[pl.ds(0, rows)])
    loads = []
    for at, mask in enumerate(given):
        for side in range(2):
            piece = pieces[2 * at + side]
            part = pl.ds(side * middle, middle)
            target = weights.at[part, peers[mask], pl.ds(0, piece.shape[1])]
            loads.append((copies.local(piece, target), None))
    last = pl.ds(units - extras[0].shape[1], extras[0].shape[1])

    def extra_slot(origin):
        return weights.at[jnp.clip(origin, 0, tiles - 1), :, last]

    for at, extra in enumerate(extras):
        origin = z - (at if at < steps else steps - 1 - at)
        there = (origin >= 0) & (origin < tiles)
        loads.append((copies.local_when(extra, extra_slot(origin), there), there))
    greet(
        [other]
        + [{"rz": (z + step) % rz_count} for step in range(1, rz_count)]
        + [{"pos": peers[mask]} for mask in range(1, pos_count)]
    )
    for mask in range(1, pos_count):
        copies.send(
            ("branch", mask),
            branch.at[token_rows(peers[mask])],
            tokens.at[:, channels(pos)],
            {"pos": peers[mask]},
        )
    grad_load.wait()
    own_half, other_half = pl.ds(0, rows), pl.ds(rows, rows)
    copies.send(("grad",), grad.at[own_half], grad.at[other_half], other)

    full = pieces[0].shape[1]
    arriving = []
    for side in range(2):
        part = pl.ds(side * middle, middle)
        for mask, bit in lane_masks(orders[side]):
            if mask in given:
                continue
            arriving.append((side, mask, bit))
            before = mask ^ bit
            slot = weights.at[part, peers[before], pl.ds(0, full)]
            if before in given:
                source = pieces[2 * given.index(before) + side]
            else:
                source = slot
                prior = [item for item in arriving if item[:2] == (side, before)][0]
                copies.got(("weights", side, before), slot, {"pos": peers[prior[2]]})
            copies.send(("weights", side, mask), source, slot, {"pos": peers[bit]})
    ends = ((1, {"rz": z + 1}, {"rz": z - 1}), (-1, {"rz": z - 1}, {"rz": z + 1}))
    for side, (direction, onward, _) in enumerate(ends):
        origin = z - direction * (steps - 1)
        sends = (origin >= 0) & (origin < tiles)
        sends = sends & (z + direction >= 0) & (z + direction < tiles)
        source = extras[steps - 1 if side == 0 else 2 * steps - 2] if steps > 1 else extras[0]
        copies.send(("extra", side), source, extra_slot(origin), onward, sends)

    tokens[:, channels(pos)] = branch[token_rows(pos), :]
    for mask in range(1, pos_count):
        copies.got(("branch", mask), tokens.at[:, channels(peers[mask])], {"pos": peers[mask]})
    line = [lines[NORM_ROW + at : NORM_ROW + at + 1, :] for at in range(6)]

    def project_out(at, _):
        part = pl.ds(pl.multiple_of(at * BLOCK, BLOCK), BLOCK)
        value = inputs[part, :].astype(F32) + line[2]
        value += jnp.dot(tokens[part, :], out_weight[...], preferred_element_type=F32)
        residual[part, :] = value
        unit, _ = norm_parts(value)
        normed[part, :] = (unit * line[3] + line[4]).astype(BF16)
        return 0

    lax.fori_loop(0, rows // BLOCK, project_out, 0)
    copies.send(("normed",), normed.at[own_half], normed.at[other_half], other)
    out_total[...] = jnp.zeros_like(out_total)
    back_total[...] = jnp.zeros_like(back_total)
    for copy, there in loads:
        if there is None:
            copy.wait()
        else:
            pl.when(there)(copy.wait)
    sent = {item[:2] for item in arriving}
    for side, mask, bit in arriving:
        onward = [item for item in arriving if item[0] == side and item[1] ^ item[2] == mask]
        if not onward:
            slot = weights.at[pl.ds(side * middle, middle), peers[mask], pl.ds(0, full)]
            copies.got(("weights", side, mask), slot, {"pos": peers[bit]})
    for side, (direction, _, back) in enumerate(ends):
        origin = z - direction * steps

        def take(side=side, origin=origin, back=back):
            copies.got(("extra", side), extra_slot(origin), back)

        pl.when((origin >= 0) & (origin < tiles))(take)
    copies.got(("grad",), grad.at[other_half], other)
    copies.got(("normed",), normed.at[other_half], other)

    def step(tile, _):
        up = jnp.concatenate(
            [
                weights[block, :, side * tiles + tile].reshape(pos_count * own_width, width)
                for block in range(tiles)
                for side in range(2)
            ],
            axis=0,
        )
        down = jnp.concatenate(
            [
                weights[
                    tile, :, 2 * tiles + at * down_units : 2 * tiles + (at + 1) * down_units
                ].reshape(width, width)
                for at in range(columns)
            ],
            axis=1,
        )
        pre = jnp.dot(normed[: 2 * rows], up, preferred_element_type=F32) + up_bias[pl.ds(tile, 1), :]
        hidden, slope = gelu_pair(pre)
        hidden = hidden.astype(BF16)
        hidden_grad = lax.dot_general(
            grad[...], down, (((1,), (1,)), ((), ())), preferred_element_type=F32
        )
        pre_grad = hidden_grad * slope
        bias_grad[pl.ds(tile, 1), :] = jnp.sum(pre_grad, axis=0, keepdims=True)
        pre_grad = pre_grad.astype(BF16)
        out_total[...] += jnp.dot(hidden, down, preferred_element_type=F32)
        back_total[...] += lax.dot_general(
            pre_grad, up, (((1,), (1,)), ((), ())), preferred_element_type=F32
        )
        down_grad = lax.dot_general(
            hidden, grad[...], (((0,), (0,)), ((), ())), preferred_element_type=F32
        ).astype(BF16)
        for at in range(columns):
            grads[tile, :, 2 * tiles + at * down_units : 2 * tiles + (at + 1) * down_units] = (
                down_grad[:, at * width : (at + 1) * width].reshape(
                    pos_count, down_units, own_width, width
                )
            )
        up_grad = lax.dot_general(
            normed[: 2 * rows], pre_grad, (((0,), (0,)), ((), ())), preferred_element_type=F32
        ).astype(BF16)
        size = pos_count * own_width
        for block in range(tiles):
            for side in range(2):
                low = (2 * block + side) * size
                grads[block, :, side * tiles + tile] = up_grad[low : low + size].reshape(
                    pos_count, own_width, width
                )
        return 0

    lax.fori_loop(0, tiles, step, 0)
    copies.settle(("normed",))
    normed[:rows] = back_total[rows:].astype(BF16)
    copies.send(("back",), normed.at[own_half], back_got, other)
    normed[rows : 2 * rows] = out_total[rows:].astype(BF16)
    copies.send(("out",), normed.at[other_half], out_got, other)
    stores = []
    for mask in range(pos_count):
        for side in range(2):
            source = grads.at[pl.ds(side * middle, middle), peers[mask]]
            stores.append(copies.local(source, piece_grads[2 * mask + side]))

    copies.got(("back",), back_got, other)
    zero = jnp.zeros((1, depth), F32)

    def norm_back(at, sums):
        part = pl.ds(pl.multiple_of(at * BLOCK, BLOCK), BLOCK)
        unit, scale = norm_parts(residual[part, :])
        back = back_total[part, :] + back_got[part, :].astype(F32)
        scaled = back * line[3]
        out = grad[part, :].astype(F32)
        value = out + scale * (
            scaled
            - jnp.mean(scaled, axis=-1, keepdims=True)
            - unit * jnp.mean(scaled * unit, axis=-1, keepdims=True)
        )
        back_total[part, :] = value
        grad_q[part, :] = value.astype(BF16)

        def total(value):
            return jnp.sum(value, axis=0, keepdims=True)

        return (
            sums[0] + total(value),
            sums[1] + total(back * unit),
            sums[2] + total(back),
            sums[3] + total(out),
        )

    sums = lax.fori_loop(0, rows // BLOCK, norm_back, (zero,) * 4)
    turned = lax.dot_general(
        grad_q[...], out_weight[...], (((1,), (1,)), ((), ())), preferred_element_type=F32
    ).astype(BF16)
    copies.settle(("grad",))
    grad[own_half, :] = turned
    for mask in range(1, pos_count):
        copies.send(
            ("branch grad", mask),
            grad.at[own_half, channels(peers[mask])],
            branch_grad.at[token_rows(pos)],
            {"pos": peers[mask]},
        )
    branch_grad[token_rows(pos), :] = grad[own_half, channels(pos)]
    copies.got(("out",), out_got, other)

    def add_result(at, _):
        part = pl.ds(pl.multiple_of(at * BLOCK, BLOCK), BLOCK)
        value = residual[part, :] + (out_total[part, :] + out_got[part, :].astype(F32)) + line[5]
        result[part, :] = value.astype(BF16)
        residual[part, :] = back_total[part, :]
        return 0

    lax.fori_loop(0, rows // BLOCK, add_result, 0)
    token_lines[...] = jnp.zeros_like(token_lines)
    for at in range(4):
        token_lines[2 + at : 3 + at, :] = sums[at]
    per_tile = width // 128
    per = 2 * tiles * width // depth // per_tile
    for tile in range(tiles):
        owner = 2 * tile + core
        lanes = pl.ds(pl.multiple_of(owner // per * 128, 128), 128)
        for at in range(per * per_tile):
            low = at % per_tile * 128
            value = bias_grad[tile : tile + 1, low : low + 128]
            token_lines[6 + at : 7 + at, lanes] = jnp.where(
                owner % per == at // per_tile, value, 0.0
            )

    copies.settle(("back",))
    copies.settle(("out",))
    normed[:depth] = lax.dot_general(
        tokens[...], grad_q[...], (((0,), (0,)), ((), ())), preferred_element_type=F32
    ).astype(BF16)
    size = pos_count * own_width

    def block_rows(block, side):
        return pl.ds(pl.multiple_of((2 * block + side) * size, size), size)

    for block in range(tiles):
        copies.send(
            ("turned", block),
            normed.at[block_rows(block, 1 - core)],
            turned_got.at[block],
            other,
        )
    for block in range(tiles):
        copies.got(("turned", block), turned_got.at[block], other)
        value = normed[block_rows(block, core), :].astype(F32)
        out_parts[block] = (value + turned_got[block].astype(F32)).astype(BF16)
    for mask in range(1, pos_count):
        copies.got(
            ("branch grad", mask), branch_grad.at[token_rows(peers[mask])], {"pos": peers[mask]}
        )
    for copy in stores:
        copy.wait()
    copies.finish()


def middle(dims, given, branch, inputs, out_weight, lines, out_grad, up_bias, pieces, extras):
    rz_count, pos_count = dims
    rows, depth = inputs.shape
    tiles, width = up_bias.shape
    length, chan = branch.shape
    piece = pieces[0].shape
    piece = piece[:1] + (piece[1] + extras[0].shape[1],) + piece[2:]
    own_width = piece[2]
    whole = (tiles, pos_count) + piece[1:]
    size = pos_count * own_width
    anywhere = pl.BlockSpec(memory_space=pl.ANY)
    inside = pl.BlockSpec(memory_space=pltpu.VMEM)
    vmem = pltpu.VMEM
    local_count = 1 + len(pieces) + len(extras) + 2 * pos_count
    remote_count = 2 * (pos_count - 1) + 2 * pos_count + 6 + tiles
    return pl.pallas_call(
        functools.partial(middle_kernel, dims, given),
        out_shape=(
            jax.ShapeDtypeStruct((rows, depth), BF16),
            jax.ShapeDtypeStruct((rows, depth), F32),
            jax.ShapeDtypeStruct((length, chan), BF16),
            jax.ShapeDtypeStruct((tiles, size, depth), BF16),
            jax.ShapeDtypeStruct((16, depth), F32),
        )
        + (jax.ShapeDtypeStruct(piece, BF16),) * (2 * pos_count),
        in_specs=[inside] * 4 + [anywhere, inside] + [anywhere] * (len(pieces) + len(extras)),
        out_specs=(inside,) * 5 + (anywhere,) * (2 * pos_count),
        scratch_shapes=[
            vmem((rows, depth), BF16),
            vmem((max(2 * rows, depth), depth), BF16),
            vmem((2 * rows, depth), BF16),
            vmem((2 * rows, depth), F32),
            vmem((2 * rows, depth), F32),
            vmem(whole, BF16),
            vmem(whole, BF16),
            vmem((rows, depth), BF16),
            vmem((rows, depth), BF16),
            vmem((rows, depth), BF16),
            vmem((tiles, size, depth), BF16),
            vmem((tiles, width), F32),
            pltpu.SemaphoreType.DMA((local_count,)),
            pltpu.SemaphoreType.DMA((remote_count,)),
            pltpu.SemaphoreType.DMA((remote_count,)),
        ],
        compiler_params=pltpu.CompilerParams(
            collective_id=2, has_side_effects=True, vmem_limit_bytes=VMEM_LIMIT
        ),
        cost_estimate=pl.CostEstimate(flops=10**7, bytes_accessed=10**7, transcendentals=0),
        name="middle",
    )(branch, inputs, out_weight, lines, out_grad, up_bias, *pieces, *extras)


def swap(value, axis, bit):
    count = lax.axis_size(axis)
    return lax.ppermute(value, axis, [(at, at ^ bit) for at in range(count)])


def gather_kernel(
    dims,
    inputs,
    weight,
    up,
    down,
    out,
    vectors,
    filter_in,
    row_in,
    weight_in,
    bundle,
    extra,
    owned,
    lines,
    mine,
    up_lines,
    layers,
    pack,
    small,
    small_mine,
    local_sems,
    send_sems,
    got_sems,
):
    rz_count, pos_count = dims
    z, core, pos = lax.axis_index("rz"), lax.axis_index("core"), lax.axis_index("pos")
    bits = bits_of(pos_count)
    lanes = [lane_masks(bits), lane_masks(bits[::-1])]
    own_width, model_width = out.shape
    chan = model_width // pos_count
    tile = bundle.shape[3]
    columns = model_width // tile
    half = model_width // 2
    middle = rz_count // 2
    copies = Copies(local_sems, send_sems, got_sems)
    other = {"core": 1 - core}
    right, left = {"rz": z + 1}, {"rz": z - 1}
    has_right, has_left = z + 1 < rz_count, z > 0
    greet(
        [other]
        + [{"rz": (z + step) % rz_count} for step in range(1, rz_count)]
        + [{"pos": jnp.bitwise_xor(pos, mask)} for mask in range(1, pos_count)]
    )

    def branch_cols(owner):
        return pl.ds(pl.multiple_of(owner * chan, chan), chan)

    for mask in range(1, pos_count):
        owner = jnp.bitwise_xor(pos, mask)
        for at in range(3):
            copies.send(
                ("in", mask, at),
                weight.at[at, :, branch_cols(owner)],
                weight_in.at[z, core, pos, :, pl.ds(at * chan, chan)],
                {"pos": owner},
            )

    def send_extra(lane, mask, bit):
        part = pl.ds(lane * (down_units // 2), down_units // 2)
        block = extra.at[jnp.bitwise_xor(pos, mask ^ bit), part]
        copies.send(("extra", lane, mask), block, block, {"pos": jnp.bitwise_xor(pos, bit)})

    def got_extra(lane, mask, bit):
        part = pl.ds(lane * (down_units // 2), down_units // 2)
        block = extra.at[jnp.bitwise_xor(pos, mask), part]
        copies.got(("extra", lane, mask), block, {"pos": jnp.bitwise_xor(pos, bit)})
        later = (bits, bits[::-1])[lane]
        for onward in later[later.index(bit) + 1 :]:
            send_extra(lane, mask ^ onward, onward)

    down_units = down.shape[0] // own_width
    local_extra = []
    for at in range(down_units):
        source = down.at[pl.ds(at * own_width, own_width), pl.ds((columns - 1) * tile, tile)]
        local_extra.append(copies.local(source, extra.at[pos, at]))
    for copy in local_extra:
        copy.wait()
    for at in range(len(bits)):
        for lane in range(2):
            bit = (bits, bits[::-1])[lane][at]
            send_extra(lane, bit, bit)

    def lane_cols(lane):
        return pl.ds(lane * half, half)

    def send_rows(lane, mask, bit):
        origin = jnp.bitwise_xor(pos, mask ^ bit)
        cols = lane_cols(lane)
        source = inputs.at[:, cols] if mask == bit else row_in.at[origin, :, cols]
        copies.send(
            ("rows", lane, mask),
            source,
            row_in.at[origin, :, cols],
            {"pos": jnp.bitwise_xor(pos, bit)},
        )

    for at in range(len(bits)):
        for lane in range(2):
            bit = (bits, bits[::-1])[lane][at]
            send_rows(lane, bit, bit)

    def up_cols(at, side):
        return pl.ds(pl.multiple_of((2 * at + side) * tile, tile), tile)

    for at in range(rz_count):
        copies.send(
            ("up", at),
            up.at[:, up_cols(at, 1 - core)],
            bundle.at[z, core * rz_count + at],
            other,
        )
    local_in = [
        copies.local(
            weight.at[at, :, branch_cols(pos)],
            weight_in.at[z, core, pos, :, pl.ds(at * chan, chan)],
        )
        for at in range(3)
    ]
    local_owned = [copies.local(out, owned.at[z, core, pos])]
    local_bundle = [
        copies.local(up.at[:, up_cols(at, core)], bundle.at[z, core * rz_count + at])
        for at in range(rz_count)
    ]
    for col in range(columns - 1):
        for at in range(down_units):
            source = down.at[pl.ds(at * own_width, own_width), pl.ds(col * tile, tile)]
            target = bundle.at[z, 2 * rz_count + col * down_units + at]
            local_bundle.append(copies.local(source, target))
    local_rows = copies.local(inputs, row_in.at[pos])

    flows = {
        "in": lambda origin: weight_in.at[origin, core],
        "owned": lambda origin: owned.at[origin, core, pos],
        "small": lambda origin: small.at[origin, core, pos],
        "bundle": lambda origin: bundle.at[origin],
    }

    def line_start(flow):
        block = flows[flow](z)
        copies.send((flow, "right", 1), block, block, right, has_right)
        copies.send((flow, "left", 1), block, block, left, has_left)

    def line_step(flow, distance, arrived=None):
        for side, origin, there, onward, has_next in (
            ("right", z - distance, z >= distance, right, has_right),
            ("left", z + distance, z + distance < rz_count, left, has_left),
        ):
            safe = jnp.clip(origin, 0, rz_count - 1)
            block = flows[flow](safe)

            def wait(block=block, side=side, onward=onward):
                copies.got((flow, side, distance), block, onward)

            pl.when(there)(wait)
            if distance + 1 < rz_count:
                copies.send((flow, side, distance + 1), block, block, onward, there & has_next)
            if arrived is not None:
                arrived(side, distance, safe, there)

    def share_in(side, distance, origin, there):
        block = weight_in.at[origin, core]
        copies.send(("in core", side, distance), block, block, other, there)

    for copy in local_in:
        copy.wait()
    for mask in range(1, pos_count):
        owner = jnp.bitwise_xor(pos, mask)
        for at in range(3):
            copies.got(
                ("in", mask, at),
                weight_in.at[z, core, owner, :, pl.ds(at * chan, chan)],
                {"pos": owner},
            )
    for lane in range(2):
        got_extra(lane, *lanes[lane][0])
    line_start("in")
    block = weight_in.at[z, core]
    copies.send(("in core", "own", 0), block, block, other)
    for copy in local_owned:
        copy.wait()
    line_start("owned")
    pack[...] = jnp.zeros_like(pack)
    row = 0
    for value in vectors:
        value = value[...].astype(F32)
        value = value.reshape(-1, value.shape[-1])
        pack[row : row + value.shape[0], : value.shape[1]] = value
        row += value.shape[0]
    small[z, core, pos] = pack[...].astype(BF16)
    line_start("small")
    for copy in local_bundle:
        copy.wait()
    for at in range(rz_count):
        copies.got(("up", at), bundle.at[z, (1 - core) * rz_count + at], other)
    line_start("bundle")

    for distance in range(1, rz_count):
        line_step("in", distance, share_in)
        line_step("owned", distance)
        line_step("small", distance)

    def owned_half(side, origin, lane):
        part = pl.ds(lane * middle, middle)
        return (owned.at[part, side, origin], small.at[part, side, origin])

    def send_owned(lane, mask, bit):
        for at, block in enumerate(owned_half(core, jnp.bitwise_xor(pos, mask ^ bit), lane)):
            copies.send(
                ("owned pos", at, lane, mask), block, block, {"pos": jnp.bitwise_xor(pos, bit)}
            )

    def share_owned(lane, mask):
        for at, block in enumerate(owned_half(core, jnp.bitwise_xor(pos, mask), lane)):
            copies.send(("owned core", at, lane, mask), block, block, other)

    def got_rows(lane, mask, bit):
        block = row_in.at[jnp.bitwise_xor(pos, mask), :, lane_cols(lane)]
        copies.got(("rows", lane, mask), block, {"pos": jnp.bitwise_xor(pos, bit)})
        later = (bits, bits[::-1])[lane]
        for onward in later[later.index(bit) + 1 :]:
            send_rows(lane, mask ^ onward, onward)

    def got_owned(lane, mask, bit):
        for at, block in enumerate(owned_half(core, jnp.bitwise_xor(pos, mask), lane)):
            copies.got(("owned pos", at, lane, mask), block, {"pos": jnp.bitwise_xor(pos, bit)})
        later = (bits, bits[::-1])[lane]
        for onward in later[later.index(bit) + 1 :]:
            send_owned(lane, mask ^ onward, onward)
        share_owned(lane, mask)

    first = [lanes[lane][0] for lane in range(2)]
    for lane in range(2):
        got_rows(lane, *first[lane])
    for at in range(len(bits)):
        for lane in range(2):
            bit = (bits, bits[::-1])[lane][at]
            send_owned(lane, bit, bit)
    for lane in range(2):
        share_owned(lane, 0)
    for distance in range(1, rz_count - 1):
        line_step("bundle", distance)
    filter_layers(filter_in, layers, small_mine)
    for at in range(1, pos_count - 1):
        for lane in range(2):
            got_rows(lane, *lanes[lane][at])
            got_extra(lane, *lanes[lane][at])
    for at in range(pos_count - 1):
        for lane in range(2):
            got_owned(lane, *lanes[lane][at])
    line_step("bundle", rz_count - 1)
    local_rows.wait()
    for at in range(pos_count):
        for lane in range(2):
            for part, block in enumerate(
                owned_half(1 - core, jnp.bitwise_xor(pos, at), lane)
            ):
                copies.got(("owned core", part, lane, at), block, other)
    copies.got(("in core", "own", 0), weight_in.at[z, 1 - core], other)
    for distance in range(1, rz_count):
        for side, origin, there in (
            ("right", z - distance, z >= distance),
            ("left", z + distance, z + distance < rz_count),
        ):
            block = weight_in.at[jnp.clip(origin, 0, rz_count - 1), 1 - core]

            def wait(block=block, side=side, distance=distance):
                copies.got(("in core", side, distance), block, other)

            pl.when(there)(wait)

    per_group = 128 // own_width
    for group in range(model_width // 128):
        total = jnp.zeros((LINES, 128), F32)
        for at in range(per_group):
            owner = group * per_group + at
            value = small[
                owner // (2 * pos_count), owner // pos_count % 2, owner % pos_count
            ].astype(F32)
            value = jnp.where(
                lax.broadcasted_iota(jnp.int32, value.shape, 1) < own_width, value, 0.0
            )
            total += pltpu.roll(value, at * own_width, 1) if at else value
        lines[:, group * 128 : (group + 1) * 128] = total
    mine[...] = lines[:NORM_ROW, pl.ds(pl.multiple_of(pos * chan, chan), chan)]
    ff_own = down.shape[0]
    per_lanes = 128 // ff_own
    for at in range(rz_count):
        for group in range(pos_count // per_lanes):
            total = jnp.zeros((1, 128), F32)
            for part in range(per_lanes):
                value = small[at, core, group * per_lanes + part][UP_ROW : UP_ROW + 1]
                value = value.astype(F32)
                total += pltpu.roll(value, part * ff_own, 1) if part else value
            up_lines[at : at + 1, group * 128 : (group + 1) * 128] = total
    copies.finish()


def filter_layers(filter_in, layers, padded):
    embedding, w_one, w_two, columns = filter_in
    padded[...] = jnp.zeros_like(padded)
    padded[: w_one.shape[0], :] = w_one[...].astype(F32)
    frequency = columns[:, 2:3]
    sums = exact(padded[...], embedding[...], ((0,), (0,))) + columns[:, 0:1]
    layers[2] = sums
    layers[4] = jnp.cos(frequency * sums)
    layers[0] = jnp.sin(frequency * sums)
    sums = exact(w_two[...].astype(F32), layers[0], ((0,), (0,))) + columns[:, 1:2]
    layers[3] = sums
    layers[5] = jnp.cos(frequency * sums)
    layers[1] = jnp.sin(frequency * sums)


def gather(dims, inputs, weight, up, down, out, vectors, filter_in):
    rz_count, pos_count = dims
    part_len, model_width = inputs.shape
    own_width = out.shape[0]
    tile = pos_count * down.shape[0]
    down_units = down.shape[0] // own_width
    units = 2 * rz_count + down_units * (model_width // tile - 1)
    anywhere = pl.BlockSpec(memory_space=pl.ANY)
    locals_count = 3 + 1 + units + down_units + 1
    count = len(vectors)
    order, length = filter_in[2].shape[0], filter_in[0].shape[1]
    remote_count = (
        3 * (pos_count - 1)
        + 4 * (pos_count - 1)
        + rz_count
        + 4 * 2 * rz_count
        + 2 * rz_count
        + 2 * 2 * 2 * pos_count
    )

    def kernel(*refs):
        head, refs = refs[:5], refs[5:]
        gather_kernel(dims, *head, refs[:count], refs[count : count + 4], *refs[count + 4 :])

    return pl.pallas_call(
        kernel,
        out_shape=(
            jax.ShapeDtypeStruct((pos_count, part_len, model_width), BF16),
            jax.ShapeDtypeStruct(
                (rz_count, 2, pos_count, own_width, 3 * model_width // pos_count), BF16
            ),
            jax.ShapeDtypeStruct((rz_count, units, own_width, tile), BF16),
            jax.ShapeDtypeStruct((pos_count, down_units, own_width, tile), BF16),
            jax.ShapeDtypeStruct((rz_count, 2, pos_count, own_width, model_width), BF16),
            jax.ShapeDtypeStruct((LINES, model_width), F32),
            jax.ShapeDtypeStruct((NORM_ROW, model_width // pos_count), F32),
            jax.ShapeDtypeStruct((rz_count, tile), F32),
            jax.ShapeDtypeStruct((6, order, length), F32),
        ),
        in_specs=[pl.BlockSpec(memory_space=pltpu.VMEM)] * (5 + count + 4),
        out_specs=(anywhere,) * 5 + (pl.BlockSpec(memory_space=pltpu.VMEM),) * 4,
        scratch_shapes=[
            pltpu.VMEM((LINES, 128), F32),
            pltpu.VMEM((rz_count, 2, pos_count, LINES, 128), BF16),
            pltpu.VMEM((FEATURES, order), F32),
            pltpu.SemaphoreType.DMA((locals_count,)),
            pltpu.SemaphoreType.DMA((remote_count,)),
            pltpu.SemaphoreType.DMA((remote_count,)),
        ],
        compiler_params=pltpu.CompilerParams(
            collective_id=1, has_side_effects=True, vmem_limit_bytes=VMEM_LIMIT
        ),
        cost_estimate=pl.CostEstimate(flops=10**6, bytes_accessed=10**7, transcendentals=0),
        name="gather",
    )(inputs, weight, up, down, out, *vectors, *filter_in)


class LineSum:
    def __init__(self, copies, name, count, z, chunk, sent, got):
        self.copies, self.name, self.count, self.z = copies, name, count, z
        self.chunk, self.sent, self.got_ref = chunk, sent, got

    def sides(self):
        last = self.count - 1
        return (
            (0, self.z, 1, {"rz": self.z + 1}, {"rz": self.z - 1}),
            (1, last - self.z, -1, {"rz": self.z - 1}, {"rz": self.z + 1}),
        )

    def step(self, step):
        count = self.count
        for side, place, direction, onward, back in self.sides():
            sends = (place < step) & (place + 1 < count)
            at = count - step + place
            at = jnp.clip(at if direction == 1 else count - 1 - at, 0, count - 1)
            target = self.sent.at[side, step - 1]

            def first(at=at, side=side):
                self.sent[side, step - 1] = self.chunk(at).astype(BF16)

            def later(at=at, side=side, back=back):
                self.copies.got((self.name, side, step - 1), self.got_ref.at[side, step - 2], back)
                self.sent[side, step - 1] = (
                    self.chunk(at) + self.got_ref[side, step - 2].astype(F32)
                ).astype(BF16)

            pl.when(sends & (place == 0))(first)
            if step > 1:
                pl.when(sends & (place > 0))(later)
            self.copies.send(
                (self.name, side, step), target, self.got_ref.at[side, step - 1], onward, sends
            )

    def total(self, result):
        last = self.count - 1
        result[...] = self.chunk(self.z)
        for side, place, _, _, back in self.sides():

            def add(side=side, back=back):
                self.copies.got((self.name, side, last), self.got_ref.at[side, last - 1], back)
                result[...] += self.got_ref[side, last - 1].astype(F32)

            pl.when(place > 0)(add)


class PieceSum:
    def __init__(self, copies, name, pos, orders, piece, got):
        self.copies, self.name, self.pos, self.orders = copies, name, pos, orders
        self.piece, self.got_ref = piece, got

    def masks(self, side, stage):
        order = self.orders[side]
        found = [0]
        for bit in order[stage:]:
            found += [mask ^ bit for mask in found]
        return [mask for mask in found if mask & order[stage]]

    def device(self, side, stage):
        return {"pos": jnp.bitwise_xor(self.pos, self.orders[side][stage])}

    def send(self, side, stage, mask):
        self.copies.send(
            (self.name, side, mask),
            self.piece(side, mask),
            self.got_ref(side, mask),
            self.device(side, stage),
        )

    def got(self, side, stage, mask):
        self.copies.got(
            (self.name, side, mask), self.got_ref(side, mask), self.device(side, stage)
        )

    def add(self, side, stage, mask):
        target = self.piece(side, mask ^ self.orders[side][stage])
        target[...] = (
            target[...].astype(F32) + self.got_ref(side, mask)[...].astype(F32)
        ).astype(BF16)

    def settle(self, stage):
        for side in range(2):
            onward = self.masks(side, stage + 1) if stage + 1 < len(self.orders[side]) else []
            masks = self.masks(side, stage)
            bit = self.orders[side][stage]
            for mask in sorted(masks, key=lambda mask: (mask ^ bit) not in onward):
                self.got(side, stage, mask)
                self.add(side, stage, mask)
                if mask ^ bit in onward:
                    self.send(side, stage + 1, mask ^ bit)


def last_sums_kernel(
    dims,
    kept,
    row_in,
    proj_grad,
    weight_in,
    lines,
    grad_residual,
    out_parts,
    token_lines,
    chan_sums,
    filt_grad,
    layers,
    mine,
    embedding,
    w_two,
    filter_columns,
    *rest,
):
    rz_count, pos_count = dims
    norm = lines.at[pl.ds(NORM_ROW, 8)]
    count = 2 * len(kept[0])
    own_pieces, moved_pieces, rest = rest[:count], rest[count : 2 * count], rest[2 * count :]
    input_grad, in_grad, up_grad, down_grad, out_grad, lines_out, inner_out = rest[:7]
    rest = rest[7:]
    (
        rows_v,
        proj_v,
        pieces_v,
        moved_v,
        pieces_got,
        bundle_sent,
        bundle_got,
        bundle_total,
        up_sent,
        up_got,
        e_v,
        e_got,
        in_total,
        in_sent,
        in_got,
        in_line_sent,
        in_line_got,
        in_mine,
        in_out,
        in_back,
        outs_v,
        outs_got,
        outs_line_sent,
        outs_line_got,
        outs_total,
        packed,
        packed_got,
        packed_pos,
        packed_total,
        inner,
        local_sems,
        send_sems,
        got_sems,
    ) = rest
    z, core, pos = lax.axis_index("rz"), lax.axis_index("core"), lax.axis_index("pos")
    rows_count = 2 * rz_count
    row = z * 2 + core
    bits = bits_of(pos_count)
    orders = (bits, bits[::-1])
    middle = rz_count // 2
    part_len, model_width = grad_residual.shape
    half = model_width // 2
    own_width, tile = up_sent.shape[1:]
    width = weight_in.shape[1]
    chan = width // 3
    columns = model_width // tile
    copies = Copies(local_sems, send_sems, got_sems)
    other = {"core": 1 - core}

    def row_device(at):
        return {"rz": at // 2, "core": at % 2}

    loads = []
    for side in range(2):
        for mask in kept[side]:
            at = 2 * kept[side].index(mask) + side
            part = pl.ds(side * middle, middle)
            loads.append(copies.local(own_pieces[at], pieces_v.at[kept[side].index(mask), part]))
            loads.append(copies.local(moved_pieces[at], moved_v.at[kept[side].index(mask), part]))
    masks = sorted(range(pos_count), key=lambda mask: -bin(mask).count("1"))
    slots = rows_v.shape[0]

    def load_rows(at):
        start = jnp.bitwise_xor(pos, masks[at]) * part_len
        block = pl.ds(pl.multiple_of(start, part_len), part_len)
        return (
            copies.local(row_in.at[block], rows_v.at[at % slots]),
            copies.local(proj_grad.at[block], proj_v.at[at % slots]),
        )

    row_loads = [load_rows(at) for at in range(slots)]
    greet(
        [row_device((row + step) % rows_count) for step in range(1, rows_count)]
        + [{"pos": jnp.bitwise_xor(pos, mask)} for mask in range(1, pos_count)]
    )

    def half_ref(ref, slot, side):
        return ref.at[slot, pl.ds(side * middle, middle)]

    bundle = PieceSum(
        copies,
        "bundle",
        pos,
        orders,
        lambda side, mask: half_ref(pieces_v, kept[side].index(mask), side),
        lambda side, mask: half_ref(pieces_got, kept[side].index(mask) - 1, side),
    )
    for copy in loads:
        copy.wait()
    for side in range(2):
        second = bundle.masks(side, 1)
        for mask in sorted(kept[side], key=lambda mask: mask not in second):
            slot = kept[side].index(mask)
            for at in range(middle):
                place = side * middle + at
                pieces_v[slot, place] = (
                    pieces_v[slot, place].astype(F32) + moved_v[slot, place].astype(F32)
                ).astype(BF16)
            if mask in second:
                bundle.send(side, 1, mask)

    outs = PieceSum(
        copies,
        "outs",
        pos,
        orders,
        lambda side, mask: outs_v.at[pl.ds(side * middle, middle), jnp.bitwise_xor(pos, mask)],
        lambda side, mask: outs_got.at[mask, pl.ds(side * middle, middle)],
    )
    outs_v[...] = out_parts[...]
    for side in range(2):
        for mask in outs.masks(side, 0):
            outs.send(side, 0, mask)

    e_sums = PieceSum(
        copies,
        "rows",
        pos,
        orders,
        lambda side, mask: e_v.at[side, mask],
        lambda side, mask: e_got.at[side, mask - 1],
    )
    in_total[...] = jnp.zeros_like(in_total)
    packed_total[...] = jnp.zeros_like(packed_total)
    packed[...] = jnp.zeros_like(packed)
    sums = (jnp.zeros((1, model_width), F32), jnp.zeros((1, model_width), F32))
    for index, mask in enumerate(masks):
        if 1 <= index <= pos_count - slots:
            row_loads.append(load_rows(slots + index - 1))
        for copy in row_loads[index]:
            copy.wait()

        def tile_step(at, sums, mask=mask, slot=index % slots):
            rows = pl.ds(pl.multiple_of(at * BLOCK, BLOCK), BLOCK)
            unit, _ = norm_parts(rows_v[slot, rows].astype(F32))
            normed = (unit * norm[0:1, :] + norm[1:2, :]).astype(BF16)
            grad = proj_v[slot, rows]
            cotangent = lax.dot_general(
                grad, weight_in[...], (((1,), (1,)), ((), ())), preferred_element_type=F32
            )
            e_v[0, mask, rows] = cotangent[:, :half].astype(BF16)
            e_v[1, mask, rows] = cotangent[:, half:].astype(BF16)
            in_total[...] += lax.dot_general(
                normed, grad, (((0,), (0,)), ((), ())), preferred_element_type=F32
            )
            return (
                sums[0] + jnp.sum(cotangent * unit, axis=0, keepdims=True),
                sums[1] + jnp.sum(cotangent, axis=0, keepdims=True),
            )

        sums = lax.fori_loop(0, part_len // BLOCK, tile_step, sums)
        for side in range(2):
            if mask in e_sums.masks(side, 0):
                e_sums.send(side, 0, mask)

    block_rows = pos_count * own_width
    for at in range(rz_count):
        rows = pl.ds(pl.multiple_of((2 * at + 1 - core) * block_rows, block_rows), block_rows)
        in_sent[at] = in_total[rows, :].astype(BF16)
    copies.send(("in core",), in_sent, in_got, other)

    groups = model_width // 128
    per = rows_count // groups
    token_rows, chan_rows = token_lines.shape[0], mine.shape[0]
    inner_rows = inner.shape[0] // groups
    line_rows = token_rows + chan_rows
    three_grad = filter_back(
        filt_grad, layers, mine[THREE_ROW:NORM_ROW, :], embedding, w_two, filter_columns, inner
    )
    for at in range(groups):
        lanes = pl.ds(at * 128, 128)
        packed[at, 0:token_rows] = token_lines[:, lanes]
        packed[at, 0:1] = sums[0][:, at * 128 : (at + 1) * 128]
        packed[at, 1:2] = sums[1][:, at * 128 : (at + 1) * 128]
        packed[at, line_rows:] = inner[pl.ds(at * inner_rows, inner_rows), :]
    for at in range(chan // 128):
        group, lanes = pos * (chan // 128) + at, pl.ds(at * 128, 128)
        packed[group, token_rows : token_rows + THREE_ROW] = chan_sums[:, lanes]
        packed[group, token_rows + THREE_ROW : line_rows] = three_grad[
            :, at * 128 : (at + 1) * 128
        ]

    def owns(at):
        return None if per == 1 else at % per == 0

    def when(condition, action):
        if condition is None:
            action()
        else:
            pl.when(condition)(action)

    for step in range(1, rows_count):
        to = (row + step) % rows_count
        copies.send(
            ("lines", step), packed.at[to // per], packed_got.at[step], row_device(to), owns(to)
        )

    for stage in range(1, len(bits)):
        bundle.settle(stage)
    outs.settle(0)
    zero_slot = kept[0].index(0)
    bundle_line = LineSum(
        copies,
        "bundle line",
        rz_count,
        z,
        lambda at: pieces_v[zero_slot, at].astype(F32),
        bundle_sent,
        bundle_got,
    )
    bundle_line.step(1)
    copies.got(("in core",), in_got, other)

    def in_chunk(at):
        rows = pl.ds(pl.multiple_of((2 * at + core) * block_rows, block_rows), block_rows)
        return in_total[rows, :] + in_got[at].astype(F32)

    in_line = LineSum(copies, "in line", rz_count, z, in_chunk, in_line_sent, in_line_got)
    in_line.step(1)
    e_sums.settle(0)

    def add_lines():
        packed_total[...] = packed[row // per]
        for step in range(1, rows_count):
            copies.got(("lines", step), packed_got.at[step], row_device((row - step) % rows_count))
            packed_total[...] += packed_got[step]
        packed_pos[pos] = packed_total[...]

    when(owns(row), add_lines)
    for mask in range(1, pos_count):
        copies.send(
            ("lines pos", mask),
            packed_total,
            packed_pos.at[pos],
            {"pos": jnp.bitwise_xor(pos, mask)},
            owns(row),
        )
    for stage in range(1, len(bits)):
        outs.settle(stage)
    outs_line = LineSum(
        copies,
        "outs line",
        rz_count,
        z,
        lambda at: outs_v[at, pos].astype(F32),
        outs_line_sent,
        outs_line_got,
    )
    outs_line.step(1)
    for step in range(2, rz_count):
        in_line.step(step)
        outs_line.step(step)
        bundle_line.step(step)
        if step == 2:
            for stage in range(1, len(bits)):
                e_sums.settle(stage)

    def input_step(at, _):
        rows = pl.ds(pl.multiple_of(at * BLOCK, BLOCK), BLOCK)
        unit, scale = norm_parts(rows_v[(pos_count - 1) % slots, rows].astype(F32))
        cotangent = jnp.concatenate(
            [e_v[0, 0, rows].astype(F32), e_v[1, 0, rows].astype(F32)], axis=1
        )
        scaled = cotangent * norm[0:1, :]
        grad = scale * (
            scaled
            - jnp.mean(scaled, axis=-1, keepdims=True)
            - unit * jnp.mean(scaled * unit, axis=-1, keepdims=True)
        )
        input_grad[rows, :] = (grad_residual[rows, :] + grad).astype(BF16)
        return 0

    lax.fori_loop(0, part_len // BLOCK, input_step, 0)

    def sum_lines():
        for mask in range(1, pos_count):
            owner = jnp.bitwise_xor(pos, mask)
            copies.got(("lines pos", mask), packed_pos.at[owner], {"pos": owner})
        total = packed_pos[0]
        for at in range(1, pos_count):
            total = total + packed_pos[at]
        lines_out[...] = total[:line_rows]
        inner_out[row // per] = total[line_rows:]

    when(owns(row), sum_lines)
    for step in range(1, rows_count):
        to = (row + step) % rows_count
        block = inner_out.at[row // per]
        copies.send(("inner", step), block, block, row_device(to), owns(row))
        if step < per:
            copies.send(
                ("lines row", step),
                lines_out,
                lines_out,
                row_device(to),
                owns(row),
            )

    in_line.total(in_mine)
    for mask in range(1, pos_count):
        owner = jnp.bitwise_xor(pos, mask)
        rows = pl.ds(pl.multiple_of(owner * own_width, own_width), own_width)
        in_out[mask] = in_mine[rows, :].astype(BF16)
        copies.send(("in pos", mask), in_out.at[mask], in_back.at[mask], {"pos": owner})
    mine = in_mine[pl.ds(pl.multiple_of(pos * own_width, own_width), own_width), :]
    cols = pl.ds(pl.multiple_of(pos * chan, chan), chan)
    for at in range(3):
        in_grad[at, :, cols] = mine[:, at * chan : (at + 1) * chan]

    outs_line.total(outs_total)
    out_grad[...] = outs_total[...]
    bundle_line.total(bundle_total)
    up_sent[...] = bundle_total[
        pl.ds(pl.multiple_of((1 - core) * rz_count, rz_count), rz_count)
    ].astype(BF16)
    copies.send(("up core",), up_sent, up_got, other)
    down_units = (bundle_total.shape[0] - 2 * rz_count) // columns
    for col in range(columns):
        for at in range(down_units):
            down_grad[at * own_width : (at + 1) * own_width, col * tile : (col + 1) * tile] = (
                bundle_total[2 * rz_count + col * down_units + at]
            )
    for at in range(rz_count):
        cols = pl.ds(pl.multiple_of((2 * at + core) * tile, tile), tile)
        up_grad[:, cols] = bundle_total[core * rz_count + at]
    for mask in range(1, pos_count):
        owner = jnp.bitwise_xor(pos, mask)
        copies.got(("in pos", mask), in_back.at[mask], {"pos": owner})
        cols = pl.ds(pl.multiple_of(owner * chan, chan), chan)
        for at in range(3):
            in_grad[at, :, cols] = in_back[mask, :, at * chan : (at + 1) * chan].astype(F32)
    copies.got(("up core",), up_got, other)
    for at in range(rz_count):
        cols = pl.ds(pl.multiple_of((2 * at + 1 - core) * tile, tile), tile)
        up_grad[:, cols] = up_got[at].astype(F32)
    for step in range(1, rows_count):
        origin = (row - step) % rows_count

        def take(step=step, origin=origin):
            copies.got(("inner", step), inner_out.at[origin // per], row_device(origin))

        when(owns(origin), take)
        if step < per:

            def take_lines(step=step, origin=origin):
                copies.got(("lines row", step), lines_out, row_device(origin))

            when(origin == row // per * per, take_lines)
    copies.finish()


def filter_back(filt_grad, layers, three, embedding, w_two, columns, inner):
    frequency = columns[:, 2:3]
    three_grad = exact(layers[1], filt_grad[...], ((1,), (0,)))
    grad = exact(three, filt_grad[...], ((1,), (1,))) * layers[5]
    freq_grad = jnp.sum(grad * layers[3], axis=1, keepdims=True)
    grad = grad * frequency
    bias_two = jnp.sum(grad, axis=1, keepdims=True)
    order = grad.shape[0]
    inner[...] = jnp.zeros_like(inner)
    inner[FEATURES : FEATURES + order, :order] = exact(layers[0], grad, ((1,), (1,)))
    grad = exact(w_two[...].astype(F32), grad, ((1,), (0,))) * layers[4]
    freq_grad += jnp.sum(grad * layers[2], axis=1, keepdims=True)
    grad = grad * frequency
    bias_one = jnp.sum(grad, axis=1, keepdims=True)
    inner[:FEATURES, :order] = exact(embedding[...], grad, ((1,), (1,)))
    held = inner[:order, :]
    lane = lax.broadcasted_iota(jnp.int32, held.shape, 1)
    for at, value in enumerate((bias_one, bias_two, freq_grad)):
        held = jnp.where(lane == order + at, value, held)
    inner[:order, :] = held
    return three_grad


def finish_kernel(place, total, shared, *outs):
    own_width = outs[0].shape[1]
    moved = pltpu.roll(total[...], 128 - place[0], 1)[:, :own_width]
    (
        pre_gain,
        pre_bias,
        out_bias,
        post_gain,
        post_bias,
        down_bias,
        short_weight,
        short_bias,
        in_bias,
        skip,
        three,
        up_bias,
        w_one,
        b_one,
        w_two,
        b_two,
        frequency,
    ) = outs
    for at, out in enumerate((pre_gain, pre_bias, out_bias, post_gain, post_bias, down_bias)):
        out[...] = moved[at : at + 1]
    for at in range(3):
        short_weight[at] = moved[16 + 3 * at : 19 + 3 * at]
    short_bias[...] = moved[25:28]
    in_bias[...] = moved[28:31]
    skip[...] = moved[31:32]
    three[...] = moved[32:96]
    rows = pltpu.roll(total[0:16, :], 128 - place[2], 1)[:, : up_bias.shape[1]]
    line = lax.broadcasted_iota(jnp.int32, rows.shape, 0)
    up_bias[...] = jnp.sum(jnp.where(line == 6 + place[1], rows, 0.0), axis=0, keepdims=True)
    inner = shared[...].reshape(-1, 128)
    order = w_two.shape[0]
    w_one[...] = inner[: w_one.shape[0], :order]
    w_two[...] = inner[FEATURES : FEATURES + order, :order]
    turned = inner[:128, :].T
    b_one[...] = turned[order : order + 1, :order]
    b_two[...] = turned[order + 1 : order + 2, :order]
    frequency[...] = turned[order + 2 : order + 3, :order]


def finish(place, total, shared, own_width, ff_own, features, order):
    shapes = [(1, own_width)] * 6
    shapes += [(3, 3, own_width), (3, own_width), (3, own_width), (1, own_width)]
    shapes += [(order, own_width), (1, ff_own), (features, order), (1, order), (order, order)]
    shapes += [(1, order), (1, order)]
    inside = pl.BlockSpec(memory_space=pltpu.VMEM)
    return pl.pallas_call(
        finish_kernel,
        out_shape=[jax.ShapeDtypeStruct(shape, F32) for shape in shapes],
        in_specs=[pl.BlockSpec(memory_space=pltpu.SMEM), inside, inside],
        out_specs=[inside] * len(shapes),
        name="finish",
    )(place, total, shared)


def last_sums(
    dims,
    kept,
    row_in,
    proj_grad,
    weight_in,
    lines,
    grad_residual,
    out_parts,
    token_lines,
    chan_sums,
    filt_grad,
    layers,
    mine,
    embedding,
    w_two,
    filter_columns,
    own_pieces,
    moved_pieces,
):
    rz_count, pos_count = dims
    part_len, model_width = grad_residual.shape
    piece = own_pieces[0].shape
    units, own_width, tile = piece[1:]
    width = weight_in.shape[1]
    block_rows = pos_count * own_width
    groups = model_width // 128
    line_rows = token_lines.shape[0] + mine.shape[0]
    inner_rows = 2 * FEATURES // groups
    slots = len(kept[0])
    steps = rz_count - 1
    rows_count = 2 * rz_count
    ff_own = (units - 2 * rz_count) * own_width * tile // model_width
    anywhere = pl.BlockSpec(memory_space=pl.ANY)
    inside = pl.BlockSpec(memory_space=pltpu.VMEM)
    local_count = 4 * len(kept[0]) + 2 * pos_count
    remote_count = (
        3 * 2 * pos_count + 3 * 2 * steps + 2 + 3 * rows_count + 3 * pos_count
    )
    half = model_width // 2
    vmem = pltpu.VMEM
    return pl.pallas_call(
        functools.partial(last_sums_kernel, dims, kept),
        out_shape=(
            jax.ShapeDtypeStruct((part_len, model_width), BF16),
            jax.ShapeDtypeStruct((3, own_width, model_width), F32),
            jax.ShapeDtypeStruct((own_width, 2 * rz_count * tile), F32),
            jax.ShapeDtypeStruct((ff_own, model_width), F32),
            jax.ShapeDtypeStruct((own_width, model_width), F32),
            jax.ShapeDtypeStruct((line_rows, 128), F32),
            jax.ShapeDtypeStruct((groups, inner_rows, 128), F32),
        ),
        in_specs=[anywhere, anywhere] + [inside] * 12 + [anywhere] * (2 * len(own_pieces)),
        out_specs=(inside,) * 7,
        scratch_shapes=[
            vmem((pos_count - 1, part_len, model_width), BF16),
            vmem((pos_count - 1, part_len, width), BF16),
            vmem((slots, rz_count, units, own_width, tile), BF16),
            vmem((slots, rz_count, units, own_width, tile), BF16),
            vmem((slots - 1, rz_count, units, own_width, tile), BF16),
            vmem((2, steps, units, own_width, tile), BF16),
            vmem((2, steps, units, own_width, tile), BF16),
            vmem((units, own_width, tile), F32),
            vmem((rz_count, own_width, tile), BF16),
            vmem((rz_count, own_width, tile), BF16),
            vmem((2, pos_count, part_len, half), BF16),
            vmem((2, pos_count - 1, part_len, half), BF16),
            vmem((model_width, width), F32),
            vmem((rz_count, block_rows, width), BF16),
            vmem((rz_count, block_rows, width), BF16),
            vmem((2, steps, block_rows, width), BF16),
            vmem((2, steps, block_rows, width), BF16),
            vmem((block_rows, width), F32),
            vmem((pos_count, own_width, width), BF16),
            vmem((pos_count, own_width, width), BF16),
            vmem((rz_count, pos_count, own_width, model_width), BF16),
            vmem((pos_count, rz_count, own_width, model_width), BF16),
            vmem((2, steps, own_width, model_width), BF16),
            vmem((2, steps, own_width, model_width), BF16),
            vmem((own_width, model_width), F32),
            vmem((groups, line_rows + inner_rows, 128), F32),
            vmem((rows_count, line_rows + inner_rows, 128), F32),
            vmem((pos_count, line_rows + inner_rows, 128), F32),
            vmem((line_rows + inner_rows, 128), F32),
            vmem((2 * FEATURES, 128), F32),
            pltpu.SemaphoreType.DMA((local_count,)),
            pltpu.SemaphoreType.DMA((remote_count,)),
            pltpu.SemaphoreType.DMA((remote_count,)),
        ],
        compiler_params=pltpu.CompilerParams(
            collective_id=0, has_side_effects=True, vmem_limit_bytes=VMEM_LIMIT
        ),
        cost_estimate=pl.CostEstimate(flops=10**7, bytes_accessed=10**7, transcendentals=0),
        name="last_sums",
    )(
        row_in,
        proj_grad,
        weight_in,
        lines,
        grad_residual,
        out_parts,
        token_lines,
        chan_sums,
        filt_grad,
        layers,
        mine,
        embedding,
        w_two,
        filter_columns,
        *own_pieces,
        *moved_pieces,
    )


def bits_of(count):
    return [1 << at for at in range(count.bit_length() - 1)]


def on_device(
    activations,
    out_grad,
    doc_bounds,
    doc_ids,
    pre_gain,
    pre_bias,
    in_weight,
    in_bias,
    short_weight,
    short_bias,
    skip_gain,
    out_weight,
    out_bias,
    post_gain,
    post_bias,
    up_weight,
    up_bias,
    down_weight,
    down_bias,
    filter_one,
    filter_bias_one,
    filter_two,
    filter_bias_two,
    filter_freq,
    filter_three,
):
    rz_count, pos_count = lax.axis_size("rz"), lax.axis_size("pos")
    pos, core = lax.axis_index("pos"), lax.axis_index("core")
    everything = ("rz", "core", "pos")
    owners = rz_count * 2 * pos_count
    own_at = (lax.axis_index("rz") * 2 + core) * pos_count + pos
    part_len, model_width = activations.shape[1:]
    length = part_len * pos_count
    own_width = pre_gain.shape[0]
    chan = model_width // pos_count
    ff_own = down_weight.shape[0]
    ff_half = rz_count * pos_count * ff_own
    docs = doc_bounds.shape[1]
    order = filter_two.shape[0]
    tables = transform_tables()
    meta = unit_table(doc_bounds[0], length, (pos * chan).astype(jnp.int32))

    single = functools.partial(jnp.reshape, shape=(1, -1))
    vectors = [
        short_weight,
        short_bias,
        single(skip_gain),
        in_bias,
        filter_three,
        single(pre_gain),
        single(pre_bias),
        single(out_bias),
        single(post_gain),
        single(post_bias),
        single(down_bias),
        single(up_bias),
    ]
    filter_columns = jnp.stack([filter_bias_one, filter_bias_two, filter_freq], 1).astype(F32)
    embedding = positions_table(length, filter_one.shape[0])
    row_in, weight_in, bundle, extra, out_all, lines, mine, up_bias_half, layers = gather(
        (rz_count, pos_count),
        activations[0],
        in_weight.transpose(1, 0, 2),
        up_weight,
        down_weight,
        out_weight,
        vectors,
        (embedding, filter_one, filter_two, filter_columns),
    )
    row_in = row_in.reshape(length, model_width)
    weight_in = weight_in.reshape(model_width, -1)
    out_all = out_all.reshape(model_width, model_width)
    tile = pos_count * ff_own
    columns = model_width // tile
    bits = bits_of(pos_count)
    orders = (bits, bits[::-1])
    place = jnp.stack([pos, lax.axis_index("rz")]).astype(jnp.int32)

    own_in = activations[0]
    projected = project(row_in, lines, weight_in, mine)
    sides = [{0: bundle[: rz_count // 2]}, {0: bundle[rz_count // 2 :]}]
    firsts = [[swap(sides[side][0], "pos", bit) for bit in bits] for side in range(2)]

    def along(values, distance):
        ups = [(at, at + 1) for at in range(distance - 1, rz_count - 1)]
        downs = [(at + 1, at) for at in range(rz_count - distance)]
        return [lax.ppermute(values[0], "rz", ups), lax.ppermute(values[1], "rz", downs)]

    moved = [along([extra, extra], 1)]
    projected, moved = lax.optimization_barrier((projected, moved))
    for distance in range(2, rz_count - 1):
        moved.append(along(moved[-1], distance))
    branch, mixed = mixer_forward(meta, docs, projected, layers, mine, model_width, tables)
    branch, firsts, moved = lax.optimization_barrier((branch, firsts, moved))
    extras = [extra] + [pair[0] for pair in moved] + [pair[1] for pair in moved]
    given = [0] + bits
    pieces = [
        sides[side][0] if bit == 0 else firsts[side][bits.index(bit)]
        for bit in given
        for side in range(2)
    ]
    result, grad_residual, branch_grad, out_parts, token_lines, *piece_grads = middle(
        (rz_count, pos_count),
        given,
        branch,
        activations[0],
        out_all,
        lines,
        out_grad[0],
        up_bias_half,
        pieces,
        extras,
    )
    out_parts = out_parts.reshape(rz_count, pos_count, own_width, model_width)
    result = result[None]

    masks = list(range(pos_count))
    kept = [[mask for mask in masks if not mask & orders[side][0]] for side in range(2)]
    by_mask = {
        (side, mask): piece_grads[2 * at + side]
        for at, mask in enumerate(masks)
        for side in range(2)
    }
    own_pieces = [by_mask[side, kept[side][at]] for at in range(len(kept[0])) for side in range(2)]
    moved_pieces = [
        swap(by_mask[side, kept[side][at] ^ orders[side][0]], "pos", orders[side][0])
        for at in range(len(kept[0]))
        for side in range(2)
    ]

    proj_grad, filt_grad, chan_sums = mixer_backward(
        meta, docs, projected, layers, mine, model_width, tables, mixed, branch_grad
    )
    input_grad, weight_in_grad, up_weight_grad, down_weight_grad, out_weight_grad, total, shared = (
        last_sums(
            (rz_count, pos_count),
            kept,
            row_in,
            proj_grad,
            weight_in,
            lines,
            grad_residual,
            out_parts,
            token_lines,
            chan_sums,
            filt_grad,
            layers,
            mine,
            embedding,
            filter_two,
            filter_columns,
            own_pieces,
            moved_pieces,
        )
    )
    input_grad = input_grad[None]
    weight_in_grad = weight_in_grad.transpose(1, 0, 2)
    lane = lax.rem(own_at * own_width, 128)
    up_place = lax.rem(own_at * ff_own, owners * ff_own * 128 // model_width)
    place = jnp.stack([lane, up_place // 128, up_place % 128]).astype(jnp.int32)
    (
        pre_gain_grad,
        pre_bias_grad,
        out_bias_grad,
        post_gain_grad,
        post_bias_grad,
        down_bias_grad,
        short_weight_grad,
        short_bias_grad,
        in_bias_grad,
        skip_grad,
        three_grad,
        up_bias_grad,
        one_grad,
        bias_one_grad,
        two_grad,
        bias_two_grad,
        freq_grad,
    ) = finish(place, total, shared, own_width, ff_own, filter_one.shape[0], order)
    return (
        result,
        input_grad,
        pre_gain_grad[0],
        pre_bias_grad[0],
        weight_in_grad,
        in_bias_grad,
        short_weight_grad,
        short_bias_grad,
        skip_grad[0],
        out_weight_grad,
        out_bias_grad[0],
        post_gain_grad[0],
        post_bias_grad[0],
        up_weight_grad,
        up_bias_grad[0],
        down_weight_grad,
        down_bias_grad[0],
        one_grad,
        bias_one_grad[0],
        two_grad,
        bias_two_grad[0],
        freq_grad[0],
        three_grad,
    )


def solution(mesh):
    rows_count, pos_count = mesh.devices.shape
    fine = Mesh(mesh.devices.reshape(rows_count // 2, 2, pos_count), ("rz", "core", "pos"))
    rows = ("rz", "core")
    every = ("rz", "core", "pos")
    tokens = P(rows, "pos", None)
    vector = P(every)
    matrix = P(every, None)
    return jax.shard_map(
        on_device,
        mesh=fine,
        in_specs=(
            tokens,
            tokens,
            P(rows, None),
            P(rows, None),
            vector,
            vector,
            P(every, None, None),
            P(None, every),
            P(None, None, every),
            P(None, every),
            vector,
            matrix,
            vector,
            vector,
            vector,
            matrix,
            vector,
            matrix,
            vector,
            P(),
            P(),
            P(),
            P(),
            P(),
            P(None, every),
        ),
        out_specs=(
            tokens,
            tokens,
            vector,
            vector,
            P(every, None, None),
            P(None, every),
            P(None, None, every),
            P(None, every),
            vector,
            matrix,
            vector,
            vector,
            vector,
            matrix,
            vector,
            matrix,
            vector,
            P(),
            P(),
            P(),
            P(),
            P(),
            P(None, every),
        ),
        check_vma=False,
    )
```

```python
import functools
import math

import jax
import jax.numpy as jnp
import ml_dtypes
import numpy as np
from jax import lax
from jax.experimental import pallas as pl
from jax.experimental.pallas import tpu as pltpu
from jax.sharding import Mesh
from jax.sharding import PartitionSpec as P

HIGHEST = lax.Precision.HIGHEST
F32 = jnp.float32
BF16 = jnp.bfloat16
BLOCK = 256
FREQ_CHUNK = 64
VMEM_LIMIT = 60 * 1024 * 1024


def layer_norm(values, norm_gain, norm_shift):
    centre = values - jnp.mean(values, axis=-1, keepdims=True)
    spread = jnp.mean(centre * centre, axis=-1, keepdims=True)
    return centre * lax.rsqrt(spread + 1e-05) * norm_gain + norm_shift


FEATURES = 64
THREE_ROW, NORM_ROW, UP_ROW, LINES = 16, 80, 86, 96


def positions_table(length, features):
    band_count = (features - 1) // 2
    places = np.arange(length, dtype=np.float64)
    ladder = 0.0001 + (band_count - 1 - 0.0001) * np.arange(band_count) / (band_count - 1)
    angles = 2.0 * math.pi / length * places[:, None] * ladder[None, :]
    table = np.zeros((FEATURES, length), np.float32)
    table[0] = places / (length - 1)
    table[1 : 1 + band_count] = np.cos(angles).T
    table[1 + band_count : features] = -np.sin(angles).T
    return jnp.asarray(table)


def decay_of(block, length, first_channel, model_width, width):
    place = lax.broadcasted_iota(jnp.int32, (BLOCK, width), 0) + block * BLOCK
    channel = lax.broadcasted_iota(jnp.int32, (BLOCK, width), 1) + first_channel
    slow_rate = math.log(0.01) / 1.5
    fast_rate = math.log(0.01) / 0.3
    rates = jnp.abs(
        slow_rate + (fast_rate - slow_rate) * channel.astype(F32) * (1.0 / (model_width - 1))
    )
    return jnp.exp(-(place.astype(F32) * (1.0 / (length - 1))) * rates) + 0.05


def exact(left, right, contract):
    return lax.dot_general(
        left, right, (contract, ((), ())), precision=HIGHEST, preferred_element_type=F32
    )


def filter_block(layers, lines, block, units, length, width, model_width):
    layer_two = layers[1, :, rows_of(block)]
    three = lines[THREE_ROW : THREE_ROW + layer_two.shape[0], :].astype(BF16)
    decay = decay_of(block, length, units.channel(), model_width, width)
    high = layer_two.astype(BF16)
    low = (layer_two - high.astype(F32)).astype(BF16)
    filt = lax.dot_general(
        jnp.concatenate([high, low], axis=0),
        jnp.concatenate([three, three], axis=0),
        (((0,), (0,)), ((), ())),
        preferred_element_type=F32,
    )
    return filt, decay


def transform_tables():
    order = np.concatenate([np.arange(0, BLOCK, 2), np.arange(1, BLOCK, 2)])
    angle = math.pi / BLOCK * (order[:, None] + 0.5) * np.arange(BLOCK)[None, :]
    forward = np.concatenate([np.cos(angle), -np.sin(angle)], axis=0)
    tables = []
    for table in (forward, forward.T / BLOCK):
        high = table.astype(ml_dtypes.bfloat16)
        low = (table - high.astype(np.float64)).astype(ml_dtypes.bfloat16)
        tables.append(jnp.asarray(high))
    return tables


def unit_table(bounds, length, first_channel):
    docs = bounds.shape[0]
    units = length // BLOCK + docs - 1
    ends = jnp.concatenate([bounds[1:], jnp.full((1,), length, jnp.int32)])
    first = bounds // BLOCK
    count = jnp.where(ends > bounds, (ends - 1) // BLOCK - first + 1, 0)
    earlier = jnp.arange(docs)[:, None] >= jnp.arange(docs)[None, :]
    stops = jnp.sum(jnp.where(earlier, count[None, :], 0), axis=1)
    starts = stops - count
    unit = jnp.arange(units, dtype=jnp.int32)
    doc = jnp.sum((unit[:, None] >= stops[None, :]).astype(jnp.int32), axis=1)
    doc = jnp.minimum(doc, docs - 1)
    pick = (doc[:, None] == jnp.arange(docs)[None, :]).astype(jnp.int32)

    def of_doc(values):
        return jnp.sum(pick * values[None, :], axis=1)

    block = jnp.clip(of_doc(first - starts) + unit, 0, length // BLOCK - 1)
    return jnp.concatenate(
        [
            block,
            of_doc(bounds),
            of_doc(ends),
            of_doc(starts),
            of_doc(stops),
            starts,
            stops,
            bounds,
            stops[docs - 1 :],
            jnp.reshape(first_channel, (1,)),
        ]
    ).astype(jnp.int32)


class Units:
    def __init__(self, meta, length, docs):
        self.meta = meta
        self.docs = docs
        self.units = length // BLOCK + docs - 1

    def block(self, unit):
        return self.meta[unit]

    def low(self, unit):
        return self.meta[self.units + unit]

    def high(self, unit):
        return self.meta[2 * self.units + unit]

    def start(self, unit):
        return self.meta[3 * self.units + unit]

    def stop(self, unit):
        return self.meta[4 * self.units + unit]

    def doc_start(self, doc):
        return self.meta[5 * self.units + doc]

    def doc_stop(self, doc):
        return self.meta[5 * self.units + self.docs + doc]

    def bound(self, doc):
        return self.meta[5 * self.units + 2 * self.docs + doc]

    def total(self):
        return self.meta[5 * self.units + 3 * self.docs]

    def channel(self):
        return self.meta[5 * self.units + 3 * self.docs + 1]

    def inside(self, unit, width):
        place = lax.broadcasted_iota(jnp.int32, (BLOCK, width), 0) + self.block(unit) * BLOCK
        return (place >= self.low(unit)) & (place < self.high(unit))


def rows_of(block):
    return pl.ds(pl.multiple_of(block * BLOCK, BLOCK), BLOCK)


def times(table, value):
    high = value.astype(BF16)
    low = (value - high.astype(F32)).astype(BF16)
    return jnp.dot(
        table[...], high, preferred_element_type=F32
    )


def tap_masks(units, block, width, ahead=0):
    place = lax.broadcasted_iota(jnp.int32, (BLOCK, width), 0) + (block * BLOCK + ahead)
    first = place == units.bound(0)
    second = place == units.bound(0) + 1
    for doc in range(1, units.docs):
        first = first | (place == units.bound(doc))
        second = second | (place == units.bound(doc) + 1)
    return jnp.logical_not(first), jnp.logical_not(first | second)


def delayed(ref, block):
    start = block * BLOCK
    here = ref[rows_of(block), :].astype(F32)
    before = ref[pl.ds(pl.multiple_of(jnp.maximum(start - 16, 0), 16), 16), :].astype(F32)
    joined = jnp.concatenate([before, here], axis=0)
    return (here, pltpu.roll(joined, 1, 0)[16:], pltpu.roll(joined, 2, 0)[16:])


def short_conv(parts, small, branch, masks):
    total = small[9 + branch : 10 + branch, :] + small[branch : branch + 1, :] * parts[0]
    total += jnp.where(masks[0], small[3 + branch : 4 + branch, :] * parts[1], 0.0)
    total += jnp.where(masks[1], small[6 + branch : 7 + branch, :] * parts[2], 0.0)
    return total


def mixer_forward_kernel(
    docs, model_width, meta, post, pre, val, layers, small, fwd, inv, branch, mixed, gated, spec, taps, prod
):
    length, width = gated.shape
    blocks = length // BLOCK
    units = Units(meta, length, docs)

    def gate(block, _):
        masks = tap_masks(units, block, width)
        part = short_conv(delayed(val, block), small, 2, masks)
        part *= short_conv(delayed(pre, block), small, 1, masks)
        gated[rows_of(block), :] = part
        mixed[rows_of(block), :] = small[12:13, :] * part
        filt, decay = filter_block(layers, small, block, units, length, width, model_width)
        taps[block] = times(fwd, filt * decay)
        return 0

    lax.fori_loop(0, blocks, gate, 0)

    def transform(unit, _):
        value = gated[rows_of(units.block(unit)), :]
        spec[unit] = times(fwd, jnp.where(units.inside(unit, width), value, 0.0))
        return 0

    lax.fori_loop(0, units.total(), transform, 0)

    def multiply(unit, _):
        for low in range(0, BLOCK, FREQ_CHUNK):
            re, im = pl.ds(low, FREQ_CHUNK), pl.ds(BLOCK + low, FREQ_CHUNK)

            def step(back, total):
                at = unit - back
                s_re, s_im, t_re, t_im = spec[at, re], spec[at, im], taps[back, re], taps[back, im]
                return (
                    total[0] + (s_re * t_re - s_im * t_im),
                    total[1] + (s_re * t_im + s_im * t_re),
                )

            zero = jnp.zeros((FREQ_CHUNK, width), F32)
            total = lax.fori_loop(0, unit - units.start(unit) + 1, step, (zero, zero))
            prod[unit, re] = total[0]
            prod[unit, im] = total[1]
        return 0

    lax.fori_loop(0, units.total(), multiply, 0)

    half = BLOCK // 2

    def bring_back(unit, _):
        last = jnp.maximum(unit - 1, 0)
        old = jnp.where(unit > units.start(unit), prod[last], 0.0)
        new = prod[unit]
        joined = jnp.concatenate(
            [
                new[:half] - old[BLOCK : BLOCK + half],
                new[half:BLOCK] + old[BLOCK + half :],
                new[BLOCK : BLOCK + half] + old[:half],
                new[BLOCK + half :] - old[half:BLOCK],
            ],
            axis=0,
        )
        value = times(inv, joined)
        rows = rows_of(units.block(unit))
        mixed[rows, :] += jnp.where(units.inside(unit, width), value, 0.0)
        return 0

    lax.fori_loop(0, units.total(), bring_back, 0)

    def finish(block, _):
        masks = tap_masks(units, block, width)
        gate_value = short_conv(delayed(post, block), small, 0, masks)
        branch[rows_of(block), :] = (gate_value * mixed[rows_of(block), :]).astype(BF16)
        return 0

    lax.fori_loop(0, blocks, finish, 0)


def mixer_backward_kernel(
    docs,
    model_width,
    meta,
    post,
    pre,
    val,
    layers,
    small,
    fwd,
    inv,
    mixed,
    branch_grad,
    proj_grad,
    filt_grad,
    sums,
    gated,
    gm,
    conv_grad,
    spec,
    taps,
    prod,
):
    length, width = gated.shape
    blocks = length // BLOCK
    units = Units(meta, length, docs)
    half = BLOCK // 2
    sums[...] = jnp.zeros_like(sums)

    def total_rows(value):
        return jnp.sum(value, axis=0, keepdims=True)

    def gate(block, _):
        rows = rows_of(block)
        masks = tap_masks(units, block, width)
        part = short_conv(delayed(val, block), small, 2, masks)
        part *= short_conv(delayed(pre, block), small, 1, masks)
        gated[rows, :] = part
        grad = branch_grad[rows, :].astype(F32)
        mix_grad = grad * short_conv(delayed(post, block), small, 0, masks)
        gm[rows, :] = mix_grad
        conv_grad[0, rows, :] = grad * mixed[rows, :]
        conv_grad[1, rows, :] = small[12:13, :] * mix_grad
        sums[15:16, :] += total_rows(part * mix_grad)
        filt, decay = filter_block(layers, small, block, units, length, width, model_width)
        taps[block] = times(fwd, filt * decay)
        return 0

    lax.fori_loop(0, blocks, gate, 0)

    def transform(unit, _):
        rows = rows_of(units.block(unit))
        inside = units.inside(unit, width)
        spec[unit] = times(fwd, jnp.where(inside, gated[rows, :], 0.0))
        prod[unit] = times(fwd, jnp.where(inside, gm[rows, :], 0.0))
        return 0

    lax.fori_loop(0, units.total(), transform, 0)

    def spread(unit, _):
        after = jnp.minimum(unit + 1, units.units - 1)
        new = jnp.where(unit + 1 < units.stop(unit), prod[after], 0.0)
        prod[unit, pl.ds(0, half)] += new[BLOCK : BLOCK + half]
        prod[unit, pl.ds(half, half)] -= new[BLOCK + half :]
        prod[unit, pl.ds(BLOCK, half)] -= new[:half]
        prod[unit, pl.ds(BLOCK + half, half)] += new[half:BLOCK]
        return 0

    lax.fori_loop(0, units.total(), spread, 0)

    def signal_grad(unit, _):
        pieces = []
        for low in range(0, BLOCK, FREQ_CHUNK):
            re, im = pl.ds(low, FREQ_CHUNK), pl.ds(BLOCK + low, FREQ_CHUNK)

            def step(ahead, total):
                at = unit + ahead
                g_re, g_im, t_re, t_im = (
                    prod[at, re],
                    prod[at, im],
                    taps[ahead, re],
                    taps[ahead, im],
                )
                return (
                    total[0] + (g_re * t_re + g_im * t_im),
                    total[1] + (g_im * t_re - g_re * t_im),
                )

            zero = jnp.zeros((FREQ_CHUNK, width), F32)
            pieces.append(lax.fori_loop(0, units.stop(unit) - unit, step, (zero, zero)))
        joined = jnp.concatenate([piece[0] for piece in pieces] + [piece[1] for piece in pieces])
        value = times(inv, joined)
        rows = rows_of(units.block(unit))
        conv_grad[1, rows, :] += jnp.where(units.inside(unit, width), value, 0.0)
        return 0

    lax.fori_loop(0, units.total(), signal_grad, 0)

    def tap_grad(back, _):
        pieces = []
        for low in range(0, BLOCK, FREQ_CHUNK):
            re, im = pl.ds(low, FREQ_CHUNK), pl.ds(BLOCK + low, FREQ_CHUNK)

            def step(unit, total):
                at = unit - back
                g_re, g_im, s_re, s_im = (
                    prod[unit, re],
                    prod[unit, im],
                    spec[at, re],
                    spec[at, im],
                )
                return (
                    total[0] + (g_re * s_re + g_im * s_im),
                    total[1] + (g_im * s_re - g_re * s_im),
                )

            zero = jnp.zeros((FREQ_CHUNK, width), F32)
            total = (zero, zero)
            for doc in range(docs):
                total = lax.fori_loop(
                    units.doc_start(doc) + back, units.doc_stop(doc), step, total
                )
            pieces.append(total)
        joined = jnp.concatenate([piece[0] for piece in pieces] + [piece[1] for piece in pieces])
        decay = decay_of(back, length, units.channel(), model_width, width)
        filt_grad[rows_of(back), :] = times(inv, joined) * decay
        return 0

    lax.fori_loop(0, blocks, tap_grad, 0)

    def conv_back(block, _):
        rows = rows_of(block)
        masks = tap_masks(units, block, width)
        val_parts, pre_parts, post_parts = (
            delayed(val, block),
            delayed(pre, block),
            delayed(post, block),
        )
        gated_grad = conv_grad[1, rows, :]
        pre_grad = gated_grad * short_conv(val_parts, small, 2, masks)
        val_grad = gated_grad * short_conv(pre_parts, small, 1, masks)
        post_grad = conv_grad[0, rows, :]
        conv_grad[1, rows, :] = pre_grad
        conv_grad[2, rows, :] = val_grad
        for branch, (grad, parts) in enumerate(
            ((post_grad, post_parts), (pre_grad, pre_parts), (val_grad, val_parts))
        ):
            sums[branch : branch + 1, :] += total_rows(grad * parts[0])
            sums[3 + branch : 4 + branch, :] += total_rows(
                jnp.where(masks[0], grad * parts[1], 0.0)
            )
            sums[6 + branch : 7 + branch, :] += total_rows(
                jnp.where(masks[1], grad * parts[2], 0.0)
            )
            sums[9 + branch : 10 + branch, :] += total_rows(grad)
        return 0

    lax.fori_loop(0, blocks, conv_back, 0)

    def spread_taps(block, _):
        start = block * BLOCK
        one, _two = tap_masks(units, block, width, 1)
        _one, two = tap_masks(units, block, width, 2)
        place = lax.broadcasted_iota(jnp.int32, (BLOCK, width), 0) + start
        one = one & (place + 1 < length)
        two = two & (place + 2 < length)
        for branch in range(3):
            here = conv_grad[branch, rows_of(block), :]
            after = conv_grad[
                branch, pl.ds(pl.multiple_of(jnp.minimum(start + BLOCK, length - 8), 8), 8), :
            ]
            joined = jnp.concatenate([here, after], axis=0)
            size = BLOCK + 8
            next_one = pltpu.roll(joined, size - 1, 0)[:BLOCK]
            next_two = pltpu.roll(joined, size - 2, 0)[:BLOCK]
            total = small[branch : branch + 1, :] * here
            total += jnp.where(one, small[3 + branch : 4 + branch, :] * next_one, 0.0)
            total += jnp.where(two, small[6 + branch : 7 + branch, :] * next_two, 0.0)
            rounded = total.astype(BF16)
            proj_grad[rows_of(block), branch * width : (branch + 1) * width] = rounded
            sums[12 + branch : 13 + branch, :] += total_rows(rounded.astype(F32))
        return 0

    lax.fori_loop(0, blocks, spread_taps, 0)


def whole_spec(shape, column=0):
    place = (0,) * (len(shape) - 1) + (column,)
    return pl.BlockSpec(shape, lambda i, meta: place, pipeline_mode=pl.Buffered(1))


def mixer_forward(meta, docs, projected, layers, small, model_width, tables):
    length, width = layers.shape[2], small.shape[1]
    units = length // BLOCK + docs - 1
    column = [whole_spec((length, width), at) for at in range(3)]
    return pl.pallas_call(
        functools.partial(mixer_forward_kernel, docs, model_width),
        out_shape=(
            jax.ShapeDtypeStruct((length, width), BF16),
            jax.ShapeDtypeStruct((length, width), F32),
        ),
        grid_spec=pltpu.PrefetchScalarGridSpec(
            num_scalar_prefetch=1,
            grid=(1,),
            in_specs=column
            + [whole_spec(value.shape) for value in (layers, small, tables[0], tables[1])],
            out_specs=(column[0], column[0]),
            scratch_shapes=[
                pltpu.VMEM((length, width), F32),
                pltpu.VMEM((units, 2 * BLOCK, width), F32),
                pltpu.VMEM((length // BLOCK, 2 * BLOCK, width), F32),
                pltpu.VMEM((units, 2 * BLOCK, width), F32),
            ],
        ),
        compiler_params=pltpu.CompilerParams(vmem_limit_bytes=VMEM_LIMIT),
        cost_estimate=pl.CostEstimate(
            flops=40 * 10**9, bytes_accessed=10 * 10**6, transcendentals=0
        ),
        name="mixer_forward",
    )(meta, projected, projected, projected, layers, small, *tables)


def mixer_backward(meta, docs, projected, layers, small, model_width, tables, mixed, branch_grad):
    length, width = layers.shape[2], small.shape[1]
    units = length // BLOCK + docs - 1
    column = [whole_spec((length, width), at) for at in range(3)]
    return pl.pallas_call(
        functools.partial(mixer_backward_kernel, docs, model_width),
        out_shape=(
            jax.ShapeDtypeStruct((length, 3 * width), BF16),
            jax.ShapeDtypeStruct((length, width), F32),
            jax.ShapeDtypeStruct((16, width), F32),
        ),
        grid_spec=pltpu.PrefetchScalarGridSpec(
            num_scalar_prefetch=1,
            grid=(1,),
            in_specs=column
            + [
                whole_spec(value.shape)
                for value in (layers, small, tables[0], tables[1], mixed, branch_grad)
            ],
            out_specs=(
                whole_spec((length, 3 * width)),
                column[0],
                whole_spec((16, width)),
            ),
            scratch_shapes=[
                pltpu.VMEM((length, width), F32),
                pltpu.VMEM((length, width), F32),
                pltpu.VMEM((3, length, width), F32),
                pltpu.VMEM((units, 2 * BLOCK, width), F32),
                pltpu.VMEM((length // BLOCK, 2 * BLOCK, width), F32),
                pltpu.VMEM((units, 2 * BLOCK, width), F32),
            ],
        ),
        compiler_params=pltpu.CompilerParams(vmem_limit_bytes=VMEM_LIMIT),
        cost_estimate=pl.CostEstimate(
            flops=80 * 10**9, bytes_accessed=16 * 10**6, transcendentals=0
        ),
        name="mixer_backward",
    )(meta, projected, projected, projected, layers, small, *tables, mixed, branch_grad)


def norm_parts(values):
    centre = values - jnp.mean(values, axis=-1, keepdims=True)
    spread = jnp.mean(centre * centre, axis=-1, keepdims=True)
    scale = lax.rsqrt(spread + 1e-05)
    return centre * scale, scale


def project_kernel(inputs, norm, weight, lines, out):
    unit, _ = norm_parts(inputs[...].astype(F32))
    normed = (unit * norm[0:1, :] + norm[1:2, :]).astype(BF16)
    bias = jnp.concatenate([lines[13 + at : 14 + at, :] for at in range(3)], axis=1)
    total = jnp.dot(normed, weight[...], preferred_element_type=F32) + bias
    out[...] = total.astype(BF16)


def project(inputs, lines, weight, mine):
    length, depth = inputs.shape
    width = weight.shape[1]
    return pl.pallas_call(
        project_kernel,
        out_shape=jax.ShapeDtypeStruct((length, width), BF16),
        grid=(length // BLOCK,),
        in_specs=[
            pl.BlockSpec((BLOCK, depth), lambda i: (i, 0)),
            pl.BlockSpec((8, depth), lambda i: (NORM_ROW // 8, 0)),
            pl.BlockSpec(weight.shape, lambda i: (0, 0)),
            pl.BlockSpec((16, mine.shape[1]), lambda i: (0, 0)),
        ],
        out_specs=pl.BlockSpec((BLOCK, width), lambda i: (i, 0)),
        compiler_params=pltpu.CompilerParams(vmem_limit_bytes=VMEM_LIMIT),
        cost_estimate=pl.CostEstimate(
            flops=2 * length * depth * width, bytes_accessed=10 * 10**6, transcendentals=0
        ),
        name="project",
    )(inputs, lines, weight, mine)


def gelu_pair(u):
    root = math.sqrt(2.0 / math.pi)
    square = u * u
    curve = jnp.tanh(root * (u + 0.044715 * (u * square)))
    value = 0.5 * u * (1.0 + curve)
    slope = 0.5 * (1.0 + curve) + 0.5 * u * (1.0 - curve * curve) * (
        root * (1.0 + 3.0 * 0.044715 * square)
    )
    return value, slope


class Copies:
    def __init__(self, local_sems, send_sems, got_sems):
        self.local_sems, self.send_sems, self.got_sems = local_sems, send_sems, got_sems
        self.locals = 0
        self.names = {}
        self.pending = []

    def local(self, source, target):
        copy = pltpu.make_async_copy(source, target, self.local_sems.at[self.locals])
        self.locals += 1
        copy.start()
        return copy

    def remote(self, name, source, target, device):
        at = self.names.setdefault(name, len(self.names))
        return pltpu.make_async_remote_copy(
            src_ref=source,
            dst_ref=target,
            send_sem=self.send_sems.at[at],
            recv_sem=self.got_sems.at[at],
            device_id=device,
            device_id_type=pl.DeviceIdType.MESH,
        )

    def send(self, name, source, target, device, when=None):
        copy = self.remote(name, source, target, device)
        if when is None:
            copy.start()
        else:
            pl.when(when)(copy.start)
        self.pending.append((name, copy, when))

    def got(self, name, target, device):
        self.remote(name, target, target, device).wait_recv()

    def local_when(self, source, target, when):
        copy = pltpu.make_async_copy(source, target, self.local_sems.at[self.locals])
        self.locals += 1
        pl.when(when)(copy.start)
        return copy

    def settle(self, name):
        for at, (found, copy, when) in enumerate(self.pending):
            if found == name:
                copy.wait_send()
                del self.pending[at]
                return

    def finish(self):
        for _, copy, when in self.pending:
            if when is None:
                copy.wait_send()
            else:
                pl.when(when)(copy.wait_send)


def greet(devices):
    barrier = pltpu.get_barrier_semaphore()
    for device in devices:
        pl.semaphore_signal(
            barrier, inc=1, device_id=device, device_id_type=pl.DeviceIdType.MESH
        )
    pl.semaphore_wait(barrier, len(devices))


def lane_masks(bits):
    masks, found = [0], []
    for bit in bits:
        found += [(mask ^ bit, bit) for mask in masks]
        masks += [mask ^ bit for mask in masks]
    return found


def middle_kernel(
    dims,
    given,
    branch,
    inputs,
    out_weight,
    lines,
    out_grad,
    up_bias,
    *rest,
):
    rz_count, pos_count = dims
    count = 2 * len(given)
    pieces, rest = rest[:count], rest[count:]
    steps = rz_count - 1
    extras, rest = rest[: 2 * steps - 1], rest[2 * steps - 1 :]
    result, residual, branch_grad, token_lines = rest[:4]
    piece_grads, rest = rest[4 : 4 + 2 * pos_count], rest[4 + 2 * pos_count :]
    (
        tokens,
        normed,
        grad,
        out_total,
        back_total,
        weights,
        grads,
        out_got,
        back_got,
        grad_q,
        turned_got,
        out_parts,
        bias_grad,
        local_sems,
        send_sems,
        got_sems,
    ) = rest
    z, core, pos = lax.axis_index("rz"), lax.axis_index("core"), lax.axis_index("pos")
    rows, depth = inputs.shape
    tiles, _, units, own_width, width = weights.shape
    middle = tiles // 2
    columns = depth // width
    chan = branch.shape[1]
    down_units = (units - 2 * tiles) // columns
    bits = bits_of(pos_count)
    orders = (bits, bits[::-1])
    copies = Copies(local_sems, send_sems, got_sems)
    other = {"core": 1 - core}
    peers = [jnp.bitwise_xor(pos, mask) for mask in range(pos_count)]

    def token_rows(owner):
        return pl.ds(pl.multiple_of(owner * rows, rows), rows)

    def channels(owner):
        return pl.ds(pl.multiple_of(owner * chan, chan), chan)

    grad_load = copies.local(out_grad, grad.at[pl.ds(0, rows)])
    loads = []
    for at, mask in enumerate(given):
        for side in range(2):
            piece = pieces[2 * at + side]
            part = pl.ds(side * middle, middle)
            target = weights.at[part, peers[mask], pl.ds(0, piece.shape[1])]
            loads.append((copies.local(piece, target), None))
    last = pl.ds(units - extras[0].shape[1], extras[0].shape[1])

    def extra_slot(origin):
        return weights.at[jnp.clip(origin, 0, tiles - 1), :, last]

    for at, extra in enumerate(extras):
        origin = z - (at if at < steps else steps - 1 - at)
        there = (origin >= 0) & (origin < tiles)
        loads.append((copies.local_when(extra, extra_slot(origin), there), there))
    greet(
        [other]
        + [{"rz": (z + step) % rz_count} for step in range(1, rz_count)]
        + [{"pos": peers[mask]} for mask in range(1, pos_count)]
    )
    for mask in range(1, pos_count):
        copies.send(
            ("branch", mask),
            branch.at[token_rows(peers[mask])],
            tokens.at[:, channels(pos)],
            {"pos": peers[mask]},
        )
    grad_load.wait()
    own_half, other_half = pl.ds(0, rows), pl.ds(rows, rows)
    copies.send(("grad",), grad.at[own_half], grad.at[other_half], other)

    full = pieces[0].shape[1]
    arriving = []
    for side in range(2):
        part = pl.ds(side * middle, middle)
        for mask, bit in lane_masks(orders[side]):
            if mask in given:
                continue
            arriving.append((side, mask, bit))
            before = mask ^ bit
            slot = weights.at[part, peers[before], pl.ds(0, full)]
            if before in given:
                source = pieces[2 * given.index(before) + side]
            else:
                source = slot
                prior = [item for item in arriving if item[:2] == (side, before)][0]
                copies.got(("weights", side, before), slot, {"pos": peers[prior[2]]})
            copies.send(("weights", side, mask), source, slot, {"pos": peers[bit]})
    ends = ((1, {"rz": z + 1}, {"rz": z - 1}), (-1, {"rz": z - 1}, {"rz": z + 1}))
    for side, (direction, onward, _) in enumerate(ends):
        origin = z - direction * (steps - 1)
        sends = (origin >= 0) & (origin < tiles)
        sends = sends & (z + direction >= 0) & (z + direction < tiles)
        source = extras[steps - 1 if side == 0 else 2 * steps - 2] if steps > 1 else extras[0]
        copies.send(("extra", side), source, extra_slot(origin), onward, sends)

    tokens[:, channels(pos)] = branch[token_rows(pos), :]
    for mask in range(1, pos_count):
        copies.got(("branch", mask), tokens.at[:, channels(peers[mask])], {"pos": peers[mask]})
    line = [lines[NORM_ROW + at : NORM_ROW + at + 1, :] for at in range(6)]

    def project_out(at, _):
        part = pl.ds(pl.multiple_of(at * BLOCK, BLOCK), BLOCK)
        value = inputs[part, :].astype(F32) + line[2]
        value += jnp.dot(tokens[part, :], out_weight[...], preferred_element_type=F32)
        residual[part, :] = value
        unit, _ = norm_parts(value)
        normed[part, :] = (unit * line[3] + line[4]).astype(BF16)
        return 0

    lax.fori_loop(0, rows // BLOCK, project_out, 0)
    copies.send(("normed",), normed.at[own_half], normed.at[other_half], other)
    out_total[...] = jnp.zeros_like(out_total)
    back_total[...] = jnp.zeros_like(back_total)
    for copy, there in loads:
        if there is None:
            copy.wait()
        else:
            pl.when(there)(copy.wait)
    sent = {item[:2] for item in arriving}
    for side, mask, bit in arriving:
        onward = [item for item in arriving if item[0] == side and item[1] ^ item[2] == mask]
        if not onward:
            slot = weights.at[pl.ds(side * middle, middle), peers[mask], pl.ds(0, full)]
            copies.got(("weights", side, mask), slot, {"pos": peers[bit]})
    for side, (direction, _, back) in enumerate(ends):
        origin = z - direction * steps

        def take(side=side, origin=origin, back=back):
            copies.got(("extra", side), extra_slot(origin), back)

        pl.when((origin >= 0) & (origin < tiles))(take)
    copies.got(("grad",), grad.at[other_half], other)
    copies.got(("normed",), normed.at[other_half], other)

    def step(tile, _):
        up = jnp.concatenate(
            [
                weights[block, :, side * tiles + tile].reshape(pos_count * own_width, width)
                for block in range(tiles)
                for side in range(2)
            ],
            axis=0,
        )
        down = jnp.concatenate(
            [
                weights[
                    tile, :, 2 * tiles + at * down_units : 2 * tiles + (at + 1) * down_units
                ].reshape(width, width)
                for at in range(columns)
            ],
            axis=1,
        )
        pre = jnp.dot(normed[: 2 * rows], up, preferred_element_type=F32) + up_bias[pl.ds(tile, 1), :]
        hidden, slope = gelu_pair(pre)
        hidden = hidden.astype(BF16)
        hidden_grad = lax.dot_general(
            grad[...], down, (((1,), (1,)), ((), ())), preferred_element_type=F32
        )
        pre_grad = hidden_grad * slope
        bias_grad[pl.ds(tile, 1), :] = jnp.sum(pre_grad, axis=0, keepdims=True)
        pre_grad = pre_grad.astype(BF16)
        out_total[...] += jnp.dot(hidden, down, preferred_element_type=F32)
        back_total[...] += lax.dot_general(
            pre_grad, up, (((1,), (1,)), ((), ())), preferred_element_type=F32
        )
        down_grad = lax.dot_general(
            hidden, grad[...], (((0,), (0,)), ((), ())), preferred_element_type=F32
        ).astype(BF16)
        for at in range(columns):
            grads[tile, :, 2 * tiles + at * down_units : 2 * tiles + (at + 1) * down_units] = (
                down_grad[:, at * width : (at + 1) * width].reshape(
                    pos_count, down_units, own_width, width
                )
            )
        up_grad = lax.dot_general(
            normed[: 2 * rows], pre_grad, (((0,), (0,)), ((), ())), preferred_element_type=F32
        ).astype(BF16)
        size = pos_count * own_width
        for block in range(tiles):
            for side in range(2):
                low = (2 * block + side) * size
                grads[block, :, side * tiles + tile] = up_grad[low : low + size].reshape(
                    pos_count, own_width, width
                )
        return 0

    lax.fori_loop(0, tiles, step, 0)
    copies.settle(("normed",))
    normed[:rows] = back_total[rows:].astype(BF16)
    copies.send(("back",), normed.at[own_half], back_got, other)
    normed[rows : 2 * rows] = out_total[rows:].astype(BF16)
    copies.send(("out",), normed.at[other_half], out_got, other)
    stores = []
    for mask in range(pos_count):
        for side in range(2):
            source = grads.at[pl.ds(side * middle, middle), peers[mask]]
            target = piece_grads[2 * mask + side].at[:, pl.ds(0, units)]
            stores.append(copies.local(source, target))

    copies.got(("back",), back_got, other)
    zero = jnp.zeros((1, depth), F32)

    def norm_back(at, sums):
        part = pl.ds(pl.multiple_of(at * BLOCK, BLOCK), BLOCK)
        unit, scale = norm_parts(residual[part, :])
        back = back_total[part, :] + back_got[part, :].astype(F32)
        scaled = back * line[3]
        out = grad[part, :].astype(F32)
        value = out + scale * (
            scaled
            - jnp.mean(scaled, axis=-1, keepdims=True)
            - unit * jnp.mean(scaled * unit, axis=-1, keepdims=True)
        )
        back_total[part, :] = value
        grad_q[part, :] = value.astype(BF16)

        def total(value):
            return jnp.sum(value, axis=0, keepdims=True)

        return (
            sums[0] + total(value),
            sums[1] + total(back * unit),
            sums[2] + total(back),
            sums[3] + total(out),
        )

    sums = lax.fori_loop(0, rows // BLOCK, norm_back, (zero,) * 4)
    turned = lax.dot_general(
        grad_q[...], out_weight[...], (((1,), (1,)), ((), ())), preferred_element_type=F32
    ).astype(BF16)
    copies.settle(("grad",))
    grad[own_half, :] = turned
    for mask in range(1, pos_count):
        copies.send(
            ("branch grad", mask),
            grad.at[own_half, channels(peers[mask])],
            branch_grad.at[token_rows(pos)],
            {"pos": peers[mask]},
        )
    branch_grad[token_rows(pos), :] = grad[own_half, channels(pos)]
    copies.got(("out",), out_got, other)

    def add_result(at, _):
        part = pl.ds(pl.multiple_of(at * BLOCK, BLOCK), BLOCK)
        value = residual[part, :] + (out_total[part, :] + out_got[part, :].astype(F32)) + line[5]
        result[part, :] = value.astype(BF16)
        residual[part, :] = back_total[part, :]
        return 0

    lax.fori_loop(0, rows // BLOCK, add_result, 0)
    token_lines[...] = jnp.zeros_like(token_lines)
    for at in range(4):
        token_lines[2 + at : 3 + at, :] = sums[at]
    per_tile = width // 128
    per = 2 * tiles * width // depth // per_tile
    for tile in range(tiles):
        owner = 2 * tile + core
        lanes = pl.ds(pl.multiple_of(owner // per * 128, 128), 128)
        for at in range(per * per_tile):
            low = at % per_tile * 128
            value = bias_grad[tile : tile + 1, low : low + 128]
            token_lines[6 + at : 7 + at, lanes] = jnp.where(
                owner % per == at // per_tile, value, 0.0
            )

    copies.settle(("back",))
    copies.settle(("out",))
    normed[:depth] = lax.dot_general(
        tokens[...], grad_q[...], (((0,), (0,)), ((), ())), preferred_element_type=F32
    ).astype(BF16)
    size = pos_count * own_width

    def block_rows(block, side):
        return pl.ds(pl.multiple_of((2 * block + side) * size, size), size)

    for block in range(tiles):
        copies.send(
            ("turned", block),
            normed.at[block_rows(block, 1 - core)],
            turned_got.at[block],
            other,
        )
    for block in range(tiles):
        copies.got(("turned", block), turned_got.at[block], other)
        value = normed[block_rows(block, core), :].astype(F32)
        value = (value + turned_got[block].astype(F32)).astype(BF16)
        for at in range(columns):
            out_parts[block, :, at] = value[:, at * width : (at + 1) * width].reshape(
                pos_count, own_width, width
            )
    for mask in range(pos_count):
        for side in range(2):
            source = out_parts.at[pl.ds(side * middle, middle), peers[mask]]
            target = piece_grads[2 * mask + side].at[:, pl.ds(units, columns)]
            stores.append(copies.local(source, target))
    for mask in range(1, pos_count):
        copies.got(
            ("branch grad", mask), branch_grad.at[token_rows(peers[mask])], {"pos": peers[mask]}
        )
    for copy in stores:
        copy.wait()
    copies.finish()


def middle(dims, given, branch, inputs, out_weight, lines, out_grad, up_bias, pieces, extras):
    rz_count, pos_count = dims
    rows, depth = inputs.shape
    tiles, width = up_bias.shape
    length, chan = branch.shape
    piece = pieces[0].shape
    piece = piece[:1] + (piece[1] + extras[0].shape[1],) + piece[2:]
    own_width = piece[2]
    whole = (tiles, pos_count) + piece[1:]
    piece_grad = piece[:1] + (piece[1] + depth // width,) + piece[2:]
    size = pos_count * own_width
    anywhere = pl.BlockSpec(memory_space=pl.ANY)
    inside = pl.BlockSpec(memory_space=pltpu.VMEM)
    vmem = pltpu.VMEM
    local_count = 1 + len(pieces) + len(extras) + 4 * pos_count
    remote_count = 2 * (pos_count - 1) + 2 * pos_count + 6 + tiles
    return pl.pallas_call(
        functools.partial(middle_kernel, dims, given),
        out_shape=(
            jax.ShapeDtypeStruct((rows, depth), BF16),
            jax.ShapeDtypeStruct((rows, depth), F32),
            jax.ShapeDtypeStruct((length, chan), BF16),
            jax.ShapeDtypeStruct((16, depth), F32),
        )
        + (jax.ShapeDtypeStruct(piece_grad, BF16),) * (2 * pos_count),
        in_specs=[inside] * 4 + [anywhere, inside] + [anywhere] * (len(pieces) + len(extras)),
        out_specs=(inside,) * 4 + (anywhere,) * (2 * pos_count),
        scratch_shapes=[
            vmem((rows, depth), BF16),
            vmem((max(2 * rows, depth), depth), BF16),
            vmem((2 * rows, depth), BF16),
            vmem((2 * rows, depth), F32),
            vmem((2 * rows, depth), F32),
            vmem(whole, BF16),
            vmem(whole, BF16),
            vmem((rows, depth), BF16),
            vmem((rows, depth), BF16),
            vmem((rows, depth), BF16),
            vmem((tiles, size, depth), BF16),
            vmem((tiles, pos_count, depth // width, own_width, width), BF16),
            vmem((tiles, width), F32),
            pltpu.SemaphoreType.DMA((local_count,)),
            pltpu.SemaphoreType.DMA((remote_count,)),
            pltpu.SemaphoreType.DMA((remote_count,)),
        ],
        compiler_params=pltpu.CompilerParams(
            collective_id=2, has_side_effects=True, vmem_limit_bytes=VMEM_LIMIT
        ),
        cost_estimate=pl.CostEstimate(flops=10**7, bytes_accessed=10**7, transcendentals=0),
        name="middle",
    )(branch, inputs, out_weight, lines, out_grad, up_bias, *pieces, *extras)


def swap(value, axis, bit):
    count = lax.axis_size(axis)
    return lax.ppermute(value, axis, [(at, at ^ bit) for at in range(count)])


def gather_kernel(
    dims,
    inputs,
    weight,
    up,
    down,
    out,
    vectors,
    filter_in,
    row_in,
    weight_in,
    bundle,
    extra,
    owned,
    lines,
    mine,
    up_lines,
    layers,
    pack,
    small,
    small_mine,
    local_sems,
    send_sems,
    got_sems,
):
    rz_count, pos_count = dims
    z, core, pos = lax.axis_index("rz"), lax.axis_index("core"), lax.axis_index("pos")
    bits = bits_of(pos_count)
    lanes = [lane_masks(bits), lane_masks(bits[::-1])]
    own_width, model_width = out.shape
    chan = model_width // pos_count
    tile = bundle.shape[3]
    columns = model_width // tile
    half = model_width // 2
    middle = rz_count // 2
    copies = Copies(local_sems, send_sems, got_sems)
    other = {"core": 1 - core}
    right, left = {"rz": z + 1}, {"rz": z - 1}
    has_right, has_left = z + 1 < rz_count, z > 0
    greet(
        [other]
        + [{"rz": (z + step) % rz_count} for step in range(1, rz_count)]
        + [{"pos": jnp.bitwise_xor(pos, mask)} for mask in range(1, pos_count)]
    )

    def branch_cols(owner):
        return pl.ds(pl.multiple_of(owner * chan, chan), chan)

    for mask in range(1, pos_count):
        owner = jnp.bitwise_xor(pos, mask)
        for at in range(3):
            copies.send(
                ("in", mask, at),
                weight.at[at, :, branch_cols(owner)],
                weight_in.at[z, core, pos, :, pl.ds(at * chan, chan)],
                {"pos": owner},
            )

    def send_extra(lane, mask, bit):
        part = pl.ds(lane * (down_units // 2), down_units // 2)
        block = extra.at[jnp.bitwise_xor(pos, mask ^ bit), part]
        copies.send(("extra", lane, mask), block, block, {"pos": jnp.bitwise_xor(pos, bit)})

    def got_extra(lane, mask, bit):
        part = pl.ds(lane * (down_units // 2), down_units // 2)
        block = extra.at[jnp.bitwise_xor(pos, mask), part]
        copies.got(("extra", lane, mask), block, {"pos": jnp.bitwise_xor(pos, bit)})
        later = (bits, bits[::-1])[lane]
        for onward in later[later.index(bit) + 1 :]:
            send_extra(lane, mask ^ onward, onward)

    down_units = down.shape[0] // own_width
    local_extra = []
    for at in range(down_units):
        source = down.at[pl.ds(at * own_width, own_width), pl.ds((columns - 1) * tile, tile)]
        local_extra.append(copies.local(source, extra.at[pos, at]))
    for copy in local_extra:
        copy.wait()
    for at in range(len(bits)):
        for lane in range(2):
            bit = (bits, bits[::-1])[lane][at]
            send_extra(lane, bit, bit)

    def lane_cols(lane):
        return pl.ds(lane * half, half)

    def send_rows(lane, mask, bit):
        origin = jnp.bitwise_xor(pos, mask ^ bit)
        cols = lane_cols(lane)
        source = inputs.at[:, cols] if mask == bit else row_in.at[origin, :, cols]
        copies.send(
            ("rows", lane, mask),
            source,
            row_in.at[origin, :, cols],
            {"pos": jnp.bitwise_xor(pos, bit)},
        )

    for at in range(len(bits)):
        for lane in range(2):
            bit = (bits, bits[::-1])[lane][at]
            send_rows(lane, bit, bit)

    def up_cols(at, side):
        return pl.ds(pl.multiple_of((2 * at + side) * tile, tile), tile)

    for at in range(rz_count):
        copies.send(
            ("up", at),
            up.at[:, up_cols(at, 1 - core)],
            bundle.at[z, core * rz_count + at],
            other,
        )
    local_in = [
        copies.local(
            weight.at[at, :, branch_cols(pos)],
            weight_in.at[z, core, pos, :, pl.ds(at * chan, chan)],
        )
        for at in range(3)
    ]
    local_owned = [copies.local(out, owned.at[z, core, pos])]
    local_bundle = [
        copies.local(up.at[:, up_cols(at, core)], bundle.at[z, core * rz_count + at])
        for at in range(rz_count)
    ]
    for col in range(columns - 1):
        for at in range(down_units):
            source = down.at[pl.ds(at * own_width, own_width), pl.ds(col * tile, tile)]
            target = bundle.at[z, 2 * rz_count + col * down_units + at]
            local_bundle.append(copies.local(source, target))
    local_rows = copies.local(inputs, row_in.at[pos])

    flows = {
        "in": lambda origin: weight_in.at[origin, core],
        "owned": lambda origin: owned.at[origin, core, pos],
        "small": lambda origin: small.at[origin, core, pos],
        "bundle": lambda origin: bundle.at[origin],
    }

    def line_start(flow):
        block = flows[flow](z)
        copies.send((flow, "right", 1), block, block, right, has_right)
        copies.send((flow, "left", 1), block, block, left, has_left)

    def line_step(flow, distance, arrived=None):
        for side, origin, there, onward, has_next in (
            ("right", z - distance, z >= distance, right, has_right),
            ("left", z + distance, z + distance < rz_count, left, has_left),
        ):
            safe = jnp.clip(origin, 0, rz_count - 1)
            block = flows[flow](safe)

            def wait(block=block, side=side, onward=onward):
                copies.got((flow, side, distance), block, onward)

            pl.when(there)(wait)
            if distance + 1 < rz_count:
                copies.send((flow, side, distance + 1), block, block, onward, there & has_next)
            if arrived is not None:
                arrived(side, distance, safe, there)

    def share_in(side, distance, origin, there):
        block = weight_in.at[origin, core]
        copies.send(("in core", side, distance), block, block, other, there)

    for copy in local_in:
        copy.wait()
    for mask in range(1, pos_count):
        owner = jnp.bitwise_xor(pos, mask)
        for at in range(3):
            copies.got(
                ("in", mask, at),
                weight_in.at[z, core, owner, :, pl.ds(at * chan, chan)],
                {"pos": owner},
            )
    for lane in range(2):
        got_extra(lane, *lanes[lane][0])
    line_start("in")
    block = weight_in.at[z, core]
    copies.send(("in core", "own", 0), block, block, other)
    for copy in local_owned:
        copy.wait()
    line_start("owned")
    pack[...] = jnp.zeros_like(pack)
    row = 0
    for value in vectors:
        value = value[...].astype(F32)
        value = value.reshape(-1, value.shape[-1])
        pack[row : row + value.shape[0], : value.shape[1]] = value
        row += value.shape[0]
    small[z, core, pos] = pack[...].astype(BF16)
    line_start("small")
    for copy in local_bundle:
        copy.wait()
    for at in range(rz_count):
        copies.got(("up", at), bundle.at[z, (1 - core) * rz_count + at], other)
    line_start("bundle")

    for distance in range(1, rz_count):
        line_step("in", distance, share_in)
        line_step("owned", distance)
        line_step("small", distance)

    def owned_half(side, origin, lane):
        part = pl.ds(lane * middle, middle)
        return (owned.at[part, side, origin], small.at[part, side, origin])

    def send_owned(lane, mask, bit):
        for at, block in enumerate(owned_half(core, jnp.bitwise_xor(pos, mask ^ bit), lane)):
            copies.send(
                ("owned pos", at, lane, mask), block, block, {"pos": jnp.bitwise_xor(pos, bit)}
            )

    def share_owned(lane, mask):
        for at, block in enumerate(owned_half(core, jnp.bitwise_xor(pos, mask), lane)):
            copies.send(("owned core", at, lane, mask), block, block, other)

    def got_rows(lane, mask, bit):
        block = row_in.at[jnp.bitwise_xor(pos, mask), :, lane_cols(lane)]
        copies.got(("rows", lane, mask), block, {"pos": jnp.bitwise_xor(pos, bit)})
        later = (bits, bits[::-1])[lane]
        for onward in later[later.index(bit) + 1 :]:
            send_rows(lane, mask ^ onward, onward)

    def got_owned(lane, mask, bit):
        for at, block in enumerate(owned_half(core, jnp.bitwise_xor(pos, mask), lane)):
            copies.got(("owned pos", at, lane, mask), block, {"pos": jnp.bitwise_xor(pos, bit)})
        later = (bits, bits[::-1])[lane]
        for onward in later[later.index(bit) + 1 :]:
            send_owned(lane, mask ^ onward, onward)
        share_owned(lane, mask)

    first = [lanes[lane][0] for lane in range(2)]
    for lane in range(2):
        got_rows(lane, *first[lane])
    for at in range(len(bits)):
        for lane in range(2):
            bit = (bits, bits[::-1])[lane][at]
            send_owned(lane, bit, bit)
    for lane in range(2):
        share_owned(lane, 0)
    for distance in range(1, rz_count - 1):
        line_step("bundle", distance)
    filter_layers(filter_in, layers, small_mine)
    for at in range(1, pos_count - 1):
        for lane in range(2):
            got_rows(lane, *lanes[lane][at])
            got_extra(lane, *lanes[lane][at])
    for at in range(pos_count - 1):
        for lane in range(2):
            got_owned(lane, *lanes[lane][at])
    line_step("bundle", rz_count - 1)
    local_rows.wait()
    for at in range(pos_count):
        for lane in range(2):
            for part, block in enumerate(
                owned_half(1 - core, jnp.bitwise_xor(pos, at), lane)
            ):
                copies.got(("owned core", part, lane, at), block, other)
    copies.got(("in core", "own", 0), weight_in.at[z, 1 - core], other)
    for distance in range(1, rz_count):
        for side, origin, there in (
            ("right", z - distance, z >= distance),
            ("left", z + distance, z + distance < rz_count),
        ):
            block = weight_in.at[jnp.clip(origin, 0, rz_count - 1), 1 - core]

            def wait(block=block, side=side, distance=distance):
                copies.got(("in core", side, distance), block, other)

            pl.when(there)(wait)

    per_group = 128 // own_width
    for group in range(model_width // 128):
        total = jnp.zeros((LINES, 128), F32)
        for at in range(per_group):
            owner = group * per_group + at
            value = small[
                owner // (2 * pos_count), owner // pos_count % 2, owner % pos_count
            ].astype(F32)
            value = jnp.where(
                lax.broadcasted_iota(jnp.int32, value.shape, 1) < own_width, value, 0.0
            )
            total += pltpu.roll(value, at * own_width, 1) if at else value
        lines[:, group * 128 : (group + 1) * 128] = total
    mine[...] = lines[:NORM_ROW, pl.ds(pl.multiple_of(pos * chan, chan), chan)]
    ff_own = down.shape[0]
    per_lanes = 128 // ff_own
    for at in range(rz_count):
        for group in range(pos_count // per_lanes):
            total = jnp.zeros((1, 128), F32)
            for part in range(per_lanes):
                value = small[at, core, group * per_lanes + part][UP_ROW : UP_ROW + 1]
                value = value.astype(F32)
                total += pltpu.roll(value, part * ff_own, 1) if part else value
            up_lines[at : at + 1, group * 128 : (group + 1) * 128] = total
    copies.finish()


def filter_layers(filter_in, layers, padded):
    embedding, w_one, w_two, columns = filter_in
    padded[...] = jnp.zeros_like(padded)
    padded[: w_one.shape[0], :] = w_one[...].astype(F32)
    frequency = columns[:, 2:3]
    sums = exact(padded[...], embedding[...], ((0,), (0,))) + columns[:, 0:1]
    layers[2] = sums
    layers[4] = jnp.cos(frequency * sums)
    layers[0] = jnp.sin(frequency * sums)
    sums = exact(w_two[...].astype(F32), layers[0], ((0,), (0,))) + columns[:, 1:2]
    layers[3] = sums
    layers[5] = jnp.cos(frequency * sums)
    layers[1] = jnp.sin(frequency * sums)


def gather(dims, inputs, weight, up, down, out, vectors, filter_in):
    rz_count, pos_count = dims
    part_len, model_width = inputs.shape
    own_width = out.shape[0]
    tile = pos_count * down.shape[0]
    down_units = down.shape[0] // own_width
    units = 2 * rz_count + down_units * (model_width // tile - 1)
    anywhere = pl.BlockSpec(memory_space=pl.ANY)
    locals_count = 3 + 1 + units + down_units + 1
    count = len(vectors)
    order, length = filter_in[2].shape[0], filter_in[0].shape[1]
    remote_count = (
        3 * (pos_count - 1)
        + 4 * (pos_count - 1)
        + rz_count
        + 4 * 2 * rz_count
        + 2 * rz_count
        + 2 * 2 * 2 * pos_count
    )

    def kernel(*refs):
        head, refs = refs[:5], refs[5:]
        gather_kernel(dims, *head, refs[:count], refs[count : count + 4], *refs[count + 4 :])

    return pl.pallas_call(
        kernel,
        out_shape=(
            jax.ShapeDtypeStruct((pos_count, part_len, model_width), BF16),
            jax.ShapeDtypeStruct(
                (rz_count, 2, pos_count, own_width, 3 * model_width // pos_count), BF16
            ),
            jax.ShapeDtypeStruct((rz_count, units, own_width, tile), BF16),
            jax.ShapeDtypeStruct((pos_count, down_units, own_width, tile), BF16),
            jax.ShapeDtypeStruct((rz_count, 2, pos_count, own_width, model_width), BF16),
            jax.ShapeDtypeStruct((LINES, model_width), F32),
            jax.ShapeDtypeStruct((NORM_ROW, model_width // pos_count), F32),
            jax.ShapeDtypeStruct((rz_count, tile), F32),
            jax.ShapeDtypeStruct((6, order, length), F32),
        ),
        in_specs=[pl.BlockSpec(memory_space=pltpu.VMEM)] * (5 + count + 4),
        out_specs=(anywhere,) * 5 + (pl.BlockSpec(memory_space=pltpu.VMEM),) * 4,
        scratch_shapes=[
            pltpu.VMEM((LINES, 128), F32),
            pltpu.VMEM((rz_count, 2, pos_count, LINES, 128), BF16),
            pltpu.VMEM((FEATURES, order), F32),
            pltpu.SemaphoreType.DMA((locals_count,)),
            pltpu.SemaphoreType.DMA((remote_count,)),
            pltpu.SemaphoreType.DMA((remote_count,)),
        ],
        compiler_params=pltpu.CompilerParams(
            collective_id=1, has_side_effects=True, vmem_limit_bytes=VMEM_LIMIT
        ),
        cost_estimate=pl.CostEstimate(flops=10**6, bytes_accessed=10**7, transcendentals=0),
        name="gather",
    )(inputs, weight, up, down, out, *vectors, *filter_in)


class LineSum:
    def __init__(self, copies, name, count, z, chunk, sent, got):
        self.copies, self.name, self.count, self.z = copies, name, count, z
        self.chunk, self.sent, self.got_ref = chunk, sent, got

    def sides(self):
        last = self.count - 1
        return (
            (0, self.z, 1, {"rz": self.z + 1}, {"rz": self.z - 1}),
            (1, last - self.z, -1, {"rz": self.z - 1}, {"rz": self.z + 1}),
        )

    def step(self, step):
        count = self.count
        for side, place, direction, onward, back in self.sides():
            sends = (place < step) & (place + 1 < count)
            at = count - step + place
            at = jnp.clip(at if direction == 1 else count - 1 - at, 0, count - 1)
            target = self.sent.at[side, step - 1]

            def first(at=at, side=side):
                self.sent[side, step - 1] = self.chunk(at).astype(BF16)

            def later(at=at, side=side, back=back):
                self.copies.got((self.name, side, step - 1), self.got_ref.at[side, step - 2], back)
                self.sent[side, step - 1] = (
                    self.chunk(at) + self.got_ref[side, step - 2].astype(F32)
                ).astype(BF16)

            pl.when(sends & (place == 0))(first)
            if step > 1:
                pl.when(sends & (place > 0))(later)
            self.copies.send(
                (self.name, side, step), target, self.got_ref.at[side, step - 1], onward, sends
            )

    def total(self, result):
        last = self.count - 1
        result[...] = self.chunk(self.z)
        for side, place, _, _, back in self.sides():

            def add(side=side, back=back):
                self.copies.got((self.name, side, last), self.got_ref.at[side, last - 1], back)
                result[...] += self.got_ref[side, last - 1].astype(F32)

            pl.when(place > 0)(add)


class PieceSum:
    def __init__(self, copies, name, pos, orders, piece, got):
        self.copies, self.name, self.pos, self.orders = copies, name, pos, orders
        self.piece, self.got_ref = piece, got

    def masks(self, side, stage):
        order = self.orders[side]
        found = [0]
        for bit in order[stage:]:
            found += [mask ^ bit for mask in found]
        return [mask for mask in found if mask & order[stage]]

    def device(self, side, stage):
        return {"pos": jnp.bitwise_xor(self.pos, self.orders[side][stage])}

    def send(self, side, stage, mask):
        self.copies.send(
            (self.name, side, mask),
            self.piece(side, mask),
            self.got_ref(side, mask),
            self.device(side, stage),
        )

    def got(self, side, stage, mask):
        self.copies.got(
            (self.name, side, mask), self.got_ref(side, mask), self.device(side, stage)
        )

    def add(self, side, stage, mask):
        target = self.piece(side, mask ^ self.orders[side][stage])
        target[...] = (
            target[...].astype(F32) + self.got_ref(side, mask)[...].astype(F32)
        ).astype(BF16)

    def settle(self, stage):
        for side in range(2):
            onward = self.masks(side, stage + 1) if stage + 1 < len(self.orders[side]) else []
            masks = self.masks(side, stage)
            bit = self.orders[side][stage]
            for mask in sorted(masks, key=lambda mask: (mask ^ bit) not in onward):
                self.got(side, stage, mask)
                self.add(side, stage, mask)
                if mask ^ bit in onward:
                    self.send(side, stage + 1, mask ^ bit)


class ChunkSum(PieceSum):
    def send_chunk(self, side, stage, mask, place):
        self.copies.send(
            (self.name, side, mask, place),
            self.piece(side, mask, place),
            self.got_ref(side, mask, place),
            self.device(side, stage),
        )

    def settle_chunk(self, side, stage, place):
        bit = self.orders[side][stage]
        onward = self.masks(side, stage + 1) if stage + 1 < len(self.orders[side]) else []
        for mask in sorted(self.masks(side, stage), key=lambda mask: (mask ^ bit) not in onward):
            got = self.got_ref(side, mask, place)
            self.copies.got((self.name, side, mask, place), got, self.device(side, stage))
            target = self.piece(side, mask ^ bit, place)
            target[...] = (target[...].astype(F32) + got[...].astype(F32)).astype(BF16)
            if mask ^ bit in onward:
                self.send_chunk(side, stage + 1, mask ^ bit, place)


def last_sums_kernel(
    dims,
    kept,
    row_in,
    proj_grad,
    weight_in,
    lines,
    grad_residual,
    token_lines,
    chan_sums,
    filt_grad,
    layers,
    mine,
    embedding,
    w_two,
    filter_columns,
    *rest,
):
    rz_count, pos_count = dims
    norm = lines.at[pl.ds(NORM_ROW, 8)]
    count = 2 * len(kept[0])
    own_pieces, moved_pieces, rest = rest[:count], rest[count : 2 * count], rest[2 * count :]
    input_grad, in_grad, up_grad, down_grad, out_grad, lines_out, inner_out = rest[:7]
    rest = rest[7:]
    (
        rows_v,
        proj_v,
        pieces_v,
        moved_v,
        pieces_got,
        bundle_sent,
        bundle_got,
        bundle_total,
        up_sent,
        up_got,
        e_v,
        e_got,
        in_total,
        in_sent,
        in_got,
        in_line_sent,
        in_line_got,
        in_mine,
        in_out,
        in_back,
        packed,
        packed_got,
        packed_pos,
        packed_total,
        inner,
        local_sems,
        send_sems,
        got_sems,
    ) = rest
    z, core, pos = lax.axis_index("rz"), lax.axis_index("core"), lax.axis_index("pos")
    rows_count = 2 * rz_count
    row = z * 2 + core
    bits = bits_of(pos_count)
    orders = (bits, bits[::-1])
    middle = rz_count // 2
    part_len, model_width = grad_residual.shape
    half = model_width // 2
    own_width, tile = up_sent.shape[1:]
    width = weight_in.shape[1]
    chan = width // 3
    columns = model_width // tile
    copies = Copies(local_sems, send_sems, got_sems)
    other = {"core": 1 - core}

    def row_device(at):
        return {"rz": at // 2, "core": at % 2}

    later = [[mask for mask in kept[side] if len(bits) > 1 and mask & orders[side][1]] for side in range(2)]
    loads = {}
    for first in (True, False):
        for side in range(2):
            for mask in kept[side]:
                if (mask in later[side]) == first:
                    slot = kept[side].index(mask)
                    at, part = 2 * slot + side, pl.ds(side * middle, middle)
                    loads[side, mask] = (
                        copies.local(own_pieces[at], pieces_v.at[slot, part]),
                        copies.local(moved_pieces[at], moved_v.at[slot, part]),
                    )
    masks = sorted(range(pos_count), key=lambda mask: -bin(mask).count("1"))
    slots = rows_v.shape[0]

    def load_rows(at):
        start = jnp.bitwise_xor(pos, masks[at]) * part_len
        block = pl.ds(pl.multiple_of(start, part_len), part_len)
        return (
            copies.local(row_in.at[block], rows_v.at[at % slots]),
            copies.local(proj_grad.at[block], proj_v.at[at % slots]),
        )

    row_loads = [load_rows(at) for at in range(slots)]
    greet(
        [row_device((row + step) % rows_count) for step in range(1, rows_count)]
        + [{"pos": jnp.bitwise_xor(pos, mask)} for mask in range(1, pos_count)]
    )

    bundle = ChunkSum(
        copies,
        "bundle",
        pos,
        orders,
        lambda side, mask, place: pieces_v.at[kept[side].index(mask), place],
        lambda side, mask, place: pieces_got.at[kept[side].index(mask) - 1, place],
    )
    for side, mask in loads:
        slot = kept[side].index(mask)
        for copy in loads[side, mask]:
            copy.wait()
        for at in range(middle):
            place = side * middle + (at if side == 0 else middle - 1 - at)
            pieces_v[slot, place] = (
                pieces_v[slot, place].astype(F32) + moved_v[slot, place].astype(F32)
            ).astype(BF16)
            if mask in later[side]:
                bundle.send_chunk(side, 1, mask, place)

    e_sums = PieceSum(
        copies,
        "rows",
        pos,
        orders,
        lambda side, mask: e_v.at[side, mask],
        lambda side, mask: e_got.at[side, mask - 1],
    )
    in_total[...] = jnp.zeros_like(in_total)
    packed_total[...] = jnp.zeros_like(packed_total)
    packed[...] = jnp.zeros_like(packed)
    sums = (jnp.zeros((1, model_width), F32), jnp.zeros((1, model_width), F32))
    for index, mask in enumerate(masks):
        if 1 <= index <= pos_count - slots:
            row_loads.append(load_rows(slots + index - 1))
        for copy in row_loads[index]:
            copy.wait()

        def tile_step(at, sums, mask=mask, slot=index % slots):
            rows = pl.ds(pl.multiple_of(at * BLOCK, BLOCK), BLOCK)
            unit, _ = norm_parts(rows_v[slot, rows].astype(F32))
            normed = (unit * norm[0:1, :] + norm[1:2, :]).astype(BF16)
            grad = proj_v[slot, rows]
            cotangent = lax.dot_general(
                grad, weight_in[...], (((1,), (1,)), ((), ())), preferred_element_type=F32
            )
            e_v[0, mask, rows] = cotangent[:, :half].astype(BF16)
            e_v[1, mask, rows] = cotangent[:, half:].astype(BF16)
            in_total[...] += lax.dot_general(
                normed, grad, (((0,), (0,)), ((), ())), preferred_element_type=F32
            )
            return (
                sums[0] + jnp.sum(cotangent * unit, axis=0, keepdims=True),
                sums[1] + jnp.sum(cotangent, axis=0, keepdims=True),
            )

        sums = lax.fori_loop(0, part_len // BLOCK, tile_step, sums)
        for side in range(2):
            if mask in e_sums.masks(side, 0):
                e_sums.send(side, 0, mask)

    block_rows = pos_count * own_width
    for at in range(rz_count):
        rows = pl.ds(pl.multiple_of((2 * at + 1 - core) * block_rows, block_rows), block_rows)
        in_sent[at] = in_total[rows, :].astype(BF16)
    copies.send(("in core",), in_sent, in_got, other)

    groups = model_width // 128
    per = rows_count // groups
    token_rows, chan_rows = token_lines.shape[0], mine.shape[0]
    inner_rows = inner.shape[0] // groups
    line_rows = token_rows + chan_rows
    three_grad = filter_back(
        filt_grad, layers, mine[THREE_ROW:NORM_ROW, :], embedding, w_two, filter_columns, inner
    )
    for at in range(groups):
        lanes = pl.ds(at * 128, 128)
        packed[at, 0:token_rows] = token_lines[:, lanes]
        packed[at, 0:1] = sums[0][:, at * 128 : (at + 1) * 128]
        packed[at, 1:2] = sums[1][:, at * 128 : (at + 1) * 128]
        packed[at, line_rows:] = inner[pl.ds(at * inner_rows, inner_rows), :]
    for at in range(chan // 128):
        group, lanes = pos * (chan // 128) + at, pl.ds(at * 128, 128)
        packed[group, token_rows : token_rows + THREE_ROW] = chan_sums[:, lanes]
        packed[group, token_rows + THREE_ROW : line_rows] = three_grad[
            :, at * 128 : (at + 1) * 128
        ]

    def owns(at):
        return None if per == 1 else at % per == 0

    def when(condition, action):
        if condition is None:
            action()
        else:
            pl.when(condition)(action)

    for step in range(1, rows_count):
        to = (row + step) % rows_count
        copies.send(
            ("lines", step), packed.at[to // per], packed_got.at[step], row_device(to), owns(to)
        )

    bundle_line = LineSum(
        copies,
        "bundle line",
        rz_count,
        z,
        lambda at: pieces_v[kept[0].index(0), at].astype(F32),
        bundle_sent,
        bundle_got,
    )
    for at in range(middle):
        for stage in range(1, len(bits)):
            bundle.settle_chunk(0, stage, at)
            bundle.settle_chunk(1, stage, rz_count - 1 - at)
        if at == 0:
            bundle_line.step(1)
    copies.got(("in core",), in_got, other)

    def in_chunk(at):
        rows = pl.ds(pl.multiple_of((2 * at + core) * block_rows, block_rows), block_rows)
        return in_total[rows, :] + in_got[at].astype(F32)

    in_line = LineSum(copies, "in line", rz_count, z, in_chunk, in_line_sent, in_line_got)
    in_line.step(1)
    e_sums.settle(0)

    def add_lines():
        packed_total[...] = packed[row // per]
        for step in range(1, rows_count):
            copies.got(("lines", step), packed_got.at[step], row_device((row - step) % rows_count))
            packed_total[...] += packed_got[step]
        packed_pos[pos] = packed_total[...]

    when(owns(row), add_lines)
    for mask in range(1, pos_count):
        copies.send(
            ("lines pos", mask),
            packed_total,
            packed_pos.at[pos],
            {"pos": jnp.bitwise_xor(pos, mask)},
            owns(row),
        )
    for step in range(2, rz_count):
        bundle_line.step(step)
        in_line.step(step)
        if step == 2:
            for stage in range(1, len(bits)):
                e_sums.settle(stage)

    def input_step(at, _):
        rows = pl.ds(pl.multiple_of(at * BLOCK, BLOCK), BLOCK)
        unit, scale = norm_parts(rows_v[(pos_count - 1) % slots, rows].astype(F32))
        cotangent = jnp.concatenate(
            [e_v[0, 0, rows].astype(F32), e_v[1, 0, rows].astype(F32)], axis=1
        )
        scaled = cotangent * norm[0:1, :]
        grad = scale * (
            scaled
            - jnp.mean(scaled, axis=-1, keepdims=True)
            - unit * jnp.mean(scaled * unit, axis=-1, keepdims=True)
        )
        input_grad[rows, :] = (grad_residual[rows, :] + grad).astype(BF16)
        return 0

    lax.fori_loop(0, part_len // BLOCK, input_step, 0)

    def sum_lines():
        for mask in range(1, pos_count):
            owner = jnp.bitwise_xor(pos, mask)
            copies.got(("lines pos", mask), packed_pos.at[owner], {"pos": owner})
        total = packed_pos[0]
        for at in range(1, pos_count):
            total = total + packed_pos[at]
        lines_out[...] = total[:line_rows]
        inner_out[row // per] = total[line_rows:]

    when(owns(row), sum_lines)
    for step in range(1, rows_count):
        to = (row + step) % rows_count
        block = inner_out.at[row // per]
        copies.send(("inner", step), block, block, row_device(to), owns(row))
        if step < per:
            copies.send(
                ("lines row", step),
                lines_out,
                lines_out,
                row_device(to),
                owns(row),
            )

    in_line.total(in_mine)
    for mask in range(1, pos_count):
        owner = jnp.bitwise_xor(pos, mask)
        rows = pl.ds(pl.multiple_of(owner * own_width, own_width), own_width)
        in_out[mask] = in_mine[rows, :].astype(BF16)
        copies.send(("in pos", mask), in_out.at[mask], in_back.at[mask], {"pos": owner})
    mine = in_mine[pl.ds(pl.multiple_of(pos * own_width, own_width), own_width), :]
    cols = pl.ds(pl.multiple_of(pos * chan, chan), chan)
    for at in range(3):
        in_grad[at, :, cols] = mine[:, at * chan : (at + 1) * chan]

    bundle_line.total(bundle_total)
    up_sent[...] = bundle_total[
        pl.ds(pl.multiple_of((1 - core) * rz_count, rz_count), rz_count)
    ].astype(BF16)
    copies.send(("up core",), up_sent, up_got, other)
    down_units = (bundle_total.shape[0] - 2 * rz_count - columns) // columns
    for col in range(columns):
        out_grad[:, col * tile : (col + 1) * tile] = bundle_total[
            2 * rz_count + columns * down_units + col
        ]
        for at in range(down_units):
            down_grad[at * own_width : (at + 1) * own_width, col * tile : (col + 1) * tile] = (
                bundle_total[2 * rz_count + col * down_units + at]
            )
    for at in range(rz_count):
        cols = pl.ds(pl.multiple_of((2 * at + core) * tile, tile), tile)
        up_grad[:, cols] = bundle_total[core * rz_count + at]
    for mask in range(1, pos_count):
        owner = jnp.bitwise_xor(pos, mask)
        copies.got(("in pos", mask), in_back.at[mask], {"pos": owner})
        cols = pl.ds(pl.multiple_of(owner * chan, chan), chan)
        for at in range(3):
            in_grad[at, :, cols] = in_back[mask, :, at * chan : (at + 1) * chan].astype(F32)
    copies.got(("up core",), up_got, other)
    for at in range(rz_count):
        cols = pl.ds(pl.multiple_of((2 * at + 1 - core) * tile, tile), tile)
        up_grad[:, cols] = up_got[at].astype(F32)
    for step in range(1, rows_count):
        origin = (row - step) % rows_count

        def take(step=step, origin=origin):
            copies.got(("inner", step), inner_out.at[origin // per], row_device(origin))

        when(owns(origin), take)
        if step < per:

            def take_lines(step=step, origin=origin):
                copies.got(("lines row", step), lines_out, row_device(origin))

            when(origin == row // per * per, take_lines)
    copies.finish()


def filter_back(filt_grad, layers, three, embedding, w_two, columns, inner):
    frequency = columns[:, 2:3]
    three_grad = exact(layers[1], filt_grad[...], ((1,), (0,)))
    grad = exact(three, filt_grad[...], ((1,), (1,))) * layers[5]
    freq_grad = jnp.sum(grad * layers[3], axis=1, keepdims=True)
    grad = grad * frequency
    bias_two = jnp.sum(grad, axis=1, keepdims=True)
    order = grad.shape[0]
    inner[...] = jnp.zeros_like(inner)
    inner[FEATURES : FEATURES + order, :order] = exact(layers[0], grad, ((1,), (1,)))
    grad = exact(w_two[...].astype(F32), grad, ((1,), (0,))) * layers[4]
    freq_grad += jnp.sum(grad * layers[2], axis=1, keepdims=True)
    grad = grad * frequency
    bias_one = jnp.sum(grad, axis=1, keepdims=True)
    inner[:FEATURES, :order] = exact(embedding[...], grad, ((1,), (1,)))
    held = inner[:order, :]
    lane = lax.broadcasted_iota(jnp.int32, held.shape, 1)
    for at, value in enumerate((bias_one, bias_two, freq_grad)):
        held = jnp.where(lane == order + at, value, held)
    inner[:order, :] = held
    return three_grad


def finish_kernel(place, total, shared, *outs):
    own_width = outs[0].shape[1]
    moved = pltpu.roll(total[...], 128 - place[0], 1)[:, :own_width]
    (
        pre_gain,
        pre_bias,
        out_bias,
        post_gain,
        post_bias,
        down_bias,
        short_weight,
        short_bias,
        in_bias,
        skip,
        three,
        up_bias,
        w_one,
        b_one,
        w_two,
        b_two,
        frequency,
    ) = outs
    for at, out in enumerate((pre_gain, pre_bias, out_bias, post_gain, post_bias, down_bias)):
        out[...] = moved[at : at + 1]
    for at in range(3):
        short_weight[at] = moved[16 + 3 * at : 19 + 3 * at]
    short_bias[...] = moved[25:28]
    in_bias[...] = moved[28:31]
    skip[...] = moved[31:32]
    three[...] = moved[32:96]
    rows = pltpu.roll(total[0:16, :], 128 - place[2], 1)[:, : up_bias.shape[1]]
    line = lax.broadcasted_iota(jnp.int32, rows.shape, 0)
    up_bias[...] = jnp.sum(jnp.where(line == 6 + place[1], rows, 0.0), axis=0, keepdims=True)
    inner = shared[...].reshape(-1, 128)
    order = w_two.shape[0]
    w_one[...] = inner[: w_one.shape[0], :order]
    w_two[...] = inner[FEATURES : FEATURES + order, :order]
    turned = inner[:128, :].T
    b_one[...] = turned[order : order + 1, :order]
    b_two[...] = turned[order + 1 : order + 2, :order]
    frequency[...] = turned[order + 2 : order + 3, :order]


def finish(place, total, shared, own_width, ff_own, features, order):
    shapes = [(1, own_width)] * 6
    shapes += [(3, 3, own_width), (3, own_width), (3, own_width), (1, own_width)]
    shapes += [(order, own_width), (1, ff_own), (features, order), (1, order), (order, order)]
    shapes += [(1, order), (1, order)]
    inside = pl.BlockSpec(memory_space=pltpu.VMEM)
    return pl.pallas_call(
        finish_kernel,
        out_shape=[jax.ShapeDtypeStruct(shape, F32) for shape in shapes],
        in_specs=[pl.BlockSpec(memory_space=pltpu.SMEM), inside, inside],
        out_specs=[inside] * len(shapes),
        name="finish",
    )(place, total, shared)


def last_sums(
    dims,
    kept,
    row_in,
    proj_grad,
    weight_in,
    lines,
    grad_residual,
    token_lines,
    chan_sums,
    filt_grad,
    layers,
    mine,
    embedding,
    w_two,
    filter_columns,
    own_pieces,
    moved_pieces,
):
    rz_count, pos_count = dims
    part_len, model_width = grad_residual.shape
    piece = own_pieces[0].shape
    units, own_width, tile = piece[1:]
    width = weight_in.shape[1]
    block_rows = pos_count * own_width
    groups = model_width // 128
    line_rows = token_lines.shape[0] + mine.shape[0]
    inner_rows = 2 * FEATURES // groups
    slots = len(kept[0])
    steps = rz_count - 1
    rows_count = 2 * rz_count
    ff_own = (units - 2 * rz_count - model_width // tile) * own_width * tile // model_width
    anywhere = pl.BlockSpec(memory_space=pl.ANY)
    inside = pl.BlockSpec(memory_space=pltpu.VMEM)
    local_count = 4 * len(kept[0]) + 2 * pos_count
    remote_count = (
        2 * pos_count * (1 + rz_count) + 2 * 2 * steps + 2 + 3 * rows_count + 3 * pos_count
    )
    half = model_width // 2
    vmem = pltpu.VMEM
    return pl.pallas_call(
        functools.partial(last_sums_kernel, dims, kept),
        out_shape=(
            jax.ShapeDtypeStruct((part_len, model_width), BF16),
            jax.ShapeDtypeStruct((3, own_width, model_width), F32),
            jax.ShapeDtypeStruct((own_width, 2 * rz_count * tile), F32),
            jax.ShapeDtypeStruct((ff_own, model_width), F32),
            jax.ShapeDtypeStruct((own_width, model_width), F32),
            jax.ShapeDtypeStruct((line_rows, 128), F32),
            jax.ShapeDtypeStruct((groups, inner_rows, 128), F32),
        ),
        in_specs=[anywhere, anywhere] + [inside] * 11 + [anywhere] * (2 * len(own_pieces)),
        out_specs=(inside,) * 7,
        scratch_shapes=[
            vmem((pos_count - 1, part_len, model_width), BF16),
            vmem((pos_count - 1, part_len, width), BF16),
            vmem((slots, rz_count, units, own_width, tile), BF16),
            vmem((slots, rz_count, units, own_width, tile), BF16),
            vmem((slots - 1, rz_count, units, own_width, tile), BF16),
            vmem((2, steps, units, own_width, tile), BF16),
            vmem((2, steps, units, own_width, tile), BF16),
            vmem((units, own_width, tile), F32),
            vmem((rz_count, own_width, tile), BF16),
            vmem((rz_count, own_width, tile), BF16),
            vmem((2, pos_count, part_len, half), BF16),
            vmem((2, pos_count - 1, part_len, half), BF16),
            vmem((model_width, width), F32),
            vmem((rz_count, block_rows, width), BF16),
            vmem((rz_count, block_rows, width), BF16),
            vmem((2, steps, block_rows, width), BF16),
            vmem((2, steps, block_rows, width), BF16),
            vmem((block_rows, width), F32),
            vmem((pos_count, own_width, width), BF16),
            vmem((pos_count, own_width, width), BF16),
            vmem((groups, line_rows + inner_rows, 128), F32),
            vmem((rows_count, line_rows + inner_rows, 128), F32),
            vmem((pos_count, line_rows + inner_rows, 128), F32),
            vmem((line_rows + inner_rows, 128), F32),
            vmem((2 * FEATURES, 128), F32),
            pltpu.SemaphoreType.DMA((local_count,)),
            pltpu.SemaphoreType.DMA((remote_count,)),
            pltpu.SemaphoreType.DMA((remote_count,)),
        ],
        compiler_params=pltpu.CompilerParams(
            collective_id=0, has_side_effects=True, vmem_limit_bytes=VMEM_LIMIT
        ),
        cost_estimate=pl.CostEstimate(flops=10**7, bytes_accessed=10**7, transcendentals=0),
        name="last_sums",
    )(
        row_in,
        proj_grad,
        weight_in,
        lines,
        grad_residual,
        token_lines,
        chan_sums,
        filt_grad,
        layers,
        mine,
        embedding,
        w_two,
        filter_columns,
        *own_pieces,
        *moved_pieces,
    )


def bits_of(count):
    return [1 << at for at in range(count.bit_length() - 1)]


def on_device(
    activations,
    out_grad,
    doc_bounds,
    doc_ids,
    pre_gain,
    pre_bias,
    in_weight,
    in_bias,
    short_weight,
    short_bias,
    skip_gain,
    out_weight,
    out_bias,
    post_gain,
    post_bias,
    up_weight,
    up_bias,
    down_weight,
    down_bias,
    filter_one,
    filter_bias_one,
    filter_two,
    filter_bias_two,
    filter_freq,
    filter_three,
):
    rz_count, pos_count = lax.axis_size("rz"), lax.axis_size("pos")
    pos, core = lax.axis_index("pos"), lax.axis_index("core")
    everything = ("rz", "core", "pos")
    owners = rz_count * 2 * pos_count
    own_at = (lax.axis_index("rz") * 2 + core) * pos_count + pos
    part_len, model_width = activations.shape[1:]
    length = part_len * pos_count
    own_width = pre_gain.shape[0]
    chan = model_width // pos_count
    ff_own = down_weight.shape[0]
    ff_half = rz_count * pos_count * ff_own
    docs = doc_bounds.shape[1]
    order = filter_two.shape[0]
    tables = transform_tables()
    meta = unit_table(doc_bounds[0], length, (pos * chan).astype(jnp.int32))

    single = functools.partial(jnp.reshape, shape=(1, -1))
    vectors = [
        short_weight,
        short_bias,
        single(skip_gain),
        in_bias,
        filter_three,
        single(pre_gain),
        single(pre_bias),
        single(out_bias),
        single(post_gain),
        single(post_bias),
        single(down_bias),
        single(up_bias),
    ]
    filter_columns = jnp.stack([filter_bias_one, filter_bias_two, filter_freq], 1).astype(F32)
    embedding = positions_table(length, filter_one.shape[0])
    row_in, weight_in, bundle, extra, out_all, lines, mine, up_bias_half, layers = gather(
        (rz_count, pos_count),
        activations[0],
        in_weight.transpose(1, 0, 2),
        up_weight,
        down_weight,
        out_weight,
        vectors,
        (embedding, filter_one, filter_two, filter_columns),
    )
    row_in = row_in.reshape(length, model_width)
    weight_in = weight_in.reshape(model_width, -1)
    out_all = out_all.reshape(model_width, model_width)
    tile = pos_count * ff_own
    columns = model_width // tile
    bits = bits_of(pos_count)
    orders = (bits, bits[::-1])
    place = jnp.stack([pos, lax.axis_index("rz")]).astype(jnp.int32)

    own_in = activations[0]
    projected = project(row_in, lines, weight_in, mine)
    sides = [{0: bundle[: rz_count // 2]}, {0: bundle[rz_count // 2 :]}]
    firsts = [[swap(sides[side][0], "pos", bit) for bit in bits] for side in range(2)]

    def along(values, distance):
        ups = [(at, at + 1) for at in range(distance - 1, rz_count - 1)]
        downs = [(at + 1, at) for at in range(rz_count - distance)]
        return [lax.ppermute(values[0], "rz", ups), lax.ppermute(values[1], "rz", downs)]

    moved = [along([extra, extra], 1)]
    projected, moved = lax.optimization_barrier((projected, moved))
    for distance in range(2, rz_count - 1):
        moved.append(along(moved[-1], distance))
    branch, mixed = mixer_forward(meta, docs, projected, layers, mine, model_width, tables)
    branch, firsts, moved = lax.optimization_barrier((branch, firsts, moved))
    extras = [extra] + [pair[0] for pair in moved] + [pair[1] for pair in moved]
    given = [0] + bits
    pieces = [
        sides[side][0] if bit == 0 else firsts[side][bits.index(bit)]
        for bit in given
        for side in range(2)
    ]
    result, grad_residual, branch_grad, token_lines, *piece_grads = middle(
        (rz_count, pos_count),
        given,
        branch,
        activations[0],
        out_all,
        lines,
        out_grad[0],
        up_bias_half,
        pieces,
        extras,
    )
    result = result[None]

    masks = list(range(pos_count))
    kept = [[mask for mask in masks if not mask & orders[side][0]] for side in range(2)]
    by_mask = {
        (side, mask): piece_grads[2 * at + side]
        for at, mask in enumerate(masks)
        for side in range(2)
    }
    own_pieces = [by_mask[side, kept[side][at]] for at in range(len(kept[0])) for side in range(2)]
    moved_pieces = [
        swap(by_mask[side, kept[side][at] ^ orders[side][0]], "pos", orders[side][0])
        for at in range(len(kept[0]))
        for side in range(2)
    ]

    proj_grad, filt_grad, chan_sums = mixer_backward(
        meta, docs, projected, layers, mine, model_width, tables, mixed, branch_grad
    )
    input_grad, weight_in_grad, up_weight_grad, down_weight_grad, out_weight_grad, total, shared = (
        last_sums(
            (rz_count, pos_count),
            kept,
            row_in,
            proj_grad,
            weight_in,
            lines,
            grad_residual,
            token_lines,
            chan_sums,
            filt_grad,
            layers,
            mine,
            embedding,
            filter_two,
            filter_columns,
            own_pieces,
            moved_pieces,
        )
    )
    input_grad = input_grad[None]
    weight_in_grad = weight_in_grad.transpose(1, 0, 2)
    lane = lax.rem(own_at * own_width, 128)
    up_place = lax.rem(own_at * ff_own, owners * ff_own * 128 // model_width)
    place = jnp.stack([lane, up_place // 128, up_place % 128]).astype(jnp.int32)
    (
        pre_gain_grad,
        pre_bias_grad,
        out_bias_grad,
        post_gain_grad,
        post_bias_grad,
        down_bias_grad,
        short_weight_grad,
        short_bias_grad,
        in_bias_grad,
        skip_grad,
        three_grad,
        up_bias_grad,
        one_grad,
        bias_one_grad,
        two_grad,
        bias_two_grad,
        freq_grad,
    ) = finish(place, total, shared, own_width, ff_own, filter_one.shape[0], order)
    return (
        result,
        input_grad,
        pre_gain_grad[0],
        pre_bias_grad[0],
        weight_in_grad,
        in_bias_grad,
        short_weight_grad,
        short_bias_grad,
        skip_grad[0],
        out_weight_grad,
        out_bias_grad[0],
        post_gain_grad[0],
        post_bias_grad[0],
        up_weight_grad,
        up_bias_grad[0],
        down_weight_grad,
        down_bias_grad[0],
        one_grad,
        bias_one_grad[0],
        two_grad,
        bias_two_grad[0],
        freq_grad[0],
        three_grad,
    )


def solution(mesh):
    rows_count, pos_count = mesh.devices.shape
    fine = Mesh(mesh.devices.reshape(rows_count // 2, 2, pos_count), ("rz", "core", "pos"))
    rows = ("rz", "core")
    every = ("rz", "core", "pos")
    tokens = P(rows, "pos", None)
    vector = P(every)
    matrix = P(every, None)
    return jax.shard_map(
        on_device,
        mesh=fine,
        in_specs=(
            tokens,
            tokens,
            P(rows, None),
            P(rows, None),
            vector,
            vector,
            P(every, None, None),
            P(None, every),
            P(None, None, every),
            P(None, every),
            vector,
            matrix,
            vector,
            vector,
            vector,
            matrix,
            vector,
            matrix,
            vector,
            P(),
            P(),
            P(),
            P(),
            P(),
            P(None, every),
        ),
        out_specs=(
            tokens,
            tokens,
            vector,
            vector,
            P(every, None, None),
            P(None, every),
            P(None, None, every),
            P(None, every),
            vector,
            matrix,
            vector,
            vector,
            vector,
            matrix,
            vector,
            matrix,
            vector,
            P(),
            P(),
            P(),
            P(),
            P(),
            P(None, every),
        ),
        check_vma=False,
    )
```

```python
import functools
import math

import jax
import jax.numpy as jnp
import ml_dtypes
import numpy as np
from jax import lax
from jax.experimental import pallas as pl
from jax.experimental.pallas import tpu as pltpu
from jax.sharding import Mesh
from jax.sharding import PartitionSpec as P

HIGHEST = lax.Precision.HIGHEST
F32 = jnp.float32
BF16 = jnp.bfloat16
BLOCK = 256
FREQ_CHUNK = 64
VMEM_LIMIT = 60 * 1024 * 1024


def layer_norm(values, norm_gain, norm_shift):
    centre = values - jnp.mean(values, axis=-1, keepdims=True)
    spread = jnp.mean(centre * centre, axis=-1, keepdims=True)
    return centre * lax.rsqrt(spread + 1e-05) * norm_gain + norm_shift


FEATURES = 64
THREE_ROW, NORM_ROW, UP_ROW, LINES = 16, 80, 86, 96


def positions_table(length, features):
    band_count = (features - 1) // 2
    places = np.arange(length, dtype=np.float64)
    ladder = 0.0001 + (band_count - 1 - 0.0001) * np.arange(band_count) / (band_count - 1)
    angles = 2.0 * math.pi / length * places[:, None] * ladder[None, :]
    table = np.zeros((FEATURES, length), np.float32)
    table[0] = places / (length - 1)
    table[1 : 1 + band_count] = np.cos(angles).T
    table[1 + band_count : features] = -np.sin(angles).T
    return jnp.asarray(table)


def decay_of(block, length, first_channel, model_width, width):
    place = lax.broadcasted_iota(jnp.int32, (BLOCK, width), 0) + block * BLOCK
    channel = lax.broadcasted_iota(jnp.int32, (BLOCK, width), 1) + first_channel
    slow_rate = math.log(0.01) / 1.5
    fast_rate = math.log(0.01) / 0.3
    rates = jnp.abs(
        slow_rate + (fast_rate - slow_rate) * channel.astype(F32) * (1.0 / (model_width - 1))
    )
    return jnp.exp(-(place.astype(F32) * (1.0 / (length - 1))) * rates) + 0.05


def exact(left, right, contract):
    return lax.dot_general(
        left, right, (contract, ((), ())), precision=HIGHEST, preferred_element_type=F32
    )


def filter_block(layers, lines, block, units, length, width, model_width):
    layer_two = layers[0, :, rows_of(block)]
    three = lines[THREE_ROW : THREE_ROW + layer_two.shape[0], :].astype(BF16)
    decay = decay_of(block, length, units.channel(), model_width, width)
    high = layer_two.astype(BF16)
    low = (layer_two - high.astype(F32)).astype(BF16)
    filt = lax.dot_general(
        jnp.concatenate([high, low], axis=0),
        jnp.concatenate([three, three], axis=0),
        (((0,), (0,)), ((), ())),
        preferred_element_type=F32,
    )
    return filt, decay


def transform_tables():
    order = np.concatenate([np.arange(0, BLOCK, 2), np.arange(1, BLOCK, 2)])
    angle = math.pi / BLOCK * (order[:, None] + 0.5) * np.arange(BLOCK)[None, :]
    forward = np.concatenate([np.cos(angle), -np.sin(angle)], axis=0)
    tables = []
    for table in (forward, forward.T / BLOCK):
        high = table.astype(ml_dtypes.bfloat16)
        low = (table - high.astype(np.float64)).astype(ml_dtypes.bfloat16)
        tables.append(jnp.asarray(high))
    return tables


def unit_table(bounds, length, first_channel):
    docs = bounds.shape[0]
    units = length // BLOCK + docs - 1
    ends = jnp.concatenate([bounds[1:], jnp.full((1,), length, jnp.int32)])
    first = bounds // BLOCK
    count = jnp.where(ends > bounds, (ends - 1) // BLOCK - first + 1, 0)
    earlier = jnp.arange(docs)[:, None] >= jnp.arange(docs)[None, :]
    stops = jnp.sum(jnp.where(earlier, count[None, :], 0), axis=1)
    starts = stops - count
    unit = jnp.arange(units, dtype=jnp.int32)
    doc = jnp.sum((unit[:, None] >= stops[None, :]).astype(jnp.int32), axis=1)
    doc = jnp.minimum(doc, docs - 1)
    pick = (doc[:, None] == jnp.arange(docs)[None, :]).astype(jnp.int32)

    def of_doc(values):
        return jnp.sum(pick * values[None, :], axis=1)

    block = jnp.clip(of_doc(first - starts) + unit, 0, length // BLOCK - 1)
    return jnp.concatenate(
        [
            block,
            of_doc(bounds),
            of_doc(ends),
            of_doc(starts),
            of_doc(stops),
            starts,
            stops,
            bounds,
            stops[docs - 1 :],
            jnp.reshape(first_channel, (1,)),
        ]
    ).astype(jnp.int32)


class Units:
    def __init__(self, meta, length, docs):
        self.meta = meta
        self.docs = docs
        self.units = length // BLOCK + docs - 1

    def block(self, unit):
        return self.meta[unit]

    def low(self, unit):
        return self.meta[self.units + unit]

    def high(self, unit):
        return self.meta[2 * self.units + unit]

    def start(self, unit):
        return self.meta[3 * self.units + unit]

    def stop(self, unit):
        return self.meta[4 * self.units + unit]

    def doc_start(self, doc):
        return self.meta[5 * self.units + doc]

    def doc_stop(self, doc):
        return self.meta[5 * self.units + self.docs + doc]

    def bound(self, doc):
        return self.meta[5 * self.units + 2 * self.docs + doc]

    def total(self):
        return self.meta[5 * self.units + 3 * self.docs]

    def channel(self):
        return self.meta[5 * self.units + 3 * self.docs + 1]

    def inside(self, unit, width):
        place = lax.broadcasted_iota(jnp.int32, (BLOCK, width), 0) + self.block(unit) * BLOCK
        return (place >= self.low(unit)) & (place < self.high(unit))


def rows_of(block):
    return pl.ds(pl.multiple_of(block * BLOCK, BLOCK), BLOCK)


def times(table, value):
    high = value.astype(BF16)
    low = (value - high.astype(F32)).astype(BF16)
    return jnp.dot(
        table[...], high, preferred_element_type=F32
    )


def tap_masks(units, block, width, ahead=0):
    place = lax.broadcasted_iota(jnp.int32, (BLOCK, width), 0) + (block * BLOCK + ahead)
    first = place == units.bound(0)
    second = place == units.bound(0) + 1
    for doc in range(1, units.docs):
        first = first | (place == units.bound(doc))
        second = second | (place == units.bound(doc) + 1)
    return jnp.logical_not(first), jnp.logical_not(first | second)


def delayed(ref, block):
    start = block * BLOCK
    here = ref[rows_of(block), :].astype(F32)
    before = ref[pl.ds(pl.multiple_of(jnp.maximum(start - 16, 0), 16), 16), :].astype(F32)
    joined = jnp.concatenate([before, here], axis=0)
    return (here, pltpu.roll(joined, 1, 0)[16:], pltpu.roll(joined, 2, 0)[16:])


def short_conv(parts, small, branch, masks):
    total = small[9 + branch : 10 + branch, :] + small[branch : branch + 1, :] * parts[0]
    total += jnp.where(masks[0], small[3 + branch : 4 + branch, :] * parts[1], 0.0)
    total += jnp.where(masks[1], small[6 + branch : 7 + branch, :] * parts[2], 0.0)
    return total


def mixer_forward_kernel(
    docs, model_width, meta, post, pre, val, layers, small, fwd, inv, branch, mixed, gated, spec, taps, prod
):
    length, width = gated.shape
    blocks = length // BLOCK
    units = Units(meta, length, docs)

    def gate(block, _):
        masks = tap_masks(units, block, width)
        part = short_conv(delayed(val, block), small, 2, masks)
        part *= short_conv(delayed(pre, block), small, 1, masks)
        gated[rows_of(block), :] = part
        mixed[rows_of(block), :] = small[12:13, :] * part
        filt, decay = filter_block(layers, small, block, units, length, width, model_width)
        taps[block] = times(fwd, filt * decay)
        return 0

    lax.fori_loop(0, blocks, gate, 0)

    def transform(unit, _):
        value = gated[rows_of(units.block(unit)), :]
        spec[unit] = times(fwd, jnp.where(units.inside(unit, width), value, 0.0))
        return 0

    lax.fori_loop(0, units.total(), transform, 0)

    def multiply(unit, _):
        for low in range(0, BLOCK, FREQ_CHUNK):
            re, im = pl.ds(low, FREQ_CHUNK), pl.ds(BLOCK + low, FREQ_CHUNK)

            def step(back, total):
                at = unit - back
                s_re, s_im, t_re, t_im = spec[at, re], spec[at, im], taps[back, re], taps[back, im]
                return (
                    total[0] + (s_re * t_re - s_im * t_im),
                    total[1] + (s_re * t_im + s_im * t_re),
                )

            zero = jnp.zeros((FREQ_CHUNK, width), F32)
            total = lax.fori_loop(0, unit - units.start(unit) + 1, step, (zero, zero))
            prod[unit, re] = total[0]
            prod[unit, im] = total[1]
        return 0

    lax.fori_loop(0, units.total(), multiply, 0)

    half = BLOCK // 2

    def bring_back(unit, _):
        last = jnp.maximum(unit - 1, 0)
        old = jnp.where(unit > units.start(unit), prod[last], 0.0)
        new = prod[unit]
        joined = jnp.concatenate(
            [
                new[:half] - old[BLOCK : BLOCK + half],
                new[half:BLOCK] + old[BLOCK + half :],
                new[BLOCK : BLOCK + half] + old[:half],
                new[BLOCK + half :] - old[half:BLOCK],
            ],
            axis=0,
        )
        value = times(inv, joined)
        rows = rows_of(units.block(unit))
        mixed[rows, :] += jnp.where(units.inside(unit, width), value, 0.0)
        return 0

    lax.fori_loop(0, units.total(), bring_back, 0)

    def finish(block, _):
        masks = tap_masks(units, block, width)
        gate_value = short_conv(delayed(post, block), small, 0, masks)
        branch[rows_of(block), :] = (gate_value * mixed[rows_of(block), :]).astype(BF16)
        return 0

    lax.fori_loop(0, blocks, finish, 0)


def mixer_backward_kernel(
    docs,
    model_width,
    meta,
    post,
    pre,
    val,
    layers,
    small,
    fwd,
    inv,
    mixed,
    branch_grad,
    proj_grad,
    filt_grad,
    sums,
    gated,
    gm,
    conv_grad,
    spec,
    taps,
    prod,
):
    length, width = gated.shape
    blocks = length // BLOCK
    units = Units(meta, length, docs)
    half = BLOCK // 2
    sums[...] = jnp.zeros_like(sums)

    def total_rows(value):
        return jnp.sum(value, axis=0, keepdims=True)

    def gate(block, _):
        rows = rows_of(block)
        masks = tap_masks(units, block, width)
        part = short_conv(delayed(val, block), small, 2, masks)
        part *= short_conv(delayed(pre, block), small, 1, masks)
        gated[rows, :] = part
        grad = branch_grad[rows, :].astype(F32)
        mix_grad = grad * short_conv(delayed(post, block), small, 0, masks)
        gm[rows, :] = mix_grad
        conv_grad[0, rows, :] = grad * mixed[rows, :]
        conv_grad[1, rows, :] = small[12:13, :] * mix_grad
        sums[15:16, :] += total_rows(part * mix_grad)
        filt, decay = filter_block(layers, small, block, units, length, width, model_width)
        taps[block] = times(fwd, filt * decay)
        return 0

    lax.fori_loop(0, blocks, gate, 0)

    def transform(unit, _):
        rows = rows_of(units.block(unit))
        inside = units.inside(unit, width)
        spec[unit] = times(fwd, jnp.where(inside, gated[rows, :], 0.0))
        prod[unit] = times(fwd, jnp.where(inside, gm[rows, :], 0.0))
        return 0

    lax.fori_loop(0, units.total(), transform, 0)

    def spread(unit, _):
        after = jnp.minimum(unit + 1, units.units - 1)
        new = jnp.where(unit + 1 < units.stop(unit), prod[after], 0.0)
        prod[unit, pl.ds(0, half)] += new[BLOCK : BLOCK + half]
        prod[unit, pl.ds(half, half)] -= new[BLOCK + half :]
        prod[unit, pl.ds(BLOCK, half)] -= new[:half]
        prod[unit, pl.ds(BLOCK + half, half)] += new[half:BLOCK]
        return 0

    lax.fori_loop(0, units.total(), spread, 0)

    def signal_grad(unit, _):
        pieces = []
        for low in range(0, BLOCK, FREQ_CHUNK):
            re, im = pl.ds(low, FREQ_CHUNK), pl.ds(BLOCK + low, FREQ_CHUNK)

            def step(ahead, total):
                at = unit + ahead
                g_re, g_im, t_re, t_im = (
                    prod[at, re],
                    prod[at, im],
                    taps[ahead, re],
                    taps[ahead, im],
                )
                return (
                    total[0] + (g_re * t_re + g_im * t_im),
                    total[1] + (g_im * t_re - g_re * t_im),
                )

            zero = jnp.zeros((FREQ_CHUNK, width), F32)
            pieces.append(lax.fori_loop(0, units.stop(unit) - unit, step, (zero, zero)))
        joined = jnp.concatenate([piece[0] for piece in pieces] + [piece[1] for piece in pieces])
        value = times(inv, joined)
        rows = rows_of(units.block(unit))
        conv_grad[1, rows, :] += jnp.where(units.inside(unit, width), value, 0.0)
        return 0

    lax.fori_loop(0, units.total(), signal_grad, 0)

    def tap_grad(back, _):
        pieces = []
        for low in range(0, BLOCK, FREQ_CHUNK):
            re, im = pl.ds(low, FREQ_CHUNK), pl.ds(BLOCK + low, FREQ_CHUNK)

            def step(unit, total):
                at = unit - back
                g_re, g_im, s_re, s_im = (
                    prod[unit, re],
                    prod[unit, im],
                    spec[at, re],
                    spec[at, im],
                )
                return (
                    total[0] + (g_re * s_re + g_im * s_im),
                    total[1] + (g_im * s_re - g_re * s_im),
                )

            zero = jnp.zeros((FREQ_CHUNK, width), F32)
            total = (zero, zero)
            for doc in range(docs):
                total = lax.fori_loop(
                    units.doc_start(doc) + back, units.doc_stop(doc), step, total
                )
            pieces.append(total)
        joined = jnp.concatenate([piece[0] for piece in pieces] + [piece[1] for piece in pieces])
        decay = decay_of(back, length, units.channel(), model_width, width)
        filt_grad[rows_of(back), :] = times(inv, joined) * decay
        return 0

    lax.fori_loop(0, blocks, tap_grad, 0)

    def conv_back(block, _):
        rows = rows_of(block)
        masks = tap_masks(units, block, width)
        val_parts, pre_parts, post_parts = (
            delayed(val, block),
            delayed(pre, block),
            delayed(post, block),
        )
        gated_grad = conv_grad[1, rows, :]
        pre_grad = gated_grad * short_conv(val_parts, small, 2, masks)
        val_grad = gated_grad * short_conv(pre_parts, small, 1, masks)
        post_grad = conv_grad[0, rows, :]
        conv_grad[1, rows, :] = pre_grad
        conv_grad[2, rows, :] = val_grad
        for branch, (grad, parts) in enumerate(
            ((post_grad, post_parts), (pre_grad, pre_parts), (val_grad, val_parts))
        ):
            sums[branch : branch + 1, :] += total_rows(grad * parts[0])
            sums[3 + branch : 4 + branch, :] += total_rows(
                jnp.where(masks[0], grad * parts[1], 0.0)
            )
            sums[6 + branch : 7 + branch, :] += total_rows(
                jnp.where(masks[1], grad * parts[2], 0.0)
            )
            sums[9 + branch : 10 + branch, :] += total_rows(grad)
        return 0

    lax.fori_loop(0, blocks, conv_back, 0)

    def spread_taps(block, _):
        start = block * BLOCK
        one, _two = tap_masks(units, block, width, 1)
        _one, two = tap_masks(units, block, width, 2)
        place = lax.broadcasted_iota(jnp.int32, (BLOCK, width), 0) + start
        one = one & (place + 1 < length)
        two = two & (place + 2 < length)
        for branch in range(3):
            here = conv_grad[branch, rows_of(block), :]
            after = conv_grad[
                branch, pl.ds(pl.multiple_of(jnp.minimum(start + BLOCK, length - 8), 8), 8), :
            ]
            joined = jnp.concatenate([here, after], axis=0)
            size = BLOCK + 8
            next_one = pltpu.roll(joined, size - 1, 0)[:BLOCK]
            next_two = pltpu.roll(joined, size - 2, 0)[:BLOCK]
            total = small[branch : branch + 1, :] * here
            total += jnp.where(one, small[3 + branch : 4 + branch, :] * next_one, 0.0)
            total += jnp.where(two, small[6 + branch : 7 + branch, :] * next_two, 0.0)
            rounded = total.astype(BF16)
            proj_grad[rows_of(block), branch * width : (branch + 1) * width] = rounded
            sums[12 + branch : 13 + branch, :] += total_rows(rounded.astype(F32))
        return 0

    lax.fori_loop(0, blocks, spread_taps, 0)


def whole_spec(shape, column=0):
    place = (0,) * (len(shape) - 1) + (column,)
    return pl.BlockSpec(shape, lambda i, meta: place, pipeline_mode=pl.Buffered(1))


def layer_spec(shape):
    return pl.BlockSpec(
        (1,) + shape[1:], lambda i, meta: (1, 0, 0), pipeline_mode=pl.Buffered(1)
    )


def mixer_forward(meta, docs, projected, layers, small, model_width, tables):
    length, width = layers.shape[2], small.shape[1]
    units = length // BLOCK + docs - 1
    column = [whole_spec((length, width), at) for at in range(3)]
    return pl.pallas_call(
        functools.partial(mixer_forward_kernel, docs, model_width),
        out_shape=(
            jax.ShapeDtypeStruct((length, width), BF16),
            jax.ShapeDtypeStruct((length, width), F32),
        ),
        grid_spec=pltpu.PrefetchScalarGridSpec(
            num_scalar_prefetch=1,
            grid=(1,),
            in_specs=column
            + [layer_spec(layers.shape)]
            + [whole_spec(value.shape) for value in (small, tables[0], tables[1])],
            out_specs=(column[0], column[0]),
            scratch_shapes=[
                pltpu.VMEM((length, width), F32),
                pltpu.VMEM((units, 2 * BLOCK, width), F32),
                pltpu.VMEM((length // BLOCK, 2 * BLOCK, width), F32),
                pltpu.VMEM((units, 2 * BLOCK, width), F32),
            ],
        ),
        compiler_params=pltpu.CompilerParams(vmem_limit_bytes=VMEM_LIMIT),
        cost_estimate=pl.CostEstimate(
            flops=40 * 10**9, bytes_accessed=10 * 10**6, transcendentals=0
        ),
        name="mixer_forward",
    )(meta, projected, projected, projected, layers, small, *tables)


def mixer_backward(meta, docs, projected, layers, small, model_width, tables, mixed, branch_grad):
    length, width = layers.shape[2], small.shape[1]
    units = length // BLOCK + docs - 1
    column = [whole_spec((length, width), at) for at in range(3)]
    return pl.pallas_call(
        functools.partial(mixer_backward_kernel, docs, model_width),
        out_shape=(
            jax.ShapeDtypeStruct((length, 3 * width), BF16),
            jax.ShapeDtypeStruct((length, width), F32),
            jax.ShapeDtypeStruct((16, width), F32),
        ),
        grid_spec=pltpu.PrefetchScalarGridSpec(
            num_scalar_prefetch=1,
            grid=(1,),
            in_specs=column
            + [layer_spec(layers.shape)]
            + [
                whole_spec(value.shape)
                for value in (small, tables[0], tables[1], mixed, branch_grad)
            ],
            out_specs=(
                whole_spec((length, 3 * width)),
                column[0],
                whole_spec((16, width)),
            ),
            scratch_shapes=[
                pltpu.VMEM((length, width), F32),
                pltpu.VMEM((length, width), F32),
                pltpu.VMEM((3, length, width), F32),
                pltpu.VMEM((units, 2 * BLOCK, width), F32),
                pltpu.VMEM((length // BLOCK, 2 * BLOCK, width), F32),
                pltpu.VMEM((units, 2 * BLOCK, width), F32),
            ],
        ),
        compiler_params=pltpu.CompilerParams(vmem_limit_bytes=VMEM_LIMIT),
        cost_estimate=pl.CostEstimate(
            flops=80 * 10**9, bytes_accessed=16 * 10**6, transcendentals=0
        ),
        name="mixer_backward",
    )(meta, projected, projected, projected, layers, small, *tables, mixed, branch_grad)


def norm_parts(values):
    centre = values - jnp.mean(values, axis=-1, keepdims=True)
    spread = jnp.mean(centre * centre, axis=-1, keepdims=True)
    scale = lax.rsqrt(spread + 1e-05)
    return centre * scale, scale


def project_kernel(inputs, norm, weight, lines, out):
    unit, _ = norm_parts(inputs[...].astype(F32))
    normed = (unit * norm[0:1, :] + norm[1:2, :]).astype(BF16)
    bias = jnp.concatenate([lines[13 + at : 14 + at, :] for at in range(3)], axis=1)
    total = jnp.dot(normed, weight[...], preferred_element_type=F32) + bias
    out[...] = total.astype(BF16)


def project(inputs, lines, weight, mine):
    length, depth = inputs.shape
    width = weight.shape[1]
    return pl.pallas_call(
        project_kernel,
        out_shape=jax.ShapeDtypeStruct((length, width), BF16),
        grid=(length // BLOCK,),
        in_specs=[
            pl.BlockSpec((BLOCK, depth), lambda i: (i, 0)),
            pl.BlockSpec((8, depth), lambda i: (NORM_ROW // 8, 0)),
            pl.BlockSpec(weight.shape, lambda i: (0, 0)),
            pl.BlockSpec((16, mine.shape[1]), lambda i: (0, 0)),
        ],
        out_specs=pl.BlockSpec((BLOCK, width), lambda i: (i, 0)),
        compiler_params=pltpu.CompilerParams(vmem_limit_bytes=VMEM_LIMIT),
        cost_estimate=pl.CostEstimate(
            flops=2 * length * depth * width, bytes_accessed=10 * 10**6, transcendentals=0
        ),
        name="project",
    )(inputs, lines, weight, mine)


def gelu_pair(u):
    root = math.sqrt(2.0 / math.pi)
    square = u * u
    curve = jnp.tanh(root * (u + 0.044715 * (u * square)))
    value = 0.5 * u * (1.0 + curve)
    slope = 0.5 * (1.0 + curve) + 0.5 * u * (1.0 - curve * curve) * (
        root * (1.0 + 3.0 * 0.044715 * square)
    )
    return value, slope


class Copies:
    def __init__(self, local_sems, send_sems, got_sems):
        self.local_sems, self.send_sems, self.got_sems = local_sems, send_sems, got_sems
        self.locals = 0
        self.names = {}
        self.pending = []

    def local(self, source, target):
        copy = pltpu.make_async_copy(source, target, self.local_sems.at[self.locals])
        self.locals += 1
        copy.start()
        return copy

    def remote(self, name, source, target, device):
        at = self.names.setdefault(name, len(self.names))
        return pltpu.make_async_remote_copy(
            src_ref=source,
            dst_ref=target,
            send_sem=self.send_sems.at[at],
            recv_sem=self.got_sems.at[at],
            device_id=device,
            device_id_type=pl.DeviceIdType.MESH,
        )

    def send(self, name, source, target, device, when=None):
        copy = self.remote(name, source, target, device)
        if when is None:
            copy.start()
        else:
            pl.when(when)(copy.start)
        self.pending.append((name, copy, when))

    def got(self, name, target, device):
        self.remote(name, target, target, device).wait_recv()

    def local_when(self, source, target, when):
        copy = pltpu.make_async_copy(source, target, self.local_sems.at[self.locals])
        self.locals += 1
        pl.when(when)(copy.start)
        return copy

    def settle(self, name):
        for at, (found, copy, when) in enumerate(self.pending):
            if found == name:
                copy.wait_send()
                del self.pending[at]
                return

    def finish(self):
        for _, copy, when in self.pending:
            if when is None:
                copy.wait_send()
            else:
                pl.when(when)(copy.wait_send)


def greet(devices):
    barrier = pltpu.get_barrier_semaphore()
    for device in devices:
        pl.semaphore_signal(
            barrier, inc=1, device_id=device, device_id_type=pl.DeviceIdType.MESH
        )
    pl.semaphore_wait(barrier, len(devices))


def lane_masks(bits):
    masks, found = [0], []
    for bit in bits:
        found += [(mask ^ bit, bit) for mask in masks]
        masks += [mask ^ bit for mask in masks]
    return found


def middle_kernel(
    dims,
    given,
    branch,
    inputs,
    out_weight,
    lines,
    out_grad,
    up_bias,
    *rest,
):
    rz_count, pos_count = dims
    count = 2 * len(given)
    pieces, rest = rest[:count], rest[count:]
    steps = rz_count - 1
    extras, rest = rest[: 2 * steps - 1], rest[2 * steps - 1 :]
    result, residual, branch_grad, token_lines = rest[:4]
    piece_grads, rest = rest[4 : 4 + 2 * pos_count], rest[4 + 2 * pos_count :]
    (
        tokens,
        normed,
        grad,
        out_total,
        back_total,
        weights,
        grads,
        out_got,
        back_got,
        grad_q,
        turned_got,
        out_parts,
        bias_grad,
        local_sems,
        send_sems,
        got_sems,
    ) = rest
    z, core, pos = lax.axis_index("rz"), lax.axis_index("core"), lax.axis_index("pos")
    rows, depth = inputs.shape
    tiles, _, units, own_width, width = weights.shape
    middle = tiles // 2
    columns = depth // width
    chan = branch.shape[1]
    down_units = (units - 2 * tiles) // columns
    bits = bits_of(pos_count)
    orders = (bits, bits[::-1])
    copies = Copies(local_sems, send_sems, got_sems)
    other = {"core": 1 - core}
    peers = [jnp.bitwise_xor(pos, mask) for mask in range(pos_count)]

    def token_rows(owner):
        return pl.ds(pl.multiple_of(owner * rows, rows), rows)

    def channels(owner):
        return pl.ds(pl.multiple_of(owner * chan, chan), chan)

    grad_load = copies.local(out_grad, grad.at[pl.ds(0, rows)])
    loads = []
    for at, mask in enumerate(given):
        for side in range(2):
            piece = pieces[2 * at + side]
            part = pl.ds(side * middle, middle)
            target = weights.at[part, peers[mask], pl.ds(0, piece.shape[1])]
            loads.append((copies.local(piece, target), None))
    last = pl.ds(units - extras[0].shape[1], extras[0].shape[1])

    def extra_slot(origin):
        return weights.at[jnp.clip(origin, 0, tiles - 1), :, last]

    for at, extra in enumerate(extras):
        origin = z - (at if at < steps else steps - 1 - at)
        there = (origin >= 0) & (origin < tiles)
        loads.append((copies.local_when(extra, extra_slot(origin), there), there))
    greet(
        [other]
        + [{"rz": (z + step) % rz_count} for step in range(1, rz_count)]
        + [{"pos": peers[mask]} for mask in range(1, pos_count)]
    )
    for mask in range(1, pos_count):
        copies.send(
            ("branch", mask),
            branch.at[token_rows(peers[mask])],
            tokens.at[:, channels(pos)],
            {"pos": peers[mask]},
        )
    grad_load.wait()
    own_half, other_half = pl.ds(0, rows), pl.ds(rows, rows)
    copies.send(("grad",), grad.at[own_half], grad.at[other_half], other)

    full = pieces[0].shape[1]
    arriving = []
    for side in range(2):
        part = pl.ds(side * middle, middle)
        for mask, bit in lane_masks(orders[side]):
            if mask in given:
                continue
            arriving.append((side, mask, bit))
            before = mask ^ bit
            slot = weights.at[part, peers[before], pl.ds(0, full)]
            if before in given:
                source = pieces[2 * given.index(before) + side]
            else:
                source = slot
                prior = [item for item in arriving if item[:2] == (side, before)][0]
                copies.got(("weights", side, before), slot, {"pos": peers[prior[2]]})
            copies.send(("weights", side, mask), source, slot, {"pos": peers[bit]})
    ends = ((1, {"rz": z + 1}, {"rz": z - 1}), (-1, {"rz": z - 1}, {"rz": z + 1}))
    for side, (direction, onward, _) in enumerate(ends):
        origin = z - direction * (steps - 1)
        sends = (origin >= 0) & (origin < tiles)
        sends = sends & (z + direction >= 0) & (z + direction < tiles)
        source = extras[steps - 1 if side == 0 else 2 * steps - 2] if steps > 1 else extras[0]
        copies.send(("extra", side), source, extra_slot(origin), onward, sends)

    tokens[:, channels(pos)] = branch[token_rows(pos), :]
    for mask in range(1, pos_count):
        copies.got(("branch", mask), tokens.at[:, channels(peers[mask])], {"pos": peers[mask]})
    line = [lines[NORM_ROW + at : NORM_ROW + at + 1, :] for at in range(6)]

    def project_out(at, _):
        part = pl.ds(pl.multiple_of(at * BLOCK, BLOCK), BLOCK)
        value = inputs[part, :].astype(F32) + line[2]
        value += jnp.dot(tokens[part, :], out_weight[...], preferred_element_type=F32)
        residual[part, :] = value
        unit, _ = norm_parts(value)
        normed[part, :] = (unit * line[3] + line[4]).astype(BF16)
        return 0

    lax.fori_loop(0, rows // BLOCK, project_out, 0)
    copies.send(("normed",), normed.at[own_half], normed.at[other_half], other)
    out_total[...] = jnp.zeros_like(out_total)
    back_total[...] = jnp.zeros_like(back_total)
    for copy, there in loads:
        if there is None:
            copy.wait()
        else:
            pl.when(there)(copy.wait)
    sent = {item[:2] for item in arriving}
    for side, mask, bit in arriving:
        onward = [item for item in arriving if item[0] == side and item[1] ^ item[2] == mask]
        if not onward:
            slot = weights.at[pl.ds(side * middle, middle), peers[mask], pl.ds(0, full)]
            copies.got(("weights", side, mask), slot, {"pos": peers[bit]})
    for side, (direction, _, back) in enumerate(ends):
        origin = z - direction * steps

        def take(side=side, origin=origin, back=back):
            copies.got(("extra", side), extra_slot(origin), back)

        pl.when((origin >= 0) & (origin < tiles))(take)
    copies.got(("grad",), grad.at[other_half], other)
    copies.got(("normed",), normed.at[other_half], other)

    def step(tile, _):
        up = jnp.concatenate(
            [
                weights[block, :, side * tiles + tile].reshape(pos_count * own_width, width)
                for block in range(tiles)
                for side in range(2)
            ],
            axis=0,
        )
        down = jnp.concatenate(
            [
                weights[
                    tile, :, 2 * tiles + at * down_units : 2 * tiles + (at + 1) * down_units
                ].reshape(width, width)
                for at in range(columns)
            ],
            axis=1,
        )
        pre = jnp.dot(normed[: 2 * rows], up, preferred_element_type=F32) + up_bias[pl.ds(tile, 1), :]
        hidden, slope = gelu_pair(pre)
        hidden = hidden.astype(BF16)
        hidden_grad = lax.dot_general(
            grad[...], down, (((1,), (1,)), ((), ())), preferred_element_type=F32
        )
        pre_grad = hidden_grad * slope
        bias_grad[pl.ds(tile, 1), :] = jnp.sum(pre_grad, axis=0, keepdims=True)
        pre_grad = pre_grad.astype(BF16)
        out_total[...] += jnp.dot(hidden, down, preferred_element_type=F32)
        back_total[...] += lax.dot_general(
            pre_grad, up, (((1,), (1,)), ((), ())), preferred_element_type=F32
        )
        down_grad = lax.dot_general(
            hidden, grad[...], (((0,), (0,)), ((), ())), preferred_element_type=F32
        ).astype(BF16)
        for at in range(columns):
            grads[tile, :, 2 * tiles + at * down_units : 2 * tiles + (at + 1) * down_units] = (
                down_grad[:, at * width : (at + 1) * width].reshape(
                    pos_count, down_units, own_width, width
                )
            )
        up_grad = lax.dot_general(
            normed[: 2 * rows], pre_grad, (((0,), (0,)), ((), ())), preferred_element_type=F32
        ).astype(BF16)
        size = pos_count * own_width
        for block in range(tiles):
            for side in range(2):
                low = (2 * block + side) * size
                grads[block, :, side * tiles + tile] = up_grad[low : low + size].reshape(
                    pos_count, own_width, width
                )
        return 0

    lax.fori_loop(0, tiles, step, 0)
    copies.settle(("normed",))
    normed[:rows] = back_total[rows:].astype(BF16)
    copies.send(("back",), normed.at[own_half], back_got, other)
    normed[rows : 2 * rows] = out_total[rows:].astype(BF16)
    copies.send(("out",), normed.at[other_half], out_got, other)
    stores = []
    for mask in range(pos_count):
        for side in range(2):
            source = grads.at[pl.ds(side * middle, middle), peers[mask]]
            target = piece_grads[2 * mask + side].at[:, pl.ds(0, units)]
            stores.append(copies.local(source, target))

    copies.got(("back",), back_got, other)
    zero = jnp.zeros((1, depth), F32)

    def norm_back(at, sums):
        part = pl.ds(pl.multiple_of(at * BLOCK, BLOCK), BLOCK)
        unit, scale = norm_parts(residual[part, :])
        back = back_total[part, :] + back_got[part, :].astype(F32)
        scaled = back * line[3]
        out = grad[part, :].astype(F32)
        value = out + scale * (
            scaled
            - jnp.mean(scaled, axis=-1, keepdims=True)
            - unit * jnp.mean(scaled * unit, axis=-1, keepdims=True)
        )
        back_total[part, :] = value
        grad_q[part, :] = value.astype(BF16)

        def total(value):
            return jnp.sum(value, axis=0, keepdims=True)

        return (
            sums[0] + total(value),
            sums[1] + total(back * unit),
            sums[2] + total(back),
            sums[3] + total(out),
        )

    sums = lax.fori_loop(0, rows // BLOCK, norm_back, (zero,) * 4)
    turned = lax.dot_general(
        grad_q[...], out_weight[...], (((1,), (1,)), ((), ())), preferred_element_type=F32
    ).astype(BF16)
    copies.settle(("grad",))
    grad[own_half, :] = turned
    for mask in range(1, pos_count):
        copies.send(
            ("branch grad", mask),
            grad.at[own_half, channels(peers[mask])],
            branch_grad.at[token_rows(pos)],
            {"pos": peers[mask]},
        )
    branch_grad[token_rows(pos), :] = grad[own_half, channels(pos)]
    copies.got(("out",), out_got, other)

    def add_result(at, _):
        part = pl.ds(pl.multiple_of(at * BLOCK, BLOCK), BLOCK)
        value = residual[part, :] + (out_total[part, :] + out_got[part, :].astype(F32)) + line[5]
        result[part, :] = value.astype(BF16)
        residual[part, :] = back_total[part, :]
        return 0

    lax.fori_loop(0, rows // BLOCK, add_result, 0)
    token_lines[...] = jnp.zeros_like(token_lines)
    for at in range(4):
        token_lines[2 + at : 3 + at, :] = sums[at]
    per_tile = width // 128
    per = 2 * tiles * width // depth // per_tile
    for tile in range(tiles):
        owner = 2 * tile + core
        lanes = pl.ds(pl.multiple_of(owner // per * 128, 128), 128)
        for at in range(per * per_tile):
            low = at % per_tile * 128
            value = bias_grad[tile : tile + 1, low : low + 128]
            token_lines[6 + at : 7 + at, lanes] = jnp.where(
                owner % per == at // per_tile, value, 0.0
            )

    copies.settle(("back",))
    copies.settle(("out",))
    normed[:depth] = lax.dot_general(
        tokens[...], grad_q[...], (((0,), (0,)), ((), ())), preferred_element_type=F32
    ).astype(BF16)
    size = pos_count * own_width

    def block_rows(block, side):
        return pl.ds(pl.multiple_of((2 * block + side) * size, size), size)

    for block in range(tiles):
        copies.send(
            ("turned", block),
            normed.at[block_rows(block, 1 - core)],
            turned_got.at[block],
            other,
        )
    for block in range(tiles):
        copies.got(("turned", block), turned_got.at[block], other)
        value = normed[block_rows(block, core), :].astype(F32)
        value = (value + turned_got[block].astype(F32)).astype(BF16)
        for at in range(columns):
            out_parts[block, :, at] = value[:, at * width : (at + 1) * width].reshape(
                pos_count, own_width, width
            )
    for mask in range(pos_count):
        for side in range(2):
            source = out_parts.at[pl.ds(side * middle, middle), peers[mask]]
            target = piece_grads[2 * mask + side].at[:, pl.ds(units, columns)]
            stores.append(copies.local(source, target))
    for mask in range(1, pos_count):
        copies.got(
            ("branch grad", mask), branch_grad.at[token_rows(peers[mask])], {"pos": peers[mask]}
        )
    for copy in stores:
        copy.wait()
    copies.finish()


def middle(dims, given, branch, inputs, out_weight, lines, out_grad, up_bias, pieces, extras):
    rz_count, pos_count = dims
    rows, depth = inputs.shape
    tiles, width = up_bias.shape
    length, chan = branch.shape
    piece = pieces[0].shape
    piece = piece[:1] + (piece[1] + extras[0].shape[1],) + piece[2:]
    own_width = piece[2]
    whole = (tiles, pos_count) + piece[1:]
    piece_grad = piece[:1] + (piece[1] + depth // width,) + piece[2:]
    size = pos_count * own_width
    anywhere = pl.BlockSpec(memory_space=pl.ANY)
    inside = pl.BlockSpec(memory_space=pltpu.VMEM)
    vmem = pltpu.VMEM
    local_count = 1 + len(pieces) + len(extras) + 4 * pos_count
    remote_count = 2 * (pos_count - 1) + 2 * pos_count + 6 + tiles
    return pl.pallas_call(
        functools.partial(middle_kernel, dims, given),
        out_shape=(
            jax.ShapeDtypeStruct((rows, depth), BF16),
            jax.ShapeDtypeStruct((rows, depth), F32),
            jax.ShapeDtypeStruct((length, chan), BF16),
            jax.ShapeDtypeStruct((16, depth), F32),
        )
        + (jax.ShapeDtypeStruct(piece_grad, BF16),) * (2 * pos_count),
        in_specs=[inside] * 4 + [anywhere, inside] + [anywhere] * (len(pieces) + len(extras)),
        out_specs=(inside,) * 4 + (anywhere,) * (2 * pos_count),
        scratch_shapes=[
            vmem((rows, depth), BF16),
            vmem((max(2 * rows, depth), depth), BF16),
            vmem((2 * rows, depth), BF16),
            vmem((2 * rows, depth), F32),
            vmem((2 * rows, depth), F32),
            vmem(whole, BF16),
            vmem(whole, BF16),
            vmem((rows, depth), BF16),
            vmem((rows, depth), BF16),
            vmem((rows, depth), BF16),
            vmem((tiles, size, depth), BF16),
            vmem((tiles, pos_count, depth // width, own_width, width), BF16),
            vmem((tiles, width), F32),
            pltpu.SemaphoreType.DMA((local_count,)),
            pltpu.SemaphoreType.DMA((remote_count,)),
            pltpu.SemaphoreType.DMA((remote_count,)),
        ],
        compiler_params=pltpu.CompilerParams(
            collective_id=2, has_side_effects=True, vmem_limit_bytes=VMEM_LIMIT
        ),
        cost_estimate=pl.CostEstimate(flops=10**7, bytes_accessed=10**7, transcendentals=0),
        name="middle",
    )(branch, inputs, out_weight, lines, out_grad, up_bias, *pieces, *extras)


def swap(value, axis, bit):
    count = lax.axis_size(axis)
    return lax.ppermute(value, axis, [(at, at ^ bit) for at in range(count)])


def gather_kernel(
    dims,
    inputs,
    weight,
    up,
    down,
    out,
    vectors,
    filter_in,
    row_in,
    weight_in,
    bundle,
    extra,
    owned,
    lines,
    mine,
    up_lines,
    layers,
    pack,
    small,
    small_mine,
    local_sems,
    send_sems,
    got_sems,
):
    rz_count, pos_count = dims
    z, core, pos = lax.axis_index("rz"), lax.axis_index("core"), lax.axis_index("pos")
    bits = bits_of(pos_count)
    lanes = [lane_masks(bits), lane_masks(bits[::-1])]
    own_width, model_width = out.shape
    chan = model_width // pos_count
    tile = bundle.shape[3]
    columns = model_width // tile
    half = model_width // 2
    middle = rz_count // 2
    copies = Copies(local_sems, send_sems, got_sems)
    other = {"core": 1 - core}
    right, left = {"rz": z + 1}, {"rz": z - 1}
    has_right, has_left = z + 1 < rz_count, z > 0
    greet(
        [other]
        + [{"rz": (z + step) % rz_count} for step in range(1, rz_count)]
        + [{"pos": jnp.bitwise_xor(pos, mask)} for mask in range(1, pos_count)]
    )

    def branch_cols(owner):
        return pl.ds(pl.multiple_of(owner * chan, chan), chan)

    for mask in range(1, pos_count):
        owner = jnp.bitwise_xor(pos, mask)
        for at in range(3):
            copies.send(
                ("in", mask, at),
                weight.at[at, :, branch_cols(owner)],
                weight_in.at[z, core, pos, :, pl.ds(at * chan, chan)],
                {"pos": owner},
            )

    def send_extra(lane, mask, bit):
        part = pl.ds(lane * (down_units // 2), down_units // 2)
        block = extra.at[jnp.bitwise_xor(pos, mask ^ bit), part]
        copies.send(("extra", lane, mask), block, block, {"pos": jnp.bitwise_xor(pos, bit)})

    def got_extra(lane, mask, bit):
        part = pl.ds(lane * (down_units // 2), down_units // 2)
        block = extra.at[jnp.bitwise_xor(pos, mask), part]
        copies.got(("extra", lane, mask), block, {"pos": jnp.bitwise_xor(pos, bit)})
        later = (bits, bits[::-1])[lane]
        for onward in later[later.index(bit) + 1 :]:
            send_extra(lane, mask ^ onward, onward)

    down_units = down.shape[0] // own_width
    local_extra = []
    for at in range(down_units):
        source = down.at[pl.ds(at * own_width, own_width), pl.ds((columns - 1) * tile, tile)]
        local_extra.append(copies.local(source, extra.at[pos, at]))
    for copy in local_extra:
        copy.wait()
    for at in range(len(bits)):
        for lane in range(2):
            bit = (bits, bits[::-1])[lane][at]
            send_extra(lane, bit, bit)

    def lane_cols(lane):
        return pl.ds(lane * half, half)

    def send_rows(lane, mask, bit):
        origin = jnp.bitwise_xor(pos, mask ^ bit)
        cols = lane_cols(lane)
        source = inputs.at[:, cols] if mask == bit else row_in.at[origin, :, cols]
        copies.send(
            ("rows", lane, mask),
            source,
            row_in.at[origin, :, cols],
            {"pos": jnp.bitwise_xor(pos, bit)},
        )

    for at in range(len(bits)):
        for lane in range(2):
            bit = (bits, bits[::-1])[lane][at]
            send_rows(lane, bit, bit)

    def up_cols(at, side):
        return pl.ds(pl.multiple_of((2 * at + side) * tile, tile), tile)

    for at in range(rz_count):
        copies.send(
            ("up", at),
            up.at[:, up_cols(at, 1 - core)],
            bundle.at[z, core * rz_count + at],
            other,
        )
    local_in = [
        copies.local(
            weight.at[at, :, branch_cols(pos)],
            weight_in.at[z, core, pos, :, pl.ds(at * chan, chan)],
        )
        for at in range(3)
    ]
    local_owned = [copies.local(out, owned.at[z, core, pos])]
    local_bundle = [
        copies.local(up.at[:, up_cols(at, core)], bundle.at[z, core * rz_count + at])
        for at in range(rz_count)
    ]
    for col in range(columns - 1):
        for at in range(down_units):
            source = down.at[pl.ds(at * own_width, own_width), pl.ds(col * tile, tile)]
            target = bundle.at[z, 2 * rz_count + col * down_units + at]
            local_bundle.append(copies.local(source, target))
    local_rows = copies.local(inputs, row_in.at[pos])

    flows = {
        "in": lambda origin: weight_in.at[origin, core],
        "owned": lambda origin: owned.at[origin, core, pos],
        "small": lambda origin: small.at[origin, core, pos],
        "bundle": lambda origin: bundle.at[origin],
    }

    def line_start(flow):
        block = flows[flow](z)
        copies.send((flow, "right", 1), block, block, right, has_right)
        copies.send((flow, "left", 1), block, block, left, has_left)

    def line_step(flow, distance, arrived=None):
        for side, origin, there, onward, has_next in (
            ("right", z - distance, z >= distance, right, has_right),
            ("left", z + distance, z + distance < rz_count, left, has_left),
        ):
            safe = jnp.clip(origin, 0, rz_count - 1)
            block = flows[flow](safe)

            def wait(block=block, side=side, onward=onward):
                copies.got((flow, side, distance), block, onward)

            pl.when(there)(wait)
            if distance + 1 < rz_count:
                copies.send((flow, side, distance + 1), block, block, onward, there & has_next)
            if arrived is not None:
                arrived(side, distance, safe, there)

    def share_in(side, distance, origin, there):
        block = weight_in.at[origin, core]
        copies.send(("in core", side, distance), block, block, other, there)

    for copy in local_in:
        copy.wait()
    for mask in range(1, pos_count):
        owner = jnp.bitwise_xor(pos, mask)
        for at in range(3):
            copies.got(
                ("in", mask, at),
                weight_in.at[z, core, owner, :, pl.ds(at * chan, chan)],
                {"pos": owner},
            )
    for lane in range(2):
        got_extra(lane, *lanes[lane][0])
    line_start("in")
    block = weight_in.at[z, core]
    copies.send(("in core", "own", 0), block, block, other)
    for copy in local_owned:
        copy.wait()
    line_start("owned")
    pack[...] = jnp.zeros_like(pack)
    row = 0
    for value in vectors:
        value = value[...].astype(F32)
        value = value.reshape(-1, value.shape[-1])
        pack[row : row + value.shape[0], : value.shape[1]] = value
        row += value.shape[0]
    small[z, core, pos] = pack[...].astype(BF16)
    line_start("small")
    for copy in local_bundle:
        copy.wait()
    for at in range(rz_count):
        copies.got(("up", at), bundle.at[z, (1 - core) * rz_count + at], other)
    line_start("bundle")

    def line_steps(distance):
        line_step("in", distance, share_in)
        line_step("owned", distance)
        line_step("small", distance)

    line_steps(1)

    def owned_half(side, origin, lane):
        part = pl.ds(lane * middle, middle)
        return (owned.at[part, side, origin], small.at[part, side, origin])

    def send_owned(lane, mask, bit):
        for at, block in enumerate(owned_half(core, jnp.bitwise_xor(pos, mask ^ bit), lane)):
            copies.send(
                ("owned pos", at, lane, mask), block, block, {"pos": jnp.bitwise_xor(pos, bit)}
            )

    def share_owned(lane, mask):
        for at, block in enumerate(owned_half(core, jnp.bitwise_xor(pos, mask), lane)):
            copies.send(("owned core", at, lane, mask), block, block, other)

    def got_rows(lane, mask, bit):
        block = row_in.at[jnp.bitwise_xor(pos, mask), :, lane_cols(lane)]
        copies.got(("rows", lane, mask), block, {"pos": jnp.bitwise_xor(pos, bit)})
        later = (bits, bits[::-1])[lane]
        for onward in later[later.index(bit) + 1 :]:
            send_rows(lane, mask ^ onward, onward)

    def got_owned(lane, mask, bit):
        for at, block in enumerate(owned_half(core, jnp.bitwise_xor(pos, mask), lane)):
            copies.got(("owned pos", at, lane, mask), block, {"pos": jnp.bitwise_xor(pos, bit)})
        later = (bits, bits[::-1])[lane]
        for onward in later[later.index(bit) + 1 :]:
            send_owned(lane, mask ^ onward, onward)
        share_owned(lane, mask)

    for lane in range(2):
        got_rows(lane, *lanes[lane][0])
    for distance in range(2, rz_count):
        line_steps(distance)
    for at in range(len(bits)):
        for lane in range(2):
            bit = (bits, bits[::-1])[lane][at]
            send_owned(lane, bit, bit)
    for lane in range(2):
        share_owned(lane, 0)
    for distance in range(1, rz_count - 1):
        line_step("bundle", distance)
    filter_layers(filter_in, layers, small_mine)
    for at in range(1, pos_count - 1):
        for lane in range(2):
            got_rows(lane, *lanes[lane][at])
            got_extra(lane, *lanes[lane][at])
    for at in range(pos_count - 1):
        for lane in range(2):
            got_owned(lane, *lanes[lane][at])
    line_step("bundle", rz_count - 1)
    local_rows.wait()
    for at in range(pos_count):
        for lane in range(2):
            for part, block in enumerate(
                owned_half(1 - core, jnp.bitwise_xor(pos, at), lane)
            ):
                copies.got(("owned core", part, lane, at), block, other)
    copies.got(("in core", "own", 0), weight_in.at[z, 1 - core], other)
    for distance in range(1, rz_count):
        for side, origin, there in (
            ("right", z - distance, z >= distance),
            ("left", z + distance, z + distance < rz_count),
        ):
            block = weight_in.at[jnp.clip(origin, 0, rz_count - 1), 1 - core]

            def wait(block=block, side=side, distance=distance):
                copies.got(("in core", side, distance), block, other)

            pl.when(there)(wait)

    per_group = 128 // own_width
    for group in range(model_width // 128):
        total = jnp.zeros((LINES, 128), F32)
        for at in range(per_group):
            owner = group * per_group + at
            value = small[
                owner // (2 * pos_count), owner // pos_count % 2, owner % pos_count
            ].astype(F32)
            value = jnp.where(
                lax.broadcasted_iota(jnp.int32, value.shape, 1) < own_width, value, 0.0
            )
            total += pltpu.roll(value, at * own_width, 1) if at else value
        lines[:, group * 128 : (group + 1) * 128] = total
    mine[...] = lines[:NORM_ROW, pl.ds(pl.multiple_of(pos * chan, chan), chan)]
    ff_own = down.shape[0]
    per_lanes = 128 // ff_own
    for at in range(rz_count):
        for group in range(pos_count // per_lanes):
            total = jnp.zeros((1, 128), F32)
            for part in range(per_lanes):
                value = small[at, core, group * per_lanes + part][UP_ROW : UP_ROW + 1]
                value = value.astype(F32)
                total += pltpu.roll(value, part * ff_own, 1) if part else value
            up_lines[at : at + 1, group * 128 : (group + 1) * 128] = total
    copies.finish()


def filter_layers(filter_in, layers, padded):
    embedding, w_one, w_two, columns = filter_in
    padded[...] = jnp.zeros_like(padded)
    padded[: w_one.shape[0], :] = w_one[...].astype(F32)
    frequency = columns[:, 2:3]
    sums = exact(padded[...], embedding[...], ((0,), (0,))) + columns[:, 0:1]
    layers[2] = sums
    layers[4] = jnp.cos(frequency * sums)
    layers[0] = jnp.sin(frequency * sums)
    sums = exact(w_two[...].astype(F32), layers[0], ((0,), (0,))) + columns[:, 1:2]
    layers[3] = sums
    layers[5] = jnp.cos(frequency * sums)
    layers[1] = jnp.sin(frequency * sums)


def gather(dims, inputs, weight, up, down, out, vectors, filter_in):
    rz_count, pos_count = dims
    part_len, model_width = inputs.shape
    own_width = out.shape[0]
    tile = pos_count * down.shape[0]
    down_units = down.shape[0] // own_width
    units = 2 * rz_count + down_units * (model_width // tile - 1)
    anywhere = pl.BlockSpec(memory_space=pl.ANY)
    locals_count = 3 + 1 + units + down_units + 1
    count = len(vectors)
    order, length = filter_in[2].shape[0], filter_in[0].shape[1]
    remote_count = (
        3 * (pos_count - 1)
        + 4 * (pos_count - 1)
        + rz_count
        + 4 * 2 * rz_count
        + 2 * rz_count
        + 2 * 2 * 2 * pos_count
    )

    def kernel(*refs):
        head, refs = refs[:5], refs[5:]
        gather_kernel(dims, *head, refs[:count], refs[count : count + 4], *refs[count + 4 :])

    return pl.pallas_call(
        kernel,
        out_shape=(
            jax.ShapeDtypeStruct((pos_count, part_len, model_width), BF16),
            jax.ShapeDtypeStruct(
                (rz_count, 2, pos_count, own_width, 3 * model_width // pos_count), BF16
            ),
            jax.ShapeDtypeStruct((rz_count, units, own_width, tile), BF16),
            jax.ShapeDtypeStruct((pos_count, down_units, own_width, tile), BF16),
            jax.ShapeDtypeStruct((rz_count, 2, pos_count, own_width, model_width), BF16),
            jax.ShapeDtypeStruct((LINES, model_width), F32),
            jax.ShapeDtypeStruct((NORM_ROW, model_width // pos_count), F32),
            jax.ShapeDtypeStruct((rz_count, tile), F32),
            jax.ShapeDtypeStruct((6, order, length), F32),
        ),
        in_specs=[pl.BlockSpec(memory_space=pltpu.VMEM)] * (5 + count + 4),
        out_specs=(anywhere,) * 5 + (pl.BlockSpec(memory_space=pltpu.VMEM),) * 4,
        scratch_shapes=[
            pltpu.VMEM((LINES, 128), F32),
            pltpu.VMEM((rz_count, 2, pos_count, LINES, 128), BF16),
            pltpu.VMEM((FEATURES, order), F32),
            pltpu.SemaphoreType.DMA((locals_count,)),
            pltpu.SemaphoreType.DMA((remote_count,)),
            pltpu.SemaphoreType.DMA((remote_count,)),
        ],
        compiler_params=pltpu.CompilerParams(
            collective_id=1, has_side_effects=True, vmem_limit_bytes=VMEM_LIMIT
        ),
        cost_estimate=pl.CostEstimate(flops=10**6, bytes_accessed=10**7, transcendentals=0),
        name="gather",
    )(inputs, weight, up, down, out, *vectors, *filter_in)


class LineSum:
    def __init__(self, copies, name, count, z, chunk, sent, got):
        self.copies, self.name, self.count, self.z = copies, name, count, z
        self.chunk, self.sent, self.got_ref = chunk, sent, got

    def sides(self):
        last = self.count - 1
        return (
            (0, self.z, 1, {"rz": self.z + 1}, {"rz": self.z - 1}),
            (1, last - self.z, -1, {"rz": self.z - 1}, {"rz": self.z + 1}),
        )

    def step(self, step):
        count = self.count
        for side, place, direction, onward, back in self.sides():
            sends = (place < step) & (place + 1 < count)
            at = count - step + place
            at = jnp.clip(at if direction == 1 else count - 1 - at, 0, count - 1)
            target = self.sent.at[side, step - 1]

            def first(at=at, side=side):
                self.sent[side, step - 1] = self.chunk(at).astype(BF16)

            def later(at=at, side=side, back=back):
                self.copies.got((self.name, side, step - 1), self.got_ref.at[side, step - 2], back)
                self.sent[side, step - 1] = (
                    self.chunk(at) + self.got_ref[side, step - 2].astype(F32)
                ).astype(BF16)

            pl.when(sends & (place == 0))(first)
            if step > 1:
                pl.when(sends & (place > 0))(later)
            self.copies.send(
                (self.name, side, step), target, self.got_ref.at[side, step - 1], onward, sends
            )

    def total(self, result):
        last = self.count - 1
        result[...] = self.chunk(self.z)
        for side, place, _, _, back in self.sides():

            def add(side=side, back=back):
                self.copies.got((self.name, side, last), self.got_ref.at[side, last - 1], back)
                result[...] += self.got_ref[side, last - 1].astype(F32)

            pl.when(place > 0)(add)


class PieceSum:
    def __init__(self, copies, name, pos, orders, piece, got):
        self.copies, self.name, self.pos, self.orders = copies, name, pos, orders
        self.piece, self.got_ref = piece, got

    def masks(self, side, stage):
        order = self.orders[side]
        found = [0]
        for bit in order[stage:]:
            found += [mask ^ bit for mask in found]
        return [mask for mask in found if mask & order[stage]]

    def device(self, side, stage):
        return {"pos": jnp.bitwise_xor(self.pos, self.orders[side][stage])}

    def send(self, side, stage, mask):
        self.copies.send(
            (self.name, side, mask),
            self.piece(side, mask),
            self.got_ref(side, mask),
            self.device(side, stage),
        )

    def got(self, side, stage, mask):
        self.copies.got(
            (self.name, side, mask), self.got_ref(side, mask), self.device(side, stage)
        )

    def add(self, side, stage, mask):
        target = self.piece(side, mask ^ self.orders[side][stage])
        target[...] = (
            target[...].astype(F32) + self.got_ref(side, mask)[...].astype(F32)
        ).astype(BF16)

    def settle(self, stage):
        for side in range(2):
            onward = self.masks(side, stage + 1) if stage + 1 < len(self.orders[side]) else []
            masks = self.masks(side, stage)
            bit = self.orders[side][stage]
            for mask in sorted(masks, key=lambda mask: (mask ^ bit) not in onward):
                self.got(side, stage, mask)
                self.add(side, stage, mask)
                if mask ^ bit in onward:
                    self.send(side, stage + 1, mask ^ bit)


class ChunkSum(PieceSum):
    def send_chunk(self, side, stage, mask, place):
        self.copies.send(
            (self.name, side, mask, place),
            self.piece(side, mask, place),
            self.got_ref(side, mask, place),
            self.device(side, stage),
        )

    def settle_chunk(self, side, stage, place):
        bit = self.orders[side][stage]
        onward = self.masks(side, stage + 1) if stage + 1 < len(self.orders[side]) else []
        for mask in sorted(self.masks(side, stage), key=lambda mask: (mask ^ bit) not in onward):
            got = self.got_ref(side, mask, place)
            self.copies.got((self.name, side, mask, place), got, self.device(side, stage))
            target = self.piece(side, mask ^ bit, place)
            target[...] = (target[...].astype(F32) + got[...].astype(F32)).astype(BF16)
            if mask ^ bit in onward:
                self.send_chunk(side, stage + 1, mask ^ bit, place)


def last_sums_kernel(
    dims,
    kept,
    row_in,
    proj_grad,
    weight_in,
    lines,
    grad_residual,
    token_lines,
    chan_sums,
    filt_grad,
    layers,
    mine,
    embedding,
    w_two,
    filter_columns,
    *rest,
):
    rz_count, pos_count = dims
    norm = lines.at[pl.ds(NORM_ROW, 8)]
    count = 2 * len(kept[0])
    own_pieces, moved_pieces, rest = rest[:count], rest[count : 2 * count], rest[2 * count :]
    input_grad, in_grad, up_grad, down_grad, out_grad, lines_out, inner_out = rest[:7]
    rest = rest[7:]
    (
        rows_v,
        proj_v,
        pieces_v,
        moved_v,
        pieces_got,
        bundle_sent,
        bundle_got,
        bundle_total,
        up_sent,
        up_got,
        e_v,
        e_got,
        in_total,
        in_sent,
        in_got,
        in_line_sent,
        in_line_got,
        in_mine,
        in_out,
        in_back,
        packed,
        packed_got,
        packed_pos,
        packed_total,
        inner,
        local_sems,
        send_sems,
        got_sems,
    ) = rest
    z, core, pos = lax.axis_index("rz"), lax.axis_index("core"), lax.axis_index("pos")
    rows_count = 2 * rz_count
    row = z * 2 + core
    bits = bits_of(pos_count)
    orders = (bits, bits[::-1])
    middle = rz_count // 2
    part_len, model_width = grad_residual.shape
    half = model_width // 2
    own_width, tile = up_sent.shape[1:]
    width = weight_in.shape[1]
    chan = width // 3
    columns = model_width // tile
    copies = Copies(local_sems, send_sems, got_sems)
    other = {"core": 1 - core}

    def row_device(at):
        return {"rz": at // 2, "core": at % 2}

    later = [[mask for mask in kept[side] if len(bits) > 1 and mask & orders[side][1]] for side in range(2)]
    loads = {}
    for first in (True, False):
        for side in range(2):
            for mask in kept[side]:
                if (mask in later[side]) == first:
                    slot = kept[side].index(mask)
                    at, part = 2 * slot + side, pl.ds(side * middle, middle)
                    loads[side, mask] = (
                        copies.local(own_pieces[at], pieces_v.at[slot, part]),
                        copies.local(moved_pieces[at], moved_v.at[slot, part]),
                    )
    masks = sorted(range(pos_count), key=lambda mask: -bin(mask).count("1"))
    slots = rows_v.shape[0]

    def load_rows(at):
        start = jnp.bitwise_xor(pos, masks[at]) * part_len
        block = pl.ds(pl.multiple_of(start, part_len), part_len)
        return (
            copies.local(row_in.at[block], rows_v.at[at % slots]),
            copies.local(proj_grad.at[block], proj_v.at[at % slots]),
        )

    row_loads = [load_rows(at) for at in range(slots)]
    greet(
        [row_device((row + step) % rows_count) for step in range(1, rows_count)]
        + [{"pos": jnp.bitwise_xor(pos, mask)} for mask in range(1, pos_count)]
    )

    bundle = ChunkSum(
        copies,
        "bundle",
        pos,
        orders,
        lambda side, mask, place: pieces_v.at[kept[side].index(mask), place],
        lambda side, mask, place: pieces_got.at[kept[side].index(mask) - 1, place],
    )
    for side, mask in loads:
        slot = kept[side].index(mask)
        for copy in loads[side, mask]:
            copy.wait()
        for at in range(middle):
            place = side * middle + (at if side == 0 else middle - 1 - at)
            pieces_v[slot, place] = (
                pieces_v[slot, place].astype(F32) + moved_v[slot, place].astype(F32)
            ).astype(BF16)
            if mask in later[side]:
                bundle.send_chunk(side, 1, mask, place)

    e_sums = PieceSum(
        copies,
        "rows",
        pos,
        orders,
        lambda side, mask: e_v.at[side, mask],
        lambda side, mask: e_got.at[side, mask - 1],
    )
    in_total[...] = jnp.zeros_like(in_total)
    packed_total[...] = jnp.zeros_like(packed_total)
    packed[...] = jnp.zeros_like(packed)
    sums = (jnp.zeros((1, model_width), F32), jnp.zeros((1, model_width), F32))
    for index, mask in enumerate(masks):
        if 1 <= index <= pos_count - slots:
            row_loads.append(load_rows(slots + index - 1))
        for copy in row_loads[index]:
            copy.wait()

        def tile_step(at, sums, mask=mask, slot=index % slots):
            rows = pl.ds(pl.multiple_of(at * BLOCK, BLOCK), BLOCK)
            unit, _ = norm_parts(rows_v[slot, rows].astype(F32))
            normed = (unit * norm[0:1, :] + norm[1:2, :]).astype(BF16)
            grad = proj_v[slot, rows]
            cotangent = lax.dot_general(
                grad, weight_in[...], (((1,), (1,)), ((), ())), preferred_element_type=F32
            )
            e_v[0, mask, rows] = cotangent[:, :half].astype(BF16)
            e_v[1, mask, rows] = cotangent[:, half:].astype(BF16)
            in_total[...] += lax.dot_general(
                normed, grad, (((0,), (0,)), ((), ())), preferred_element_type=F32
            )
            return (
                sums[0] + jnp.sum(cotangent * unit, axis=0, keepdims=True),
                sums[1] + jnp.sum(cotangent, axis=0, keepdims=True),
            )

        sums = lax.fori_loop(0, part_len // BLOCK, tile_step, sums)
        for side in range(2):
            if mask in e_sums.masks(side, 0):
                e_sums.send(side, 0, mask)

    block_rows = pos_count * own_width
    for at in range(rz_count):
        rows = pl.ds(pl.multiple_of((2 * at + 1 - core) * block_rows, block_rows), block_rows)
        in_sent[at] = in_total[rows, :].astype(BF16)
    copies.send(("in core",), in_sent, in_got, other)

    groups = model_width // 128
    per = rows_count // groups
    token_rows, chan_rows = token_lines.shape[0], mine.shape[0]
    inner_rows = inner.shape[0] // groups
    line_rows = token_rows + chan_rows
    three_grad = filter_back(
        filt_grad, layers, mine[THREE_ROW:NORM_ROW, :], embedding, w_two, filter_columns, inner
    )
    for at in range(groups):
        lanes = pl.ds(at * 128, 128)
        packed[at, 0:token_rows] = token_lines[:, lanes]
        packed[at, 0:1] = sums[0][:, at * 128 : (at + 1) * 128]
        packed[at, 1:2] = sums[1][:, at * 128 : (at + 1) * 128]
        packed[at, line_rows:] = inner[pl.ds(at * inner_rows, inner_rows), :]
    for at in range(chan // 128):
        group, lanes = pos * (chan // 128) + at, pl.ds(at * 128, 128)
        packed[group, token_rows : token_rows + THREE_ROW] = chan_sums[:, lanes]
        packed[group, token_rows + THREE_ROW : line_rows] = three_grad[
            :, at * 128 : (at + 1) * 128
        ]

    def owns(at):
        return None if per == 1 else at % per == 0

    def when(condition, action):
        if condition is None:
            action()
        else:
            pl.when(condition)(action)

    for step in range(1, rows_count):
        to = (row + step) % rows_count
        copies.send(
            ("lines", step), packed.at[to // per], packed_got.at[step], row_device(to), owns(to)
        )

    bundle_line = LineSum(
        copies,
        "bundle line",
        rz_count,
        z,
        lambda at: pieces_v[kept[0].index(0), at].astype(F32),
        bundle_sent,
        bundle_got,
    )
    for at in range(middle):
        for stage in range(1, len(bits)):
            bundle.settle_chunk(0, stage, at)
            bundle.settle_chunk(1, stage, rz_count - 1 - at)
        if at == 0:
            bundle_line.step(1)
    copies.got(("in core",), in_got, other)

    def in_chunk(at):
        rows = pl.ds(pl.multiple_of((2 * at + core) * block_rows, block_rows), block_rows)
        return in_total[rows, :] + in_got[at].astype(F32)

    in_line = LineSum(copies, "in line", rz_count, z, in_chunk, in_line_sent, in_line_got)
    in_line.step(1)

    def add_lines():
        packed_total[...] = packed[row // per]
        for step in range(1, rows_count):
            copies.got(("lines", step), packed_got.at[step], row_device((row - step) % rows_count))
            packed_total[...] += packed_got[step]
        packed_pos[pos] = packed_total[...]

    when(owns(row), add_lines)
    for mask in range(1, pos_count):
        copies.send(
            ("lines pos", mask),
            packed_total,
            packed_pos.at[pos],
            {"pos": jnp.bitwise_xor(pos, mask)},
            owns(row),
        )
    for step in range(2, rz_count):
        bundle_line.step(step)
        in_line.step(step)
    e_sums.settle(0)

    def sum_lines():
        for mask in range(1, pos_count):
            owner = jnp.bitwise_xor(pos, mask)
            copies.got(("lines pos", mask), packed_pos.at[owner], {"pos": owner})
        total = packed_pos[0]
        for at in range(1, pos_count):
            total = total + packed_pos[at]
        lines_out[...] = total[:line_rows]
        inner_out[row // per] = total[line_rows:]

    when(owns(row), sum_lines)
    for step in range(1, rows_count):
        to = (row + step) % rows_count
        block = inner_out.at[row // per]
        copies.send(("inner", step), block, block, row_device(to), owns(row))
        if step < per:
            copies.send(
                ("lines row", step),
                lines_out,
                lines_out,
                row_device(to),
                owns(row),
            )

    in_line.total(in_mine)
    for mask in range(1, pos_count):
        owner = jnp.bitwise_xor(pos, mask)
        rows = pl.ds(pl.multiple_of(owner * own_width, own_width), own_width)
        in_out[mask] = in_mine[rows, :].astype(BF16)
        copies.send(("in pos", mask), in_out.at[mask], in_back.at[mask], {"pos": owner})
    mine = in_mine[pl.ds(pl.multiple_of(pos * own_width, own_width), own_width), :]
    cols = pl.ds(pl.multiple_of(pos * chan, chan), chan)
    for at in range(3):
        in_grad[at, :, cols] = mine[:, at * chan : (at + 1) * chan]

    bundle_line.total(bundle_total)
    up_sent[...] = bundle_total[
        pl.ds(pl.multiple_of((1 - core) * rz_count, rz_count), rz_count)
    ].astype(BF16)
    copies.send(("up core",), up_sent, up_got, other)
    down_units = (bundle_total.shape[0] - 2 * rz_count - columns) // columns
    for col in range(columns):
        out_grad[:, col * tile : (col + 1) * tile] = bundle_total[
            2 * rz_count + columns * down_units + col
        ]
        for at in range(down_units):
            down_grad[at * own_width : (at + 1) * own_width, col * tile : (col + 1) * tile] = (
                bundle_total[2 * rz_count + col * down_units + at]
            )
    for at in range(rz_count):
        cols = pl.ds(pl.multiple_of((2 * at + core) * tile, tile), tile)
        up_grad[:, cols] = bundle_total[core * rz_count + at]
    for stage in range(1, len(bits)):
        e_sums.settle(stage)
    def input_step(at, _):
        rows = pl.ds(pl.multiple_of(at * BLOCK, BLOCK), BLOCK)
        unit, scale = norm_parts(rows_v[(pos_count - 1) % slots, rows].astype(F32))
        cotangent = jnp.concatenate(
            [e_v[0, 0, rows].astype(F32), e_v[1, 0, rows].astype(F32)], axis=1
        )
        scaled = cotangent * norm[0:1, :]
        grad = scale * (
            scaled
            - jnp.mean(scaled, axis=-1, keepdims=True)
            - unit * jnp.mean(scaled * unit, axis=-1, keepdims=True)
        )
        input_grad[rows, :] = (grad_residual[rows, :] + grad).astype(BF16)
        return 0

    lax.fori_loop(0, part_len // BLOCK, input_step, 0)

    for mask in range(1, pos_count):
        owner = jnp.bitwise_xor(pos, mask)
        copies.got(("in pos", mask), in_back.at[mask], {"pos": owner})
        cols = pl.ds(pl.multiple_of(owner * chan, chan), chan)
        for at in range(3):
            in_grad[at, :, cols] = in_back[mask, :, at * chan : (at + 1) * chan].astype(F32)
    copies.got(("up core",), up_got, other)
    for at in range(rz_count):
        cols = pl.ds(pl.multiple_of((2 * at + 1 - core) * tile, tile), tile)
        up_grad[:, cols] = up_got[at].astype(F32)
    for step in range(1, rows_count):
        origin = (row - step) % rows_count

        def take(step=step, origin=origin):
            copies.got(("inner", step), inner_out.at[origin // per], row_device(origin))

        when(owns(origin), take)
        if step < per:

            def take_lines(step=step, origin=origin):
                copies.got(("lines row", step), lines_out, row_device(origin))

            when(origin == row // per * per, take_lines)
    copies.finish()


def filter_back(filt_grad, layers, three, embedding, w_two, columns, inner):
    frequency = columns[:, 2:3]
    three_grad = exact(layers[1], filt_grad[...], ((1,), (0,)))
    grad = exact(three, filt_grad[...], ((1,), (1,))) * layers[5]
    freq_grad = jnp.sum(grad * layers[3], axis=1, keepdims=True)
    grad = grad * frequency
    bias_two = jnp.sum(grad, axis=1, keepdims=True)
    order = grad.shape[0]
    inner[...] = jnp.zeros_like(inner)
    inner[FEATURES : FEATURES + order, :order] = exact(layers[0], grad, ((1,), (1,)))
    grad = exact(w_two[...].astype(F32), grad, ((1,), (0,))) * layers[4]
    freq_grad += jnp.sum(grad * layers[2], axis=1, keepdims=True)
    grad = grad * frequency
    bias_one = jnp.sum(grad, axis=1, keepdims=True)
    inner[:FEATURES, :order] = exact(embedding[...], grad, ((1,), (1,)))
    held = inner[:order, :]
    lane = lax.broadcasted_iota(jnp.int32, held.shape, 1)
    for at, value in enumerate((bias_one, bias_two, freq_grad)):
        held = jnp.where(lane == order + at, value, held)
    inner[:order, :] = held
    return three_grad


def finish_kernel(place, total, shared, *outs):
    own_width = outs[0].shape[1]
    moved = pltpu.roll(total[...], 128 - place[0], 1)[:, :own_width]
    (
        pre_gain,
        pre_bias,
        out_bias,
        post_gain,
        post_bias,
        down_bias,
        short_weight,
        short_bias,
        in_bias,
        skip,
        three,
        up_bias,
        w_one,
        b_one,
        w_two,
        b_two,
        frequency,
    ) = outs
    for at, out in enumerate((pre_gain, pre_bias, out_bias, post_gain, post_bias, down_bias)):
        out[...] = moved[at : at + 1]
    for at in range(3):
        short_weight[at] = moved[16 + 3 * at : 19 + 3 * at]
    short_bias[...] = moved[25:28]
    in_bias[...] = moved[28:31]
    skip[...] = moved[31:32]
    three[...] = moved[32:96]
    rows = pltpu.roll(total[0:16, :], 128 - place[2], 1)[:, : up_bias.shape[1]]
    line = lax.broadcasted_iota(jnp.int32, rows.shape, 0)
    up_bias[...] = jnp.sum(jnp.where(line == 6 + place[1], rows, 0.0), axis=0, keepdims=True)
    inner = shared[...].reshape(-1, 128)
    order = w_two.shape[0]
    w_one[...] = inner[: w_one.shape[0], :order]
    w_two[...] = inner[FEATURES : FEATURES + order, :order]
    turned = inner[:128, :].T
    b_one[...] = turned[order : order + 1, :order]
    b_two[...] = turned[order + 1 : order + 2, :order]
    frequency[...] = turned[order + 2 : order + 3, :order]


def finish(place, total, shared, own_width, ff_own, features, order):
    shapes = [(1, own_width)] * 6
    shapes += [(3, 3, own_width), (3, own_width), (3, own_width), (1, own_width)]
    shapes += [(order, own_width), (1, ff_own), (features, order), (1, order), (order, order)]
    shapes += [(1, order), (1, order)]
    inside = pl.BlockSpec(memory_space=pltpu.VMEM)
    return pl.pallas_call(
        finish_kernel,
        out_shape=[jax.ShapeDtypeStruct(shape, F32) for shape in shapes],
        in_specs=[pl.BlockSpec(memory_space=pltpu.SMEM), inside, inside],
        out_specs=[inside] * len(shapes),
        name="finish",
    )(place, total, shared)


def last_sums(
    dims,
    kept,
    row_in,
    proj_grad,
    weight_in,
    lines,
    grad_residual,
    token_lines,
    chan_sums,
    filt_grad,
    layers,
    mine,
    embedding,
    w_two,
    filter_columns,
    own_pieces,
    moved_pieces,
):
    rz_count, pos_count = dims
    part_len, model_width = grad_residual.shape
    piece = own_pieces[0].shape
    units, own_width, tile = piece[1:]
    width = weight_in.shape[1]
    block_rows = pos_count * own_width
    groups = model_width // 128
    line_rows = token_lines.shape[0] + mine.shape[0]
    inner_rows = 2 * FEATURES // groups
    slots = len(kept[0])
    steps = rz_count - 1
    rows_count = 2 * rz_count
    ff_own = (units - 2 * rz_count - model_width // tile) * own_width * tile // model_width
    anywhere = pl.BlockSpec(memory_space=pl.ANY)
    inside = pl.BlockSpec(memory_space=pltpu.VMEM)
    local_count = 4 * len(kept[0]) + 2 * pos_count
    remote_count = (
        2 * pos_count * (1 + rz_count) + 2 * 2 * steps + 2 + 3 * rows_count + 3 * pos_count
    )
    half = model_width // 2
    vmem = pltpu.VMEM
    return pl.pallas_call(
        functools.partial(last_sums_kernel, dims, kept),
        out_shape=(
            jax.ShapeDtypeStruct((part_len, model_width), BF16),
            jax.ShapeDtypeStruct((3, own_width, model_width), F32),
            jax.ShapeDtypeStruct((own_width, 2 * rz_count * tile), F32),
            jax.ShapeDtypeStruct((ff_own, model_width), F32),
            jax.ShapeDtypeStruct((own_width, model_width), F32),
            jax.ShapeDtypeStruct((line_rows, 128), F32),
            jax.ShapeDtypeStruct((groups, inner_rows, 128), F32),
        ),
        in_specs=[anywhere, anywhere] + [inside] * 11 + [anywhere] * (2 * len(own_pieces)),
        out_specs=(inside,) * 7,
        scratch_shapes=[
            vmem((pos_count - 1, part_len, model_width), BF16),
            vmem((pos_count - 1, part_len, width), BF16),
            vmem((slots, rz_count, units, own_width, tile), BF16),
            vmem((slots, rz_count, units, own_width, tile), BF16),
            vmem((slots - 1, rz_count, units, own_width, tile), BF16),
            vmem((2, steps, units, own_width, tile), BF16),
            vmem((2, steps, units, own_width, tile), BF16),
            vmem((units, own_width, tile), F32),
            vmem((rz_count, own_width, tile), BF16),
            vmem((rz_count, own_width, tile), BF16),
            vmem((2, pos_count, part_len, half), BF16),
            vmem((2, pos_count - 1, part_len, half), BF16),
            vmem((model_width, width), F32),
            vmem((rz_count, block_rows, width), BF16),
            vmem((rz_count, block_rows, width), BF16),
            vmem((2, steps, block_rows, width), BF16),
            vmem((2, steps, block_rows, width), BF16),
            vmem((block_rows, width), F32),
            vmem((pos_count, own_width, width), BF16),
            vmem((pos_count, own_width, width), BF16),
            vmem((groups, line_rows + inner_rows, 128), F32),
            vmem((rows_count, line_rows + inner_rows, 128), F32),
            vmem((pos_count, line_rows + inner_rows, 128), F32),
            vmem((line_rows + inner_rows, 128), F32),
            vmem((2 * FEATURES, 128), F32),
            pltpu.SemaphoreType.DMA((local_count,)),
            pltpu.SemaphoreType.DMA((remote_count,)),
            pltpu.SemaphoreType.DMA((remote_count,)),
        ],
        compiler_params=pltpu.CompilerParams(
            collective_id=0, has_side_effects=True, vmem_limit_bytes=VMEM_LIMIT
        ),
        cost_estimate=pl.CostEstimate(flops=10**7, bytes_accessed=10**7, transcendentals=0),
        name="last_sums",
    )(
        row_in,
        proj_grad,
        weight_in,
        lines,
        grad_residual,
        token_lines,
        chan_sums,
        filt_grad,
        layers,
        mine,
        embedding,
        w_two,
        filter_columns,
        *own_pieces,
        *moved_pieces,
    )


def bits_of(count):
    return [1 << at for at in range(count.bit_length() - 1)]


def on_device(
    activations,
    out_grad,
    doc_bounds,
    doc_ids,
    pre_gain,
    pre_bias,
    in_weight,
    in_bias,
    short_weight,
    short_bias,
    skip_gain,
    out_weight,
    out_bias,
    post_gain,
    post_bias,
    up_weight,
    up_bias,
    down_weight,
    down_bias,
    filter_one,
    filter_bias_one,
    filter_two,
    filter_bias_two,
    filter_freq,
    filter_three,
):
    rz_count, pos_count = lax.axis_size("rz"), lax.axis_size("pos")
    pos, core = lax.axis_index("pos"), lax.axis_index("core")
    everything = ("rz", "core", "pos")
    owners = rz_count * 2 * pos_count
    own_at = (lax.axis_index("rz") * 2 + core) * pos_count + pos
    part_len, model_width = activations.shape[1:]
    length = part_len * pos_count
    own_width = pre_gain.shape[0]
    chan = model_width // pos_count
    ff_own = down_weight.shape[0]
    ff_half = rz_count * pos_count * ff_own
    docs = doc_bounds.shape[1]
    order = filter_two.shape[0]
    tables = transform_tables()
    meta = unit_table(doc_bounds[0], length, (pos * chan).astype(jnp.int32))

    single = functools.partial(jnp.reshape, shape=(1, -1))
    vectors = [
        short_weight,
        short_bias,
        single(skip_gain),
        in_bias,
        filter_three,
        single(pre_gain),
        single(pre_bias),
        single(out_bias),
        single(post_gain),
        single(post_bias),
        single(down_bias),
        single(up_bias),
    ]
    filter_columns = jnp.stack([filter_bias_one, filter_bias_two, filter_freq], 1).astype(F32)
    embedding = positions_table(length, filter_one.shape[0])
    row_in, weight_in, bundle, extra, out_all, lines, mine, up_bias_half, layers = gather(
        (rz_count, pos_count),
        activations[0],
        in_weight.transpose(1, 0, 2),
        up_weight,
        down_weight,
        out_weight,
        vectors,
        (embedding, filter_one, filter_two, filter_columns),
    )
    row_in = row_in.reshape(length, model_width)
    weight_in = weight_in.reshape(model_width, -1)
    out_all = out_all.reshape(model_width, model_width)
    tile = pos_count * ff_own
    columns = model_width // tile
    bits = bits_of(pos_count)
    orders = (bits, bits[::-1])
    place = jnp.stack([pos, lax.axis_index("rz")]).astype(jnp.int32)

    own_in = activations[0]
    projected = project(row_in, lines, weight_in, mine)
    sides = [{0: bundle[: rz_count // 2]}, {0: bundle[rz_count // 2 :]}]
    firsts = [[swap(sides[side][0], "pos", bit) for bit in bits] for side in range(2)]

    def along(values, distance):
        ups = [(at, at + 1) for at in range(distance - 1, rz_count - 1)]
        downs = [(at + 1, at) for at in range(rz_count - distance)]
        return [lax.ppermute(values[0], "rz", ups), lax.ppermute(values[1], "rz", downs)]

    moved = [along([extra, extra], 1)]
    projected, moved = lax.optimization_barrier((projected, moved))
    for distance in range(2, rz_count - 1):
        moved.append(along(moved[-1], distance))
    branch, mixed = mixer_forward(meta, docs, projected, layers, mine, model_width, tables)
    branch, firsts, moved = lax.optimization_barrier((branch, firsts, moved))
    extras = [extra] + [pair[0] for pair in moved] + [pair[1] for pair in moved]
    given = [0] + bits
    pieces = [
        sides[side][0] if bit == 0 else firsts[side][bits.index(bit)]
        for bit in given
        for side in range(2)
    ]
    result, grad_residual, branch_grad, token_lines, *piece_grads = middle(
        (rz_count, pos_count),
        given,
        branch,
        activations[0],
        out_all,
        lines,
        out_grad[0],
        up_bias_half,
        pieces,
        extras,
    )
    result = result[None]

    masks = list(range(pos_count))
    kept = [[mask for mask in masks if not mask & orders[side][0]] for side in range(2)]
    by_mask = {
        (side, mask): piece_grads[2 * at + side]
        for at, mask in enumerate(masks)
        for side in range(2)
    }
    own_pieces = [by_mask[side, kept[side][at]] for at in range(len(kept[0])) for side in range(2)]
    moved_pieces = [
        swap(by_mask[side, kept[side][at] ^ orders[side][0]], "pos", orders[side][0])
        for at in range(len(kept[0]))
        for side in range(2)
    ]

    proj_grad, filt_grad, chan_sums = mixer_backward(
        meta, docs, projected, layers, mine, model_width, tables, mixed, branch_grad
    )
    input_grad, weight_in_grad, up_weight_grad, down_weight_grad, out_weight_grad, total, shared = (
        last_sums(
            (rz_count, pos_count),
            kept,
            row_in,
            proj_grad,
            weight_in,
            lines,
            grad_residual,
            token_lines,
            chan_sums,
            filt_grad,
            layers,
            mine,
            embedding,
            filter_two,
            filter_columns,
            own_pieces,
            moved_pieces,
        )
    )
    input_grad = input_grad[None]
    weight_in_grad = weight_in_grad.transpose(1, 0, 2)
    lane = lax.rem(own_at * own_width, 128)
    up_place = lax.rem(own_at * ff_own, owners * ff_own * 128 // model_width)
    place = jnp.stack([lane, up_place // 128, up_place % 128]).astype(jnp.int32)
    (
        pre_gain_grad,
        pre_bias_grad,
        out_bias_grad,
        post_gain_grad,
        post_bias_grad,
        down_bias_grad,
        short_weight_grad,
        short_bias_grad,
        in_bias_grad,
        skip_grad,
        three_grad,
        up_bias_grad,
        one_grad,
        bias_one_grad,
        two_grad,
        bias_two_grad,
        freq_grad,
    ) = finish(place, total, shared, own_width, ff_own, filter_one.shape[0], order)
    return (
        result,
        input_grad,
        pre_gain_grad[0],
        pre_bias_grad[0],
        weight_in_grad,
        in_bias_grad,
        short_weight_grad,
        short_bias_grad,
        skip_grad[0],
        out_weight_grad,
        out_bias_grad[0],
        post_gain_grad[0],
        post_bias_grad[0],
        up_weight_grad,
        up_bias_grad[0],
        down_weight_grad,
        down_bias_grad[0],
        one_grad,
        bias_one_grad[0],
        two_grad,
        bias_two_grad[0],
        freq_grad[0],
        three_grad,
    )


def solution(mesh):
    rows_count, pos_count = mesh.devices.shape
    fine = Mesh(mesh.devices.reshape(rows_count // 2, 2, pos_count), ("rz", "core", "pos"))
    rows = ("rz", "core")
    every = ("rz", "core", "pos")
    tokens = P(rows, "pos", None)
    vector = P(every)
    matrix = P(every, None)
    return jax.shard_map(
        on_device,
        mesh=fine,
        in_specs=(
            tokens,
            tokens,
            P(rows, None),
            P(rows, None),
            vector,
            vector,
            P(every, None, None),
            P(None, every),
            P(None, None, every),
            P(None, every),
            vector,
            matrix,
            vector,
            vector,
            vector,
            matrix,
            vector,
            matrix,
            vector,
            P(),
            P(),
            P(),
            P(),
            P(),
            P(None, every),
        ),
        out_specs=(
            tokens,
            tokens,
            vector,
            vector,
            P(every, None, None),
            P(None, every),
            P(None, None, every),
            P(None, every),
            vector,
            matrix,
            vector,
            vector,
            vector,
            matrix,
            vector,
            matrix,
            vector,
            P(),
            P(),
            P(),
            P(),
            P(),
            P(None, every),
        ),
        check_vma=False,
    )
```

```python
import functools
import math

import jax
import jax.numpy as jnp
import ml_dtypes
import numpy as np
from jax import lax
from jax.experimental import pallas as pl
from jax.experimental.pallas import tpu as pltpu
from jax.sharding import Mesh
from jax.sharding import PartitionSpec as P

HIGHEST = lax.Precision.HIGHEST
F32 = jnp.float32
BF16 = jnp.bfloat16
BLOCK = 256
FREQ_CHUNK = 64
VMEM_LIMIT = 60 * 1024 * 1024


def layer_norm(values, norm_gain, norm_shift):
    centre = values - jnp.mean(values, axis=-1, keepdims=True)
    spread = jnp.mean(centre * centre, axis=-1, keepdims=True)
    return centre * lax.rsqrt(spread + 1e-05) * norm_gain + norm_shift


FEATURES = 64
THREE_ROW, NORM_ROW, UP_ROW, LINES = 16, 80, 86, 96


def positions_table(length, features):
    band_count = (features - 1) // 2
    places = np.arange(length, dtype=np.float64)
    ladder = 0.0001 + (band_count - 1 - 0.0001) * np.arange(band_count) / (band_count - 1)
    angles = 2.0 * math.pi / length * places[:, None] * ladder[None, :]
    table = np.zeros((FEATURES, length), np.float32)
    table[0] = places / (length - 1)
    table[1 : 1 + band_count] = np.cos(angles).T
    table[1 + band_count : features] = -np.sin(angles).T
    return jnp.asarray(table)


def decay_of(block, length, first_channel, model_width, width):
    place = lax.broadcasted_iota(jnp.int32, (BLOCK, width), 0) + block * BLOCK
    channel = lax.broadcasted_iota(jnp.int32, (BLOCK, width), 1) + first_channel
    slow_rate = math.log(0.01) / 1.5
    fast_rate = math.log(0.01) / 0.3
    rates = jnp.abs(
        slow_rate + (fast_rate - slow_rate) * channel.astype(F32) * (1.0 / (model_width - 1))
    )
    return jnp.exp(-(place.astype(F32) * (1.0 / (length - 1))) * rates) + 0.05


def exact(left, right, contract):
    return lax.dot_general(
        left, right, (contract, ((), ())), precision=HIGHEST, preferred_element_type=F32
    )


def filter_block(layers, lines, block, units, length, width, model_width):
    layer_two = layers[0, :, rows_of(block)]
    three = lines[THREE_ROW : THREE_ROW + layer_two.shape[0], :].astype(BF16)
    decay = decay_of(block, length, units.channel(), model_width, width)
    high = layer_two.astype(BF16)
    low = (layer_two - high.astype(F32)).astype(BF16)
    filt = lax.dot_general(
        jnp.concatenate([high, low], axis=0),
        jnp.concatenate([three, three], axis=0),
        (((0,), (0,)), ((), ())),
        preferred_element_type=F32,
    )
    return filt, decay


def transform_tables():
    order = np.concatenate([np.arange(0, BLOCK, 2), np.arange(1, BLOCK, 2)])
    angle = math.pi / BLOCK * (order[:, None] + 0.5) * np.arange(BLOCK)[None, :]
    forward = np.concatenate([np.cos(angle), -np.sin(angle)], axis=0)
    tables = []
    for table in (forward, forward.T / BLOCK):
        high = table.astype(ml_dtypes.bfloat16)
        low = (table - high.astype(np.float64)).astype(ml_dtypes.bfloat16)
        tables.append(jnp.asarray(high))
    return tables


def unit_table(bounds, length, first_channel):
    docs = bounds.shape[0]
    units = length // BLOCK + docs - 1
    ends = jnp.concatenate([bounds[1:], jnp.full((1,), length, jnp.int32)])
    first = bounds // BLOCK
    count = jnp.where(ends > bounds, (ends - 1) // BLOCK - first + 1, 0)
    earlier = jnp.arange(docs)[:, None] >= jnp.arange(docs)[None, :]
    stops = jnp.sum(jnp.where(earlier, count[None, :], 0), axis=1)
    starts = stops - count
    unit = jnp.arange(units, dtype=jnp.int32)
    doc = jnp.sum((unit[:, None] >= stops[None, :]).astype(jnp.int32), axis=1)
    doc = jnp.minimum(doc, docs - 1)
    pick = (doc[:, None] == jnp.arange(docs)[None, :]).astype(jnp.int32)

    def of_doc(values):
        return jnp.sum(pick * values[None, :], axis=1)

    block = jnp.clip(of_doc(first - starts) + unit, 0, length // BLOCK - 1)
    return jnp.concatenate(
        [
            block,
            of_doc(bounds),
            of_doc(ends),
            of_doc(starts),
            of_doc(stops),
            starts,
            stops,
            bounds,
            stops[docs - 1 :],
            jnp.reshape(first_channel, (1,)),
        ]
    ).astype(jnp.int32)


class Units:
    def __init__(self, meta, length, docs):
        self.meta = meta
        self.docs = docs
        self.units = length // BLOCK + docs - 1

    def block(self, unit):
        return self.meta[unit]

    def low(self, unit):
        return self.meta[self.units + unit]

    def high(self, unit):
        return self.meta[2 * self.units + unit]

    def start(self, unit):
        return self.meta[3 * self.units + unit]

    def stop(self, unit):
        return self.meta[4 * self.units + unit]

    def doc_start(self, doc):
        return self.meta[5 * self.units + doc]

    def doc_stop(self, doc):
        return self.meta[5 * self.units + self.docs + doc]

    def bound(self, doc):
        return self.meta[5 * self.units + 2 * self.docs + doc]

    def total(self):
        return self.meta[5 * self.units + 3 * self.docs]

    def channel(self):
        return self.meta[5 * self.units + 3 * self.docs + 1]

    def inside(self, unit, width):
        place = lax.broadcasted_iota(jnp.int32, (BLOCK, width), 0) + self.block(unit) * BLOCK
        return (place >= self.low(unit)) & (place < self.high(unit))


def rows_of(block):
    return pl.ds(pl.multiple_of(block * BLOCK, BLOCK), BLOCK)


def times(table, value):
    high = value.astype(BF16)
    low = (value - high.astype(F32)).astype(BF16)
    return jnp.dot(
        table[...], high, preferred_element_type=F32
    )


def tap_masks(units, block, width, ahead=0):
    place = lax.broadcasted_iota(jnp.int32, (BLOCK, width), 0) + (block * BLOCK + ahead)
    first = place == units.bound(0)
    second = place == units.bound(0) + 1
    for doc in range(1, units.docs):
        first = first | (place == units.bound(doc))
        second = second | (place == units.bound(doc) + 1)
    return jnp.logical_not(first), jnp.logical_not(first | second)


def delayed(ref, block):
    start = block * BLOCK
    here = ref[rows_of(block), :].astype(F32)
    before = ref[pl.ds(pl.multiple_of(jnp.maximum(start - 16, 0), 16), 16), :].astype(F32)
    joined = jnp.concatenate([before, here], axis=0)
    return (here, pltpu.roll(joined, 1, 0)[16:], pltpu.roll(joined, 2, 0)[16:])


def short_conv(parts, small, branch, masks):
    total = small[9 + branch : 10 + branch, :] + small[branch : branch + 1, :] * parts[0]
    total += jnp.where(masks[0], small[3 + branch : 4 + branch, :] * parts[1], 0.0)
    total += jnp.where(masks[1], small[6 + branch : 7 + branch, :] * parts[2], 0.0)
    return total


def mixer_forward_kernel(
    docs, model_width, meta, post, pre, val, layers, small, fwd, inv, branch, mixed, gated, spec, taps, prod
):
    length, width = gated.shape
    blocks = length // BLOCK
    units = Units(meta, length, docs)

    def gate(block, _):
        masks = tap_masks(units, block, width)
        part = short_conv(delayed(val, block), small, 2, masks)
        part *= short_conv(delayed(pre, block), small, 1, masks)
        gated[rows_of(block), :] = part
        mixed[rows_of(block), :] = small[12:13, :] * part
        filt, decay = filter_block(layers, small, block, units, length, width, model_width)
        taps[block] = times(fwd, filt * decay)
        return 0

    lax.fori_loop(0, blocks, gate, 0)

    def transform(unit, _):
        value = gated[rows_of(units.block(unit)), :]
        spec[unit] = times(fwd, jnp.where(units.inside(unit, width), value, 0.0))
        return 0

    lax.fori_loop(0, units.total(), transform, 0)

    def multiply(unit, _):
        for low in range(0, BLOCK, FREQ_CHUNK):
            re, im = pl.ds(low, FREQ_CHUNK), pl.ds(BLOCK + low, FREQ_CHUNK)

            def step(back, total):
                at = unit - back
                s_re, s_im, t_re, t_im = spec[at, re], spec[at, im], taps[back, re], taps[back, im]
                return (
                    total[0] + (s_re * t_re - s_im * t_im),
                    total[1] + (s_re * t_im + s_im * t_re),
                )

            zero = jnp.zeros((FREQ_CHUNK, width), F32)
            total = lax.fori_loop(0, unit - units.start(unit) + 1, step, (zero, zero))
            prod[unit, re] = total[0]
            prod[unit, im] = total[1]
        return 0

    lax.fori_loop(0, units.total(), multiply, 0)

    half = BLOCK // 2

    def bring_back(unit, _):
        last = jnp.maximum(unit - 1, 0)
        old = jnp.where(unit > units.start(unit), prod[last], 0.0)
        new = prod[unit]
        joined = jnp.concatenate(
            [
                new[:half] - old[BLOCK : BLOCK + half],
                new[half:BLOCK] + old[BLOCK + half :],
                new[BLOCK : BLOCK + half] + old[:half],
                new[BLOCK + half :] - old[half:BLOCK],
            ],
            axis=0,
        )
        value = times(inv, joined)
        rows = rows_of(units.block(unit))
        mixed[rows, :] += jnp.where(units.inside(unit, width), value, 0.0)
        return 0

    lax.fori_loop(0, units.total(), bring_back, 0)

    def finish(block, _):
        masks = tap_masks(units, block, width)
        gate_value = short_conv(delayed(post, block), small, 0, masks)
        branch[rows_of(block), :] = (gate_value * mixed[rows_of(block), :]).astype(BF16)
        return 0

    lax.fori_loop(0, blocks, finish, 0)


def mixer_backward_kernel(
    docs,
    model_width,
    meta,
    post,
    pre,
    val,
    layers,
    small,
    fwd,
    inv,
    mixed,
    branch_grad,
    proj_grad,
    filt_grad,
    sums,
    gated,
    gm,
    conv_grad,
    spec,
    taps,
    prod,
):
    length, width = gated.shape
    blocks = length // BLOCK
    units = Units(meta, length, docs)
    half = BLOCK // 2
    sums[...] = jnp.zeros_like(sums)

    def total_rows(value):
        return jnp.sum(value, axis=0, keepdims=True)

    def gate(block, _):
        rows = rows_of(block)
        masks = tap_masks(units, block, width)
        part = short_conv(delayed(val, block), small, 2, masks)
        part *= short_conv(delayed(pre, block), small, 1, masks)
        gated[rows, :] = part
        grad = branch_grad[rows, :].astype(F32)
        mix_grad = grad * short_conv(delayed(post, block), small, 0, masks)
        gm[rows, :] = mix_grad
        conv_grad[0, rows, :] = grad * mixed[rows, :]
        conv_grad[1, rows, :] = small[12:13, :] * mix_grad
        sums[15:16, :] += total_rows(part * mix_grad)
        filt, decay = filter_block(layers, small, block, units, length, width, model_width)
        taps[block] = times(fwd, filt * decay)
        return 0

    lax.fori_loop(0, blocks, gate, 0)

    def transform(unit, _):
        rows = rows_of(units.block(unit))
        inside = units.inside(unit, width)
        spec[unit] = times(fwd, jnp.where(inside, gated[rows, :], 0.0))
        prod[unit] = times(fwd, jnp.where(inside, gm[rows, :], 0.0))
        return 0

    lax.fori_loop(0, units.total(), transform, 0)

    def spread(unit, _):
        after = jnp.minimum(unit + 1, units.units - 1)
        new = jnp.where(unit + 1 < units.stop(unit), prod[after], 0.0)
        prod[unit, pl.ds(0, half)] += new[BLOCK : BLOCK + half]
        prod[unit, pl.ds(half, half)] -= new[BLOCK + half :]
        prod[unit, pl.ds(BLOCK, half)] -= new[:half]
        prod[unit, pl.ds(BLOCK + half, half)] += new[half:BLOCK]
        return 0

    lax.fori_loop(0, units.total(), spread, 0)

    def signal_grad(unit, _):
        pieces = []
        for low in range(0, BLOCK, FREQ_CHUNK):
            re, im = pl.ds(low, FREQ_CHUNK), pl.ds(BLOCK + low, FREQ_CHUNK)

            def step(ahead, total):
                at = unit + ahead
                g_re, g_im, t_re, t_im = (
                    prod[at, re],
                    prod[at, im],
                    taps[ahead, re],
                    taps[ahead, im],
                )
                return (
                    total[0] + (g_re * t_re + g_im * t_im),
                    total[1] + (g_im * t_re - g_re * t_im),
                )

            zero = jnp.zeros((FREQ_CHUNK, width), F32)
            pieces.append(lax.fori_loop(0, units.stop(unit) - unit, step, (zero, zero)))
        joined = jnp.concatenate([piece[0] for piece in pieces] + [piece[1] for piece in pieces])
        value = times(inv, joined)
        rows = rows_of(units.block(unit))
        conv_grad[1, rows, :] += jnp.where(units.inside(unit, width), value, 0.0)
        return 0

    lax.fori_loop(0, units.total(), signal_grad, 0)

    def tap_grad(back, _):
        pieces = []
        for low in range(0, BLOCK, FREQ_CHUNK):
            re, im = pl.ds(low, FREQ_CHUNK), pl.ds(BLOCK + low, FREQ_CHUNK)

            def step(unit, total):
                at = unit - back
                g_re, g_im, s_re, s_im = (
                    prod[unit, re],
                    prod[unit, im],
                    spec[at, re],
                    spec[at, im],
                )
                return (
                    total[0] + (g_re * s_re + g_im * s_im),
                    total[1] + (g_im * s_re - g_re * s_im),
                )

            zero = jnp.zeros((FREQ_CHUNK, width), F32)
            total = (zero, zero)
            for doc in range(docs):
                total = lax.fori_loop(
                    units.doc_start(doc) + back, units.doc_stop(doc), step, total
                )
            pieces.append(total)
        joined = jnp.concatenate([piece[0] for piece in pieces] + [piece[1] for piece in pieces])
        decay = decay_of(back, length, units.channel(), model_width, width)
        filt_grad[rows_of(back), :] = times(inv, joined) * decay
        return 0

    lax.fori_loop(0, blocks, tap_grad, 0)

    def conv_back(block, _):
        rows = rows_of(block)
        masks = tap_masks(units, block, width)
        val_parts, pre_parts, post_parts = (
            delayed(val, block),
            delayed(pre, block),
            delayed(post, block),
        )
        gated_grad = conv_grad[1, rows, :]
        pre_grad = gated_grad * short_conv(val_parts, small, 2, masks)
        val_grad = gated_grad * short_conv(pre_parts, small, 1, masks)
        post_grad = conv_grad[0, rows, :]
        conv_grad[1, rows, :] = pre_grad
        conv_grad[2, rows, :] = val_grad
        for branch, (grad, parts) in enumerate(
            ((post_grad, post_parts), (pre_grad, pre_parts), (val_grad, val_parts))
        ):
            sums[branch : branch + 1, :] += total_rows(grad * parts[0])
            sums[3 + branch : 4 + branch, :] += total_rows(
                jnp.where(masks[0], grad * parts[1], 0.0)
            )
            sums[6 + branch : 7 + branch, :] += total_rows(
                jnp.where(masks[1], grad * parts[2], 0.0)
            )
            sums[9 + branch : 10 + branch, :] += total_rows(grad)
        return 0

    lax.fori_loop(0, blocks, conv_back, 0)

    def spread_taps(block, _):
        start = block * BLOCK
        one, _two = tap_masks(units, block, width, 1)
        _one, two = tap_masks(units, block, width, 2)
        place = lax.broadcasted_iota(jnp.int32, (BLOCK, width), 0) + start
        one = one & (place + 1 < length)
        two = two & (place + 2 < length)
        for branch in range(3):
            here = conv_grad[branch, rows_of(block), :]
            after = conv_grad[
                branch, pl.ds(pl.multiple_of(jnp.minimum(start + BLOCK, length - 8), 8), 8), :
            ]
            joined = jnp.concatenate([here, after], axis=0)
            size = BLOCK + 8
            next_one = pltpu.roll(joined, size - 1, 0)[:BLOCK]
            next_two = pltpu.roll(joined, size - 2, 0)[:BLOCK]
            total = small[branch : branch + 1, :] * here
            total += jnp.where(one, small[3 + branch : 4 + branch, :] * next_one, 0.0)
            total += jnp.where(two, small[6 + branch : 7 + branch, :] * next_two, 0.0)
            rounded = total.astype(BF16)
            proj_grad[rows_of(block), branch * width : (branch + 1) * width] = rounded
            sums[12 + branch : 13 + branch, :] += total_rows(rounded.astype(F32))
        return 0

    lax.fori_loop(0, blocks, spread_taps, 0)


def whole_spec(shape, column=0):
    place = (0,) * (len(shape) - 1) + (column,)
    return pl.BlockSpec(shape, lambda i, meta: place, pipeline_mode=pl.Buffered(1))


def layer_spec(shape):
    return pl.BlockSpec(
        (1,) + shape[1:], lambda i, meta: (1, 0, 0), pipeline_mode=pl.Buffered(1)
    )


def mixer_forward(meta, docs, projected, layers, small, model_width, tables):
    length, width = layers.shape[2], small.shape[1]
    units = length // BLOCK + docs - 1
    column = [whole_spec((length, width), at) for at in range(3)]
    return pl.pallas_call(
        functools.partial(mixer_forward_kernel, docs, model_width),
        out_shape=(
            jax.ShapeDtypeStruct((length, width), BF16),
            jax.ShapeDtypeStruct((length, width), F32),
        ),
        grid_spec=pltpu.PrefetchScalarGridSpec(
            num_scalar_prefetch=1,
            grid=(1,),
            in_specs=column
            + [layer_spec(layers.shape)]
            + [whole_spec(value.shape) for value in (small, tables[0], tables[1])],
            out_specs=(column[0], column[0]),
            scratch_shapes=[
                pltpu.VMEM((length, width), F32),
                pltpu.VMEM((units, 2 * BLOCK, width), F32),
                pltpu.VMEM((length // BLOCK, 2 * BLOCK, width), F32),
                pltpu.VMEM((units, 2 * BLOCK, width), F32),
            ],
        ),
        compiler_params=pltpu.CompilerParams(vmem_limit_bytes=VMEM_LIMIT),
        cost_estimate=pl.CostEstimate(
            flops=40 * 10**9, bytes_accessed=10 * 10**6, transcendentals=0
        ),
        name="mixer_forward",
    )(meta, projected, projected, projected, layers, small, *tables)


def mixer_backward(meta, docs, projected, layers, small, model_width, tables, mixed, branch_grad):
    length, width = layers.shape[2], small.shape[1]
    units = length // BLOCK + docs - 1
    column = [whole_spec((length, width), at) for at in range(3)]
    return pl.pallas_call(
        functools.partial(mixer_backward_kernel, docs, model_width),
        out_shape=(
            jax.ShapeDtypeStruct((length, 3 * width), BF16),
            jax.ShapeDtypeStruct((length, width), F32),
            jax.ShapeDtypeStruct((16, width), F32),
        ),
        grid_spec=pltpu.PrefetchScalarGridSpec(
            num_scalar_prefetch=1,
            grid=(1,),
            in_specs=column
            + [layer_spec(layers.shape)]
            + [
                whole_spec(value.shape)
                for value in (small, tables[0], tables[1], mixed, branch_grad)
            ],
            out_specs=(
                whole_spec((length, 3 * width)),
                column[0],
                whole_spec((16, width)),
            ),
            scratch_shapes=[
                pltpu.VMEM((length, width), F32),
                pltpu.VMEM((length, width), F32),
                pltpu.VMEM((3, length, width), F32),
                pltpu.VMEM((units, 2 * BLOCK, width), F32),
                pltpu.VMEM((length // BLOCK, 2 * BLOCK, width), F32),
                pltpu.VMEM((units, 2 * BLOCK, width), F32),
            ],
        ),
        compiler_params=pltpu.CompilerParams(vmem_limit_bytes=VMEM_LIMIT),
        cost_estimate=pl.CostEstimate(
            flops=80 * 10**9, bytes_accessed=16 * 10**6, transcendentals=0
        ),
        name="mixer_backward",
    )(meta, projected, projected, projected, layers, small, *tables, mixed, branch_grad)


def norm_parts(values):
    centre = values - jnp.mean(values, axis=-1, keepdims=True)
    spread = jnp.mean(centre * centre, axis=-1, keepdims=True)
    scale = lax.rsqrt(spread + 1e-05)
    return centre * scale, scale


def project_kernel(inputs, norm, weight, lines, out):
    unit, _ = norm_parts(inputs[...].astype(F32))
    normed = (unit * norm[0:1, :] + norm[1:2, :]).astype(BF16)
    bias = jnp.concatenate([lines[13 + at : 14 + at, :] for at in range(3)], axis=1)
    total = jnp.dot(normed, weight[...], preferred_element_type=F32) + bias
    out[...] = total.astype(BF16)


def project(inputs, lines, weight, mine):
    length, depth = inputs.shape
    width = weight.shape[1]
    return pl.pallas_call(
        project_kernel,
        out_shape=jax.ShapeDtypeStruct((length, width), BF16),
        grid=(length // BLOCK,),
        in_specs=[
            pl.BlockSpec((BLOCK, depth), lambda i: (i, 0)),
            pl.BlockSpec((8, depth), lambda i: (NORM_ROW // 8, 0)),
            pl.BlockSpec(weight.shape, lambda i: (0, 0)),
            pl.BlockSpec((16, mine.shape[1]), lambda i: (0, 0)),
        ],
        out_specs=pl.BlockSpec((BLOCK, width), lambda i: (i, 0)),
        compiler_params=pltpu.CompilerParams(vmem_limit_bytes=VMEM_LIMIT),
        cost_estimate=pl.CostEstimate(
            flops=2 * length * depth * width, bytes_accessed=10 * 10**6, transcendentals=0
        ),
        name="project",
    )(inputs, lines, weight, mine)


def gelu_pair(u):
    root = math.sqrt(2.0 / math.pi)
    square = u * u
    curve = jnp.tanh(root * (u + 0.044715 * (u * square)))
    value = 0.5 * u * (1.0 + curve)
    slope = 0.5 * (1.0 + curve) + 0.5 * u * (1.0 - curve * curve) * (
        root * (1.0 + 3.0 * 0.044715 * square)
    )
    return value, slope


class Copies:
    def __init__(self, local_sems, send_sems, got_sems):
        self.local_sems, self.send_sems, self.got_sems = local_sems, send_sems, got_sems
        self.locals = 0
        self.names = {}
        self.pending = []

    def local(self, source, target):
        copy = pltpu.make_async_copy(source, target, self.local_sems.at[self.locals])
        self.locals += 1
        copy.start()
        return copy

    def remote(self, name, source, target, device):
        at = self.names.setdefault(name, len(self.names))
        return pltpu.make_async_remote_copy(
            src_ref=source,
            dst_ref=target,
            send_sem=self.send_sems.at[at],
            recv_sem=self.got_sems.at[at],
            device_id=device,
            device_id_type=pl.DeviceIdType.MESH,
        )

    def send(self, name, source, target, device, when=None):
        copy = self.remote(name, source, target, device)
        if when is None:
            copy.start()
        else:
            pl.when(when)(copy.start)
        self.pending.append((name, copy, when))

    def got(self, name, target, device):
        self.remote(name, target, target, device).wait_recv()

    def local_when(self, source, target, when):
        copy = pltpu.make_async_copy(source, target, self.local_sems.at[self.locals])
        self.locals += 1
        pl.when(when)(copy.start)
        return copy

    def settle(self, name):
        for at, (found, copy, when) in enumerate(self.pending):
            if found == name:
                copy.wait_send()
                del self.pending[at]
                return

    def finish(self):
        for _, copy, when in self.pending:
            if when is None:
                copy.wait_send()
            else:
                pl.when(when)(copy.wait_send)


def greet(devices):
    barrier = pltpu.get_barrier_semaphore()
    for device in devices:
        pl.semaphore_signal(
            barrier, inc=1, device_id=device, device_id_type=pl.DeviceIdType.MESH
        )
    pl.semaphore_wait(barrier, len(devices))


def lane_masks(bits):
    masks, found = [0], []
    for bit in bits:
        found += [(mask ^ bit, bit) for mask in masks]
        masks += [mask ^ bit for mask in masks]
    return found


def middle_kernel(
    dims,
    given,
    branch,
    inputs,
    out_weight,
    lines,
    out_grad,
    up_bias,
    *rest,
):
    rz_count, pos_count = dims
    count = 2 * len(given)
    pieces, rest = rest[:count], rest[count:]
    steps = rz_count - 1
    extras, rest = rest[: 2 * steps - 1], rest[2 * steps - 1 :]
    result, residual, branch_grad, token_lines = rest[:4]
    piece_grads, rest = rest[4 : 4 + 2 * pos_count], rest[4 + 2 * pos_count :]
    down_moved, rest = rest[:pos_count], rest[pos_count:]
    (
        tokens,
        normed,
        grad,
        out_total,
        back_total,
        weights,
        grads,
        out_got,
        back_got,
        grad_q,
        turned_got,
        out_parts,
        bias_grad,
        local_sems,
        send_sems,
        got_sems,
    ) = rest
    z, core, pos = lax.axis_index("rz"), lax.axis_index("core"), lax.axis_index("pos")
    rows, depth = inputs.shape
    tiles, _, units, own_width, width = weights.shape
    middle = tiles // 2
    columns = depth // width
    chan = branch.shape[1]
    down_units = (units - 2 * tiles) // columns
    bits = bits_of(pos_count)
    orders = (bits, bits[::-1])
    copies = Copies(local_sems, send_sems, got_sems)
    other = {"core": 1 - core}
    peers = [jnp.bitwise_xor(pos, mask) for mask in range(pos_count)]

    def token_rows(owner):
        return pl.ds(pl.multiple_of(owner * rows, rows), rows)

    def channels(owner):
        return pl.ds(pl.multiple_of(owner * chan, chan), chan)

    grad_load = copies.local(out_grad, grad.at[pl.ds(0, rows)])
    loads = []
    for at, mask in enumerate(given):
        for side in range(2):
            piece = pieces[2 * at + side]
            part = pl.ds(side * middle, middle)
            target = weights.at[part, peers[mask], pl.ds(0, piece.shape[1])]
            loads.append((copies.local(piece, target), None))
    last = pl.ds(units - extras[0].shape[1], extras[0].shape[1])

    def extra_slot(origin):
        return weights.at[jnp.clip(origin, 0, tiles - 1), :, last]

    for at, extra in enumerate(extras):
        origin = z - (at if at < steps else steps - 1 - at)
        there = (origin >= 0) & (origin < tiles)
        loads.append((copies.local_when(extra, extra_slot(origin), there), there))
    greet(
        [other]
        + [{"rz": (z + step) % rz_count} for step in range(1, rz_count)]
        + [{"pos": peers[mask]} for mask in range(1, pos_count)]
    )
    for mask in range(1, pos_count):
        copies.send(
            ("branch", mask),
            branch.at[token_rows(peers[mask])],
            tokens.at[:, channels(pos)],
            {"pos": peers[mask]},
        )
    grad_load.wait()
    own_half, other_half = pl.ds(0, rows), pl.ds(rows, rows)
    copies.send(("grad",), grad.at[own_half], grad.at[other_half], other)

    full = pieces[0].shape[1]
    arriving = []
    for side in range(2):
        part = pl.ds(side * middle, middle)
        for mask, bit in lane_masks(orders[side]):
            if mask in given:
                continue
            arriving.append((side, mask, bit))
            before = mask ^ bit
            slot = weights.at[part, peers[before], pl.ds(0, full)]
            if before in given:
                source = pieces[2 * given.index(before) + side]
            else:
                source = slot
                prior = [item for item in arriving if item[:2] == (side, before)][0]
                copies.got(("weights", side, before), slot, {"pos": peers[prior[2]]})
            copies.send(("weights", side, mask), source, slot, {"pos": peers[bit]})
    ends = ((1, {"rz": z + 1}, {"rz": z - 1}), (-1, {"rz": z - 1}, {"rz": z + 1}))
    for side, (direction, onward, _) in enumerate(ends):
        origin = z - direction * (steps - 1)
        sends = (origin >= 0) & (origin < tiles)
        sends = sends & (z + direction >= 0) & (z + direction < tiles)
        source = extras[steps - 1 if side == 0 else 2 * steps - 2] if steps > 1 else extras[0]
        copies.send(("extra", side), source, extra_slot(origin), onward, sends)

    tokens[:, channels(pos)] = branch[token_rows(pos), :]
    for mask in range(1, pos_count):
        copies.got(("branch", mask), tokens.at[:, channels(peers[mask])], {"pos": peers[mask]})
    line = [lines[NORM_ROW + at : NORM_ROW + at + 1, :] for at in range(6)]

    def project_out(at, _):
        part = pl.ds(pl.multiple_of(at * BLOCK, BLOCK), BLOCK)
        value = inputs[part, :].astype(F32) + line[2]
        value += jnp.dot(tokens[part, :], out_weight[...], preferred_element_type=F32)
        residual[part, :] = value
        unit, _ = norm_parts(value)
        normed[part, :] = (unit * line[3] + line[4]).astype(BF16)
        return 0

    lax.fori_loop(0, rows // BLOCK, project_out, 0)
    copies.send(("normed",), normed.at[own_half], normed.at[other_half], other)
    out_total[...] = jnp.zeros_like(out_total)
    back_total[...] = jnp.zeros_like(back_total)
    for copy, there in loads:
        if there is None:
            copy.wait()
        else:
            pl.when(there)(copy.wait)
    sent = {item[:2] for item in arriving}
    for side, mask, bit in arriving:
        onward = [item for item in arriving if item[0] == side and item[1] ^ item[2] == mask]
        if not onward:
            slot = weights.at[pl.ds(side * middle, middle), peers[mask], pl.ds(0, full)]
            copies.got(("weights", side, mask), slot, {"pos": peers[bit]})
    for side, (direction, _, back) in enumerate(ends):
        origin = z - direction * steps

        def take(side=side, origin=origin, back=back):
            copies.got(("extra", side), extra_slot(origin), back)

        pl.when((origin >= 0) & (origin < tiles))(take)
    copies.got(("grad",), grad.at[other_half], other)
    copies.got(("normed",), normed.at[other_half], other)

    def step(tile, _):
        up = jnp.concatenate(
            [
                weights[block, :, side * tiles + tile].reshape(pos_count * own_width, width)
                for block in range(tiles)
                for side in range(2)
            ],
            axis=0,
        )
        down = jnp.concatenate(
            [
                weights[
                    tile, :, 2 * tiles + at * down_units : 2 * tiles + (at + 1) * down_units
                ].reshape(width, width)
                for at in range(columns)
            ],
            axis=1,
        )
        pre = jnp.dot(normed[: 2 * rows], up, preferred_element_type=F32) + up_bias[pl.ds(tile, 1), :]
        hidden, slope = gelu_pair(pre)
        hidden = hidden.astype(BF16)
        hidden_grad = lax.dot_general(
            grad[...], down, (((1,), (1,)), ((), ())), preferred_element_type=F32
        )
        pre_grad = hidden_grad * slope
        bias_grad[pl.ds(tile, 1), :] = jnp.sum(pre_grad, axis=0, keepdims=True)
        pre_grad = pre_grad.astype(BF16)
        out_total[...] += jnp.dot(hidden, down, preferred_element_type=F32)
        back_total[...] += lax.dot_general(
            pre_grad, up, (((1,), (1,)), ((), ())), preferred_element_type=F32
        )
        down_grad = lax.dot_general(
            hidden, grad[...], (((0,), (0,)), ((), ())), preferred_element_type=F32
        ).astype(BF16)
        for at in range(columns):
            grads[tile, :, 2 * tiles + at * down_units : 2 * tiles + (at + 1) * down_units] = (
                down_grad[:, at * width : (at + 1) * width].reshape(
                    pos_count, down_units, own_width, width
                )
            )
        up_grad = lax.dot_general(
            normed[: 2 * rows], pre_grad, (((0,), (0,)), ((), ())), preferred_element_type=F32
        ).astype(BF16)
        size = pos_count * own_width
        for block in range(tiles):
            for side in range(2):
                low = (2 * block + side) * size
                grads[block, :, side * tiles + tile] = up_grad[low : low + size].reshape(
                    pos_count, own_width, width
                )
        return 0

    kept = kept_masks(orders)
    down_part = pl.ds(2 * tiles, columns * down_units)
    early = middle // 2
    chunk_units = 2 * tiles + columns

    def down_copies(tile):
        side = tile // middle
        bit = orders[side][0]
        if tile - side * middle >= early:
            return
        for mask in range(pos_count):
            if mask & bit:
                at = 2 * kept[side].index(mask ^ bit) + side
                yield (
                    ("down", tile, mask),
                    grads.at[tile, peers[mask], down_part],
                    down_moved[at].at[tile - side * middle],
                    {"pos": peers[bit]},
                )

    for tile in sorted(range(tiles), key=lambda tile: tile % middle):
        step(tile, 0)
        for copy in down_copies(tile):
            copies.send(*copy)
    copies.settle(("normed",))
    normed[:rows] = back_total[rows:].astype(BF16)
    copies.send(("back",), normed.at[own_half], back_got, other)
    normed[rows : 2 * rows] = out_total[rows:].astype(BF16)
    copies.send(("out",), normed.at[other_half], out_got, other)
    stores = []
    for mask in range(pos_count):
        for side in range(2):
            target = piece_grads[2 * mask + side]
            if mask in kept[side]:
                source = grads.at[pl.ds(side * middle, middle), peers[mask]]
                stores.append(copies.local(source, target.at[:, pl.ds(0, units)]))
                continue
            for at in range(middle):
                source = grads.at[side * middle + at, peers[mask]]
                stores.append(
                    copies.local(
                        source.at[pl.ds(0, 2 * tiles)], target.at[pl.ds(at * chunk_units, 2 * tiles)]
                    )
                )
                if at >= early:
                    low = middle * chunk_units + (at - early) * columns * down_units
                    stores.append(
                        copies.local(
                            source.at[down_part], target.at[pl.ds(low, columns * down_units)]
                        )
                    )

    copies.got(("back",), back_got, other)
    zero = jnp.zeros((1, depth), F32)

    def norm_back(at, sums):
        part = pl.ds(pl.multiple_of(at * BLOCK, BLOCK), BLOCK)
        unit, scale = norm_parts(residual[part, :])
        back = back_total[part, :] + back_got[part, :].astype(F32)
        scaled = back * line[3]
        out = grad[part, :].astype(F32)
        value = out + scale * (
            scaled
            - jnp.mean(scaled, axis=-1, keepdims=True)
            - unit * jnp.mean(scaled * unit, axis=-1, keepdims=True)
        )
        back_total[part, :] = value
        grad_q[part, :] = value.astype(BF16)

        def total(value):
            return jnp.sum(value, axis=0, keepdims=True)

        return (
            sums[0] + total(value),
            sums[1] + total(back * unit),
            sums[2] + total(back),
            sums[3] + total(out),
        )

    sums = lax.fori_loop(0, rows // BLOCK, norm_back, (zero,) * 4)
    turned = lax.dot_general(
        grad_q[...], out_weight[...], (((1,), (1,)), ((), ())), preferred_element_type=F32
    ).astype(BF16)
    copies.settle(("grad",))
    grad[own_half, :] = turned
    for mask in range(1, pos_count):
        copies.send(
            ("branch grad", mask),
            grad.at[own_half, channels(peers[mask])],
            branch_grad.at[token_rows(pos)],
            {"pos": peers[mask]},
        )
    branch_grad[token_rows(pos), :] = grad[own_half, channels(pos)]
    copies.got(("out",), out_got, other)

    def add_result(at, _):
        part = pl.ds(pl.multiple_of(at * BLOCK, BLOCK), BLOCK)
        value = residual[part, :] + (out_total[part, :] + out_got[part, :].astype(F32)) + line[5]
        result[part, :] = value.astype(BF16)
        residual[part, :] = back_total[part, :]
        return 0

    lax.fori_loop(0, rows // BLOCK, add_result, 0)
    token_lines[...] = jnp.zeros_like(token_lines)
    for at in range(4):
        token_lines[2 + at : 3 + at, :] = sums[at]
    per_tile = width // 128
    per = 2 * tiles * width // depth // per_tile
    for tile in range(tiles):
        owner = 2 * tile + core
        lanes = pl.ds(pl.multiple_of(owner // per * 128, 128), 128)
        for at in range(per * per_tile):
            low = at % per_tile * 128
            value = bias_grad[tile : tile + 1, low : low + 128]
            token_lines[6 + at : 7 + at, lanes] = jnp.where(
                owner % per == at // per_tile, value, 0.0
            )

    copies.settle(("back",))
    copies.settle(("out",))
    normed[:depth] = lax.dot_general(
        tokens[...], grad_q[...], (((0,), (0,)), ((), ())), preferred_element_type=F32
    ).astype(BF16)
    size = pos_count * own_width

    def block_rows(block, side):
        return pl.ds(pl.multiple_of((2 * block + side) * size, size), size)

    for block in range(tiles):
        copies.send(
            ("turned", block),
            normed.at[block_rows(block, 1 - core)],
            turned_got.at[block],
            other,
        )
    for block in range(tiles):
        copies.got(("turned", block), turned_got.at[block], other)
        value = normed[block_rows(block, core), :].astype(F32)
        value = (value + turned_got[block].astype(F32)).astype(BF16)
        for at in range(columns):
            out_parts[block, :, at] = value[:, at * width : (at + 1) * width].reshape(
                pos_count, own_width, width
            )
    for mask in range(pos_count):
        for side in range(2):
            target = piece_grads[2 * mask + side]
            if mask in kept[side]:
                source = out_parts.at[pl.ds(side * middle, middle), peers[mask]]
                stores.append(copies.local(source, target.at[:, pl.ds(units, columns)]))
                continue
            for at in range(middle):
                source = out_parts.at[side * middle + at, peers[mask]]
                low = at * chunk_units + 2 * tiles
                stores.append(copies.local(source, target.at[pl.ds(low, columns)]))
    for mask in range(1, pos_count):
        copies.got(
            ("branch grad", mask), branch_grad.at[token_rows(peers[mask])], {"pos": peers[mask]}
        )
    for tile in range(tiles):
        for name, _, target, device in down_copies(tile):
            copies.got(name, target, device)
    for copy in stores:
        copy.wait()
    copies.finish()


def kept_masks(orders):
    count = 1 << len(orders[0])
    return [[mask for mask in range(count) if not mask & order[0]] for order in orders]


def middle(dims, given, branch, inputs, out_weight, lines, out_grad, up_bias, pieces, extras):
    rz_count, pos_count = dims
    rows, depth = inputs.shape
    tiles, width = up_bias.shape
    length, chan = branch.shape
    piece = pieces[0].shape
    piece = piece[:1] + (piece[1] + extras[0].shape[1],) + piece[2:]
    own_width = piece[2]
    whole = (tiles, pos_count) + piece[1:]
    columns = depth // width
    orders = (bits_of(pos_count), bits_of(pos_count)[::-1])
    kept = kept_masks(orders)

    half, downs = tiles // 2, piece[1] - 2 * tiles
    early = half // 2

    def piece_of(*units):
        return jax.ShapeDtypeStruct(units + piece[2:], BF16)

    sent = piece_of(half * (2 * tiles + columns) + (half - early) * downs)
    piece_grads = tuple(
        piece_of(half, piece[1] + columns) if mask in kept[side] else sent
        for mask in range(pos_count)
        for side in range(2)
    )
    down_moved = (piece_of(early, downs),) * pos_count
    size = pos_count * own_width
    anywhere = pl.BlockSpec(memory_space=pl.ANY)
    inside = pl.BlockSpec(memory_space=pltpu.VMEM)
    vmem = pltpu.VMEM
    local_count = 1 + len(pieces) + len(extras) + pos_count * (4 + 3 * half)
    remote_count = 2 * (pos_count - 1) + 2 * pos_count + 6 + tiles + tiles * pos_count // 2
    return pl.pallas_call(
        functools.partial(middle_kernel, dims, given),
        out_shape=(
            jax.ShapeDtypeStruct((rows, depth), BF16),
            jax.ShapeDtypeStruct((rows, depth), F32),
            jax.ShapeDtypeStruct((length, chan), BF16),
            jax.ShapeDtypeStruct((16, depth), F32),
        )
        + piece_grads
        + down_moved,
        in_specs=[inside] * 4 + [anywhere, inside] + [anywhere] * (len(pieces) + len(extras)),
        out_specs=(inside,) * 4 + (anywhere,) * (3 * pos_count),
        scratch_shapes=[
            vmem((rows, depth), BF16),
            vmem((max(2 * rows, depth), depth), BF16),
            vmem((2 * rows, depth), BF16),
            vmem((2 * rows, depth), F32),
            vmem((2 * rows, depth), F32),
            vmem(whole, BF16),
            vmem(whole, BF16),
            vmem((rows, depth), BF16),
            vmem((rows, depth), BF16),
            vmem((rows, depth), BF16),
            vmem((tiles, size, depth), BF16),
            vmem((tiles, pos_count, depth // width, own_width, width), BF16),
            vmem((tiles, width), F32),
            pltpu.SemaphoreType.DMA((local_count,)),
            pltpu.SemaphoreType.DMA((remote_count,)),
            pltpu.SemaphoreType.DMA((remote_count,)),
        ],
        compiler_params=pltpu.CompilerParams(
            collective_id=2, has_side_effects=True, vmem_limit_bytes=VMEM_LIMIT
        ),
        cost_estimate=pl.CostEstimate(flops=10**7, bytes_accessed=10**7, transcendentals=0),
        name="middle",
    )(branch, inputs, out_weight, lines, out_grad, up_bias, *pieces, *extras)


def swap(value, axis, bit):
    count = lax.axis_size(axis)
    return lax.ppermute(value, axis, [(at, at ^ bit) for at in range(count)])


def gather_kernel(
    dims,
    inputs,
    weight,
    up,
    down,
    out,
    vectors,
    filter_in,
    row_in,
    weight_in,
    bundle,
    extra,
    owned,
    lines,
    mine,
    up_lines,
    layers,
    pack,
    small,
    small_mine,
    local_sems,
    send_sems,
    got_sems,
):
    rz_count, pos_count = dims
    z, core, pos = lax.axis_index("rz"), lax.axis_index("core"), lax.axis_index("pos")
    bits = bits_of(pos_count)
    lanes = [lane_masks(bits), lane_masks(bits[::-1])]
    own_width, model_width = out.shape
    chan = model_width // pos_count
    tile = bundle.shape[3]
    columns = model_width // tile
    half = model_width // 2
    middle = rz_count // 2
    copies = Copies(local_sems, send_sems, got_sems)
    other = {"core": 1 - core}
    right, left = {"rz": z + 1}, {"rz": z - 1}
    has_right, has_left = z + 1 < rz_count, z > 0
    greet(
        [other]
        + [{"rz": (z + step) % rz_count} for step in range(1, rz_count)]
        + [{"pos": jnp.bitwise_xor(pos, mask)} for mask in range(1, pos_count)]
    )

    def branch_cols(owner):
        return pl.ds(pl.multiple_of(owner * chan, chan), chan)

    for mask in range(1, pos_count):
        owner = jnp.bitwise_xor(pos, mask)
        for at in range(3):
            copies.send(
                ("in", mask, at),
                weight.at[at, :, branch_cols(owner)],
                weight_in.at[z, core, pos, :, pl.ds(at * chan, chan)],
                {"pos": owner},
            )

    def send_extra(lane, mask, bit):
        part = pl.ds(lane * (down_units // 2), down_units // 2)
        block = extra.at[jnp.bitwise_xor(pos, mask ^ bit), part]
        copies.send(("extra", lane, mask), block, block, {"pos": jnp.bitwise_xor(pos, bit)})

    def got_extra(lane, mask, bit):
        part = pl.ds(lane * (down_units // 2), down_units // 2)
        block = extra.at[jnp.bitwise_xor(pos, mask), part]
        copies.got(("extra", lane, mask), block, {"pos": jnp.bitwise_xor(pos, bit)})
        later = (bits, bits[::-1])[lane]
        for onward in later[later.index(bit) + 1 :]:
            send_extra(lane, mask ^ onward, onward)

    down_units = down.shape[0] // own_width
    local_extra = []
    for at in range(down_units):
        source = down.at[pl.ds(at * own_width, own_width), pl.ds((columns - 1) * tile, tile)]
        local_extra.append(copies.local(source, extra.at[pos, at]))
    for copy in local_extra:
        copy.wait()
    for at in range(len(bits)):
        for lane in range(2):
            bit = (bits, bits[::-1])[lane][at]
            send_extra(lane, bit, bit)

    def lane_cols(lane):
        return pl.ds(lane * half, half)

    def send_rows(lane, mask, bit):
        origin = jnp.bitwise_xor(pos, mask ^ bit)
        cols = lane_cols(lane)
        source = inputs.at[:, cols] if mask == bit else row_in.at[origin, :, cols]
        copies.send(
            ("rows", lane, mask),
            source,
            row_in.at[origin, :, cols],
            {"pos": jnp.bitwise_xor(pos, bit)},
        )

    for at in range(len(bits)):
        for lane in range(2):
            bit = (bits, bits[::-1])[lane][at]
            send_rows(lane, bit, bit)

    def up_cols(at, side):
        return pl.ds(pl.multiple_of((2 * at + side) * tile, tile), tile)

    for at in range(rz_count):
        copies.send(
            ("up", at),
            up.at[:, up_cols(at, 1 - core)],
            bundle.at[z, core * rz_count + at],
            other,
        )
    local_in = [
        copies.local(
            weight.at[at, :, branch_cols(pos)],
            weight_in.at[z, core, pos, :, pl.ds(at * chan, chan)],
        )
        for at in range(3)
    ]
    local_owned = [copies.local(out, owned.at[z, core, pos])]
    local_bundle = [
        copies.local(up.at[:, up_cols(at, core)], bundle.at[z, core * rz_count + at])
        for at in range(rz_count)
    ]
    for col in range(columns - 1):
        for at in range(down_units):
            source = down.at[pl.ds(at * own_width, own_width), pl.ds(col * tile, tile)]
            target = bundle.at[z, 2 * rz_count + col * down_units + at]
            local_bundle.append(copies.local(source, target))
    local_rows = copies.local(inputs, row_in.at[pos])

    flows = {
        "in": lambda origin: weight_in.at[origin, core],
        "owned": lambda origin: owned.at[origin, core, pos],
        "small": lambda origin: small.at[origin, core, pos],
        "bundle": lambda origin: bundle.at[origin],
    }

    def line_start(flow):
        block = flows[flow](z)
        copies.send((flow, "right", 1), block, block, right, has_right)
        copies.send((flow, "left", 1), block, block, left, has_left)

    def line_step(flow, distance, arrived=None):
        for side, origin, there, onward, has_next in (
            ("right", z - distance, z >= distance, right, has_right),
            ("left", z + distance, z + distance < rz_count, left, has_left),
        ):
            safe = jnp.clip(origin, 0, rz_count - 1)
            block = flows[flow](safe)

            def wait(block=block, side=side, onward=onward):
                copies.got((flow, side, distance), block, onward)

            pl.when(there)(wait)
            if distance + 1 < rz_count:
                copies.send((flow, side, distance + 1), block, block, onward, there & has_next)
            if arrived is not None:
                arrived(side, distance, safe, there)

    def share_in(side, distance, origin, there):
        block = weight_in.at[origin, core]
        copies.send(("in core", side, distance), block, block, other, there)

    for copy in local_in:
        copy.wait()
    for mask in range(1, pos_count):
        owner = jnp.bitwise_xor(pos, mask)
        for at in range(3):
            copies.got(
                ("in", mask, at),
                weight_in.at[z, core, owner, :, pl.ds(at * chan, chan)],
                {"pos": owner},
            )
    for lane in range(2):
        got_extra(lane, *lanes[lane][0])
    line_start("in")
    block = weight_in.at[z, core]
    copies.send(("in core", "own", 0), block, block, other)
    for copy in local_owned:
        copy.wait()
    line_start("owned")
    pack[...] = jnp.zeros_like(pack)
    row = 0
    for value in vectors:
        value = value[...].astype(F32)
        value = value.reshape(-1, value.shape[-1])
        pack[row : row + value.shape[0], : value.shape[1]] = value
        row += value.shape[0]
    small[z, core, pos] = pack[...].astype(BF16)
    line_start("small")
    for copy in local_bundle:
        copy.wait()
    for at in range(rz_count):
        copies.got(("up", at), bundle.at[z, (1 - core) * rz_count + at], other)
    line_start("bundle")

    def line_steps(distance):
        line_step("in", distance, share_in)
        line_step("owned", distance)
        line_step("small", distance)

    line_steps(1)

    def owned_half(side, origin, lane):
        part = pl.ds(lane * middle, middle)
        return (owned.at[part, side, origin], small.at[part, side, origin])

    def send_owned(lane, mask, bit):
        for at, block in enumerate(owned_half(core, jnp.bitwise_xor(pos, mask ^ bit), lane)):
            copies.send(
                ("owned pos", at, lane, mask), block, block, {"pos": jnp.bitwise_xor(pos, bit)}
            )

    def share_owned(lane, mask):
        for at, block in enumerate(owned_half(core, jnp.bitwise_xor(pos, mask), lane)):
            copies.send(("owned core", at, lane, mask), block, block, other)

    def got_rows(lane, mask, bit):
        block = row_in.at[jnp.bitwise_xor(pos, mask), :, lane_cols(lane)]
        copies.got(("rows", lane, mask), block, {"pos": jnp.bitwise_xor(pos, bit)})
        later = (bits, bits[::-1])[lane]
        for onward in later[later.index(bit) + 1 :]:
            send_rows(lane, mask ^ onward, onward)

    def got_owned(lane, mask, bit):
        for at, block in enumerate(owned_half(core, jnp.bitwise_xor(pos, mask), lane)):
            copies.got(("owned pos", at, lane, mask), block, {"pos": jnp.bitwise_xor(pos, bit)})
        later = (bits, bits[::-1])[lane]
        for onward in later[later.index(bit) + 1 :]:
            send_owned(lane, mask ^ onward, onward)
        share_owned(lane, mask)

    for lane in range(2):
        got_rows(lane, *lanes[lane][0])
    for distance in range(2, rz_count):
        line_steps(distance)
    for at in range(len(bits)):
        for lane in range(2):
            bit = (bits, bits[::-1])[lane][at]
            send_owned(lane, bit, bit)
    for lane in range(2):
        share_owned(lane, 0)
    for distance in range(1, rz_count - 1):
        line_step("bundle", distance)
    filter_layers(filter_in, layers, small_mine)
    for at in range(1, pos_count - 1):
        for lane in range(2):
            got_rows(lane, *lanes[lane][at])
            got_extra(lane, *lanes[lane][at])
    for at in range(pos_count - 1):
        for lane in range(2):
            got_owned(lane, *lanes[lane][at])
    line_step("bundle", rz_count - 1)
    local_rows.wait()
    for at in range(pos_count):
        for lane in range(2):
            for part, block in enumerate(
                owned_half(1 - core, jnp.bitwise_xor(pos, at), lane)
            ):
                copies.got(("owned core", part, lane, at), block, other)
    copies.got(("in core", "own", 0), weight_in.at[z, 1 - core], other)
    for distance in range(1, rz_count):
        for side, origin, there in (
            ("right", z - distance, z >= distance),
            ("left", z + distance, z + distance < rz_count),
        ):
            block = weight_in.at[jnp.clip(origin, 0, rz_count - 1), 1 - core]

            def wait(block=block, side=side, distance=distance):
                copies.got(("in core", side, distance), block, other)

            pl.when(there)(wait)

    per_group = 128 // own_width
    for group in range(model_width // 128):
        total = jnp.zeros((LINES, 128), F32)
        for at in range(per_group):
            owner = group * per_group + at
            value = small[
                owner // (2 * pos_count), owner // pos_count % 2, owner % pos_count
            ].astype(F32)
            value = jnp.where(
                lax.broadcasted_iota(jnp.int32, value.shape, 1) < own_width, value, 0.0
            )
            total += pltpu.roll(value, at * own_width, 1) if at else value
        lines[:, group * 128 : (group + 1) * 128] = total
    mine[...] = lines[:NORM_ROW, pl.ds(pl.multiple_of(pos * chan, chan), chan)]
    ff_own = down.shape[0]
    per_lanes = 128 // ff_own
    for at in range(rz_count):
        for group in range(pos_count // per_lanes):
            total = jnp.zeros((1, 128), F32)
            for part in range(per_lanes):
                value = small[at, core, group * per_lanes + part][UP_ROW : UP_ROW + 1]
                value = value.astype(F32)
                total += pltpu.roll(value, part * ff_own, 1) if part else value
            up_lines[at : at + 1, group * 128 : (group + 1) * 128] = total
    copies.finish()


def filter_layers(filter_in, layers, padded):
    embedding, w_one, w_two, columns = filter_in
    padded[...] = jnp.zeros_like(padded)
    padded[: w_one.shape[0], :] = w_one[...].astype(F32)
    frequency = columns[:, 2:3]
    sums = exact(padded[...], embedding[...], ((0,), (0,))) + columns[:, 0:1]
    layers[2] = sums
    layers[4] = jnp.cos(frequency * sums)
    layers[0] = jnp.sin(frequency * sums)
    sums = exact(w_two[...].astype(F32), layers[0], ((0,), (0,))) + columns[:, 1:2]
    layers[3] = sums
    layers[5] = jnp.cos(frequency * sums)
    layers[1] = jnp.sin(frequency * sums)


def gather(dims, inputs, weight, up, down, out, vectors, filter_in):
    rz_count, pos_count = dims
    part_len, model_width = inputs.shape
    own_width = out.shape[0]
    tile = pos_count * down.shape[0]
    down_units = down.shape[0] // own_width
    units = 2 * rz_count + down_units * (model_width // tile - 1)
    anywhere = pl.BlockSpec(memory_space=pl.ANY)
    locals_count = 3 + 1 + units + down_units + 1
    count = len(vectors)
    order, length = filter_in[2].shape[0], filter_in[0].shape[1]
    remote_count = (
        3 * (pos_count - 1)
        + 4 * (pos_count - 1)
        + rz_count
        + 4 * 2 * rz_count
        + 2 * rz_count
        + 2 * 2 * 2 * pos_count
    )

    def kernel(*refs):
        head, refs = refs[:5], refs[5:]
        gather_kernel(dims, *head, refs[:count], refs[count : count + 4], *refs[count + 4 :])

    return pl.pallas_call(
        kernel,
        out_shape=(
            jax.ShapeDtypeStruct((pos_count, part_len, model_width), BF16),
            jax.ShapeDtypeStruct(
                (rz_count, 2, pos_count, own_width, 3 * model_width // pos_count), BF16
            ),
            jax.ShapeDtypeStruct((rz_count, units, own_width, tile), BF16),
            jax.ShapeDtypeStruct((pos_count, down_units, own_width, tile), BF16),
            jax.ShapeDtypeStruct((rz_count, 2, pos_count, own_width, model_width), BF16),
            jax.ShapeDtypeStruct((LINES, model_width), F32),
            jax.ShapeDtypeStruct((NORM_ROW, model_width // pos_count), F32),
            jax.ShapeDtypeStruct((rz_count, tile), F32),
            jax.ShapeDtypeStruct((6, order, length), F32),
        ),
        in_specs=[pl.BlockSpec(memory_space=pltpu.VMEM)] * (5 + count + 4),
        out_specs=(anywhere,) * 5 + (pl.BlockSpec(memory_space=pltpu.VMEM),) * 4,
        scratch_shapes=[
            pltpu.VMEM((LINES, 128), F32),
            pltpu.VMEM((rz_count, 2, pos_count, LINES, 128), BF16),
            pltpu.VMEM((FEATURES, order), F32),
            pltpu.SemaphoreType.DMA((locals_count,)),
            pltpu.SemaphoreType.DMA((remote_count,)),
            pltpu.SemaphoreType.DMA((remote_count,)),
        ],
        compiler_params=pltpu.CompilerParams(
            collective_id=1, has_side_effects=True, vmem_limit_bytes=VMEM_LIMIT
        ),
        cost_estimate=pl.CostEstimate(flops=10**6, bytes_accessed=10**7, transcendentals=0),
        name="gather",
    )(inputs, weight, up, down, out, *vectors, *filter_in)


class LineSum:
    def __init__(self, copies, name, count, z, chunk, sent, got):
        self.copies, self.name, self.count, self.z = copies, name, count, z
        self.chunk, self.sent, self.got_ref = chunk, sent, got

    def sides(self):
        last = self.count - 1
        return (
            (0, self.z, 1, {"rz": self.z + 1}, {"rz": self.z - 1}),
            (1, last - self.z, -1, {"rz": self.z - 1}, {"rz": self.z + 1}),
        )

    def step(self, step):
        count = self.count
        for side, place, direction, onward, back in self.sides():
            sends = (place < step) & (place + 1 < count)
            at = count - step + place
            at = jnp.clip(at if direction == 1 else count - 1 - at, 0, count - 1)
            target = self.sent.at[side, step - 1]

            def first(at=at, side=side):
                self.sent[side, step - 1] = self.chunk(at).astype(BF16)

            def later(at=at, side=side, back=back):
                self.copies.got((self.name, side, step - 1), self.got_ref.at[side, step - 2], back)
                self.sent[side, step - 1] = (
                    self.chunk(at) + self.got_ref[side, step - 2].astype(F32)
                ).astype(BF16)

            pl.when(sends & (place == 0))(first)
            if step > 1:
                pl.when(sends & (place > 0))(later)
            self.copies.send(
                (self.name, side, step), target, self.got_ref.at[side, step - 1], onward, sends
            )

    def total(self, result):
        last = self.count - 1
        result[...] = self.chunk(self.z)
        for side, place, _, _, back in self.sides():

            def add(side=side, back=back):
                self.copies.got((self.name, side, last), self.got_ref.at[side, last - 1], back)
                result[...] += self.got_ref[side, last - 1].astype(F32)

            pl.when(place > 0)(add)


class PieceSum:
    def __init__(self, copies, name, pos, orders, piece, got):
        self.copies, self.name, self.pos, self.orders = copies, name, pos, orders
        self.piece, self.got_ref = piece, got

    def masks(self, side, stage):
        order = self.orders[side]
        found = [0]
        for bit in order[stage:]:
            found += [mask ^ bit for mask in found]
        return [mask for mask in found if mask & order[stage]]

    def device(self, side, stage):
        return {"pos": jnp.bitwise_xor(self.pos, self.orders[side][stage])}

    def send(self, side, stage, mask):
        self.copies.send(
            (self.name, side, mask),
            self.piece(side, mask),
            self.got_ref(side, mask),
            self.device(side, stage),
        )

    def got(self, side, stage, mask):
        self.copies.got(
            (self.name, side, mask), self.got_ref(side, mask), self.device(side, stage)
        )

    def add(self, side, stage, mask):
        target = self.piece(side, mask ^ self.orders[side][stage])
        target[...] = (
            target[...].astype(F32) + self.got_ref(side, mask)[...].astype(F32)
        ).astype(BF16)

    def settle(self, stage):
        for side in range(2):
            onward = self.masks(side, stage + 1) if stage + 1 < len(self.orders[side]) else []
            masks = self.masks(side, stage)
            bit = self.orders[side][stage]
            for mask in sorted(masks, key=lambda mask: (mask ^ bit) not in onward):
                self.got(side, stage, mask)
                self.add(side, stage, mask)
                if mask ^ bit in onward:
                    self.send(side, stage + 1, mask ^ bit)


class ChunkSum(PieceSum):
    def send_chunk(self, side, stage, mask, place):
        self.copies.send(
            (self.name, side, mask, place),
            self.piece(side, mask, place),
            self.got_ref(side, mask, place),
            self.device(side, stage),
        )

    def settle_chunk(self, side, stage, place):
        bit = self.orders[side][stage]
        onward = self.masks(side, stage + 1) if stage + 1 < len(self.orders[side]) else []
        for mask in sorted(self.masks(side, stage), key=lambda mask: (mask ^ bit) not in onward):
            got = self.got_ref(side, mask, place)
            self.copies.got((self.name, side, mask, place), got, self.device(side, stage))
            target = self.piece(side, mask ^ bit, place)
            target[...] = (target[...].astype(F32) + got[...].astype(F32)).astype(BF16)
            if mask ^ bit in onward:
                self.send_chunk(side, stage + 1, mask ^ bit, place)


def last_sums_kernel(
    dims,
    kept,
    row_in,
    proj_grad,
    weight_in,
    lines,
    grad_residual,
    token_lines,
    chan_sums,
    filt_grad,
    layers,
    mine,
    embedding,
    w_two,
    filter_columns,
    *rest,
):
    rz_count, pos_count = dims
    norm = lines.at[pl.ds(NORM_ROW, 8)]
    count = 2 * len(kept[0])
    own_pieces, moved_pieces, rest = rest[:count], rest[count : 2 * count], rest[2 * count :]
    down_moved, rest = rest[:count], rest[count:]
    input_grad, in_grad, up_grad, down_grad, out_grad, lines_out, inner_out = rest[:7]
    rest = rest[7:]
    (
        rows_v,
        proj_v,
        pieces_v,
        moved_v,
        pieces_got,
        bundle_sent,
        bundle_got,
        bundle_total,
        up_sent,
        up_got,
        e_v,
        e_got,
        in_total,
        in_sent,
        in_got,
        in_line_sent,
        in_line_got,
        in_mine,
        in_out,
        in_back,
        packed,
        packed_got,
        packed_pos,
        packed_total,
        inner,
        local_sems,
        send_sems,
        got_sems,
    ) = rest
    z, core, pos = lax.axis_index("rz"), lax.axis_index("core"), lax.axis_index("pos")
    rows_count = 2 * rz_count
    row = z * 2 + core
    bits = bits_of(pos_count)
    orders = (bits, bits[::-1])
    middle = rz_count // 2
    part_len, model_width = grad_residual.shape
    half = model_width // 2
    own_width, tile = up_sent.shape[1:]
    width = weight_in.shape[1]
    chan = width // 3
    columns = model_width // tile
    copies = Copies(local_sems, send_sems, got_sems)
    other = {"core": 1 - core}

    def row_device(at):
        return {"rz": at // 2, "core": at % 2}

    later = [[mask for mask in kept[side] if len(bits) > 1 and mask & orders[side][1]] for side in range(2)]
    loads = {}
    for first in (True, False):
        for side in range(2):
            for mask in kept[side]:
                if (mask in later[side]) == first:
                    slot = kept[side].index(mask)
                    at, part = 2 * slot + side, pl.ds(side * middle, middle)
                    early, downs = down_moved[at].shape[:2]
                    ups = 2 * rz_count
                    outs = pieces_v.shape[2] - ups - downs
                    group = [copies.local(own_pieces[at], pieces_v.at[slot, part])]
                    for chunk in range(middle):
                        target = moved_v.at[slot, side * middle + chunk]
                        source, low = moved_pieces[at], chunk * (ups + outs)
                        if chunk < early:
                            down = down_moved[at].at[chunk]
                        else:
                            down_low = middle * (ups + outs) + (chunk - early) * downs
                            down = source.at[pl.ds(down_low, downs)]
                        group += [
                            copies.local(source.at[pl.ds(low, ups)], target.at[pl.ds(0, ups)]),
                            copies.local(down, target.at[pl.ds(ups, downs)]),
                            copies.local(
                                source.at[pl.ds(low + ups, outs)],
                                target.at[pl.ds(ups + downs, outs)],
                            ),
                        ]
                    loads[side, mask] = group
    masks = sorted(range(pos_count), key=lambda mask: -bin(mask).count("1"))
    slots = rows_v.shape[0]

    def load_rows(at):
        start = jnp.bitwise_xor(pos, masks[at]) * part_len
        block = pl.ds(pl.multiple_of(start, part_len), part_len)
        return (
            copies.local(row_in.at[block], rows_v.at[at % slots]),
            copies.local(proj_grad.at[block], proj_v.at[at % slots]),
        )

    row_loads = [load_rows(at) for at in range(slots)]
    greet(
        [row_device((row + step) % rows_count) for step in range(1, rows_count)]
        + [{"pos": jnp.bitwise_xor(pos, mask)} for mask in range(1, pos_count)]
    )

    bundle = ChunkSum(
        copies,
        "bundle",
        pos,
        orders,
        lambda side, mask, place: pieces_v.at[kept[side].index(mask), place],
        lambda side, mask, place: pieces_got.at[kept[side].index(mask) - 1, place],
    )
    for side, mask in loads:
        slot = kept[side].index(mask)
        for copy in loads[side, mask]:
            copy.wait()
        for at in range(middle):
            place = side * middle + (at if side == 0 else middle - 1 - at)
            pieces_v[slot, place] = (
                pieces_v[slot, place].astype(F32) + moved_v[slot, place].astype(F32)
            ).astype(BF16)
            if mask in later[side]:
                bundle.send_chunk(side, 1, mask, place)

    e_sums = PieceSum(
        copies,
        "rows",
        pos,
        orders,
        lambda side, mask: e_v.at[side, mask],
        lambda side, mask: e_got.at[side, mask - 1],
    )
    in_total[...] = jnp.zeros_like(in_total)
    packed_total[...] = jnp.zeros_like(packed_total)
    packed[...] = jnp.zeros_like(packed)
    sums = (jnp.zeros((1, model_width), F32), jnp.zeros((1, model_width), F32))
    for index, mask in enumerate(masks):
        if 1 <= index <= pos_count - slots:
            row_loads.append(load_rows(slots + index - 1))
        for copy in row_loads[index]:
            copy.wait()

        def tile_step(at, sums, mask=mask, slot=index % slots):
            rows = pl.ds(pl.multiple_of(at * BLOCK, BLOCK), BLOCK)
            unit, _ = norm_parts(rows_v[slot, rows].astype(F32))
            normed = (unit * norm[0:1, :] + norm[1:2, :]).astype(BF16)
            grad = proj_v[slot, rows]
            cotangent = lax.dot_general(
                grad, weight_in[...], (((1,), (1,)), ((), ())), preferred_element_type=F32
            )
            e_v[0, mask, rows] = cotangent[:, :half].astype(BF16)
            e_v[1, mask, rows] = cotangent[:, half:].astype(BF16)
            in_total[...] += lax.dot_general(
                normed, grad, (((0,), (0,)), ((), ())), preferred_element_type=F32
            )
            return (
                sums[0] + jnp.sum(cotangent * unit, axis=0, keepdims=True),
                sums[1] + jnp.sum(cotangent, axis=0, keepdims=True),
            )

        sums = lax.fori_loop(0, part_len // BLOCK, tile_step, sums)
        for side in range(2):
            if mask in e_sums.masks(side, 0):
                e_sums.send(side, 0, mask)

    block_rows = pos_count * own_width
    for at in range(rz_count):
        rows = pl.ds(pl.multiple_of((2 * at + 1 - core) * block_rows, block_rows), block_rows)
        in_sent[at] = in_total[rows, :].astype(BF16)
    copies.send(("in core",), in_sent, in_got, other)

    groups = model_width // 128
    per = rows_count // groups
    token_rows, chan_rows = token_lines.shape[0], mine.shape[0]
    inner_rows = inner.shape[0] // groups
    line_rows = token_rows + chan_rows
    three_grad = filter_back(
        filt_grad, layers, mine[THREE_ROW:NORM_ROW, :], embedding, w_two, filter_columns, inner
    )
    for at in range(groups):
        lanes = pl.ds(at * 128, 128)
        packed[at, 0:token_rows] = token_lines[:, lanes]
        packed[at, 0:1] = sums[0][:, at * 128 : (at + 1) * 128]
        packed[at, 1:2] = sums[1][:, at * 128 : (at + 1) * 128]
        packed[at, line_rows:] = inner[pl.ds(at * inner_rows, inner_rows), :]
    for at in range(chan // 128):
        group, lanes = pos * (chan // 128) + at, pl.ds(at * 128, 128)
        packed[group, token_rows : token_rows + THREE_ROW] = chan_sums[:, lanes]
        packed[group, token_rows + THREE_ROW : line_rows] = three_grad[
            :, at * 128 : (at + 1) * 128
        ]

    def owns(at):
        return None if per == 1 else at % per == 0

    def when(condition, action):
        if condition is None:
            action()
        else:
            pl.when(condition)(action)

    for step in range(1, rows_count):
        to = (row + step) % rows_count
        copies.send(
            ("lines", step), packed.at[to // per], packed_got.at[step], row_device(to), owns(to)
        )

    bundle_line = LineSum(
        copies,
        "bundle line",
        rz_count,
        z,
        lambda at: pieces_v[kept[0].index(0), at].astype(F32),
        bundle_sent,
        bundle_got,
    )
    for at in range(middle):
        for stage in range(1, len(bits)):
            bundle.settle_chunk(0, stage, at)
            bundle.settle_chunk(1, stage, rz_count - 1 - at)
        if at == 0:
            bundle_line.step(1)
    copies.got(("in core",), in_got, other)

    def in_chunk(at):
        rows = pl.ds(pl.multiple_of((2 * at + core) * block_rows, block_rows), block_rows)
        return in_total[rows, :] + in_got[at].astype(F32)

    in_line = LineSum(copies, "in line", rz_count, z, in_chunk, in_line_sent, in_line_got)
    in_line.step(1)

    def add_lines():
        packed_total[...] = packed[row // per]
        for step in range(1, rows_count):
            copies.got(("lines", step), packed_got.at[step], row_device((row - step) % rows_count))
            packed_total[...] += packed_got[step]
        packed_pos[pos] = packed_total[...]

    when(owns(row), add_lines)
    for mask in range(1, pos_count):
        copies.send(
            ("lines pos", mask),
            packed_total,
            packed_pos.at[pos],
            {"pos": jnp.bitwise_xor(pos, mask)},
            owns(row),
        )
    for step in range(2, rz_count):
        bundle_line.step(step)
        in_line.step(step)
    e_sums.settle(0)

    def sum_lines():
        for mask in range(1, pos_count):
            owner = jnp.bitwise_xor(pos, mask)
            copies.got(("lines pos", mask), packed_pos.at[owner], {"pos": owner})
        total = packed_pos[0]
        for at in range(1, pos_count):
            total = total + packed_pos[at]
        lines_out[...] = total[:line_rows]
        inner_out[row // per] = total[line_rows:]

    when(owns(row), sum_lines)
    for step in range(1, rows_count):
        to = (row + step) % rows_count
        block = inner_out.at[row // per]
        copies.send(("inner", step), block, block, row_device(to), owns(row))
        if step < per:
            copies.send(
                ("lines row", step),
                lines_out,
                lines_out,
                row_device(to),
                owns(row),
            )

    in_line.total(in_mine)
    for mask in range(1, pos_count):
        owner = jnp.bitwise_xor(pos, mask)
        rows = pl.ds(pl.multiple_of(owner * own_width, own_width), own_width)
        in_out[mask] = in_mine[rows, :].astype(BF16)
        copies.send(("in pos", mask), in_out.at[mask], in_back.at[mask], {"pos": owner})
    mine = in_mine[pl.ds(pl.multiple_of(pos * own_width, own_width), own_width), :]
    cols = pl.ds(pl.multiple_of(pos * chan, chan), chan)
    for at in range(3):
        in_grad[at, :, cols] = mine[:, at * chan : (at + 1) * chan]

    bundle_line.total(bundle_total)
    up_sent[...] = bundle_total[
        pl.ds(pl.multiple_of((1 - core) * rz_count, rz_count), rz_count)
    ].astype(BF16)
    copies.send(("up core",), up_sent, up_got, other)
    down_units = (bundle_total.shape[0] - 2 * rz_count - columns) // columns
    for col in range(columns):
        out_grad[:, col * tile : (col + 1) * tile] = bundle_total[
            2 * rz_count + columns * down_units + col
        ]
        for at in range(down_units):
            down_grad[at * own_width : (at + 1) * own_width, col * tile : (col + 1) * tile] = (
                bundle_total[2 * rz_count + col * down_units + at]
            )
    for at in range(rz_count):
        cols = pl.ds(pl.multiple_of((2 * at + core) * tile, tile), tile)
        up_grad[:, cols] = bundle_total[core * rz_count + at]
    for stage in range(1, len(bits)):
        e_sums.settle(stage)
    def input_step(at, _):
        rows = pl.ds(pl.multiple_of(at * BLOCK, BLOCK), BLOCK)
        unit, scale = norm_parts(rows_v[(pos_count - 1) % slots, rows].astype(F32))
        cotangent = jnp.concatenate(
            [e_v[0, 0, rows].astype(F32), e_v[1, 0, rows].astype(F32)], axis=1
        )
        scaled = cotangent * norm[0:1, :]
        grad = scale * (
            scaled
            - jnp.mean(scaled, axis=-1, keepdims=True)
            - unit * jnp.mean(scaled * unit, axis=-1, keepdims=True)
        )
        input_grad[rows, :] = (grad_residual[rows, :] + grad).astype(BF16)
        return 0

    lax.fori_loop(0, part_len // BLOCK, input_step, 0)

    for mask in range(1, pos_count):
        owner = jnp.bitwise_xor(pos, mask)
        copies.got(("in pos", mask), in_back.at[mask], {"pos": owner})
        cols = pl.ds(pl.multiple_of(owner * chan, chan), chan)
        for at in range(3):
            in_grad[at, :, cols] = in_back[mask, :, at * chan : (at + 1) * chan].astype(F32)
    copies.got(("up core",), up_got, other)
    for at in range(rz_count):
        cols = pl.ds(pl.multiple_of((2 * at + 1 - core) * tile, tile), tile)
        up_grad[:, cols] = up_got[at].astype(F32)
    for step in range(1, rows_count):
        origin = (row - step) % rows_count

        def take(step=step, origin=origin):
            copies.got(("inner", step), inner_out.at[origin // per], row_device(origin))

        when(owns(origin), take)
        if step < per:

            def take_lines(step=step, origin=origin):
                copies.got(("lines row", step), lines_out, row_device(origin))

            when(origin == row // per * per, take_lines)
    copies.finish()


def filter_back(filt_grad, layers, three, embedding, w_two, columns, inner):
    frequency = columns[:, 2:3]
    three_grad = exact(layers[1], filt_grad[...], ((1,), (0,)))
    grad = exact(three, filt_grad[...], ((1,), (1,))) * layers[5]
    freq_grad = jnp.sum(grad * layers[3], axis=1, keepdims=True)
    grad = grad * frequency
    bias_two = jnp.sum(grad, axis=1, keepdims=True)
    order = grad.shape[0]
    inner[...] = jnp.zeros_like(inner)
    inner[FEATURES : FEATURES + order, :order] = exact(layers[0], grad, ((1,), (1,)))
    grad = exact(w_two[...].astype(F32), grad, ((1,), (0,))) * layers[4]
    freq_grad += jnp.sum(grad * layers[2], axis=1, keepdims=True)
    grad = grad * frequency
    bias_one = jnp.sum(grad, axis=1, keepdims=True)
    inner[:FEATURES, :order] = exact(embedding[...], grad, ((1,), (1,)))
    held = inner[:order, :]
    lane = lax.broadcasted_iota(jnp.int32, held.shape, 1)
    for at, value in enumerate((bias_one, bias_two, freq_grad)):
        held = jnp.where(lane == order + at, value, held)
    inner[:order, :] = held
    return three_grad


def finish_kernel(place, total, shared, *outs):
    own_width = outs[0].shape[1]
    moved = pltpu.roll(total[...], 128 - place[0], 1)[:, :own_width]
    (
        pre_gain,
        pre_bias,
        out_bias,
        post_gain,
        post_bias,
        down_bias,
        short_weight,
        short_bias,
        in_bias,
        skip,
        three,
        up_bias,
        w_one,
        b_one,
        w_two,
        b_two,
        frequency,
    ) = outs
    for at, out in enumerate((pre_gain, pre_bias, out_bias, post_gain, post_bias, down_bias)):
        out[...] = moved[at : at + 1]
    for at in range(3):
        short_weight[at] = moved[16 + 3 * at : 19 + 3 * at]
    short_bias[...] = moved[25:28]
    in_bias[...] = moved[28:31]
    skip[...] = moved[31:32]
    three[...] = moved[32:96]
    rows = pltpu.roll(total[0:16, :], 128 - place[2], 1)[:, : up_bias.shape[1]]
    line = lax.broadcasted_iota(jnp.int32, rows.shape, 0)
    up_bias[...] = jnp.sum(jnp.where(line == 6 + place[1], rows, 0.0), axis=0, keepdims=True)
    inner = shared[...].reshape(-1, 128)
    order = w_two.shape[0]
    w_one[...] = inner[: w_one.shape[0], :order]
    w_two[...] = inner[FEATURES : FEATURES + order, :order]
    turned = inner[:128, :].T
    b_one[...] = turned[order : order + 1, :order]
    b_two[...] = turned[order + 1 : order + 2, :order]
    frequency[...] = turned[order + 2 : order + 3, :order]


def finish(place, total, shared, own_width, ff_own, features, order):
    shapes = [(1, own_width)] * 6
    shapes += [(3, 3, own_width), (3, own_width), (3, own_width), (1, own_width)]
    shapes += [(order, own_width), (1, ff_own), (features, order), (1, order), (order, order)]
    shapes += [(1, order), (1, order)]
    inside = pl.BlockSpec(memory_space=pltpu.VMEM)
    return pl.pallas_call(
        finish_kernel,
        out_shape=[jax.ShapeDtypeStruct(shape, F32) for shape in shapes],
        in_specs=[pl.BlockSpec(memory_space=pltpu.SMEM), inside, inside],
        out_specs=[inside] * len(shapes),
        name="finish",
    )(place, total, shared)


def last_sums(
    dims,
    kept,
    row_in,
    proj_grad,
    weight_in,
    lines,
    grad_residual,
    token_lines,
    chan_sums,
    filt_grad,
    layers,
    mine,
    embedding,
    w_two,
    filter_columns,
    own_pieces,
    moved_pieces,
    down_moved,
):
    rz_count, pos_count = dims
    part_len, model_width = grad_residual.shape
    piece = own_pieces[0].shape
    units, own_width, tile = piece[1:]
    width = weight_in.shape[1]
    block_rows = pos_count * own_width
    groups = model_width // 128
    line_rows = token_lines.shape[0] + mine.shape[0]
    inner_rows = 2 * FEATURES // groups
    slots = len(kept[0])
    steps = rz_count - 1
    rows_count = 2 * rz_count
    ff_own = (units - 2 * rz_count - model_width // tile) * own_width * tile // model_width
    anywhere = pl.BlockSpec(memory_space=pl.ANY)
    inside = pl.BlockSpec(memory_space=pltpu.VMEM)
    local_count = 2 * len(kept[0]) * (1 + 3 * (rz_count // 2)) + 2 * pos_count
    remote_count = (
        2 * pos_count * (1 + rz_count) + 2 * 2 * steps + 2 + 3 * rows_count + 3 * pos_count
    )
    half = model_width // 2
    vmem = pltpu.VMEM
    return pl.pallas_call(
        functools.partial(last_sums_kernel, dims, kept),
        out_shape=(
            jax.ShapeDtypeStruct((part_len, model_width), BF16),
            jax.ShapeDtypeStruct((3, own_width, model_width), F32),
            jax.ShapeDtypeStruct((own_width, 2 * rz_count * tile), F32),
            jax.ShapeDtypeStruct((ff_own, model_width), F32),
            jax.ShapeDtypeStruct((own_width, model_width), F32),
            jax.ShapeDtypeStruct((line_rows, 128), F32),
            jax.ShapeDtypeStruct((groups, inner_rows, 128), F32),
        ),
        in_specs=[anywhere, anywhere] + [inside] * 11 + [anywhere] * (3 * len(own_pieces)),
        out_specs=(inside,) * 7,
        scratch_shapes=[
            vmem((pos_count - 1, part_len, model_width), BF16),
            vmem((pos_count - 1, part_len, width), BF16),
            vmem((slots, rz_count, units, own_width, tile), BF16),
            vmem((slots, rz_count, units, own_width, tile), BF16),
            vmem((slots - 1, rz_count, units, own_width, tile), BF16),
            vmem((2, steps, units, own_width, tile), BF16),
            vmem((2, steps, units, own_width, tile), BF16),
            vmem((units, own_width, tile), F32),
            vmem((rz_count, own_width, tile), BF16),
            vmem((rz_count, own_width, tile), BF16),
            vmem((2, pos_count, part_len, half), BF16),
            vmem((2, pos_count - 1, part_len, half), BF16),
            vmem((model_width, width), F32),
            vmem((rz_count, block_rows, width), BF16),
            vmem((rz_count, block_rows, width), BF16),
            vmem((2, steps, block_rows, width), BF16),
            vmem((2, steps, block_rows, width), BF16),
            vmem((block_rows, width), F32),
            vmem((pos_count, own_width, width), BF16),
            vmem((pos_count, own_width, width), BF16),
            vmem((groups, line_rows + inner_rows, 128), F32),
            vmem((rows_count, line_rows + inner_rows, 128), F32),
            vmem((pos_count, line_rows + inner_rows, 128), F32),
            vmem((line_rows + inner_rows, 128), F32),
            vmem((2 * FEATURES, 128), F32),
            pltpu.SemaphoreType.DMA((local_count,)),
            pltpu.SemaphoreType.DMA((remote_count,)),
            pltpu.SemaphoreType.DMA((remote_count,)),
        ],
        compiler_params=pltpu.CompilerParams(
            collective_id=0, has_side_effects=True, vmem_limit_bytes=VMEM_LIMIT
        ),
        cost_estimate=pl.CostEstimate(flops=10**7, bytes_accessed=10**7, transcendentals=0),
        name="last_sums",
    )(
        row_in,
        proj_grad,
        weight_in,
        lines,
        grad_residual,
        token_lines,
        chan_sums,
        filt_grad,
        layers,
        mine,
        embedding,
        w_two,
        filter_columns,
        *own_pieces,
        *moved_pieces,
        *down_moved,
    )


def bits_of(count):
    return [1 << at for at in range(count.bit_length() - 1)]


def on_device(
    activations,
    out_grad,
    doc_bounds,
    doc_ids,
    pre_gain,
    pre_bias,
    in_weight,
    in_bias,
    short_weight,
    short_bias,
    skip_gain,
    out_weight,
    out_bias,
    post_gain,
    post_bias,
    up_weight,
    up_bias,
    down_weight,
    down_bias,
    filter_one,
    filter_bias_one,
    filter_two,
    filter_bias_two,
    filter_freq,
    filter_three,
):
    rz_count, pos_count = lax.axis_size("rz"), lax.axis_size("pos")
    pos, core = lax.axis_index("pos"), lax.axis_index("core")
    everything = ("rz", "core", "pos")
    owners = rz_count * 2 * pos_count
    own_at = (lax.axis_index("rz") * 2 + core) * pos_count + pos
    part_len, model_width = activations.shape[1:]
    length = part_len * pos_count
    own_width = pre_gain.shape[0]
    chan = model_width // pos_count
    ff_own = down_weight.shape[0]
    ff_half = rz_count * pos_count * ff_own
    docs = doc_bounds.shape[1]
    order = filter_two.shape[0]
    tables = transform_tables()
    meta = unit_table(doc_bounds[0], length, (pos * chan).astype(jnp.int32))

    single = functools.partial(jnp.reshape, shape=(1, -1))
    vectors = [
        short_weight,
        short_bias,
        single(skip_gain),
        in_bias,
        filter_three,
        single(pre_gain),
        single(pre_bias),
        single(out_bias),
        single(post_gain),
        single(post_bias),
        single(down_bias),
        single(up_bias),
    ]
    filter_columns = jnp.stack([filter_bias_one, filter_bias_two, filter_freq], 1).astype(F32)
    embedding = positions_table(length, filter_one.shape[0])
    row_in, weight_in, bundle, extra, out_all, lines, mine, up_bias_half, layers = gather(
        (rz_count, pos_count),
        activations[0],
        in_weight.transpose(1, 0, 2),
        up_weight,
        down_weight,
        out_weight,
        vectors,
        (embedding, filter_one, filter_two, filter_columns),
    )
    row_in = row_in.reshape(length, model_width)
    weight_in = weight_in.reshape(model_width, -1)
    out_all = out_all.reshape(model_width, model_width)
    tile = pos_count * ff_own
    columns = model_width // tile
    bits = bits_of(pos_count)
    orders = (bits, bits[::-1])
    place = jnp.stack([pos, lax.axis_index("rz")]).astype(jnp.int32)

    own_in = activations[0]
    projected = project(row_in, lines, weight_in, mine)
    sides = [{0: bundle[: rz_count // 2]}, {0: bundle[rz_count // 2 :]}]
    firsts = [[swap(sides[side][0], "pos", bit) for bit in bits] for side in range(2)]

    def along(values, distance):
        ups = [(at, at + 1) for at in range(distance - 1, rz_count - 1)]
        downs = [(at + 1, at) for at in range(rz_count - distance)]
        return [lax.ppermute(values[0], "rz", ups), lax.ppermute(values[1], "rz", downs)]

    moved = [along([extra, extra], 1)]
    projected, moved = lax.optimization_barrier((projected, moved))
    for distance in range(2, rz_count - 1):
        moved.append(along(moved[-1], distance))
    branch, mixed = mixer_forward(meta, docs, projected, layers, mine, model_width, tables)
    branch, firsts, moved = lax.optimization_barrier((branch, firsts, moved))
    extras = [extra] + [pair[0] for pair in moved] + [pair[1] for pair in moved]
    given = [0] + bits
    pieces = [
        sides[side][0] if bit == 0 else firsts[side][bits.index(bit)]
        for bit in given
        for side in range(2)
    ]
    result, grad_residual, branch_grad, token_lines, *rest = middle(
        (rz_count, pos_count),
        given,
        branch,
        activations[0],
        out_all,
        lines,
        out_grad[0],
        up_bias_half,
        pieces,
        extras,
    )
    result = result[None]

    masks = list(range(pos_count))
    piece_grads, down_moved = rest[: 2 * pos_count], rest[2 * pos_count :]
    kept = kept_masks(orders)
    by_mask = {
        (side, mask): piece_grads[2 * at + side]
        for at, mask in enumerate(masks)
        for side in range(2)
    }
    own_pieces = [by_mask[side, kept[side][at]] for at in range(len(kept[0])) for side in range(2)]
    moved_pieces = [
        swap(by_mask[side, kept[side][at] ^ orders[side][0]], "pos", orders[side][0])
        for at in range(len(kept[0]))
        for side in range(2)
    ]

    proj_grad, filt_grad, chan_sums = mixer_backward(
        meta, docs, projected, layers, mine, model_width, tables, mixed, branch_grad
    )
    input_grad, weight_in_grad, up_weight_grad, down_weight_grad, out_weight_grad, total, shared = (
        last_sums(
            (rz_count, pos_count),
            kept,
            row_in,
            proj_grad,
            weight_in,
            lines,
            grad_residual,
            token_lines,
            chan_sums,
            filt_grad,
            layers,
            mine,
            embedding,
            filter_two,
            filter_columns,
            own_pieces,
            moved_pieces,
            down_moved,
        )
    )
    input_grad = input_grad[None]
    weight_in_grad = weight_in_grad.transpose(1, 0, 2)
    lane = lax.rem(own_at * own_width, 128)
    up_place = lax.rem(own_at * ff_own, owners * ff_own * 128 // model_width)
    place = jnp.stack([lane, up_place // 128, up_place % 128]).astype(jnp.int32)
    (
        pre_gain_grad,
        pre_bias_grad,
        out_bias_grad,
        post_gain_grad,
        post_bias_grad,
        down_bias_grad,
        short_weight_grad,
        short_bias_grad,
        in_bias_grad,
        skip_grad,
        three_grad,
        up_bias_grad,
        one_grad,
        bias_one_grad,
        two_grad,
        bias_two_grad,
        freq_grad,
    ) = finish(place, total, shared, own_width, ff_own, filter_one.shape[0], order)
    return (
        result,
        input_grad,
        pre_gain_grad[0],
        pre_bias_grad[0],
        weight_in_grad,
        in_bias_grad,
        short_weight_grad,
        short_bias_grad,
        skip_grad[0],
        out_weight_grad,
        out_bias_grad[0],
        post_gain_grad[0],
        post_bias_grad[0],
        up_weight_grad,
        up_bias_grad[0],
        down_weight_grad,
        down_bias_grad[0],
        one_grad,
        bias_one_grad[0],
        two_grad,
        bias_two_grad[0],
        freq_grad[0],
        three_grad,
    )


def solution(mesh):
    rows_count, pos_count = mesh.devices.shape
    fine = Mesh(mesh.devices.reshape(rows_count // 2, 2, pos_count), ("rz", "core", "pos"))
    rows = ("rz", "core")
    every = ("rz", "core", "pos")
    tokens = P(rows, "pos", None)
    vector = P(every)
    matrix = P(every, None)
    return jax.shard_map(
        on_device,
        mesh=fine,
        in_specs=(
            tokens,
            tokens,
            P(rows, None),
            P(rows, None),
            vector,
            vector,
            P(every, None, None),
            P(None, every),
            P(None, None, every),
            P(None, every),
            vector,
            matrix,
            vector,
            vector,
            vector,
            matrix,
            vector,
            matrix,
            vector,
            P(),
            P(),
            P(),
            P(),
            P(),
            P(None, every),
        ),
        out_specs=(
            tokens,
            tokens,
            vector,
            vector,
            P(every, None, None),
            P(None, every),
            P(None, None, every),
            P(None, every),
            vector,
            matrix,
            vector,
            vector,
            vector,
            matrix,
            vector,
            matrix,
            vector,
            P(),
            P(),
            P(),
            P(),
            P(),
            P(None, every),
        ),
        check_vma=False,
    )
```
